128 devices in a mesh: grp: 2 (over z_hi), ch: 64 (over y, x, z_lo, core).
Axes of the slice: x: 4, y: 4, z: 4 (z_hi: 2, z_lo: 2; z = z_hi * 2 + z_lo), core: 2. Of those that a mesh axis runs over, the one named last changes fastest.
Arguments:
- hidden: bfloat16 [65536, 768], P(('grp', 'ch')), may hold values from -6 to 6
- cotangent: bfloat16 [65536, 768], P(('grp', 'ch')), may hold values from -6 to 6
- lengths: int32 [128], replicated, may hold values from 259 to 512, as said below
- split_at: int32 [128], replicated, may hold values from 1 to 510, as said below
- seg_table: float32 [2, 768], replicated, may hold values from -3 to 3
- w_query: bfloat16 [2, 768, 384], replicated, may hold values from -0.21875 to 0.21875
- b_query: float32 [2, 384], replicated, may hold values from -3 to 3
- w_key: bfloat16 [2, 768, 384], replicated, may hold values from -0.21875 to 0.21875
- w_value: bfloat16 [2, 768, 384], replicated, may hold values from -0.21875 to 0.21875
- b_value: float32 [2, 384], replicated, may hold values from -3 to 3
- w_depth: bfloat16 [2, 9, 768], replicated, may hold values from -2 to 2
- w_point: bfloat16 [2, 768, 384], replicated, may hold values from -0.21875 to 0.21875
- b_keyconv: float32 [2, 384], replicated, may hold values from -3 to 3
- w_kernel: bfloat16 [2, 384, 54], replicated, may hold values from -0.3125 to 0.3125
- b_kernel: float32 [2, 54], replicated, may hold values from -4 to 4
- w_conv: bfloat16 [2, 768, 384], replicated, may hold values from -0.21875 to 0.21875
- b_conv: float32 [2, 384], replicated, may hold values from -3 to 3
- w_out: bfloat16 [2, 768, 768], replicated, may hold values from -0.875 to 0.875
- b_out: float32 [2, 768], replicated, may hold values from -2 to 2
- first_gain: float32 [2, 768], replicated, may hold values from 0.25 to 1.75
- first_shift: float32 [2, 768], replicated, may hold values from -2 to 2
- w_up: bfloat16 [2, 2, 384, 1536], P(None, 'grp', None, 'ch'), may hold values from -0.3125 to 0.3125
- b_up: bfloat16 [2, 2, 1536], P(None, 'grp', 'ch'), may hold values from -3 to 3
- down_weight: bfloat16 [2, 2, 1536, 384], P(None, 'grp', 'ch'), may hold values from -0.15625 to 0.15625
- b_down: float32 [2, 768], replicated, may hold values from -2 to 2
- second_gain: float32 [2, 768], replicated, may hold values from 0.25 to 1.75
- second_shift: float32 [2, 768], replicated, may hold values from -2 to 2
Outputs:
- output: float32 [65536, 768], P(('grp', 'ch'))
- input_grad: float32 [65536, 768], P(('grp', 'ch'))
- grad_seg_table: float32 [2, 768], replicated
- grad_w_query: float32 [2, 768, 384], replicated
- grad_b_query: float32 [2, 384], replicated
- grad_w_key: float32 [2, 768, 384], replicated
- grad_w_value: float32 [2, 768, 384], replicated
- grad_b_value: float32 [2, 384], replicated
- grad_w_depth: float32 [2, 9, 768], replicated
- grad_w_point: float32 [2, 768, 384], replicated
- grad_b_keyconv: float32 [2, 384], replicated
- grad_w_kernel: float32 [2, 384, 54], replicated
- grad_b_kernel: float32 [2, 54], replicated
- grad_w_conv: float32 [2, 768, 384], replicated
- grad_b_conv: float32 [2, 384], replicated
- grad_w_out: float32 [2, 768, 768], replicated
- grad_b_out: float32 [2, 768], replicated
- grad_first_gain: float32 [2, 768], replicated
- grad_first_shift: float32 [2, 768], replicated
- grad_w_up: float32 [2, 2, 384, 1536], P(None, 'grp', None, 'ch')
- grad_b_up: float32 [2, 2, 1536], P(None, 'grp', 'ch')
- grad_w_down: float32 [2, 2, 1536, 384], P(None, 'grp', 'ch')
- grad_b_down: float32 [2, 768], replicated
- grad_second_gain: float32 [2, 768], replicated
- grad_second_shift: float32 [2, 768], replicated
The draws below stay inside these ranges and needn't reach their ends.
Inputs may be any that keep to these rules, and one draw needn't show every extreme that they name: `lengths`: one row in every draw has exactly 512 live positions and another exactly 259. `split_at`: lies between 1 and the row's length minus 2.
All inputs are finite; a program needn't handle non-finite values.
Results may differ from the reference program's by a relative error of at most 0.025.
Values may be sent and summed in bfloat16 or wider, within the bound.
A program may use at most 320 MiB of HBM per device.

```python
import math
import jax
import jax.numpy as jnp
from jax import lax

D = 768
HEADS = 6
HEAD = 64
KERNEL = 9
FF = 3072
GROUPS = 2
LAYERS = 2
LEN = 512
TOKENS = 65536
SEQS = 128


def draw_rows(key):
    drawn = jax.random.randint(jax.random.fold_in(key, 21), (SEQS,), LEN // 2 + 3, LEN + 1)
    longest = jax.random.randint(jax.random.fold_in(key, 22), (), 0, SEQS)
    shortest = (longest + 1 + jax.random.randint(jax.random.fold_in(key, 23), (), 0, SEQS - 1)) % SEQS
    drawn = drawn.at[shortest].set(LEN // 2 + 3)
    drawn = drawn.at[longest].set(LEN)
    return drawn.astype(jnp.int32)


def draw_lengths(key, part):
    return draw_rows(key)


def draw_split_at(key, part):
    row_lengths = draw_rows(key)
    key = jax.random.fold_in(key, 5)
    return jax.random.randint(key, (SEQS,), 1, row_lengths - 1).astype(jnp.int32)


def steps_of(key, extent, cuts, smallest, largest):
    def one(position, blocks):
        heights = jax.random.uniform(jax.random.fold_in(jax.random.fold_in(key, 6), position), (blocks,), jnp.float32, smallest / len(cuts), largest / len(cuts))
        return jnp.repeat(jnp.exp(heights), extent[position] // blocks).reshape((-1,) + (1,) * (len(extent) - position - 1))

    gain = one(*cuts[0])
    for cut in cuts[1:]:
        gain = gain * one(*cut)
    return gain


def scatter_about(key, extent, scale, reach, shards=(), kind=jnp.bfloat16):
    array = scale * jax.random.normal(key, extent, jnp.float32)
    if shards:
        array = array * steps_of(key, extent, shards, -0.22, 0.18)
    return jnp.clip(array, -reach, reach).astype(kind)


def setup_inputs(seed: int = 0) -> dict:
    splits = jax.random.split(jax.random.key(seed), 28)
    hidden = scatter_about(splits[0], (TOKENS, D), 1.0, 6.0, ((0, 128),))
    cotangent = scatter_about(splits[1], (TOKENS, D), 1.0, 6.0, ((0, 128),))
    lengths = draw_lengths(jax.random.fold_in(splits[27], 71), 0)
    split_at = draw_split_at(jax.random.fold_in(splits[27], 71), 0)
    seg_table = scatter_about(splits[4], (2, D), 0.5, 3.0, (), jnp.float32)
    w_query = scatter_about(splits[5], (LAYERS, D, D // 2), D ** -0.5, 0.21875)
    b_query = scatter_about(splits[6], (LAYERS, D // 2), 0.5, 3.0, (), jnp.float32)
    w_key = scatter_about(splits[7], (LAYERS, D, D // 2), D ** -0.5, 0.21875)
    w_value = scatter_about(splits[8], (LAYERS, D, D // 2), D ** -0.5, 0.21875)
    b_value = scatter_about(splits[9], (LAYERS, D // 2), 0.5, 3.0, (), jnp.float32)
    w_depth = scatter_about(splits[10], (LAYERS, KERNEL, D), KERNEL ** -0.5, 2.0)
    w_point = scatter_about(splits[11], (LAYERS, D, D // 2), D ** -0.5, 0.21875)
    b_keyconv = scatter_about(splits[12], (LAYERS, D // 2), 0.5, 3.0, (), jnp.float32)
    w_kernel = scatter_about(splits[13], (LAYERS, D // 2, HEADS * KERNEL), (D // 2) ** -0.5, 0.3125)
    b_kernel = scatter_about(splits[14], (LAYERS, HEADS * KERNEL), 1.0, 4.0, (), jnp.float32)
    w_conv = scatter_about(splits[15], (LAYERS, D, D // 2), D ** -0.5, 0.21875)
    b_conv = scatter_about(splits[16], (LAYERS, D // 2), 0.5, 3.0, (), jnp.float32)
    w_out = scatter_about(splits[17], (LAYERS, D, D), (D // 16) ** -0.5, 0.875)
    b_out = scatter_about(splits[18], (LAYERS, D), 0.3, 2.0, (), jnp.float32)
    first_gain = jnp.clip(1.0 + 0.15 * jax.random.normal(splits[19], (LAYERS, D), jnp.float32), 0.25, 1.75)
    first_shift = scatter_about(splits[20], (LAYERS, D), 0.3, 2.0, (), jnp.float32)
    w_up = scatter_about(splits[21], (LAYERS, GROUPS, D // GROUPS, FF // GROUPS), (D // GROUPS) ** -0.5, 0.3125, ((1, 2), (3, 64)))
    b_up = scatter_about(splits[22], (LAYERS, GROUPS, FF // GROUPS), 0.5, 3.0, ((1, 2), (2, 64)))
    down_weight = scatter_about(splits[23], (LAYERS, GROUPS, FF // GROUPS, D // GROUPS), (FF // GROUPS) ** -0.5, 0.15625, ((1, 2), (2, 64)))
    b_down = scatter_about(splits[24], (LAYERS, D), 0.3, 2.0, (), jnp.float32)
    second_gain = jnp.clip(1.0 + 0.15 * jax.random.normal(splits[25], (LAYERS, D), jnp.float32), 0.25, 1.75)
    second_shift = scatter_about(splits[26], (LAYERS, D), 0.3, 2.0, (), jnp.float32)
    return dict(hidden=hidden, cotangent=cotangent, lengths=lengths, split_at=split_at, seg_table=seg_table, w_query=w_query, b_query=b_query, w_key=w_key, w_value=w_value, b_value=b_value, w_depth=w_depth, w_point=w_point, b_keyconv=b_keyconv, w_kernel=w_kernel, b_kernel=b_kernel, w_conv=w_conv, b_conv=b_conv, w_out=w_out, b_out=b_out, first_gain=first_gain, first_shift=first_shift, w_up=w_up, b_up=b_up, down_weight=down_weight, b_down=b_down, second_gain=second_gain, second_shift=second_shift)


@jax.custom_vjp
def reduced_input(v):
    return lax.optimization_barrier(v.astype(jnp.bfloat16)).astype(jnp.float32)

@jax.custom_vjp
def reduced_backward(v):
    return v

def low_keep(v):
    return (reduced_input(v), None)

def low_pass(kept, grad):
    return (grad,)

def back_keep(v):
    return (v, None)

def back_low(kept, grad):
    return (reduced_input(grad),)
reduced_input.defvjp(low_keep, low_pass)
reduced_backward.defvjp(back_keep, back_low)
EPSILON = 1e-06
SCORE_SCALE = 0.125
MASK_VALUE = -1000000000.0
EXACT_PRECISION = lax.Precision.HIGHEST
PARAM_NAMES = ('seg_table', 'w_query', 'b_query', 'w_key', 'w_value', 'b_value', 'w_depth', 'w_point', 'b_keyconv', 'w_kernel', 'b_kernel', 'w_conv', 'b_conv', 'w_out', 'b_out', 'first_gain', 'first_shift', 'w_up', 'b_up', 'w_down', 'b_down', 'second_gain', 'second_shift')

def product(first_op, second_op):
    return jnp.matmul(first_op, second_op, precision=EXACT_PRECISION)

def norm_rows(residual, gains, offset):
    center = residual - lax.optimization_barrier(jnp.mean(residual, axis=-1, keepdims=True))
    spread = lax.optimization_barrier(jnp.mean(center * center, axis=-1, keepdims=True))
    return center * lax.rsqrt(spread + EPSILON) * gains + offset

def layer_forward(layer_input, model_parameters, layer_number, valid_rows, key_valid):
    batch_size = layer_input.shape[0]
    seq_len = layer_input.shape[1]
    conv_reach = KERNEL // 2
    x_low = reduced_input(layer_input)
    queries = reduced_backward(product(x_low, model_parameters['w_query'][layer_number]) + model_parameters['b_query'][layer_number])
    key_rows = reduced_backward(product(x_low, model_parameters['w_key'][layer_number]))
    value_rows = reduced_backward(product(x_low, model_parameters['w_value'][layer_number]) + model_parameters['b_value'][layer_number])
    padded = jnp.pad(x_low, ((0, 0), (conv_reach, conv_reach), (0, 0)))
    depth_taps = model_parameters['w_depth'][layer_number]
    depth_out = sum((depth_taps[tap_idx] * padded[:, tap_idx:tap_idx + seq_len] for tap_idx in range(KERNEL)))
    key_conv = reduced_backward(product(reduced_input(depth_out), model_parameters['w_point'][layer_number]) + model_parameters['b_keyconv'][layer_number])
    mixed = key_conv * queries
    kernel_logit = reduced_backward(product(reduced_input(mixed), model_parameters['w_kernel'][layer_number]) + model_parameters['b_kernel'][layer_number])
    kernels = jax.nn.softmax(kernel_logit.reshape(batch_size, seq_len, HEADS, KERNEL), axis=-1)
    conv_rows = reduced_backward(product(x_low, model_parameters['w_conv'][layer_number]) + model_parameters['b_conv'][layer_number])
    conv_pad = jnp.pad(conv_rows, ((0, 0), (conv_reach, conv_reach), (0, 0))).reshape(batch_size, seq_len + 2 * conv_reach, HEADS, HEAD)
    conv_mix = sum((kernels[..., tap_idx:tap_idx + 1] * conv_pad[:, tap_idx:tap_idx + seq_len] for tap_idx in range(KERNEL)))
    conv_mix = conv_mix.reshape(batch_size, seq_len, HEADS * HEAD)
    query_heads = reduced_input(queries).reshape(batch_size, seq_len, HEADS, HEAD)
    key_heads = reduced_input(key_rows).reshape(batch_size, seq_len, HEADS, HEAD)
    value_heads = reduced_input(value_rows).reshape(batch_size, seq_len, HEADS, HEAD)
    scores = jnp.einsum('bqhd,bkhd->bhqk', query_heads, key_heads, precision=EXACT_PRECISION) * SCORE_SCALE
    scores = reduced_backward(jnp.where(key_valid[:, None, None, :], scores, MASK_VALUE))
    probs = jax.nn.softmax(scores, axis=-1)
    context = jnp.einsum('bhqk,bkhd->bqhd', reduced_input(probs), value_heads, precision=EXACT_PRECISION).reshape(batch_size, seq_len, HEADS * HEAD)
    joined = reduced_input(reduced_backward(jnp.concatenate([context, conv_mix], axis=-1)))
    resid_one = layer_input + reduced_backward(product(joined, model_parameters['w_out'][layer_number]) + model_parameters['b_out'][layer_number])
    normed = norm_rows(resid_one, model_parameters['first_gain'][layer_number], model_parameters['first_shift'][layer_number])
    grouped = reduced_input(normed).reshape(batch_size, seq_len, GROUPS, D // GROUPS)
    pre_act = reduced_backward(jnp.einsum('btgc,gcf->btgf', grouped, model_parameters['w_up'][layer_number], precision=EXACT_PRECISION) + model_parameters['b_up'][layer_number])
    activated_rows = reduced_input(jax.nn.gelu(pre_act, approximate=False))
    grouped_output = reduced_input(reduced_backward(jnp.einsum('purh,rhw->purw', activated_rows, model_parameters['w_down'][layer_number], precision=EXACT_PRECISION)))
    resid_two = normed + grouped_output.reshape(batch_size, seq_len, D) + model_parameters['b_down'][layer_number]
    return norm_rows(resid_two, model_parameters['second_gain'][layer_number], model_parameters['second_shift'][layer_number]) * valid_rows

def reference(hidden, cotangent, lengths, split_at, seg_table, w_query, b_query, w_key, w_value, b_value, w_depth, w_point, b_keyconv, w_kernel, b_kernel, w_conv, b_conv, w_out, b_out, first_gain, first_shift, w_up, b_up, down_weight, b_down, second_gain, second_shift):
    arrays = (seg_table, w_query, b_query, w_key, w_value, b_value, w_depth, w_point, b_keyconv, w_kernel, b_kernel, w_conv, b_conv, w_out, b_out, first_gain, first_shift, w_up, b_up, down_weight, b_down, second_gain, second_shift)
    model_parameters = dict(zip(PARAM_NAMES, [array_in.astype(jnp.float32) for array_in in arrays]))
    block_seqs = math.gcd(SEQS, max(1, 4096 // LEN))
    block_count = SEQS // block_seqs
    hidden_blocks = hidden.astype(jnp.float32).reshape(block_count, block_seqs, LEN, D)
    cot_blocks = cotangent.astype(jnp.float32).reshape(block_count, block_seqs, LEN, D)
    length_blocks = lengths.reshape(block_count, block_seqs)
    split_blocks = split_at.reshape(block_count, block_seqs)
    positions = jnp.arange(LEN, dtype=jnp.int32)

    def one_block(totals, inputs):
        hidden_in, cot_in, length_in, split_in = inputs
        key_valid = positions[None, :] < length_in[:, None]
        valid_rows = key_valid.astype(jnp.float32)[:, :, None]
        second_seg = (positions[None, :] > split_in[:, None])[:, :, None]

        def run(weights, start_in):
            current = (start_in + jnp.where(second_seg, weights['seg_table'][1], weights['seg_table'][0])) * valid_rows
            for layer_number in range(LAYERS):
                current = layer_forward(current, weights, layer_number, valid_rows, key_valid)
            return current
        result, pullback = jax.vjp(run, model_parameters, hidden_in)
        d_params, d_hidden = pullback(cot_in)
        return (jax.tree.map(jnp.add, totals, d_params), (result, d_hidden))
    zeros_tree = jax.tree.map(jnp.zeros_like, model_parameters)
    totals, (results, d_hiddens) = lax.scan(one_block, zeros_tree, (hidden_blocks, cot_blocks, length_blocks, split_blocks))
    return (results.reshape(TOKENS, D), d_hiddens.reshape(TOKENS, D), totals['seg_table'], totals['w_query'], totals['b_query'], totals['w_key'], totals['w_value'], totals['b_value'], totals['w_depth'], totals['w_point'], totals['b_keyconv'], totals['w_kernel'], totals['b_kernel'], totals['w_conv'], totals['b_conv'], totals['w_out'], totals['b_out'], totals['first_gain'], totals['first_shift'], totals['w_up'], totals['b_up'], totals['w_down'], totals['b_down'], totals['second_gain'], totals['second_shift'])
```

```python
import functools

import jax
import jax.numpy as jnp
from jax import lax
from jax.experimental import pallas as pl
from jax.experimental.pallas import tpu as pltpu
from jax.sharding import Mesh
from jax.sharding import PartitionSpec as P

HEADS = 6
HEAD = 64
KERNEL = 9
LAYERS = 2
LEN = 512
CH = ("ch_0", "ch_1", "ch_2", "ch_3")
GRP_CH = ("grp", "ch_0", "ch_1", "ch_2", "ch_3")


EPSILON = 1e-06
SCORE_SCALE = 0.125
MASK_VALUE = -1000000000.0


MESH = pl.DeviceIdType.MESH
LANES = 384
PARTS = 3
ORDERS = ("xyz", "yzx", "zxy")


def here():
    x, y = lax.axis_index("ch_1"), lax.axis_index("ch_0")
    z = lax.axis_index("grp") * 2 + lax.axis_index("ch_2")
    return {"x": x, "y": y, "z": z, "core": lax.axis_index("ch_3")}


def device_at(axis, place):
    if axis == "x":
        return {"ch_1": place}
    if axis == "y":
        return {"ch_0": place}
    if axis == "z":
        return {"grp": place // 2, "ch_2": place % 2}
    return {"ch_3": place}


def greet(at):
    barrier = pltpu.get_barrier_semaphore()
    peers = [("core", 1 - at["core"])]
    for axis in "xyz":
        peers += [(axis, (at[axis] + 1) % 4), (axis, (at[axis] + 3) % 4)]
    for axis, place in peers:
        pl.semaphore_signal(barrier, inc=1, device_id=device_at(axis, place), device_id_type=MESH)
    pl.semaphore_wait(barrier, len(peers))


class Sends:
    def __init__(self, send_sems, recv_sems):
        self.send_sems, self.recv_sems, self.count, self.all = send_sems, recv_sems, 0, []

    def start(self, src, dst, axis, place):
        copy = pltpu.make_async_remote_copy(
            src_ref=src, dst_ref=dst,
            send_sem=self.send_sems.at[self.count], recv_sem=self.recv_sems.at[self.count],
            device_id=device_at(axis, place), device_id_type=MESH)
        self.count += 1
        copy.start()
        self.all.append(copy)
        return copy

    def finish(self):
        for copy in self.all:
            copy.wait_send()


def add_into(dst, *srcs):
    lead = dst.shape[:-2]
    total = 1
    for n in lead:
        total *= n

    def one(i):
        idx, rest = [], i
        for n in reversed(lead):
            idx.append(rest % n)
            rest = rest // n
        idx = tuple(reversed(idx))
        acc = dst[idx].astype(jnp.float32) if idx else dst[...].astype(jnp.float32)
        for s in srcs:
            acc = acc + (s[idx] if idx else s[...]).astype(jnp.float32)
        if idx:
            dst[idx] = acc.astype(jnp.bfloat16)
        else:
            dst[...] = acc.astype(jnp.bfloat16)

    if total == 1 and not lead:
        one(0)
    else:
        pl.loop(0, total)(one)


def halves(ref):
    n = ref.shape[0] // 2
    return ref.at[pl.ds(0, n)], ref.at[pl.ds(n, n)]


class Scatter:
    def __init__(self, at, sends, x, sums, core_in, bufs):
        self.at, self.sends, self.x, self.sums, self.core_in, self.bufs = at, sends, x, sums, core_in, bufs

    def places(self, p, s):
        axis = ORDERS[p][s]
        i = self.at[axis]
        return axis, i, (i + 1) % 4, (i + 2) % 4, (i + 3) % 4

    def begin(self):
        c = self.at["core"]
        self.core = {}
        for turn in (2, 1, 3, 0):
            for p in range(PARTS):
                k = (self.at[ORDERS[p][0]] + turn) % 4
                self.core[p, turn] = self.sends.start(
                    self.x.at[p, 1 - c, k], self.core_in.at[p, k], "core", 1 - c)

    def arrive(self, p, turn):
        k = (self.at[ORDERS[p][0]] + turn) % 4
        self.core[p, turn].wait_recv()
        add_into(self.sums.at[p, k], self.core_in.at[p, k])

    def block(self, p, s, k):
        if s == 0:
            return self.sums.at[p, k]
        if s == 1:
            return self.sums.at[p, self.at[ORDERS[p][0]], k]
        return self.sums.at[p, self.at[ORDERS[p][0]], self.at[ORDERS[p][1]], k]

    def split(self, s):
        return s < 2 or self.x.shape[-2] % 32 == 0

    def first(self, p, s):
        axis, i, up, far, down = self.places(p, s)
        t = self.bufs[s].at[p, 0]
        src = self.block(p, s, far)
        if self.split(s):
            (s0, s1), (t0, t1) = halves(src), halves(t)
            return (self.sends.start(s0, t0, axis, up), self.sends.start(s1, t1, axis, down))
        return (self.sends.start(src, t, axis, up),)

    def second_early(self, p, s):
        axis, i, up, far, down = self.places(p, s)
        u0, u1 = self.bufs[s].at[p, 1], self.bufs[s].at[p, 2]
        if self.split(s):
            a = self.sends.start(halves(self.block(p, s, up))[1], halves(u0)[1], axis, up)
            b = self.sends.start(halves(self.block(p, s, down))[0], halves(u1)[0], axis, down)
            return [a, b]
        return [self.sends.start(self.block(p, s, down), u1, axis, down)]

    def second_late(self, p, s, firsts):
        axis, i, up, far, down = self.places(p, s)
        t, u0, u1 = (self.bufs[s].at[p, n] for n in range(3))
        out = []
        if self.split(s):
            firsts[0].wait_recv()
            half = halves(self.block(p, s, up))[0]
            add_into(half, halves(t)[0])
            out.append(self.sends.start(half, halves(u0)[0], axis, up))
            firsts[1].wait_recv()
            half = halves(self.block(p, s, down))[1]
            add_into(half, halves(t)[1])
            out.append(self.sends.start(half, halves(u1)[1], axis, down))
        else:
            firsts[0].wait_recv()
            whole = self.block(p, s, up)
            add_into(whole, t)
            out.append(self.sends.start(whole, u0, axis, up))
        return out

    def last(self, p, s, copies):
        for copy in copies:
            copy.wait_recv()
        axis, i, up, far, down = self.places(p, s)
        add_into(self.block(p, s, i), self.bufs[s].at[p, 1], self.bufs[s].at[p, 2])

    def run(self):
        self.begin()
        firsts, seconds = {}, {}
        for p in range(PARTS):
            self.arrive(p, 2)
            firsts[p] = self.first(p, 0)
        for p in range(PARTS):
            self.arrive(p, 1)
            self.arrive(p, 3)
            seconds[p] = self.second_early(p, 0)
        for p in range(PARTS):
            self.arrive(p, 0)
        for p in range(PARTS):
            seconds[p] += self.second_late(p, 0, firsts[p])
        for s in (1, 2):
            for p in range(PARTS):
                self.last(p, s - 1, seconds[p])
                firsts[p] = self.first(p, s)
                seconds[p] = self.second_early(p, s)
            for p in range(PARTS):
                seconds[p] += self.second_late(p, s, firsts[p])
        for p in range(PARTS):
            self.last(p, 2, seconds[p])

    def own(self, p):
        o = ORDERS[p]
        return self.sums.at[p, self.at[o[0]], self.at[o[1]], self.at[o[2]]]


def scatter_scratch(R):
    bf = jnp.bfloat16
    return [pltpu.VMEM((PARTS, 4, 4, 4, R, LANES), bf), pltpu.VMEM((PARTS, 4, 4, 4, R, LANES), bf),
            pltpu.VMEM((PARTS, 3, 4, 4, R, LANES), bf), pltpu.VMEM((PARTS, 3, 4, R, LANES), bf),
            pltpu.VMEM((PARTS, 3, R, LANES), bf)]


class Gather:
    def __init__(self, at, sends, g):
        self.at, self.sends, self.g = at, sends, g

    def block(self, p, s, k):
        c, o = self.at["core"], ORDERS[p]
        if s == 0:
            return self.g.at[p, c, k]
        if s == 1:
            return self.g.at[p, c, self.at[o[0]], k]
        return self.g.at[p, c, self.at[o[0]], self.at[o[1]], k]

    def split(self, s):
        return s < 2 or self.g.shape[-2] % 32 == 0

    def first(self, p, s):
        axis = ORDERS[p][s]
        i = self.at[axis]
        mine = self.block(p, s, i)
        return (self.sends.start(mine, mine, axis, (i + 1) % 4), self.sends.start(mine, mine, axis, (i + 3) % 4))

    def second(self, p, s, firsts):
        axis = ORDERS[p][s]
        i = self.at[axis]
        firsts[0].wait_recv()
        low = self.block(p, s, (i + 3) % 4)
        if not self.split(s):
            out = [self.sends.start(low, low, axis, (i + 1) % 4)]
            firsts[1].wait_recv()
            return out
        low = halves(low)[0]
        out = [self.sends.start(low, low, axis, (i + 1) % 4)]
        firsts[1].wait_recv()
        high = halves(self.block(p, s, (i + 1) % 4))[1]
        return out + [self.sends.start(high, high, axis, (i + 3) % 4)]

    def across(self, p, turn):
        k = (self.at[ORDERS[p][0]] + turn) % 4
        mine = self.g.at[p, self.at["core"], k]
        return self.sends.start(mine, mine, "core", 1 - self.at["core"])

    def run(self):
        firsts, seconds, cores = {}, {}, []
        for s in (2, 1):
            for p in range(PARTS):
                firsts[p] = self.first(p, s)
            for p in range(PARTS):
                seconds[p] = self.second(p, s, firsts[p])
            for p in range(PARTS):
                for copy in seconds[p]:
                    copy.wait_recv()
        for p in range(PARTS):
            firsts[p] = self.first(p, 0)
        for p in range(PARTS):
            cores.append(self.across(p, 0))
        for p in range(PARTS):
            seconds[p] = self.second(p, 0, firsts[p])
            cores.append(self.across(p, 3))
            cores.append(self.across(p, 1))
        for p in range(PARTS):
            for copy in seconds[p]:
                copy.wait_recv()
            cores.append(self.across(p, 2))
        for copy in cores:
            copy.wait_recv()


def exchange_kernel(R, Rg, x, g, own_out, sums, core_in, b0, b1, b2, local, ss, rs):
    at = here()
    greet(at)
    sends = Sends(ss, rs)
    load = pltpu.make_async_copy(x.at[:, at["core"]], sums, local.at[0])
    load.start()
    sc = Scatter(at, sends, x, sums, core_in, (b0, b1, b2))
    load.wait()
    sc.run()
    put = []
    for p in range(PARTS):
        own_out[p] = sc.own(p)[...]
        if Rg:
            o = ORDERS[p]
            g[p, at["core"], at[o[0]], at[o[1]], at[o[2]]] = sc.own(p)[pl.ds(R - Rg, Rg)]
    if Rg:
        Gather(at, sends, g).run()
    sends.finish()


def exchange(x, R, Rg, cid):
    bf = jnp.bfloat16
    return pl.pallas_call(
        functools.partial(exchange_kernel, R, Rg),
        out_shape=(jax.ShapeDtypeStruct((PARTS, 2, 4, 4, 4, Rg, LANES), bf),
                   jax.ShapeDtypeStruct((PARTS, R, LANES), bf)),
        in_specs=[pl.BlockSpec(memory_space=pl.ANY)],
        out_specs=(pl.BlockSpec(memory_space=pltpu.VMEM), pl.BlockSpec(memory_space=pltpu.VMEM)),
        scratch_shapes=scatter_scratch(R) + [pltpu.SemaphoreType.DMA((1,)), pltpu.SemaphoreType.DMA((120,)), pltpu.SemaphoreType.DMA((120,))],
        compiler_params=pltpu.CompilerParams(collective_id=cid, has_side_effects=True, vmem_limit_bytes=60 << 20),
    )(x)


def gather_kernel(R, own, g, ss, rs):
    at = here()
    for p in range(PARTS):
        o = ORDERS[p]
        g[p, at["core"], at[o[0]], at[o[1]], at[o[2]]] = own[p]
    greet(at)
    sends = Sends(ss, rs)
    Gather(at, sends, g).run()
    sends.finish()


def gather(own, R, cid):
    return pl.pallas_call(
        functools.partial(gather_kernel, R),
        out_shape=jax.ShapeDtypeStruct((PARTS, 2, 4, 4, 4, R, LANES), jnp.bfloat16),
        in_specs=[pl.BlockSpec(memory_space=pltpu.VMEM)],
        out_specs=pl.BlockSpec(memory_space=pltpu.VMEM),
        scratch_shapes=[pltpu.SemaphoreType.DMA((60,)), pltpu.SemaphoreType.DMA((60,))],
        compiler_params=pltpu.CompilerParams(collective_id=cid, has_side_effects=True, vmem_limit_bytes=60 << 20),
    )(own)


PLACES = {"xyz": (2, 1, 0, 3), "yzx": (1, 0, 3, 2), "zxy": (0, 3, 2, 1)}


def to_part(rows, p):
    r = rows.shape[1]
    cut = rows.reshape(2, 4, 4, 2, 2, r, LANES)
    return jnp.transpose(cut, (4,) + PLACES[ORDERS[p]] + (5, 6)).reshape(2, 4, 4, 4, r, LANES)


def from_part(part, p):
    r = part.shape[-2]
    order = (4,) + PLACES[ORDERS[p]] + (5, 6)
    sizes = (2, 4, 4, 2, 2, r, LANES)
    cut = part.reshape([sizes[d] for d in order])
    back = [order.index(d) for d in range(7)]
    return jnp.transpose(cut, back).reshape(128, r, LANES)


def norm_rows(residual, gains, offset):
    center = residual - jnp.mean(residual, axis=-1, keepdims=True)
    spread = jnp.mean(center * center, axis=-1, keepdims=True)
    return center * lax.rsqrt(spread + EPSILON) * gains + offset


def product(first_op, second_op):
    return jnp.dot(first_op, second_op, preferred_element_type=jnp.float32)


def product_t(first_op, second_op):
    return lax.dot_general(
        first_op, second_op, (((1,), (1,)), ((), ())), preferred_element_type=jnp.float32
    )


def inner_rows(first_op, second_op):
    return lax.dot_general(
        first_op, second_op, (((0,), (0,)), ((), ())), preferred_element_type=jnp.float32
    )


def exact_gelu(inputs):
    return jax.nn.gelu(inputs, approximate=False)


def column_sum(inputs):
    return jnp.sum(inputs.astype(jnp.float32), axis=0)


def attend_forward(operands):
    query_low, key_heads, value_heads, key_valid = operands
    scores = (
        jnp.einsum("qhd,khd->hqk", query_low, key_heads, preferred_element_type=jnp.float32)
        * SCORE_SCALE
    )
    scores = jnp.where(key_valid[None, None, :], scores, MASK_VALUE)
    peak = jnp.max(scores, axis=-1, keepdims=True)
    log_total = peak + jnp.log(jnp.sum(jnp.exp(scores - peak), axis=-1, keepdims=True))
    probs_low = jnp.exp(scores - log_total).astype(jnp.bfloat16)
    context = jnp.einsum("hqk,khd->qhd", probs_low, value_heads, preferred_element_type=jnp.float32)
    return (context.reshape(context.shape[0], -1), log_total)


def attend_backward(operands):
    query_low, key_heads, value_heads, d_context, log_total, key_valid = operands
    scores = (
        jnp.einsum("qhd,khd->hqk", query_low, key_heads, preferred_element_type=jnp.float32)
        * SCORE_SCALE
    )
    scores = jnp.where(key_valid[None, None, :], scores, MASK_VALUE)
    probs = jnp.exp(scores - log_total)
    d_probs = jnp.einsum("qhd,khd->hqk", d_context, value_heads, preferred_element_type=jnp.float32)
    row_dot = jnp.sum(probs * d_probs, axis=-1, keepdims=True)
    d_scores = (probs * (d_probs - row_dot)).astype(jnp.bfloat16)
    d_query_att = (
        jnp.einsum("hqk,khd->qhd", d_scores, key_heads, preferred_element_type=jnp.float32)
        * SCORE_SCALE
    )
    d_key = (
        jnp.einsum("hqk,qhd->khd", d_scores, query_low, preferred_element_type=jnp.float32)
        * SCORE_SCALE
    ).astype(jnp.bfloat16)
    d_value = jnp.einsum(
        "hqk,qhd->khd", probs.astype(jnp.bfloat16), d_context, preferred_element_type=jnp.float32
    ).astype(jnp.bfloat16)
    seq_rows = query_low.shape[0]
    return (
        d_query_att.reshape(seq_rows, -1),
        d_key.reshape(seq_rows, -1),
        d_value.reshape(seq_rows, -1),
    )


def shards(
    hidden,
    cotangent,
    lengths,
    split_at,
    seg_table,
    w_query,
    b_query,
    w_key,
    w_value,
    b_value,
    w_depth,
    w_point,
    b_keyconv,
    w_kernel,
    b_kernel,
    w_conv,
    b_conv,
    w_out,
    b_out,
    first_gain,
    first_shift,
    w_up,
    b_up,
    down_weight,
    b_down,
    second_gain,
    second_shift,
):
    num_rows = hidden.shape[0]
    model_width = hidden.shape[1]
    attend = w_query.shape[2]
    half_width = model_width // 2
    conv_reach = KERNEL // 2
    seq_count = num_rows // LEN
    block_index = lax.axis_index("grp") * lax.axis_size(CH) + lax.axis_index(CH)
    first_seq = block_index * seq_count
    my_lengths = lax.dynamic_slice_in_dim(lengths, first_seq, seq_count)
    my_splits = lax.dynamic_slice_in_dim(split_at, first_seq, seq_count)
    positions = jnp.arange(LEN, dtype=jnp.int32)
    key_valid = positions[None, :] < my_lengths[:, None]
    valid_rows = key_valid.astype(jnp.float32).reshape(num_rows, 1)
    second_seg = (positions[None, :] > my_splits[:, None]).reshape(num_rows, 1)
    start_x = (
        hidden.astype(jnp.float32) + jnp.where(second_seg, seg_table[1], seg_table[0])
    ) * valid_rows

    def rows_three(matrix):
        return matrix.reshape(seq_count, LEN, matrix.shape[-1])

    def pad_rows(matrix):
        return jnp.pad(matrix, ((0, 0), (conv_reach, conv_reach), (0, 0)))

    def heads_four(matrix):
        return matrix.reshape(seq_count, LEN, HEADS, HEAD)

    def conv_kernels(queries, key_conv, layer_number):
        mixed = key_conv * queries
        kernel_logit = (
            product(mixed.astype(jnp.bfloat16), w_kernel[layer_number]) + b_kernel[layer_number]
        )
        return (mixed, jax.nn.softmax(kernel_logit.reshape(seq_count, LEN, HEADS, KERNEL), axis=-1))

    def forward_layer(layer_input, layer_number):
        x_low = layer_input.astype(jnp.bfloat16)
        queries = product(x_low, w_query[layer_number]) + b_query[layer_number]
        key_low = product(x_low, w_key[layer_number]).astype(jnp.bfloat16)
        value_low = (product(x_low, w_value[layer_number]) + b_value[layer_number]).astype(
            jnp.bfloat16
        )
        x_pad = pad_rows(rows_three(x_low)).astype(jnp.float32)
        depth_taps = w_depth[layer_number].astype(jnp.float32)
        depth_out = sum(
            (depth_taps[tap_idx] * x_pad[:, tap_idx : tap_idx + LEN] for tap_idx in range(KERNEL))
        ).reshape(num_rows, model_width)
        depth_low = depth_out.astype(jnp.bfloat16)
        key_conv = product(depth_low, w_point[layer_number]) + b_keyconv[layer_number]
        mixed, kernels = conv_kernels(queries, key_conv, layer_number)
        conv_rows = product(x_low, w_conv[layer_number]) + b_conv[layer_number]
        conv_pad = pad_rows(rows_three(conv_rows)).reshape(
            seq_count, LEN + 2 * conv_reach, HEADS, HEAD
        )
        conv_mix = sum(
            (
                kernels[..., tap_idx : tap_idx + 1] * conv_pad[:, tap_idx : tap_idx + LEN]
                for tap_idx in range(KERNEL)
            )
        ).reshape(num_rows, attend)
        query_low = queries.astype(jnp.bfloat16)
        context, log_total = lax.map(
            attend_forward,
            (heads_four(query_low), heads_four(key_low), heads_four(value_low), key_valid),
        )
        joined = jnp.concatenate([context.reshape(num_rows, attend), conv_mix], axis=1).astype(
            jnp.bfloat16
        )
        resid_one = layer_input + product(joined, w_out[layer_number]) + b_out[layer_number]
        normed = norm_rows(resid_one, first_gain[layer_number], first_shift[layer_number])
        group_rows = normed.astype(jnp.bfloat16).reshape(num_rows, 2, half_width)
        up_full, down_full, bias_full = ffn_weights[layer_number]
        pre_act = jnp.einsum(
            "tgc,ghc->gth", group_rows, up_full, preferred_element_type=jnp.float32
        ) + bias_full[:, None]
        back_rows = jnp.einsum(
            "gth,ghc->tgc",
            exact_gelu(pre_act).astype(jnp.bfloat16),
            down_full,
            preferred_element_type=jnp.float32,
        ).astype(jnp.bfloat16).reshape(num_rows, model_width)
        weights_kept = (up_full, down_full, pre_act)
        resid_two = normed + back_rows.astype(jnp.float32) + b_down[layer_number]
        result = (
            norm_rows(resid_two, second_gain[layer_number], second_shift[layer_number]) * valid_rows
        )
        kept = {
            "layer_input": layer_input,
            "queries": queries,
            "key_low": key_low,
            "value_low": value_low,
            "depth_low": depth_low,
            "key_conv": key_conv,
            "conv_pad": conv_pad,
            "log_total": log_total,
            "joined": joined,
            "resid_one": resid_one,
            "group_rows": group_rows,
            "weights": weights_kept,
            "resid_two": resid_two,
        }
        return (result, kept)

    def backward_layer(grad_out, layer_number, kept):
        pull_two = jax.vjp(
            norm_rows, kept["resid_two"], second_gain[layer_number], second_shift[layer_number]
        )[1]
        d_resid_two, d_gain_two, d_shift_two = pull_two(grad_out * valid_rows)
        d_bdown = jnp.sum(d_resid_two, axis=0)
        d_group = d_resid_two.astype(jnp.bfloat16).reshape(num_rows, 2, half_width)
        group_rows = kept["group_rows"]
        up_full, down_full, pre_act = kept["weights"]
        gelu_out, gelu_pull = jax.vjp(exact_gelu, pre_act)
        d_pre = gelu_pull(
            jnp.einsum("tgc,ghc->gth", d_group, down_full, preferred_element_type=jnp.float32)
        )[0].astype(jnp.bfloat16)
        d_back = (
            jnp.einsum("gth,ghc->tgc", d_pre, up_full, preferred_element_type=jnp.float32)
            .astype(jnp.bfloat16)
            .astype(jnp.float32)
            .reshape(num_rows, model_width)
        )
        d_up = jnp.einsum("gth,tgc->ghc", d_pre, group_rows, preferred_element_type=jnp.float32)
        d_down = jnp.einsum(
            "gth,tgc->ghc",
            gelu_out.astype(jnp.bfloat16),
            d_group,
            preferred_element_type=jnp.float32,
        )
        d_upbias = jnp.sum(d_pre.astype(jnp.float32), axis=1)
        pull_one = jax.vjp(
            norm_rows, kept["resid_one"], first_gain[layer_number], first_shift[layer_number]
        )[1]
        d_resid_one, d_gain_one, d_shift_one = pull_one(d_resid_two + d_back)
        d_proj = d_resid_one.astype(jnp.bfloat16)
        d_wout = inner_rows(kept["joined"], d_proj)
        d_bout = column_sum(d_proj)
        d_joined = product_t(d_proj, w_out[layer_number]).astype(jnp.bfloat16)
        d_context = heads_four(d_joined[:, :attend])
        d_mix = heads_four(d_joined[:, attend:].astype(jnp.float32))
        queries = kept["queries"]
        query_low = queries.astype(jnp.bfloat16)
        d_query_att, d_key, d_value = lax.map(
            attend_backward,
            (
                heads_four(query_low),
                heads_four(kept["key_low"]),
                heads_four(kept["value_low"]),
                d_context,
                kept["log_total"],
                key_valid,
            ),
        )
        d_query_att = d_query_att.reshape(num_rows, attend)
        d_key = d_key.reshape(num_rows, attend)
        d_value = d_value.reshape(num_rows, attend)
        key_conv = kept["key_conv"]
        mixed, kernels = conv_kernels(queries, key_conv, layer_number)
        conv_pad = kept["conv_pad"]
        d_kernels = jnp.stack(
            [
                jnp.sum(d_mix * conv_pad[:, tap_idx : tap_idx + LEN], axis=-1)
                for tap_idx in range(KERNEL)
            ],
            axis=-1,
        )
        d_conv_pad = sum(
            (
                jnp.pad(
                    kernels[..., tap_idx : tap_idx + 1] * d_mix,
                    ((0, 0), (tap_idx, 2 * conv_reach - tap_idx), (0, 0), (0, 0)),
                )
                for tap_idx in range(KERNEL)
            )
        )
        d_conv = (
            d_conv_pad[:, conv_reach : conv_reach + LEN]
            .reshape(num_rows, attend)
            .astype(jnp.bfloat16)
        )
        d_logit = (
            (kernels * (d_kernels - jnp.sum(kernels * d_kernels, axis=-1, keepdims=True)))
            .reshape(num_rows, HEADS * KERNEL)
            .astype(jnp.bfloat16)
        )
        d_wkernel = inner_rows(mixed.astype(jnp.bfloat16), d_logit)
        d_bkernel = column_sum(d_logit)
        d_mixed = product_t(d_logit, w_kernel[layer_number])
        d_keyconv = (d_mixed * queries).astype(jnp.bfloat16)
        d_query = (d_query_att + d_mixed * key_conv).astype(jnp.bfloat16)
        d_wpoint = inner_rows(kept["depth_low"], d_keyconv)
        d_bkeyconv = column_sum(d_keyconv)
        d_depth = rows_three(product_t(d_keyconv, w_point[layer_number]))
        x_low = kept["layer_input"].astype(jnp.bfloat16)
        x_pad = pad_rows(rows_three(x_low)).astype(jnp.float32)
        d_wdepth = jnp.stack(
            [
                jnp.sum(d_depth * x_pad[:, tap_idx : tap_idx + LEN], axis=(0, 1))
                for tap_idx in range(KERNEL)
            ]
        )
        depth_taps = w_depth[layer_number].astype(jnp.float32)
        d_extended = sum(
            (
                jnp.pad(
                    depth_taps[tap_idx] * d_depth,
                    ((0, 0), (tap_idx, 2 * conv_reach - tap_idx), (0, 0)),
                )
                for tap_idx in range(KERNEL)
            )
        )
        d_input = d_resid_one + d_extended[:, conv_reach : conv_reach + LEN].reshape(
            num_rows, model_width
        )
        d_input = (
            d_input
            + product_t(d_query, w_query[layer_number])
            + product_t(d_key, w_key[layer_number])
        )
        d_input = (
            d_input
            + product_t(d_value, w_value[layer_number])
            + product_t(d_conv, w_conv[layer_number])
        )
        layer_grads = (
            inner_rows(x_low, d_query),
            column_sum(d_query),
            inner_rows(x_low, d_key),
            inner_rows(x_low, d_value),
            column_sum(d_value),
            d_wdepth,
            d_wpoint,
            d_bkeyconv,
            d_wkernel,
            d_bkernel,
            inner_rows(x_low, d_conv),
            column_sum(d_conv),
            d_wout,
            d_bout,
            d_gain_one,
            d_shift_one,
            d_bdown,
            d_gain_two,
            d_shift_two,
            d_upbias,
        )
        return (d_input, layer_grads, (d_up, d_down))

    hidden_piece = w_up.shape[3]
    pieces = jnp.concatenate([jnp.swapaxes(w_up[:, 0], 1, 2), down_weight[:, 0]], axis=1)
    pieces = pieces.reshape(LAYERS, PARTS, 16, LANES).swapaxes(0, 1)
    arrived = gather(pieces.reshape(PARTS, LAYERS * 16, LANES), LAYERS * 16, 1)
    whole = jnp.stack([from_part(arrived[p], p) for p in range(PARTS)], axis=1)
    whole = whole.reshape(2, 64, PARTS, LAYERS, 16, LANES)
    whole = jnp.moveaxis(whole, 3, 0).reshape(LAYERS, 2, 64, 2, hidden_piece, LANES)
    bias = lax.all_gather(b_up[:, 0], GRP_CH, axis=0).reshape(2, 64, LAYERS, hidden_piece)
    bias = jnp.moveaxis(bias, 2, 0).reshape(LAYERS, 2, -1).astype(jnp.float32)
    ffn_weights = [
        (
            whole[layer_pos, :, :, 0].reshape(2, -1, LANES),
            whole[layer_pos, :, :, 1].reshape(2, -1, LANES),
            bias[layer_pos],
        )
        for layer_pos in range(LAYERS)
    ]
    current = start_x
    kept_all = []
    for layer_number in range(LAYERS):
        current, kept = forward_layer(current, layer_number)
        kept_all.append(kept)
    grad_flow = cotangent.astype(jnp.float32)
    shared = [None] * LAYERS
    sharded = [None] * LAYERS
    seg_local = jnp.zeros_like(seg_table)
    for layer_number in reversed(range(LAYERS)):
        grad_flow, layer_grads, group_grads = backward_layer(
            grad_flow, layer_number, kept_all[layer_number]
        )
        sharded[layer_number] = group_grads
        if layer_number == 0:
            grad_flow = grad_flow * valid_rows
            seg_local = jnp.stack(
                [
                    jnp.sum(jnp.where(second_seg, 0.0, grad_flow), axis=0),
                    jnp.sum(jnp.where(second_seg, grad_flow, 0.0), axis=0),
                ]
            )
        shared[layer_number] = layer_grads
    members = [jnp.stack([shared[layer_pos][member] for layer_pos in range(LAYERS)]) for member in range(20)]
    members.append(seg_local)
    flat = [m.astype(jnp.bfloat16).reshape(-1) for m in members]
    sizes = [f.shape[0] for f in flat]
    total_rows = 128 * PARTS * 32
    flat.append(jnp.zeros((total_rows * LANES - sum(sizes),), jnp.bfloat16))
    small = jnp.concatenate(flat).reshape(PARTS, 2, 4, 4, 4, 32, LANES)
    own = []
    for layer_pos in range(LAYERS):
        d_up, d_down = sharded[layer_pos]
        rows = jnp.concatenate(
            [d_up.reshape(128, hidden_piece, LANES), d_down.reshape(128, hidden_piece, LANES)], axis=1
        ).astype(jnp.bfloat16)
        own.append([to_part(rows[:, 16 * p : 16 * p + 16], p) for p in range(PARTS)])
    both = jnp.concatenate([jnp.stack(own[0]), jnp.stack(own[1]), small], axis=-2)
    summed, mine = exchange(both, 64, 32, 2)
    summed = summed.reshape(-1).astype(jnp.float32)
    totals, start = [], 0
    for m, size in zip(members, sizes):
        totals.append(summed[start : start + size].reshape(m.shape))
        start += size
    mine = mine[:, :32].astype(jnp.float32).reshape(PARTS, LAYERS, 16, LANES)
    mine = jnp.moveaxis(mine, 1, 0).reshape(LAYERS, 2, hidden_piece, LANES)
    grad_up = jnp.swapaxes(mine[:, 0], 1, 2)[:, None]
    grad_down = mine[:, 1][:, None]
    here_grp, here_ch = lax.axis_index("grp"), lax.axis_index(CH)
    grad_upbias = lax.dynamic_slice(
        totals[19], (0, here_grp, here_ch * hidden_piece), (LAYERS, 1, hidden_piece)
    )
    return (
        current,
        grad_flow,
        totals[20],
        totals[0],
        totals[1],
        totals[2],
        totals[3],
        totals[4],
        totals[5],
        totals[6],
        totals[7],
        totals[8],
        totals[9],
        totals[10],
        totals[11],
        totals[12],
        totals[13],
        totals[14],
        totals[15],
        grad_up,
        grad_upbias,
        grad_down,
        totals[16],
        totals[17],
        totals[18],
    )


def solution(mesh):
    finer = Mesh(
        mesh.devices.reshape(mesh.shape["grp"], 4, 4, 2, 2), ("grp", "ch_0", "ch_1", "ch_2", "ch_3")
    )
    placed = (
        P(GRP_CH, None),
        P(GRP_CH, None),
        P(),
        P(),
        P(),
        P(),
        P(),
        P(),
        P(),
        P(),
        P(),
        P(),
        P(),
        P(),
        P(),
        P(),
        P(),
        P(),
        P(),
        P(),
        P(),
        P(None, "grp", None, CH),
        P(None, "grp", CH),
        P(None, "grp", CH, None),
        P(),
        P(),
        P(),
    )
    return jax.shard_map(
        shards,
        mesh=finer,
        in_specs=placed,
        out_specs=(
            P(GRP_CH, None),
            P(GRP_CH, None),
            P(),
            P(),
            P(),
            P(),
            P(),
            P(),
            P(),
            P(),
            P(),
            P(),
            P(),
            P(),
            P(),
            P(),
            P(),
            P(),
            P(),
            P(None, "grp", None, CH),
            P(None, "grp", CH),
            P(None, "grp", CH, None),
            P(),
            P(),
            P(),
        ),
        check_vma=False,
    )
```

```python
import functools
from typing import NamedTuple

import jax
import jax.numpy as jnp
import ml_dtypes
import numpy as np
from jax import lax
from jax.experimental import pallas as pl
from jax.experimental.pallas import tpu as pltpu
from jax.sharding import Mesh
from jax.sharding import PartitionSpec as P

HEADS = 6
HEAD = 64
KERNEL = 9
LAYERS = 2
LEN = 512
CH = ("ch_0", "ch_1", "ch_2", "ch_3")
GRP_CH = ("grp",) + CH
EPSILON = 1e-06
SCORE_SCALE = 0.125
MASK_VALUE = -1000000000.0
BF, F32 = jnp.bfloat16, jnp.float32
MESH = pl.DeviceIdType.MESH
LANES = 384
PARTS = 3
ORDERS = ("xyz", "yzx", "zxy")


def here():
    x, y = lax.axis_index("ch_1"), lax.axis_index("ch_0")
    z = lax.axis_index("grp") * 2 + lax.axis_index("ch_2")
    return {"x": x, "y": y, "z": z, "core": lax.axis_index("ch_3")}


def device_at(axis, place):
    if axis == "x":
        return {"ch_1": place}
    if axis == "y":
        return {"ch_0": place}
    if axis == "z":
        return {"grp": place // 2, "ch_2": place % 2}
    return {"ch_3": place}


def greet(at):
    peers = [("core", 1 - at["core"])]
    for axis in "xyz":
        peers += [(axis, (at[axis] + turn) % 4) for turn in (1, 2, 3)]
    for axis, place in peers:
        pl.semaphore_signal(
            pltpu.get_barrier_semaphore(), inc=1, device_id=device_at(axis, place), device_id_type=MESH)


def met():
    pl.semaphore_wait(pltpu.get_barrier_semaphore(), 10)


class Sends:
    def __init__(self, send_sems, recv_sems):
        self.send_sems, self.recv_sems, self.made = send_sems, recv_sems, {}

    def copy(self, key):
        number, make = self.made[key]
        src, dst, axis, place = make()
        return pltpu.make_async_remote_copy(
            src_ref=src, dst_ref=dst, send_sem=self.send_sems.at[number], recv_sem=self.recv_sems.at[number],
            device_id=device_at(axis, place), device_id_type=MESH)

    def start(self, key, make):
        if key not in self.made:
            self.made[key] = (len(self.made), make)
        self.copy(key).start()

    def arrived(self, *keys):
        for key in keys:
            self.copy(key).wait_recv()

    def finish(self):
        for key in self.made:
            self.copy(key).wait_send()


def all_in(lead, work):
    @pl.loop(0, int(np.prod(lead)))
    def one(i):
        at, rest = [], i
        for n in reversed(lead):
            at.append(rest % n)
            rest = rest // n
        work(tuple(reversed(at)))


class Scatter:
    def __init__(self, name, at, sends, x, scratch, together=False):
        self.name, self.at, self.sends, self.x, self.together = name, at, sends, x, together
        self.sums, self.core_in, self.bufs, self.load_sem = scratch[0], scratch[1], scratch[2:5], scratch[5]

    def load(self):
        return pltpu.make_async_copy(self.x.at[:, self.at["core"]], self.sums, self.load_sem.at[0])

    def place(self, p, s, turn):
        return (self.at[ORDERS[p][s]] + turn) % 4

    def block(self, p, s, turn):
        lead = [self.at[ORDERS[p][n]] for n in range(s)]
        return self.sums.at[(p, *lead, self.place(p, s, turn))]

    def begin(self):
        self.load().start()
        for turn in (2, 1, 3, 0):
            for p in range(PARTS):
                self.sends.start((self.name, 3, p, turn), lambda p=p, turn=turn: (
                    self.x.at[p, 1 - self.at["core"], self.place(p, 0, turn)],
                    self.core_in.at[p, self.place(p, 0, turn)], "core", 1 - self.at["core"]))

    def take(self, turn):
        for p in range(PARTS):
            self.sends.arrived((self.name, 3, p, turn))
            mine, other = self.block(p, 0, turn), self.core_in.at[p, self.place(p, 0, turn)]

            def add(at):
                mine[at] = mine[at] + other[at]

            all_in(mine.shape[:1], add)
            if turn:
                self.send(p, 0, turn)

    def send(self, p, s, turn):
        self.sends.start((self.name, s, p, turn), lambda: (
            self.block(p, s, turn), self.bufs[s].at[p, turn - 1], ORDERS[p][s], self.place(p, s, turn)))

    def send_same(self, p, turn):
        def make():
            slot = self.bufs[2].at[p, self.at[ORDERS[p][2]]]
            return slot, slot, ORDERS[p][2], self.place(p, 2, turn)

        self.sends.start((self.name, 2, p, turn), make)

    def onward(self, s):
        for p in range(PARTS):
            self.join(p, s - 1)
            if s == 2 and self.together:
                self.bufs[2][p, self.at[ORDERS[p][2]]] = self.own(p)[...]
            for turn in (2, 1, 3):
                if s == 2 and self.together:
                    self.send_same(p, turn)
                else:
                    self.send(p, s, turn)

    def join(self, p, s):
        for turn in (1, 3, 2):
            self.sends.arrived((self.name, s, p, turn))
        if s == 2 and self.together:
            own, slots = self.own(p), self.bufs[2].at[p]
            total = slots[0].astype(F32) + slots[1].astype(F32)
            own[...] = (total + slots[2].astype(F32) + slots[3].astype(F32)).astype(BF)
            return
        mine, came = self.block(p, s, 0), self.bufs[s].at[p]

        def add(at):
            total = mine[at].astype(F32)
            for n in range(3):
                total += came[(n, *at)].astype(F32)
            mine[at] = total.astype(BF)

        if len(mine.shape) > 2:
            all_in(mine.shape[:1], add)
        else:
            add((Ellipsis,))

    def steps(self):
        def start():
            self.load().wait()
            self.take(2)

        return [self.begin, start, lambda: self.take(1), lambda: self.take(3), lambda: self.take(0),
                lambda: self.onward(1), lambda: self.onward(2), lambda: [self.join(p, 2) for p in range(PARTS)] and None]

    def own(self, p):
        order = ORDERS[p][:2] if self.together else ORDERS[p]
        return self.sums.at[(p, *[self.at[axis] for axis in order])]


def scatter_scratch(rows, together=False):
    lead = (PARTS, 4, 4, 4)
    last = (PARTS, 4, 4, rows, LANES) if together else (PARTS, 3, rows, LANES)
    return [pltpu.VMEM(lead + (rows, LANES), BF), pltpu.VMEM(lead + (rows, LANES), BF),
            pltpu.VMEM((PARTS, 3, 4, 4, rows, LANES), BF), pltpu.VMEM((PARTS, 3, 4, rows, LANES), BF),
            pltpu.VMEM(last, BF), pltpu.SemaphoreType.DMA((1,))]


class Gather:
    def __init__(self, name, at, sends, parts, together=False):
        self.name, self.at, self.sends, self.parts, self.together = name, at, sends, parts, together

    def place(self, p, s, turn):
        return (self.at[self.parts[p][1][s]] + turn) % 4

    def block(self, p, s, turn):
        ref, order = self.parts[p]
        lead = [self.at[order[n]] for n in range(s)]
        return ref.at[(self.at["core"], *lead, self.place(p, s, turn))]

    def own(self, p):
        ref, order = self.parts[p]
        order = order[:2] if self.together else order
        return ref.at[(self.at["core"], *[self.at[axis] for axis in order])]

    def send(self, s):
        for turn in (2, 1, 3):
            for p in range(len(self.parts)):
                def make(p=p, turn=turn):
                    ref = self.block(p, s, 0)
                    return ref, ref, self.parts[p][1][s], self.place(p, s, turn)

                self.sends.start((self.name, s, p, turn), make)

    def arrived(self, s, *turns):
        for turn in turns:
            for p in range(len(self.parts)):
                self.sends.arrived((self.name, s, p, turn))

    def across(self, turn):
        for p in range(len(self.parts)):
            def make(p=p):
                ref = self.block(p, 0, turn)
                return ref, ref, "core", 1 - self.at["core"]

            self.sends.start((self.name, 3, p, turn), make)

    def steps(self):
        def onward(s):
            self.arrived(s + 1, 1, 3, 2)
            self.send(s)

        def near():
            onward(0)
            self.across(0)

        def more():
            self.arrived(0, 1)
            self.across(3)
            self.arrived(0, 3)
            self.across(1)

        def rest():
            self.arrived(0, 2)
            self.across(2)

        first = [lambda: self.send(1)] if self.together else [lambda: self.send(2), lambda: onward(1)]
        return first + [near, more, rest, lambda: self.arrived(3, 0, 3, 1, 2)]


def steps_in(i, table):
    for turn, step in table:
        pl.when(i == turn)(step)


D = 768
HALF = 384
HIDDEN = 1536
TILE = 128
TAPW = 128
PADDED = LEN + 16
SHARED_ROWS = 6144
VMEM_BYTES = 60 << 20
SMALL_AT = 5440
SMALL_DEPTH, SMALL_FFN, SMALL_BIAS, SMALL_SEG = 0, 18, 36, 44


class Params(NamedTuple):
    hidden: jax.Array
    cotangent: jax.Array
    lengths: jax.Array
    split_at: jax.Array
    seg_table: jax.Array
    w_query: jax.Array
    b_query: jax.Array
    w_key: jax.Array
    w_value: jax.Array
    b_value: jax.Array
    w_depth: jax.Array
    w_point: jax.Array
    b_keyconv: jax.Array
    w_kernel: jax.Array
    b_kernel: jax.Array
    w_conv: jax.Array
    b_conv: jax.Array
    w_out: jax.Array
    b_out: jax.Array
    first_gain: jax.Array
    first_shift: jax.Array
    w_up: jax.Array
    b_up: jax.Array
    down_weight: jax.Array
    b_down: jax.Array
    second_gain: jax.Array
    second_shift: jax.Array


class Kept(NamedTuple):
    x_low: jax.Array
    query: jax.Array
    key_low: jax.Array
    value_low: jax.Array
    depth_low: jax.Array
    key_conv: jax.Array
    kernels: jax.Array
    conv_pad: jax.Array
    joined: jax.Array
    resid: jax.Array
    log_total: jax.Array


KEPT_SHAPES = (((LEN, D), BF), ((LEN, HALF), F32), ((LEN, HALF), BF), ((LEN, HALF), BF), ((LEN, D), BF),
               ((LEN, HALF), F32), ((PADDED, KERNEL * TAPW), F32), ((PADDED, HALF), F32), ((LEN, D), BF),
               ((LEN, D), F32))


def dims(lhs, rhs):
    return (((lhs,), (rhs,)), ((), ()))


def dot(a, b):
    return lax.dot_general(a, b, dims(1, 0), preferred_element_type=F32)


def dot_nt(a, b):
    return lax.dot_general(a, b, dims(1, 1), preferred_element_type=F32)


def dot_tn(a, b):
    return lax.dot_general(a, b, dims(0, 0), preferred_element_type=F32)


def tile_rows(i, n=TILE, start=0):
    return pl.ds(pl.multiple_of(i * n + start, 8 if start % 16 else 16), n)


def lanes_at(start, n=128):
    return pl.ds(pl.multiple_of(start, 128), n)


def rows_iota(n, width=1):
    return lax.broadcasted_iota(jnp.int32, (n, width), 0)


class Moves:
    def __init__(self, sems):
        self.sems, self.all = sems, []

    def start(self, src, dst):
        copy = pltpu.make_async_copy(src, dst, self.sems.at[len(self.all)])
        copy.start()
        self.all.append(copy)
        return copy

    def start_cat(self, layer, matrices, w_cat):
        return [self.start(ref.at[layer], w_cat.at[:, pl.ds(n * HALF, HALF)]) for n, ref in enumerate(matrices)]


def wait_all(copies):
    for copy in copies:
        copy.wait()


def my_row():
    row = lax.axis_index("grp")
    for name, size in zip(CH, (4, 4, 2, 2)):
        row = row * size + lax.axis_index(name)
    return row


def widen_matrix():
    lane = np.arange(HALF)[None, :] // HEAD
    return (np.arange(TAPW)[:, None] == lane).astype(ml_dtypes.bfloat16)


def tap_matrix():
    out = np.zeros((TAPW, KERNEL * TAPW), np.float32)
    for h in range(HEADS):
        for j in range(KERNEL):
            out[h * KERNEL + j, j * TAPW + h] = 1.0
    return out.astype(ml_dtypes.bfloat16)


def norm_stats(residual):
    mean = jnp.mean(residual, axis=-1, keepdims=True)
    center = residual - mean
    scale = lax.rsqrt(jnp.mean(center * center, axis=-1, keepdims=True) + EPSILON)
    return center * scale, scale


def norm_grad(gy, hat, scale, gain):
    d_hat = gy * gain
    mean_one = jnp.mean(d_hat, axis=-1, keepdims=True)
    mean_two = jnp.mean(d_hat * hat, axis=-1, keepdims=True)
    return scale * (d_hat - mean_one - hat * mean_two)


def gelu_both(pre):
    base = 1.0 + (0.3275911 * 0.7071067811865476) * jnp.abs(pre)
    t = pl.reciprocal(base, approx=True)
    t = t * (2.0 - base * t)
    poly = t * (0.127414796 + t * (-0.142248368 + t * (0.7107068705 + t * (-0.7265760135 + t * 0.5307027145))))
    bell = jnp.exp(-0.5 * pre * pre)
    tail = poly * bell
    cdf = jnp.where(pre >= 0, 1.0 - tail, tail)
    return pre * cdf, cdf + pre * (bell * 0.3989422804014327)


def far():
    return pl.BlockSpec(memory_space=pl.ANY)


def whole():
    return pl.BlockSpec(memory_space=pltpu.VMEM)


def scalars():
    return pl.BlockSpec(memory_space=pltpu.SMEM)


def dma(n):
    return pltpu.SemaphoreType.DMA((n,))


def shape(dims, dtype):
    return jax.ShapeDtypeStruct(dims, dtype)


def block_shape(rows, lanes=LANES):
    return shape((PARTS, 2, 4, 4, 4, rows, lanes), BF)


def call(kernel, ins, outs, scratch, name, **comm):
    return pl.pallas_call(
        kernel,
        out_shape=[out for out, _ in outs],
        in_specs=[place for _, place in ins],
        out_specs=[place for _, place in outs],
        scratch_shapes=scratch,
        compiler_params=pltpu.CompilerParams(vmem_limit_bytes=VMEM_BYTES, **comm),
        name=name,
    )(*[array for array, _ in ins])


def remote(number):
    return {"collective_id": number, "has_side_effects": True}


def tap_weights(layer, w_kernel, rows):
    rows[...] = jnp.zeros_like(rows)
    for n in range(HEADS * KERNEL):
        rows[n : n + 1, :] = w_kernel[n].astype(F32)[layer : layer + 1, :]


def clear_edges(*refs):
    for ref in refs:
        ref[pl.ds(0, 8), :] = jnp.zeros((8, ref.shape[1]), F32)
        ref[pl.ds(LEN + 8, 8), :] = jnp.zeros((8, ref.shape[1]), F32)


def attention_forward_kernel(layer, *refs):
    first = layer == 0
    (lengths, splits, x_in, seg, w_query, w_key, w_value, w_conv, w_point, w_out, w_depth, w_kernel, b_query, b_value,
     b_conv, b_keyconv, b_kernel, b_out, widen, spread, pieces) = refs[:21]
    kept_out, log_total, gathered, refs = refs[21:31], refs[31], refs[32], refs[33:]
    if first:
        bias_all, refs = refs[0], refs[1:]
    kept, refs = refs[:10], refs[10:]
    x_low, query, key_low, value_low, depth_low, key_conv, kernels, conv_pad, joined, resid = kept
    (x_all, hidden, w_cat, point, out_w, x_pad, query_low, mixed_low, tap_rows, taps_w, tap_bias, sems, send_sems,
     recv_sems) = refs
    length = lengths[my_row()]
    one = slice(layer, layer + 1)
    at = here()
    greet(at)
    moves = Moves(sems)
    load_x = moves.start(x_in, hidden if first else x_all)
    load_cat = moves.start_cat(layer, (w_query, w_key, w_value, w_conv), w_cat)
    load_rest = [moves.start(w_point.at[layer], point), moves.start(w_out.at[layer], out_w)]
    sends = Sends(send_sems, recv_sems)
    parts = [(gathered.at[p], ORDERS[p]) for p in range(PARTS)]
    mine = [pieces.at[layer * PARTS + p] for p in range(PARTS)]
    if first:
        parts.append((bias_all, ORDERS[0]))
        mine.append(pieces.at[LAYERS * PARTS, :, pl.ds(0, TAPW)])
    gather = Gather(0, at, sends, parts)
    steps = gather.steps()
    wait_all([moves.start(src, gather.own(p)) for p, src in enumerate(mine)])
    met()
    steps[0]()

    clear_edges(x_pad, conv_pad, kernels)
    tap_weights(layer, w_kernel, tap_rows)
    for c in range(0, KERNEL * TAPW, 384):
        taps_w[:, c : c + 384] = dot_tn(tap_rows[...].astype(BF), spread[:, c : c + 384]).astype(BF)
    tap_bias[...] = jnp.zeros_like(tap_bias)
    tap_bias[0:1, 0 : HEADS * KERNEL] = b_kernel[one, :]
    left, bias = tap_bias[:, :TAPW], jnp.zeros((8, KERNEL * TAPW), F32)
    for _ in range(3):
        bias += dot(left.astype(BF), spread[...])
        left = left - left.astype(BF).astype(F32)
    tap_bias[...] = bias

    load_x.wait()

    @pl.loop(0, LEN // TILE)
    def enter(i):
        rows = tile_rows(i)
        if first:
            place = rows_iota(TILE) + i * TILE
            x = hidden[rows, :].astype(F32) + jnp.where(place > splits[my_row()], seg[1:2, :], seg[0:1, :])
            x = x * (place < length).astype(F32)
            x_all[rows, :] = x
        else:
            x = x_all[rows, :]
        low = x.astype(BF)
        x_low[rows, :] = low
        x_pad[tile_rows(i, TILE, 8), :] = low.astype(F32)

    steps[1]()
    wait_all(load_cat)
    for n in range(6):
        proj = dot(x_low[...], w_cat[:, n * 256 : n * 256 + 256])
        for h in range(2):
            which, c = (2 * n + h) // 3, (2 * n + h) % 3 * 128
            cols = slice(c, c + 128)
            part = proj[:, h * 128 : h * 128 + 128]
            if which == 0:
                part += b_query[one, cols]
                query[:, cols] = part
                query_low[:, cols] = part.astype(BF)
            elif which == 1:
                key_low[:, cols] = part.astype(BF)
            elif which == 2:
                value_low[:, cols] = (part + b_value[one, cols]).astype(BF)
            else:
                conv_pad[pl.ds(8, LEN), cols] = part + b_conv[one, cols]
    steps[2]()
    stores = [moves.start(kept[n], kept_out[n]) for n in (0, 1, 2, 3, 7)]

    @pl.loop(0, LEN // TILE)
    def depth(i):
        rows = tile_rows(i)
        around = pl.ds(pl.multiple_of(i * TILE, TILE), TILE + 16)
        for c in range(0, D, 256):
            window = x_pad[around, c : c + 256]
            total = jnp.zeros((TILE, 256), F32)
            for j in range(KERNEL):
                total += w_depth[j, one, c : c + 256].astype(F32) * window[4 + j : 4 + j + TILE]
            depth_low[rows, c : c + 256] = total.astype(BF)

    wait_all(load_rest)
    for c, n in ((0, 256), (256, 128)):
        cols = slice(c, c + n)
        key = dot(depth_low[...], point[:, cols]) + b_keyconv[one, cols]
        key_conv[:, cols] = key
        mixed_low[:, cols] = (key * query[:, cols]).astype(BF)
    for c in range(0, KERNEL * TAPW, 384):
        cols = slice(c, c + 384)
        kernels[pl.ds(8, LEN), cols] = dot(mixed_low[...], taps_w[:, cols]) + tap_bias[0:1, cols]
    steps[3]()
    stores += [moves.start(kept[n], kept_out[n]) for n in (4, 5)]

    @pl.loop(0, LEN // TILE)
    def convolve(i):
        rows = tile_rows(i)
        around = pl.ds(pl.multiple_of(i * TILE, TILE), TILE + 16)
        padded = tile_rows(i, TILE, 8)
        taps = [kernels[padded, j * TAPW : (j + 1) * TAPW] for j in range(KERNEL)]
        peak = functools.reduce(jnp.maximum, taps)
        taps = [jnp.exp(t - peak) for t in taps]
        share = 1.0 / sum(taps)
        window = conv_pad[around, :]
        mix = jnp.zeros((TILE, HALF), F32)
        for j in range(KERNEL):
            tap = taps[j] * share
            kernels[padded, j * TAPW : (j + 1) * TAPW] = tap
            mix += dot(tap.astype(BF), widen[...]) * window[4 + j : 4 + j + TILE]
        joined[rows, HALF:] = mix.astype(BF)

    steps[4]()
    stores += [moves.start(kept[6], kept_out[6])]

    @pl.loop(0, HEADS // 2)
    def attend(pair):
        lanes = lanes_at(pair * 128)
        keys = key_low[:, lanes] * jnp.asarray(SCORE_SCALE, BF)
        side = lax.broadcasted_iota(jnp.int32, (LEN, 128), 1) // HEAD
        values = jnp.transpose(value_low[:, lanes].astype(F32)).astype(BF)
        for block in range(2):
            cols = slice(block * 256, block * 256 + 256)
            queries = query_low[cols, lanes]
            pieces_t = []
            for head in range(2):
                mine = jnp.where(side == head, keys, jnp.zeros_like(keys))
                scores = dot_nt(mine, queries)
                scores = jnp.where(rows_iota(LEN, 256) < length, scores, MASK_VALUE)
                peak = jnp.max(scores, axis=0, keepdims=True)
                probs = jnp.exp(scores - peak)
                total = jnp.sum(probs, axis=0, keepdims=True)
                log_total[pair * 2 + head, :, cols] = peak + jnp.log(total)
                probs = (probs * (1.0 / total)).astype(BF)
                pieces_t.append(dot(values[head * HEAD : (head + 1) * HEAD, :], probs))
            joined[cols, lanes] = jnp.transpose(jnp.concatenate(pieces_t, axis=0)).astype(BF)

    stores += [moves.start(kept[8], kept_out[8])]
    steps[5]()
    for c in range(0, D, 256):
        cols = slice(c, c + 256)
        resid[:, cols] = x_all[:, cols] + dot(joined[...], out_w[:, cols]) + b_out[one, cols]
    stores += [moves.start(kept[9], kept_out[9])]
    wait_all(stores)
    sends.finish()


def attention_forward(layer, x, pieces, w):
    ins = [(w.lengths, scalars()), (w.split_at, scalars()), (x, far()), (w.seg_table, whole())]
    ins += [(m, far()) for m in (w.w_query, w.w_key, w.w_value, w.w_conv, w.w_point, w.w_out)]
    ins += [(m, whole()) for m in (w.w_depth, w.w_kernel, w.b_query, w.b_value, w.b_conv, w.b_keyconv, w.b_kernel,
                                   w.b_out, widen_matrix(), tap_matrix())]
    ins += [(pieces, far())]
    outs = [(shape(*s), far()) for s in KEPT_SHAPES]
    outs += [(shape((HEADS, 1, LEN), F32), whole()), (block_shape(16), far())]
    if layer == 0:
        outs += [(shape((2, 4, 4, 4, 16, TAPW), BF), far())]
    scratch = [pltpu.VMEM(*s) for s in KEPT_SHAPES]
    scratch += [pltpu.VMEM((LEN, D), F32), pltpu.VMEM((LEN, D), BF), pltpu.VMEM((D, 4 * HALF), BF),
                pltpu.VMEM((D, HALF), BF), pltpu.VMEM((D, D), BF), pltpu.VMEM((PADDED, D), F32),
                pltpu.VMEM((LEN, HALF), BF), pltpu.VMEM((LEN, HALF), BF), pltpu.VMEM((TAPW, HALF), F32),
                pltpu.VMEM((HALF, KERNEL * TAPW), BF), pltpu.VMEM((8, KERNEL * TAPW), F32), dma(24), dma(64), dma(64)]
    return call(functools.partial(attention_forward_kernel, layer), ins, outs, scratch, "fa", **remote(1 + layer))


def part_block(ref, p, core, x, y, z):
    if p == 0:
        return ref.at[0, core, x, y, z]
    if p == 1:
        return ref.at[1, core, y, z, x]
    return ref.at[2, core, z, x, y]


def ffn_forward_kernel(layer, *refs):
    (lengths, resid_in, gathered_in, bias_all, first_gain, first_shift, b_down, second_gain, second_shift) = refs[:9]
    outs, (up, down, acted, slope, resid_two, x_next), refs = refs[9:15], refs[15:21], refs[21:]
    resid, gathered, low, pre, bias_rows, bias, sems = refs
    one = slice(layer, layer + 1)
    length = lengths[my_row()]
    moves = Moves(sems)
    load = moves.start(resid_in, resid)
    load_weights = moves.start(gathered_in, gathered)
    load.wait()

    @pl.loop(0, LEN // TILE)
    def enter(i):
        rows = tile_rows(i)
        hat, _ = norm_stats(resid[rows, :])
        normed = hat * first_gain[one, :] + first_shift[one, :]
        resid[rows, :] = normed
        low[rows, :] = normed.astype(BF)

    load_weights.wait()

    @pl.loop(0, 64)
    def unpack(chip):
        z, y, x = (chip // 32) * 2 + chip % 2, (chip // 8) % 4, (chip // 2) % 4
        ups, downs = [], []
        for core in range(2):
            piece = jnp.concatenate(
                [part_block(gathered, p, core, x, y, z)[...].astype(F32) for p in range(PARTS)], axis=0)
            ups.append(piece[:24])
            downs.append(piece[24:])
            bias_rows[core, pl.ds(chip, 1), :] = bias_all[core, x, y, z].astype(F32)[one, :]
        rows = tile_rows(chip, 48)
        up[rows, :] = jnp.concatenate(ups, axis=0).astype(BF)
        down[rows, :] = jnp.concatenate(downs, axis=0).astype(BF)

    stores = [moves.start(up, outs[0]), moves.start(down, outs[1])]
    for c in range(0, 2 * HIDDEN, 512):
        spot = lax.broadcasted_iota(jnp.int32, (64, 512), 1) + c
        slot = (lax.broadcasted_iota(jnp.int32, (TAPW, 512), 1) + c) % 24
        repeat = (slot == rows_iota(TAPW, 512)).astype(F32).astype(BF)
        total = jnp.zeros((1, 512), F32)
        for core in range(2):
            spread = dot(bias_rows[core].astype(BF), repeat)
            mine = spot // 24 == 2 * rows_iota(64, 512) + core
            total += jnp.sum(jnp.where(mine, spread, 0.0), axis=0, keepdims=True)
        bias[:, c : c + 512] = total

    for g in range(2):
        @pl.loop(0, HIDDEN // 512)
        def feed(k):
            at = g * HIDDEN + k * 512
            hidden = pl.ds(pl.multiple_of(at, 512), 512)
            pre[...] = dot_nt(low[:, g * HALF : (g + 1) * HALF], up[hidden, :]) + bias[:, hidden]

            @pl.loop(0, LEN // 32)
            def act(i):
                few = tile_rows(i, 32)
                for c in range(0, 512, 256):
                    value, grad = gelu_both(pre[few, c : c + 256])
                    cols = lanes_at(at + c, 256)
                    acted[few, cols] = value.astype(BF)
                    slope[few, cols] = grad.astype(BF)

    stores += [moves.start(acted, outs[2]), moves.start(slope, outs[3])]

    @pl.loop(0, LEN // 256)
    def leave(i):
        rows = tile_rows(i, 256)
        out = []
        for g in range(2):
            hidden = slice(g * HIDDEN, (g + 1) * HIDDEN)
            out.append(dot(acted[rows, hidden], down[hidden, :]).astype(BF).astype(F32))
        two = resid[rows, :] + jnp.concatenate(out, axis=1) + b_down[one, :]
        resid_two[rows, :] = two
        hat, _ = norm_stats(two)
        valid = (rows_iota(256) + i * 256 < length).astype(F32)
        x_next[rows, :] = (hat * second_gain[one, :] + second_shift[one, :]) * valid

    stores += [moves.start(resid_two, outs[4]), moves.start(x_next, outs[5])]
    wait_all(stores)


def ffn_forward(layer, resid, gathered, bias, w):
    ins = [(w.lengths, scalars()), (resid, far()), (gathered, far())]
    ins += [(m, whole()) for m in (bias, w.first_gain, w.first_shift, w.b_down, w.second_gain, w.second_shift)]
    shapes = [((2 * HIDDEN, HALF), BF)] * 2 + [((LEN, 2 * HIDDEN), BF)] * 2 + [((LEN, D), F32)] * 2
    outs = [(shape(*s), far()) for s in shapes]
    scratch = [pltpu.VMEM(*s) for s in shapes]
    scratch += [pltpu.VMEM((LEN, D), F32), pltpu.VMEM(block_shape(16).shape, BF), pltpu.VMEM((LEN, D), BF),
                pltpu.VMEM((LEN, 512), F32), pltpu.VMEM((2, 64, TAPW), F32), pltpu.VMEM((1, 2 * HIDDEN), F32), dma(8)]
    return call(functools.partial(ffn_forward_kernel, layer), ins, outs, scratch, "ff")


def ffn_backward_kernel(layer, *refs):
    comm = layer == 0
    lengths, ins, (first_gain, first_shift, second_gain), refs = refs[0], refs[1:8], refs[8:11], refs[11:]
    if comm:
        above, refs = refs[0], refs[1:]
    d_resid_out, grads_out, small, refs = *refs[:3], refs[3:]
    if comm:
        own, refs = refs[0], refs[1:]
    (gy, resid_two, resid, slope, down, up, acted), refs = refs[:7], refs[7:]
    (d_resid, grads, d_two, d_pre, d_group, normed_low, sems), refs = refs[:7], refs[7:]
    one = slice(layer, layer + 1)
    length = lengths[my_row()]
    moves = Moves(sems)
    loads = [moves.start(src, dst) for src, dst in zip(ins, (gy, resid_two, resid, slope, down, up, acted))]
    steps = [lambda: None] * 8
    if comm:
        scratch, (send_sems, recv_sems) = refs[:6], refs[6:]
        at = here()
        greet(at)
        sends = Sends(send_sems, recv_sems)
        scatter = Scatter(0, at, sends, above, scratch, together=True)
        steps = scatter.steps()
        met()
    steps[0]()
    small[...] = jnp.zeros_like(small)

    def note(slot, value):
        total = jnp.sum(value, axis=0, keepdims=True)
        small[slot : slot + 1, :] += total[:, :HALF]
        small[slot + 1 : slot + 2, :] += total[:, HALF:]

    wait_all(loads[:3])

    @pl.loop(0, LEN // TILE)
    def enter(i):
        rows = tile_rows(i)
        valid = (rows_iota(TILE) + i * TILE < length).astype(F32)
        grad = gy[rows, :].astype(F32) * valid
        hat, scale = norm_stats(resid_two[rows, :])
        note(0, grad * hat)
        note(2, grad)
        two = norm_grad(grad, hat, scale, second_gain[one, :])
        note(4, two)
        d_two[rows, :] = two
        d_group[rows, :] = two.astype(BF)
        hat, _ = norm_stats(resid[rows, :])
        normed_low[rows, :] = (hat * first_gain[one, :] + first_shift[one, :]).astype(BF)

    steps[1]()
    wait_all(loads[3:5])
    for g in range(2):
        @pl.loop(0, HIDDEN // 256)
        def feed(k):
            hidden = pl.ds(pl.multiple_of(g * HIDDEN + k * 256, 256), 256)
            d_act = dot_nt(d_group[:, g * HALF : (g + 1) * HALF], down[hidden, :])
            d_pre[:, hidden] = (d_act * slope[:, hidden].astype(F32)).astype(BF)

        steps[2 + g]()

    wait_all(loads[5:])

    @pl.loop(0, LEN // 256)
    def back(i):
        rows = tile_rows(i, 256)
        got = []
        for g in range(2):
            hidden = slice(g * HIDDEN, (g + 1) * HIDDEN)
            got.append(dot(d_pre[rows, hidden], up[hidden, :]).astype(BF).astype(F32))
        d_normed = d_two[rows, :] + jnp.concatenate(got, axis=1)
        hat, scale = norm_stats(resid[rows, :])
        note(6, d_normed * hat)
        note(8, d_normed)
        d_resid[rows, :] = norm_grad(d_normed, hat, scale, first_gain[one, :])

    stores = [moves.start(d_resid, d_resid_out)]
    steps[4]()
    ones = jnp.ones((8, LEN), BF)
    for k in range(8):
        small[10 + k : 11 + k, :] = dot(ones, d_pre[:, k * HALF : (k + 1) * HALF])[0:1, :]

    for g in range(2):
        @pl.loop(0, 4)
        def grad(y):
            steps_in(y, ((1 + g, steps[5 + g]),))
            hidden = lanes_at(g * HIDDEN + y * HALF, HALF)
            cols = slice(g * HALF, (g + 1) * HALF)
            d_up = dot_tn(d_pre[:, hidden], normed_low[:, cols])
            d_down = dot_tn(acted[:, hidden], d_group[:, cols])
            for d in range(16):
                x, z, core = d // 4, g * 2 + (d // 2) % 2, d % 2
                piece = jnp.concatenate([d_up[24 * d : 24 * d + 24], d_down[24 * d : 24 * d + 24]], axis=0).astype(BF)
                for p in range(PARTS):
                    part_block(grads, p, core, x, y, z)[...] = piece[16 * p : 16 * p + 16]

        zs = pl.ds(2 * g, 2)
        for index in ((0, slice(None), slice(None), slice(None), zs), (1, slice(None), slice(None), zs),
                      (2, slice(None), zs)):
            stores.append(moves.start(grads.at[index], grads_out.at[index]))

    steps[7]()
    if comm:
        for p in range(PARTS):
            own[p] = scatter.own(p)[...]
        sends.finish()
    wait_all(stores)


def ffn_backward(layer, gy, kept, ffn, above, w):
    up, down, acted, slope, resid_two = ffn
    ins = [(w.lengths, scalars())] + [(m, far()) for m in (gy, resid_two, kept.resid, slope, down, up, acted)]
    ins += [(m, whole()) for m in (w.first_gain, w.first_shift, w.second_gain)]
    outs = [(shape((LEN, D), F32), far()), (block_shape(16), far()), (shape((32, HALF), F32), whole())]
    scratch = [pltpu.VMEM(m.shape, m.dtype) for m in (gy, resid_two, kept.resid, slope, down, up, acted)]
    scratch += [pltpu.VMEM((LEN, D), F32), pltpu.VMEM(block_shape(16).shape, BF), pltpu.VMEM((LEN, D), F32),
                pltpu.VMEM((LEN, 2 * HIDDEN), BF), pltpu.VMEM((LEN, D), BF), pltpu.VMEM((LEN, D), BF), dma(16)]
    comm = {}
    if layer == 0:
        ins += [(above, far())]
        outs += [(shape((PARTS, 4, 16, LANES), BF), whole())]
        scratch += scatter_scratch(16, True) + [dma(48), dma(48)]
        comm = remote(3)
    return call(functools.partial(ffn_backward_kernel, layer), ins, outs, scratch, "bf", **comm)


def attention_backward_kernel(layer, *refs):
    first = layer == 0
    (lengths, splits, d_resid_in), kept_in, log_total, refs = refs[:3], refs[3:12], refs[12], refs[13:]
    (ffn_small, w_query, w_key, w_value, w_conv, w_point, w_out, w_depth, w_kernel, widen, spread, ffn_grads) = refs[:12]
    refs = refs[12:]
    if first:
        above_own, refs = refs[0], refs[1:]
    d_input_out, shared_out, own, refs = *refs[:3], refs[3:]
    if first:
        above_all, refs = refs[0], refs[1:]
    d_resid, kept, d_input, shared, refs = refs[0], refs[1:10], refs[10], refs[11], refs[12:]
    x_low, query, key_low, value_low, depth_low, key_conv, kernels, conv_pad, joined = kept
    (w_cat, point, out_w, d_proj, d_cat, d_join, query_low, d_att, mix_pad, depth_pad, small, d_tap, tap_rows,
     sems) = refs[:14]
    scratch, (send_sems, recv_sems) = refs[14:20], refs[20:]
    length = lengths[my_row()]
    at = here()
    greet(at)
    moves = Moves(sems)
    load_first = [moves.start(d_resid_in, d_resid), moves.start(w_out.at[layer], out_w)]
    load = [moves.start(kept_in[n], kept[n]) for n in (8, 1, 2, 3, 6, 7, 5, 4, 0)]
    load_cat = moves.start_cat(layer, (w_query, w_key, w_value, w_conv), w_cat)
    load_point = moves.start(w_point.at[layer], point)
    sends = Sends(send_sems, recv_sems)
    scatter = Scatter(0, at, sends, ffn_grads, scratch)
    steps = scatter.steps()
    more = [lambda: None] * 5
    if first:
        gather = Gather(1, at, sends, [(above_all.at[p], ORDERS[p]) for p in range(PARTS)], together=True)
        more = gather.steps()
        wait_all([moves.start(above_own.at[p], gather.own(p)) for p in range(PARTS)])
    met()
    steps[0]()
    more[0]()
    clear_edges(mix_pad, depth_pad)
    small[...] = jnp.zeros_like(small)
    small[SMALL_FFN : SMALL_FFN + 18, :] = ffn_small[0:18, :]
    shared[SMALL_AT + 64 :, :] = jnp.zeros((SHARED_ROWS - SMALL_AT - 64, HALF), BF)
    tap_weights(layer, w_kernel, tap_rows)

    def note(slot, value):
        total = jnp.sum(value, axis=0, keepdims=True)
        for n in range(total.shape[1] // HALF):
            small[slot + n : slot + n + 1, :] += total[:, n * HALF : (n + 1) * HALF]

    wait_all(load_first)

    @pl.loop(0, LEN // TILE)
    def enter(i):
        rows = tile_rows(i)
        low = d_resid[rows, :].astype(BF)
        d_proj[rows, :] = low
        note(SMALL_BIAS + 5, low.astype(F32))

    for c in range(0, D, 256):
        d_join[:, c : c + 256] = dot_nt(d_proj[...], out_w[c : c + 256, :]).astype(BF)
    mix_pad[pl.ds(8, LEN), :] = d_join[:, HALF:].astype(F32)
    steps[1]()
    load[0].wait()

    @pl.loop(0, D // 256)
    def out_grad(c):
        part = dot_tn(joined[:, lanes_at(c * 256, 256)], d_proj[...])
        for n in range(2):
            shared[pl.ds(pl.multiple_of(3840 + n * D + c * 256, 16), 256), :] = part[:, n * HALF : (n + 1) * HALF].astype(BF)

    steps[2]()
    steps[3]()
    wait_all(load[1:4])
    query_low[...] = query[...].astype(BF)

    @pl.loop(0, HEADS // 2)
    def attend(pair):
        steps_in(pair, ((1, steps[4]), (2, steps[5])) + (((1, more[1]), (2, more[2])) if first else ()))
        lanes = lanes_at(pair * 128)
        keys = key_low[:, lanes]
        values = value_low[:, lanes]
        scaled = keys * jnp.asarray(SCORE_SCALE, BF)
        keys_t = jnp.transpose(keys.astype(F32)).astype(BF)
        side = lax.broadcasted_iota(jnp.int32, (LEN, 128), 1) // HEAD
        nothing = jnp.zeros_like(keys)
        d_keys = [None, None]
        d_values = [None, None]
        for block in range(2):
            cols = slice(block * 256, block * 256 + 256)
            queries = query_low[cols, lanes]
            d_context = d_join[cols, lanes]
            pieces = []
            for head in range(2):
                scores = dot_nt(jnp.where(side == head, scaled, nothing), queries)
                scores = jnp.where(rows_iota(LEN, 256) < length, scores, MASK_VALUE)
                probs = jnp.exp(scores - log_total[pair * 2 + head, :, cols])
                d_probs = dot_nt(jnp.where(side == head, values, nothing), d_context)
                weighted = probs * d_probs
                row_dot = jnp.sum(weighted, axis=0, keepdims=True)
                d_scores = (weighted - probs * row_dot).astype(BF)
                pieces.append(dot(keys_t[head * HEAD : (head + 1) * HEAD, :], d_scores))
                part = dot(d_scores, queries)
                d_keys[head] = part if block == 0 else d_keys[head] + part
                part = dot(probs.astype(BF), d_context)
                d_values[head] = part if block == 0 else d_values[head] + part
            d_att[cols, lanes] = jnp.transpose(jnp.concatenate(pieces, axis=0)) * SCORE_SCALE
        d_cat[:, lanes_at(HALF + pair * 128)] = (jnp.where(side == 0, d_keys[0], d_keys[1]) * SCORE_SCALE).astype(BF)
        d_cat[:, lanes_at(2 * HALF + pair * 128)] = jnp.where(side == 0, d_values[0], d_values[1]).astype(BF)

    steps[6]()
    wait_all(load[4:7])

    @pl.loop(0, LEN // TILE)
    def taps(i):
        rows = tile_rows(i)
        around = pl.ds(pl.multiple_of(i * TILE, TILE), TILE + 16)
        padded = tile_rows(i, TILE, 8)
        mix = mix_pad[padded, :]
        window = conv_pad[around, :]
        mix_window = mix_pad[around, :]
        d_kernel, d_conv = [], jnp.zeros((TILE, HALF), F32)
        dotted = jnp.zeros((TILE, TAPW), F32)
        for j in range(KERNEL):
            part = dot_nt((mix * window[4 + j : 4 + j + TILE]).astype(BF), widen[...])
            d_kernel.append(part)
            dotted += part * kernels[padded, j * TAPW : (j + 1) * TAPW]
            share = kernels[around, j * TAPW : (j + 1) * TAPW][12 - j : 12 - j + TILE]
            d_conv += dot(share.astype(BF), widen[...]) * mix_window[12 - j : 12 - j + TILE]
        d_cat[rows, 3 * HALF :] = d_conv.astype(BF)
        wide = [kernels[padded, j * TAPW : (j + 1) * TAPW] * (d_kernel[j] - dotted) for j in range(KERNEL)]
        d_logit = dot_nt(jnp.concatenate(wide, axis=1).astype(BF), spread[...]).astype(BF)
        d_tap[rows, :] = d_logit
        d_mixed = dot(d_logit, tap_rows[...].astype(BF))
        q = query[rows, :]
        key = key_conv[rows, :]
        d_keyconv = (d_mixed * q).astype(BF)
        d_cat[rows, :HALF] = (d_att[rows, :] + d_mixed * key).astype(BF)
        note(SMALL_BIAS + 2, d_keyconv.astype(F32))
        cat = d_cat[rows, :].astype(F32)
        note(SMALL_BIAS, cat[:, :HALF])
        note(SMALL_BIAS + 1, cat[:, 2 * HALF : 3 * HALF])
        note(SMALL_BIAS + 3, cat[:, 3 * HALF :])
        small[SMALL_BIAS + 4 : SMALL_BIAS + 5, :TAPW] += jnp.sum(d_logit.astype(F32), axis=0, keepdims=True)
        d_join[rows, HALF:] = d_keyconv
        d_join[rows, :HALF] = (key * q).astype(BF)

    steps[7]()
    more[3]()
    shared[5376:5440, :] = dot_tn(d_tap[...], d_join[:, :HALF])[:64].astype(BF)
    load_point.wait()
    for c in range(0, D, 256):
        depth_pad[pl.ds(8, LEN), c : c + 256] = dot_nt(d_join[:, HALF:], point[c : c + 256, :])
    wait_all(load[7:])

    @pl.loop(0, D // 256)
    def point_grad(c):
        part = dot_tn(depth_low[:, lanes_at(c * 256, 256)], d_join[:, HALF:])
        shared[pl.ds(pl.multiple_of(3072 + c * 256, 16), 256), :] = part.astype(BF)

    more[4]()

    @pl.loop(0, D // 256)
    def cat_grad(c):
        low = x_low[:, lanes_at(c * 256, 256)]
        for n in range(4):
            part = dot_tn(low, d_cat[:, n * HALF : (n + 1) * HALF])
            shared[pl.ds(pl.multiple_of(n * D + c * 256, 16), 256), :] = part.astype(BF)

    wait_all(load_cat)
    store = moves.start(shared.at[pl.ds(0, SMALL_AT)], shared_out.at[pl.ds(0, SMALL_AT)])
    for n in range(3):
        cols = slice(n * 256, n * 256 + 256)
        d_input[:, cols] = d_resid[:, cols] + dot_nt(d_cat[...], w_cat[cols, :])

        @pl.loop(0, LEN // TILE)
        def leave(i):
            rows = tile_rows(i)
            window = depth_pad[pl.ds(pl.multiple_of(i * TILE, TILE), TILE + 16), cols]
            low = x_low[rows, cols].astype(F32)
            total = d_input[rows, cols]
            for j in range(KERNEL):
                moved = window[12 - j : 12 - j + TILE]
                total += w_depth[j, layer : layer + 1, cols].astype(F32) * moved
                tap = jnp.sum(low * moved, axis=0, keepdims=True)
                if n == 0:
                    small[SMALL_DEPTH + j : SMALL_DEPTH + j + 1, 0:256] += tap
                elif n == 1:
                    small[SMALL_DEPTH + j : SMALL_DEPTH + j + 1, 256:] += tap[:, :128]
                    small[SMALL_DEPTH + 9 + j : SMALL_DEPTH + 10 + j, :128] += tap[:, 128:]
                else:
                    small[SMALL_DEPTH + 9 + j : SMALL_DEPTH + 10 + j, 128:] += tap
            d_input[rows, cols] = total

    if first:
        @pl.loop(0, LEN // TILE)
        def seg_grad(i):
            rows = tile_rows(i)
            place = rows_iota(TILE) + i * TILE
            grad = d_input[rows, :] * (place < length).astype(F32)
            later = (place > splits[my_row()]).astype(F32)
            note(SMALL_SEG + 2, grad * later)
            note(SMALL_SEG, grad * (1.0 - later))
            d_input[rows, :] = grad

    shared[SMALL_AT : SMALL_AT + 64, :] = small[...].astype(BF)
    stores = [store, moves.start(d_input, d_input_out),
              moves.start(shared.at[pl.ds(SMALL_AT, SHARED_ROWS - SMALL_AT)],
                          shared_out.at[pl.ds(SMALL_AT, SHARED_ROWS - SMALL_AT)])]
    for p in range(PARTS):
        own[p] = scatter.own(p)[...]

    sends.finish()
    wait_all(stores)


def attention_backward(layer, d_resid, ffn_small, ffn_grads, above_own, kept, w):
    ins = [(w.lengths, scalars()), (w.split_at, scalars()), (d_resid, far())] + [(m, far()) for m in kept[:9]]
    ins += [(kept.log_total, whole()), (ffn_small, whole())]
    ins += [(m, far()) for m in (w.w_query, w.w_key, w.w_value, w.w_conv, w.w_point, w.w_out)]
    ins += [(m, whole()) for m in (w.w_depth, w.w_kernel, widen_matrix(), tap_matrix())] + [(ffn_grads, far())]
    outs = [(shape((LEN, D), F32), far()), (shape((SHARED_ROWS, HALF), BF), far()),
            (shape((PARTS, 16, LANES), BF), whole())]
    if layer == 0:
        ins += [(above_own, far())]
        outs += [(block_shape(16), far())]
    scratch = [pltpu.VMEM((LEN, D), F32)] + [pltpu.VMEM(*s) for s in KEPT_SHAPES[:9]]
    scratch += [pltpu.VMEM((LEN, D), F32), pltpu.VMEM((SHARED_ROWS, HALF), BF), pltpu.VMEM((D, 4 * HALF), BF),
                pltpu.VMEM((D, HALF), BF), pltpu.VMEM((D, D), BF), pltpu.VMEM((LEN, D), BF),
                pltpu.VMEM((LEN, 4 * HALF), BF), pltpu.VMEM((LEN, D), BF), pltpu.VMEM((LEN, HALF), BF),
                pltpu.VMEM((LEN, HALF), F32), pltpu.VMEM((PADDED, HALF), F32), pltpu.VMEM((PADDED, D), F32),
                pltpu.VMEM((64, HALF), F32), pltpu.VMEM((LEN, TAPW), BF), pltpu.VMEM((TAPW, HALF), F32), dma(24)]
    scratch += scatter_scratch(16) + [dma(96), dma(96)]
    return call(functools.partial(attention_backward_kernel, layer), ins, outs, scratch, "ba", **remote(4 + layer))


def last_sums_kernel(x, gathered, *refs):
    scratch, (sems, send_sems, recv_sems) = refs[:6], refs[6:]
    at = here()
    greet(at)
    sends = Sends(send_sems, recv_sems)
    scatter = Scatter(0, at, sends, x, scratch, together=True)
    gather = Gather(1, at, sends, [(gathered.at[p], ORDERS[p]) for p in range(PARTS)], together=True)
    met()
    for step in scatter.steps():
        step()
    moves = Moves(sems)
    wait_all([moves.start(scatter.own(p), gather.own(p)) for p in range(PARTS)])
    for step in gather.steps():
        step()
    sends.finish()


def last_sums(x):
    return call(last_sums_kernel, [(x, far())], [(block_shape(16), far())],
                scatter_scratch(16, True) + [dma(3), dma(96), dma(96)], "sums", **remote(6))[0]


def hand_out_kernel(shared_0, shared_1, ffn_0, ffn_1, *refs):
    (seg, w_query, b_query, w_key, w_value, b_value, w_depth, w_point, b_keyconv, w_kernel, b_kernel, w_conv, b_conv,
     w_out, b_out, first_gain, first_shift, w_up, b_up, w_down, b_down, second_gain, second_shift) = refs[:23]
    low, high, load_sems, store_sems = refs[23:]
    group = lax.axis_index("grp")
    place = my_row() - group * 64
    loads, stores = Moves(load_sems), Moves(store_sems)
    sources = (shared_0, shared_1)
    for layer in range(LAYERS):
        for n in range(8):
            rows = pl.ds(n * D, D)
            loads.start(sources[layer].at[rows], low.at[layer, rows])
    for layer in range(LAYERS):
        for n in range(7):
            loads.all[layer * 8 + n].wait()

            @pl.loop(0, D // 256)
            def widen(c):
                high[layer * 7 + n, tile_rows(c, 256), :] = low[layer, tile_rows(c + 3 * n, 256), :].astype(F32)

            out = (w_query, w_key, w_value, w_conv, w_point, w_out, w_out)[n].at[layer]
            if n >= 5:
                out = out.at[:, pl.ds((n - 5) * HALF, HALF)]
            stores.start(high.at[layer * 7 + n], out)
    smalls, taps, ups = [], [], []
    for layer, ffn in enumerate((ffn_0, ffn_1)):
        loads.all[layer * 8 + 7].wait()
        taps.append(low[layer, 5376:5440, :].astype(F32))
        smalls.append(low[layer, SMALL_AT : SMALL_AT + 64, :].astype(F32))
        rows = jnp.concatenate([ffn[p].astype(F32) for p in range(PARTS)], axis=0)
        w_up[layer, 0] = rows[:24]
        w_down[layer, 0] = rows[24:]
        mine = jnp.sum(jnp.where(rows_iota(8, HALF) == group * 4 + place // 16,
                                 smalls[layer][SMALL_FFN + 10 : SMALL_FFN + 18], 0.0), axis=0, keepdims=True)
        mine = jnp.broadcast_to(mine, (8, HALF))
        b_up[layer] = pltpu.roll(mine, (HALF - (place % 16) * 24) % HALF, 1)[:1, :24]

    def both(start, n=1):
        return jnp.concatenate(
            [jnp.concatenate([s[start + k : start + k + 1] for k in range(n)], axis=1) for s in smalls], axis=0)

    for j in range(KERNEL):
        w_depth[j] = jnp.concatenate([both(SMALL_DEPTH + j), both(SMALL_DEPTH + 9 + j)], axis=1)
    for j in range(HEADS * KERNEL):
        w_kernel[j] = jnp.concatenate([t[j : j + 1] for t in taps], axis=0)
    for n, out in enumerate((second_gain, second_shift, b_down, first_gain, first_shift)):
        out[...] = both(SMALL_FFN + 2 * n, 2)
    for n, out in enumerate((b_query, b_value, b_keyconv, b_conv)):
        out[...] = both(SMALL_BIAS + n)
    b_kernel[...] = both(SMALL_BIAS + 4)[:, : HEADS * KERNEL]
    b_out[...] = both(SMALL_BIAS + 5, 2)
    for n in range(2):
        s = smalls[0][SMALL_SEG + 2 * n : SMALL_SEG + 2 * n + 2]
        seg[n : n + 1, :] = jnp.concatenate([s[0:1], s[1:2]], axis=1)
    wait_all(stores.all)


def hand_out(shared, ffn):
    proj, half_row, full_row = (LAYERS, D, HALF), (LAYERS, HALF), (LAYERS, D)
    shapes = [(2, D), proj, half_row, proj, proj, half_row, (KERNEL, LAYERS, D), proj, half_row,
              (HEADS * KERNEL, LAYERS, HALF), (LAYERS, HEADS * KERNEL), proj, half_row, (LAYERS, D, D), full_row,
              full_row, full_row, (LAYERS, 1, 24, HALF), (LAYERS, 1, 24), (LAYERS, 1, 24, HALF), full_row, full_row,
              full_row]
    big = (proj, (LAYERS, D, D))
    outs = list(call(
        hand_out_kernel,
        [(m, far()) for m in shared] + [(m, whole()) for m in ffn],
        [(shape(s, F32), far() if s in big else whole()) for s in shapes],
        [pltpu.VMEM((LAYERS, SHARED_ROWS, HALF), BF), pltpu.VMEM((14, D, HALF), F32), dma(16), dma(14)],
        "hand_out",
    ))
    outs[6] = jnp.swapaxes(outs[6], 0, 1)
    outs[9] = jnp.transpose(outs[9], (1, 2, 0))
    outs[17] = jnp.swapaxes(outs[17], 2, 3)
    return tuple(outs)


def shards(*args):
    w = Params(*args)
    w = w._replace(w_depth=jnp.swapaxes(w.w_depth, 0, 1), w_kernel=jnp.transpose(w.w_kernel, (2, 0, 1)))
    pieces = jnp.concatenate([jnp.swapaxes(w.w_up[:, 0], 1, 2), w.down_weight[:, 0]], axis=1)
    bias = jnp.pad(w.b_up[:, 0], ((0, 16 - LAYERS), (0, LANES - w.b_up.shape[2])))
    pieces = jnp.concatenate([pieces.reshape(LAYERS * PARTS, 16, LANES), bias[None]])
    x, kept, ffn = w.hidden, [], []
    for layer in range(LAYERS):
        outs = attention_forward(layer, x, pieces, w)
        kept.append(Kept(*outs[:11]))
        if layer == 0:
            bias = outs[12]
        *more, x = ffn_forward(layer, kept[layer].resid, outs[11], bias, w)
        ffn.append(more)
    output, grad = x, w.cotangent
    shared, ffn_own, above, above_own = [None] * LAYERS, [None] * LAYERS, None, None
    for layer in reversed(range(LAYERS)):
        d_resid, ffn_grads, small, *own = ffn_backward(layer, grad, kept[layer], ffn[layer], above, w)
        grad, mine, ffn_own[layer], *others = attention_backward(
            layer, d_resid, small, ffn_grads, own[0] if own else None, kept[layer], w)
        above = mine.reshape(block_shape(16).shape)
        if others:
            shared[1] = others[0].reshape(SHARED_ROWS, HALF)
    shared[0] = last_sums(above).reshape(SHARED_ROWS, HALF)
    return (output, grad) + hand_out(shared, ffn_own)


def solution(mesh):
    finer = Mesh(mesh.devices.reshape(mesh.shape["grp"], 4, 4, 2, 2), GRP_CH)
    rows, up = P(GRP_CH, None), P(None, "grp", None, CH)
    bias, down = P(None, "grp", CH), P(None, "grp", CH, None)
    placed = Params(*[P()] * len(Params._fields))._replace(
        hidden=rows, cotangent=rows, w_up=up, b_up=bias, down_weight=down)
    given = [P()] * 23
    given[17:20] = [up, bias, down]
    return jax.shard_map(
        shards,
        mesh=finer,
        in_specs=tuple(placed),
        out_specs=(rows, rows, *given),
        check_vma=False,
    )
```

```python
import functools
from typing import NamedTuple

import jax
import jax.numpy as jnp
import ml_dtypes
import numpy as np
from jax import lax
from jax.experimental import pallas as pl
from jax.experimental.pallas import tpu as pltpu
from jax.sharding import Mesh
from jax.sharding import PartitionSpec as P

HEADS = 6
HEAD = 64
KERNEL = 9
LAYERS = 2
LEN = 512
CH = ("ch_0", "ch_1", "ch_2", "ch_3")
GRP_CH = ("grp",) + CH
EPSILON = 1e-06
SCORE_SCALE = 0.125
MASK_VALUE = -1000000000.0
BF, F32 = jnp.bfloat16, jnp.float32
MESH = pl.DeviceIdType.MESH
LANES = 384
PARTS = 3
ORDERS = ("xyz", "yzx", "zxy")


def here():
    x, y = lax.axis_index("ch_1"), lax.axis_index("ch_0")
    z = lax.axis_index("grp") * 2 + lax.axis_index("ch_2")
    return {"x": x, "y": y, "z": z, "core": lax.axis_index("ch_3")}


def device_at(axis, place):
    if axis == "x":
        return {"ch_1": place}
    if axis == "y":
        return {"ch_0": place}
    if axis == "z":
        return {"grp": place // 2, "ch_2": place % 2}
    return {"ch_3": place}


def greet(at):
    peers = [("core", 1 - at["core"])]
    for axis in "xyz":
        peers += [(axis, (at[axis] + turn) % 4) for turn in (1, 2, 3)]
    for axis, place in peers:
        pl.semaphore_signal(
            pltpu.get_barrier_semaphore(), inc=1, device_id=device_at(axis, place), device_id_type=MESH)


def met():
    pl.semaphore_wait(pltpu.get_barrier_semaphore(), 10)


class Sends:
    def __init__(self, send_sems, recv_sems):
        self.send_sems, self.recv_sems, self.made = send_sems, recv_sems, {}

    def copy(self, key):
        number, make = self.made[key]
        src, dst, axis, place = make()
        return pltpu.make_async_remote_copy(
            src_ref=src, dst_ref=dst, send_sem=self.send_sems.at[number], recv_sem=self.recv_sems.at[number],
            device_id=device_at(axis, place), device_id_type=MESH)

    def start(self, key, make):
        if key not in self.made:
            self.made[key] = (len(self.made), make)
        self.copy(key).start()

    def arrived(self, *keys):
        for key in keys:
            self.copy(key).wait_recv()

    def finish(self):
        for key in self.made:
            self.copy(key).wait_send()


def all_in(lead, work):
    @pl.loop(0, int(np.prod(lead)))
    def one(i):
        at, rest = [], i
        for n in reversed(lead):
            at.append(rest % n)
            rest = rest // n
        work(tuple(reversed(at)))


class Scatter:
    def __init__(self, name, at, sends, x, scratch):
        self.name, self.at, self.sends, self.x = name, at, sends, x
        self.sums, self.core_in, self.bufs, self.load_sem = scratch[0], scratch[1], scratch[2:5], scratch[5]

    def load(self):
        return pltpu.make_async_copy(self.x.at[:, self.at["core"]], self.sums, self.load_sem.at[0])

    def place(self, p, s, turn):
        return (self.at[ORDERS[p][s]] + turn) % 4

    def block(self, p, s, turn):
        lead = [self.at[ORDERS[p][n]] for n in range(s)]
        return self.sums.at[(p, *lead, self.place(p, s, turn))]

    def begin(self):
        self.load().start()
        for turn in (2, 1, 3, 0):
            for p in range(PARTS):
                self.sends.start((self.name, 3, p, turn), lambda p=p, turn=turn: (
                    self.x.at[p, 1 - self.at["core"], self.place(p, 0, turn)],
                    self.core_in.at[p, self.place(p, 0, turn)], "core", 1 - self.at["core"]))

    def take(self, turn):
        for p in range(PARTS):
            self.sends.arrived((self.name, 3, p, turn))
            mine, other = self.block(p, 0, turn), self.core_in.at[p, self.place(p, 0, turn)]

            def add(at):
                mine[at] = mine[at] + other[at]

            all_in(mine.shape[:1], add)
            if turn:
                self.send(p, 0, turn)

    def send(self, p, s, turn):
        self.sends.start((self.name, s, p, turn), lambda: (
            self.block(p, s, turn), self.bufs[s].at[p, turn - 1], ORDERS[p][s], self.place(p, s, turn)))

    def onward(self, s):
        for p in range(PARTS):
            self.join(p, s - 1)
            for turn in (2, 1, 3):
                self.send(p, s, turn)

    def join(self, p, s):
        for turn in (1, 3, 2):
            self.sends.arrived((self.name, s, p, turn))
        mine, came = self.block(p, s, 0), self.bufs[s].at[p]

        def add(at):
            total = mine[at].astype(F32)
            for n in range(3):
                total += came[(n, *at)].astype(F32)
            mine[at] = total.astype(BF)

        if len(mine.shape) > 2:
            all_in(mine.shape[:1], add)
        else:
            add((Ellipsis,))

    def steps(self):
        def start():
            self.load().wait()
            self.take(2)

        return [self.begin, start, lambda: self.take(1), lambda: self.take(3), lambda: self.take(0),
                lambda: self.onward(1), lambda: self.onward(2), lambda: [self.join(p, 2) for p in range(PARTS)] and None]

    def own(self, p):
        return self.sums.at[(p, *[self.at[axis] for axis in ORDERS[p]])]


def scatter_scratch(rows):
    lead = (PARTS, 4, 4, 4)
    return [pltpu.VMEM(lead + (rows, LANES), BF), pltpu.VMEM(lead + (rows, LANES), BF),
            pltpu.VMEM((PARTS, 3, 4, 4, rows, LANES), BF), pltpu.VMEM((PARTS, 3, 4, rows, LANES), BF),
            pltpu.VMEM((PARTS, 3, rows, LANES), BF), dma(1)]


def chunk(start, size):
    return pl.ds(pl.multiple_of(start, 16), size)


class FirstSum:
    def __init__(self, name, at, sends, x, mid, scratch):
        self.name, self.at, self.sends, self.x, self.mid = name, at, sends, x, mid
        self.sums, self.core_in, self.came, self.load_sem = scratch
        self.c = x.shape[0] // (PARTS * 32)

    def place(self, p, turn):
        return (self.at[ORDERS[p][0]] + turn) % 4

    def loads(self):
        c = self.c
        return [pltpu.make_async_copy(self.x.at[chunk((p * 2 + self.at["core"]) * 16 * c, 16 * c)], self.sums.at[p],
                                      self.load_sem.at[p]) for p in range(PARTS)]

    def begin(self):
        c = self.c
        for load in self.loads():
            load.start()
        for turn in (2, 1, 3, 0):
            for p in range(PARTS):
                def make(p=p, turn=turn):
                    start = self.place(p, turn) * 4 * c
                    other = 1 - self.at["core"]
                    return (self.x.at[chunk((p * 2 + other) * 16 * c + start, 4 * c)],
                            self.core_in.at[p, chunk(start, 4 * c)], "core", other)

                self.sends.start((self.name, 3, p, turn), make)

    def take(self, turn):
        size = 4 * self.c
        for p in range(PARTS):
            self.sends.arrived((self.name, 3, p, turn))
            start = self.place(p, turn) * size

            @pl.loop(0, size // 64)
            def add(i):
                rows = chunk(start + i * 64, 64)
                self.sums[p, rows] = self.sums[p, rows] + self.core_in[p, rows]

            if turn:
                self.sends.start((self.name, 0, p, turn), lambda p=p: (
                    self.sums.at[p, chunk(self.place(p, turn) * size, size)], self.came.at[p, turn - 1], ORDERS[p][0],
                    self.place(p, turn)))

    def join(self):
        size = 4 * self.c
        for p in range(PARTS):
            for turn in (1, 3, 2):
                self.sends.arrived((self.name, 0, p, turn))
            start = self.place(p, 0) * size

            @pl.loop(0, size // 64)
            def add(i):
                rows = chunk(i * 64, 64)
                total = self.sums[p, chunk(start + i * 64, 64)].astype(F32)
                for n in range(3):
                    total += self.came[p, n, rows].astype(F32)
                self.mid[p, rows] = total.astype(BF)

    def steps(self):
        def start():
            for load in self.loads():
                load.wait()
            self.take(2)

        return [self.begin, start, lambda: self.take(1), lambda: self.take(3), lambda: self.take(0), self.join]


def first_scratch(c):
    return [pltpu.VMEM((PARTS, 16 * c, LANES), BF), pltpu.VMEM((PARTS, 16 * c, LANES), BF),
            pltpu.VMEM((PARTS, 3, 4 * c, LANES), BF), dma(PARTS)]


class SecondSum:
    def __init__(self, name, at, sends, mid, gathered, scratch):
        self.name, self.at, self.sends, self.mid, self.gathered = name, at, sends, mid, gathered
        self.came, self.slots, self.final, self.sems = scratch
        self.c = mid.shape[1] // 4

    def place(self, p, s, turn):
        return (self.at[ORDERS[p][s]] + turn) % 4

    def rows(self, p, first, second=None):
        c = self.c
        start = (p * 2 + self.at["core"]) * 16 * c + self.place(p, 0, first) * 4 * c
        if second is None:
            return self.gathered.at[chunk(start, 4 * c)]
        return self.gathered.at[chunk(start + self.place(p, 1, second) * c, c)]

    def scatter(self):
        c = self.c
        for p in range(PARTS):
            for turn in (2, 1, 3):
                self.sends.start((self.name, 1, p, turn), lambda p=p, turn=turn: (
                    self.mid.at[p, chunk(self.place(p, 1, turn) * c, c)], self.came.at[p, turn - 1], ORDERS[p][1],
                    self.place(p, 1, turn)))

    def share(self):
        for p in range(PARTS):
            for turn in (1, 3, 2):
                self.sends.arrived((self.name, 1, p, turn))
            total = self.mid[p, chunk(self.place(p, 1, 0) * self.c, self.c)].astype(F32)
            for n in range(3):
                total += self.came[p, n].astype(F32)
            self.slots[p, self.at[ORDERS[p][2]]] = total.astype(BF)
            for turn in (2, 1, 3):
                def make(p=p, turn=turn):
                    slot = self.slots.at[p, self.at[ORDERS[p][2]]]
                    return slot, slot, ORDERS[p][2], self.place(p, 2, turn)

                self.sends.start((self.name, 2, p, turn), make)

    def puts(self):
        return [pltpu.make_async_copy(self.final.at[p], self.rows(p, 0, 0), self.sems.at[p]) for p in range(PARTS)]

    def settle(self):
        for p in range(PARTS):
            for turn in (1, 3, 2):
                self.sends.arrived((self.name, 2, p, turn))
            total = self.slots[p, 0].astype(F32) + self.slots[p, 1].astype(F32)
            self.final[p] = (total + self.slots[p, 2].astype(F32) + self.slots[p, 3].astype(F32)).astype(BF)
            for turn in (2, 1, 3):
                self.sends.start((self.name, 4, p, turn), lambda p=p, turn=turn: (
                    self.final.at[p], self.rows(p, 0, 0), ORDERS[p][1], self.place(p, 1, turn)))
        for put in self.puts():
            put.start()

    def across(self, p, turn):
        def make():
            ref = self.rows(p, turn)
            return ref, ref, "core", 1 - self.at["core"]

        self.sends.start((self.name, 6, p, turn), make)

    def near(self):
        for put in self.puts():
            put.wait()
        for p in range(PARTS):
            for turn in (1, 3, 2):
                self.sends.arrived((self.name, 4, p, turn))
            for turn in (2, 1, 3):
                def make(p=p, turn=turn):
                    ref = self.rows(p, 0)
                    return ref, ref, ORDERS[p][0], self.place(p, 0, turn)

                self.sends.start((self.name, 5, p, turn), make)
            self.across(p, 0)

    def over(self, *turns):
        for turn in turns:
            for p in range(PARTS):
                self.sends.arrived((self.name, 5, p, turn))
                self.across(p, 4 - turn)

    def end(self):
        for turn in (0, 3, 1, 2):
            for p in range(PARTS):
                self.sends.arrived((self.name, 6, p, turn))

    def steps(self):
        return [self.scatter, self.share, self.settle, self.near, lambda: self.over(1, 3), lambda: self.over(2), self.end]


def second_scratch(c):
    return [pltpu.VMEM((PARTS, 3, c, LANES), BF), pltpu.VMEM((PARTS, 4, c, LANES), BF),
            pltpu.VMEM((PARTS, c, LANES), BF), dma(PARTS)]


class Gather:
    def __init__(self, name, at, sends, parts, sems):
        self.name, self.at, self.sends, self.parts, self.sems = name, at, sends, parts, sems

    def place(self, p, s, turn):
        return (self.at[self.parts[p][3][s]] + turn) % 4

    def in_plane(self, p):
        _, plane, _, order = self.parts[p]
        return plane.at[self.at[order[1]], self.at[order[2]]]

    def block(self, p, turn):
        return self.parts[p][2].at[self.at["core"], self.place(p, 0, turn)]

    def puts(self):
        return [pltpu.make_async_copy(part[0], self.in_plane(p), self.sems.at[p]) for p, part in enumerate(self.parts)]

    def last_puts(self):
        return [pltpu.make_async_copy(part[1], self.block(p, 0), self.sems.at[p]) for p, part in enumerate(self.parts)]

    def send(self, s, pick):
        for turn in (2, 1, 3):
            for p in range(len(self.parts)):
                self.sends.start((self.name, s, p, turn), lambda p=p, turn=turn: (
                    *pick(p), self.parts[p][3][s], self.place(p, s, turn)))

    def arrived(self, s, *turns):
        for turn in turns:
            for p in range(len(self.parts)):
                self.sends.arrived((self.name, s, p, turn))

    def across(self, turn):
        for p in range(len(self.parts)):
            def make(p=p):
                ref = self.block(p, turn)
                return self.parts[p][1] if turn == 0 else ref, ref, "core", 1 - self.at["core"]

            self.sends.start((self.name, 3, p, turn), make)

    def plane_steps(self):
        def first():
            for put in self.puts():
                put.start()
            self.send(2, lambda p: (self.parts[p][0], self.in_plane(p)))

        def second():
            for put in self.puts():
                put.wait()
            self.arrived(2, 1, 3, 2)

            def row(p):
                ref = self.parts[p][1].at[self.at[self.parts[p][3][1]]]
                return ref, ref

            self.send(1, row)

        return [first, second, lambda: self.arrived(1, 1, 3, 2)]

    def whole_steps(self):
        def first():
            for put in self.last_puts():
                put.start()
            self.send(0, lambda p: (self.parts[p][1], self.block(p, 0)))
            self.across(0)

        def more():
            self.arrived(0, 1)
            self.across(3)
            self.arrived(0, 3)
            self.across(1)

        def rest():
            self.arrived(0, 2)
            self.across(2)

        def end():
            self.arrived(3, 0, 3, 1, 2)
            for put in self.last_puts():
                put.wait()

        return [first, more, rest, end]


class SmallSum:
    def __init__(self, name, at, sends, x, core_in, slots):
        self.name, self.at, self.sends, self.x, self.core_in, self.slots = name, at, sends, x, core_in, slots

    def begin(self):
        for p in range(PARTS):
            self.sends.start((self.name, 3, p, 0), lambda p=p: (
                self.x.at[pl.ds(16 * p, 16)], self.core_in.at[p], "core", 1 - self.at["core"]))

    def total(self, p, s):
        if s == 0:
            self.sends.arrived((self.name, 3, p, 0))
            return self.x[16 * p : 16 * p + 16].astype(F32) + self.core_in[p].astype(F32)
        for turn in (1, 3, 2):
            self.sends.arrived((self.name, s - 1, p, turn))
        slots = self.slots.at[p, s - 1]
        return slots[0].astype(F32) + slots[1].astype(F32) + slots[2].astype(F32) + slots[3].astype(F32)

    def stage(self, s):
        for p in range(PARTS):
            self.slots[p, s, self.at[ORDERS[p][s]]] = self.total(p, s).astype(BF)
            for turn in (2, 1, 3):
                def make(p=p, turn=turn):
                    slot = self.slots.at[p, s, self.at[ORDERS[p][s]]]
                    return slot, slot, ORDERS[p][s], (self.at[ORDERS[p][s]] + turn) % 4

                self.sends.start((self.name, s, p, turn), make)

    def steps(self, out):
        def end():
            for p in range(PARTS):
                out[16 * p : 16 * p + 16] = self.total(p, 3).astype(BF)

        return [self.begin, lambda: self.stage(0), lambda: self.stage(1), lambda: self.stage(2), end]


def steps_in(i, *table):
    for turn, *steps in table:
        @pl.when(i == turn)
        def run():
            for step in steps:
                step()


D = 768
HALF = 384
HIDDEN = 1536
TILE = 128
TAPW = 128
PADDED = LEN + 16
SHARED_ROWS = 6144
VMEM_BYTES = 60 << 20
EARLY = 3072
POINT_AT, TAPS_AT, SMALL_AT = EARLY + 1536, EARLY + 2304, EARLY + 2368
SMALL_DEPTH, SMALL_FFN, SMALL_BIAS, SMALL_SEG, SMALL = 0, 18, 36, 43, 48


class Params(NamedTuple):
    hidden: jax.Array
    cotangent: jax.Array
    lengths: jax.Array
    split_at: jax.Array
    seg_table: jax.Array
    w_query: jax.Array
    b_query: jax.Array
    w_key: jax.Array
    w_value: jax.Array
    b_value: jax.Array
    w_depth: jax.Array
    w_point: jax.Array
    b_keyconv: jax.Array
    w_kernel: jax.Array
    b_kernel: jax.Array
    w_conv: jax.Array
    b_conv: jax.Array
    w_out: jax.Array
    b_out: jax.Array
    first_gain: jax.Array
    first_shift: jax.Array
    w_up: jax.Array
    b_up: jax.Array
    down_weight: jax.Array
    b_down: jax.Array
    second_gain: jax.Array
    second_shift: jax.Array


class Kept(NamedTuple):
    x_low: jax.Array
    query: jax.Array
    key_low: jax.Array
    value_low: jax.Array
    depth_low: jax.Array
    key_conv: jax.Array
    kernels: jax.Array
    conv_pad: jax.Array
    joined: jax.Array
    resid: jax.Array
    log_total: jax.Array


KEPT_SHAPES = (((LEN, D), BF), ((LEN, HALF), F32), ((LEN, HALF), BF), ((LEN, HALF), BF), ((LEN, D), BF),
               ((LEN, HALF), F32), ((PADDED, KERNEL * TAPW), F32), ((PADDED, HALF), F32), ((LEN, D), BF),
               ((LEN, D), F32))


def dims(lhs, rhs):
    return (((lhs,), (rhs,)), ((), ()))


def dot(a, b):
    return lax.dot_general(a, b, dims(1, 0), preferred_element_type=F32)


def dot_nt(a, b):
    return lax.dot_general(a, b, dims(1, 1), preferred_element_type=F32)


def dot_tn(a, b):
    return lax.dot_general(a, b, dims(0, 0), preferred_element_type=F32)


def tile_rows(i, n=TILE, start=0):
    return pl.ds(pl.multiple_of(i * n + start, 8 if start % 16 else 16), n)


def lanes_at(start, n=128):
    return pl.ds(pl.multiple_of(start, 128), n)


def rows_iota(n, width=1):
    return lax.broadcasted_iota(jnp.int32, (n, width), 0)


class Moves:
    def __init__(self, sems):
        self.sems, self.all = sems, []

    def start(self, src, dst):
        copy = pltpu.make_async_copy(src, dst, self.sems.at[len(self.all)])
        copy.start()
        self.all.append(copy)
        return copy

    def start_cat(self, layer, matrices, w_cat):
        return [self.start(ref.at[layer], w_cat.at[:, pl.ds(n * HALF, HALF)]) for n, ref in enumerate(matrices)]


def wait_all(copies):
    for copy in copies:
        copy.wait()


def my_row():
    row = lax.axis_index("grp")
    for name, size in zip(CH, (4, 4, 2, 2)):
        row = row * size + lax.axis_index(name)
    return row


def widen_matrix():
    lane = np.arange(HALF)[None, :] // HEAD
    return (np.arange(TAPW)[:, None] == lane).astype(ml_dtypes.bfloat16)


def tap_matrix():
    out = np.zeros((TAPW, KERNEL * TAPW), np.float32)
    for h in range(HEADS):
        for j in range(KERNEL):
            out[h * KERNEL + j, j * TAPW + h] = 1.0
    return out.astype(ml_dtypes.bfloat16)


def norm_stats(residual):
    mean = jnp.mean(residual, axis=-1, keepdims=True)
    center = residual - mean
    scale = lax.rsqrt(jnp.mean(center * center, axis=-1, keepdims=True) + EPSILON)
    return center * scale, scale


def norm_grad(gy, hat, scale, gain):
    d_hat = gy * gain
    mean_one = jnp.mean(d_hat, axis=-1, keepdims=True)
    mean_two = jnp.mean(d_hat * hat, axis=-1, keepdims=True)
    return scale * (d_hat - mean_one - hat * mean_two)


def gelu_both(pre):
    base = 1.0 + (0.3275911 * 0.7071067811865476) * jnp.abs(pre)
    t = pl.reciprocal(base, approx=True)
    t = t * (2.0 - base * t)
    poly = t * (0.127414796 + t * (-0.142248368 + t * (0.7107068705 + t * (-0.7265760135 + t * 0.5307027145))))
    bell = jnp.exp(-0.5 * pre * pre)
    tail = poly * bell
    cdf = jnp.where(pre >= 0, 1.0 - tail, tail)
    return pre * cdf, cdf + pre * (bell * 0.3989422804014327)


def far():
    return pl.BlockSpec(memory_space=pl.ANY)


def whole():
    return pl.BlockSpec(memory_space=pltpu.VMEM)


def scalars():
    return pl.BlockSpec(memory_space=pltpu.SMEM)


def dma(n):
    return pltpu.SemaphoreType.DMA((n,))


def shape(dims, dtype):
    return jax.ShapeDtypeStruct(dims, dtype)


def block_shape(rows, lanes=LANES):
    return shape((PARTS, 2, 4, 4, 4, rows, lanes), BF)


def call(kernel, ins, outs, scratch, name, **comm):
    return pl.pallas_call(
        kernel,
        out_shape=[out for out, _ in outs],
        in_specs=[place for _, place in ins],
        out_specs=[place for _, place in outs],
        scratch_shapes=scratch,
        compiler_params=pltpu.CompilerParams(vmem_limit_bytes=VMEM_BYTES, **comm),
        name=name,
    )(*[array for array, _ in ins])


def remote(number):
    return {"collective_id": number, "has_side_effects": True}


def tap_weights(layer, w_kernel, rows):
    rows[...] = jnp.zeros_like(rows)
    for n in range(HEADS * KERNEL):
        rows[n : n + 1, :] = w_kernel[n].astype(F32)[layer : layer + 1, :]


def clear_edges(*refs):
    for ref in refs:
        ref[pl.ds(0, 8), :] = jnp.zeros((8, ref.shape[1]), F32)
        ref[pl.ds(LEN + 8, 8), :] = jnp.zeros((8, ref.shape[1]), F32)


def attention_forward_kernel(layer, *refs):
    first = layer == 0
    (lengths, splits, x_in, seg, w_query, w_key, w_value, w_conv, w_point, w_out, w_depth, w_kernel, b_query, b_value,
     b_conv, b_keyconv, b_kernel, b_out, widen, spread, pieces) = refs[:21]
    kept_out, log_total, gathered, refs = refs[21:31], refs[31], refs[32], refs[33:]
    if first:
        bias_all, refs = refs[0], refs[1:]
    kept, refs = refs[:10], refs[10:]
    x_low, query, key_low, value_low, depth_low, key_conv, kernels, conv_pad, joined, resid = kept
    (x_all, hidden, w_cat, point, out_w, x_pad, query_low, mixed_low, tap_rows, taps_w, tap_bias, sems, own_sems,
     send_sems, recv_sems), refs = refs[:15], refs[15:]
    length = lengths[my_row()]
    one = slice(layer, layer + 1)
    at = here()
    greet(at)
    moves = Moves(sems)
    load_x = moves.start(x_in, hidden if first else x_all)
    load_cat = moves.start_cat(layer, (w_query, w_key, w_value, w_conv), w_cat)
    load_rest = [moves.start(w_point.at[layer], point), moves.start(w_out.at[layer], out_w)]
    sends = Sends(send_sems, recv_sems)
    if first:
        planes, bias_plane = refs
        parts = [(pieces.at[p], planes.at[p], gathered.at[p], ORDERS[p]) for p in range(PARTS)]
        bias_piece = pieces.at[LAYERS * PARTS, :, pl.ds(0, TAPW)]
        parts.append((bias_piece, bias_plane, bias_all, ORDERS[0]))
    else:
        parts = [(None, pieces.at[p], gathered.at[p], ORDERS[p]) for p in range(PARTS)]
    gather = Gather(0, at, sends, parts, own_sems)
    planar = gather.plane_steps() if first else [lambda: None] * 3
    steps = gather.whole_steps()
    met()
    planar[0]()
    if not first:
        steps[0]()
    clear_edges(x_pad, conv_pad, kernels)
    tap_weights(layer, w_kernel, tap_rows)
    for c in range(0, KERNEL * TAPW, 384):
        taps_w[:, c : c + 384] = dot_tn(tap_rows[...].astype(BF), spread[:, c : c + 384]).astype(BF)
    tap_bias[...] = jnp.zeros_like(tap_bias)
    tap_bias[0:1, 0 : HEADS * KERNEL] = b_kernel[one, :]
    left, bias = tap_bias[:, :TAPW], jnp.zeros((8, KERNEL * TAPW), F32)
    for _ in range(3):
        bias += dot(left.astype(BF), spread[...])
        left = left - left.astype(BF).astype(F32)
    tap_bias[...] = bias

    load_x.wait()
    planar[1]()

    @pl.loop(0, LEN // TILE)
    def enter(i):
        rows = tile_rows(i)
        if first:
            place = rows_iota(TILE) + i * TILE
            x = hidden[rows, :].astype(F32) + jnp.where(place > splits[my_row()], seg[1:2, :], seg[0:1, :])
            x = x * (place < length).astype(F32)
            x_all[rows, :] = x
        else:
            x = x_all[rows, :]
        low = x.astype(BF)
        x_low[rows, :] = low
        x_pad[tile_rows(i, TILE, 8), :] = low.astype(F32)

    wait_all(load_cat)
    for n in range(6):
        proj = dot(x_low[...], w_cat[:, n * 256 : n * 256 + 256])
        for h in range(2):
            which, c = (2 * n + h) // 3, (2 * n + h) % 3 * 128
            cols = slice(c, c + 128)
            part = proj[:, h * 128 : h * 128 + 128]
            if which == 0:
                part += b_query[one, cols]
                query[:, cols] = part
                query_low[:, cols] = part.astype(BF)
            elif which == 1:
                key_low[:, cols] = part.astype(BF)
            elif which == 2:
                value_low[:, cols] = (part + b_value[one, cols]).astype(BF)
            else:
                conv_pad[pl.ds(8, LEN), cols] = part + b_conv[one, cols]
    stores = [moves.start(kept[n], kept_out[n]) for n in (0, 1, 2, 3, 7)]

    @pl.loop(0, LEN // TILE)
    def depth(i):
        rows = tile_rows(i)
        around = pl.ds(pl.multiple_of(i * TILE, TILE), TILE + 16)
        for c in range(0, D, 256):
            window = x_pad[around, c : c + 256]
            total = jnp.zeros((TILE, 256), F32)
            for j in range(KERNEL):
                total += w_depth[j, one, c : c + 256].astype(F32) * window[4 + j : 4 + j + TILE]
            depth_low[rows, c : c + 256] = total.astype(BF)

    planar[2]()
    if first:
        steps[0]()
    wait_all(load_rest)
    for c, n in ((0, 256), (256, 128)):
        cols = slice(c, c + n)
        key = dot(depth_low[...], point[:, cols]) + b_keyconv[one, cols]
        key_conv[:, cols] = key
        mixed_low[:, cols] = (key * query[:, cols]).astype(BF)
    for c in range(0, KERNEL * TAPW, 384):
        cols = slice(c, c + 384)
        kernels[pl.ds(8, LEN), cols] = dot(mixed_low[...], taps_w[:, cols]) + tap_bias[0:1, cols]
    stores += [moves.start(kept[n], kept_out[n]) for n in (4, 5)]

    @pl.loop(0, LEN // TILE)
    def convolve(i):
        rows = tile_rows(i)
        around = pl.ds(pl.multiple_of(i * TILE, TILE), TILE + 16)
        padded = tile_rows(i, TILE, 8)
        taps = [kernels[padded, j * TAPW : (j + 1) * TAPW] for j in range(KERNEL)]
        peak = functools.reduce(jnp.maximum, taps)
        taps = [jnp.exp(t - peak) for t in taps]
        share = 1.0 / sum(taps)
        window = conv_pad[around, :]
        mix = jnp.zeros((TILE, HALF), F32)
        for j in range(KERNEL):
            tap = taps[j] * share
            kernels[padded, j * TAPW : (j + 1) * TAPW] = tap
            mix += dot(tap.astype(BF), widen[...]) * window[4 + j : 4 + j + TILE]
        joined[rows, HALF:] = mix.astype(BF)

    stores += [moves.start(kept[6], kept_out[6])]

    @pl.loop(0, HEADS // 2)
    def attend(pair):
        if not first:
            steps_in(pair, (1, steps[1]), (2, steps[2]))
        lanes = lanes_at(pair * 128)
        keys = key_low[:, lanes] * jnp.asarray(SCORE_SCALE, BF)
        side = lax.broadcasted_iota(jnp.int32, (LEN, 128), 1) // HEAD
        values = jnp.transpose(value_low[:, lanes].astype(F32)).astype(BF)
        for block in range(2):
            cols = slice(block * 256, block * 256 + 256)
            queries = query_low[cols, lanes]
            pieces_t = []
            for head in range(2):
                mine = jnp.where(side == head, keys, jnp.zeros_like(keys))
                scores = dot_nt(mine, queries)
                scores = jnp.where(rows_iota(LEN, 256) < length, scores, MASK_VALUE)
                peak = jnp.max(scores, axis=0, keepdims=True)
                probs = jnp.exp(scores - peak)
                total = jnp.sum(probs, axis=0, keepdims=True)
                log_total[pair * 2 + head, :, cols] = peak + jnp.log(total)
                probs = (probs * (1.0 / total)).astype(BF)
                pieces_t.append(dot(values[head * HEAD : (head + 1) * HEAD, :], probs))
            joined[cols, lanes] = jnp.transpose(jnp.concatenate(pieces_t, axis=0)).astype(BF)

    stores += [moves.start(kept[8], kept_out[8])]
    if first:
        steps[1]()
    for c in range(0, D, 256):
        cols = slice(c, c + 256)
        resid[:, cols] = x_all[:, cols] + dot(joined[...], out_w[:, cols]) + b_out[one, cols]
    stores += [moves.start(kept[9], kept_out[9])]
    if first:
        steps[2]()
    steps[3]()
    wait_all(stores)
    sends.finish()


def attention_forward(layer, x, pieces, w):
    ins = [(w.lengths, scalars()), (w.split_at, scalars()), (x, far()), (w.seg_table, whole())]
    ins += [(m, far()) for m in (w.w_query, w.w_key, w.w_value, w.w_conv, w.w_point, w.w_out)]
    ins += [(m, whole()) for m in (w.w_depth, w.w_kernel, w.b_query, w.b_value, w.b_conv, w.b_keyconv, w.b_kernel,
                                   w.b_out, widen_matrix(), tap_matrix())]
    ins += [(pieces, far() if layer == 0 else whole())]
    outs = [(shape(*s), far()) for s in KEPT_SHAPES]
    outs += [(shape((HEADS, 1, LEN), F32), whole()), (block_shape(16), far())]
    if layer == 0:
        outs += [(shape((2, 4, 4, 4, 16, TAPW), BF), far())]
    scratch = [pltpu.VMEM(*s) for s in KEPT_SHAPES]
    scratch += [pltpu.VMEM((LEN, D), F32), pltpu.VMEM((LEN, D), BF), pltpu.VMEM((D, 4 * HALF), BF),
                pltpu.VMEM((D, HALF), BF), pltpu.VMEM((D, D), BF), pltpu.VMEM((PADDED, D), F32),
                pltpu.VMEM((LEN, HALF), BF), pltpu.VMEM((LEN, HALF), BF), pltpu.VMEM((TAPW, HALF), F32),
                pltpu.VMEM((HALF, KERNEL * TAPW), BF), pltpu.VMEM((8, KERNEL * TAPW), F32), dma(24), dma(4), dma(64), dma(64)]
    if layer == 0:
        scratch += [pltpu.VMEM(PLANES, BF), pltpu.VMEM((4, 4, 16, TAPW), BF)]
    return call(functools.partial(attention_forward_kernel, layer), ins, outs, scratch, "fa", **remote(1 + layer))


PLANES = (PARTS, 4, 4, 16, LANES)


def part_block(ref, p, core, x, y, z):
    if p == 0:
        return ref.at[0, core, x, y, z]
    if p == 1:
        return ref.at[1, core, y, z, x]
    return ref.at[2, core, z, x, y]


def ffn_forward_kernel(layer, *refs):
    (lengths, resid_in, gathered_in, bias_all, first_gain, first_shift, b_down, second_gain, second_shift) = refs[:9]
    refs = refs[9:]
    comm = layer + 1 < LAYERS
    if comm:
        pieces, refs = refs[0], refs[1:]
    outs, refs = refs[:6], refs[6:]
    if comm:
        planes, refs = refs[0], refs[1:]
    (up, down, acted, slope, resid_two, x_next), refs = refs[:6], refs[6:]
    (resid, gathered, low, pre, bias_rows, bias, sems, block_sems), refs = refs[:8], refs[8:]
    steps = [lambda: None] * 3
    if comm:
        own_sems, send_sems, recv_sems = refs
        at = here()
        greet(at)
        sends = Sends(send_sems, recv_sems)
        parts = [(pieces.at[(layer + 1) * PARTS + p], planes.at[p], None, ORDERS[p]) for p in range(PARTS)]
        steps = Gather(0, at, sends, parts, own_sems).plane_steps()
    one = slice(layer, layer + 1)
    length = lengths[my_row()]
    moves = Moves(sems)
    load = moves.start(resid_in, resid)
    load_weights = moves.start(gathered_in, gathered)
    if comm:
        met()
    steps[0]()
    load.wait()

    @pl.loop(0, LEN // TILE)
    def enter(i):
        rows = tile_rows(i)
        hat, _ = norm_stats(resid[rows, :])
        normed = hat * first_gain[one, :] + first_shift[one, :]
        resid[rows, :] = normed
        low[rows, :] = normed.astype(BF)

    load_weights.wait()

    @pl.loop(0, 64)
    def unpack(chip):
        z, y, x = (chip // 32) * 2 + chip % 2, (chip // 8) % 4, (chip // 2) % 4
        ups, downs = [], []
        for core in range(2):
            piece = jnp.concatenate(
                [part_block(gathered, p, core, x, y, z)[...].astype(F32) for p in range(PARTS)], axis=0)
            ups.append(piece[:24])
            downs.append(piece[24:])
            bias_rows[core, pl.ds(chip, 1), :] = bias_all[core, x, y, z].astype(F32)[one, :]
        rows = tile_rows(chip, 48)
        up[rows, :] = jnp.concatenate(ups, axis=0).astype(BF)
        down[rows, :] = jnp.concatenate(downs, axis=0).astype(BF)

    stores = [moves.start(up, outs[0]), moves.start(down, outs[1])]
    steps[1]()
    for c in range(0, 2 * HIDDEN, 512):
        spot = lax.broadcasted_iota(jnp.int32, (64, 512), 1) + c
        slot = (lax.broadcasted_iota(jnp.int32, (TAPW, 512), 1) + c) % 24
        repeat = (slot == rows_iota(TAPW, 512)).astype(F32).astype(BF)
        total = jnp.zeros((1, 512), F32)
        for core in range(2):
            spread = dot(bias_rows[core].astype(BF), repeat)
            mine = spot // 24 == 2 * rows_iota(64, 512) + core
            total += jnp.sum(jnp.where(mine, spread, 0.0), axis=0, keepdims=True)
        bias[:, c : c + 512] = total

    def block_stores(n):
        cols = lanes_at(n * 512, 512)
        return [pltpu.make_async_copy(src.at[:, cols], out.at[:, cols], block_sems.at[2 * n + m])
                for m, (src, out) in enumerate(((acted, outs[2]), (slope, outs[3])))]

    for g in range(2):
        @pl.loop(0, HIDDEN // 512)
        def feed(k):
            at = g * HIDDEN + k * 512
            hidden = pl.ds(pl.multiple_of(at, 512), 512)
            pre[...] = dot_nt(low[:, g * HALF : (g + 1) * HALF], up[hidden, :]) + bias[:, hidden]

            @pl.loop(0, LEN // 32)
            def act(i):
                few = tile_rows(i, 32)
                for c in range(0, 512, 256):
                    value, grad = gelu_both(pre[few, c : c + 256])
                    cols = lanes_at(at + c, 256)
                    acted[few, cols] = value.astype(BF)
                    slope[few, cols] = grad.astype(BF)

            for store in block_stores(g * (HIDDEN // 512) + k):
                store.start()

    @pl.loop(0, LEN // 256)
    def leave(i):
        rows = tile_rows(i, 256)
        out = []
        for g in range(2):
            hidden = slice(g * HIDDEN, (g + 1) * HIDDEN)
            out.append(dot(acted[rows, hidden], down[hidden, :]).astype(BF).astype(F32))
        two = resid[rows, :] + jnp.concatenate(out, axis=1) + b_down[one, :]
        resid_two[rows, :] = two
        hat, _ = norm_stats(two)
        valid = (rows_iota(256) + i * 256 < length).astype(F32)
        x_next[rows, :] = (hat * second_gain[one, :] + second_shift[one, :]) * valid

    stores += [moves.start(resid_two, outs[4]), moves.start(x_next, outs[5])]
    steps[2]()
    for n in range(2 * HIDDEN // 512):
        wait_all(block_stores(n))
    wait_all(stores)
    if comm:
        sends.finish()


def ffn_forward(layer, resid, gathered, bias, pieces, w):
    ins = [(w.lengths, scalars()), (resid, far()), (gathered, far())]
    ins += [(m, whole()) for m in (bias, w.first_gain, w.first_shift, w.b_down, w.second_gain, w.second_shift)]
    shapes = [((2 * HIDDEN, HALF), BF)] * 2 + [((LEN, 2 * HIDDEN), BF)] * 2 + [((LEN, D), F32)] * 2
    outs = [(shape(*s), far()) for s in shapes]
    scratch = [pltpu.VMEM(*s) for s in shapes]
    scratch += [pltpu.VMEM((LEN, D), F32), pltpu.VMEM(block_shape(16).shape, BF), pltpu.VMEM((LEN, D), BF),
                pltpu.VMEM((LEN, 512), F32), pltpu.VMEM((2, 64, TAPW), F32), pltpu.VMEM((1, 2 * HIDDEN), F32), dma(8), dma(12)]
    comm = {}
    if layer + 1 < LAYERS:
        ins += [(pieces, far())]
        outs += [(shape(PLANES, BF), whole())]
        scratch += [dma(PARTS), dma(18), dma(18)]
        comm = remote(7)
    return call(functools.partial(ffn_forward_kernel, layer), ins, outs, scratch, "ff", **comm)


def ffn_backward_kernel(layer, *refs):
    comm = layer == 0
    lengths, ins, (first_gain, first_shift, second_gain), refs = refs[0], refs[1:8], refs[8:11], refs[11:]
    if comm:
        late, early_mid, refs = *refs[:2], refs[2:]
    d_resid_out, grads_out, small, refs = *refs[:3], refs[3:]
    if comm:
        late_mid, early_all, refs = *refs[:2], refs[2:]
    (gy, resid_two, resid, slope, down, up, acted), refs = refs[:7], refs[7:]
    (d_resid, grads, d_two, d_pre, d_group, normed_low, sems), refs = refs[:7], refs[7:]
    one = slice(layer, layer + 1)
    length = lengths[my_row()]
    moves = Moves(sems)
    loads = [moves.start(src, dst) for src, dst in zip(ins, (gy, resid_two, resid, slope, down, up, acted))]
    first, second = [lambda: None] * 6, [lambda: None] * 7
    if comm:
        scratch, (send_sems, recv_sems) = refs[:8], refs[8:]
        at = here()
        greet(at)
        sends = Sends(send_sems, recv_sems)
        first = FirstSum(0, at, sends, late, late_mid, scratch[:4]).steps()
        second = SecondSum(1, at, sends, early_mid, early_all, scratch[4:]).steps()
        met()
    first[0]()
    second[0]()
    small[...] = jnp.zeros_like(small)

    def note(slot, value):
        total = jnp.sum(value, axis=0, keepdims=True)
        small[slot : slot + 1, :] += total[:, :HALF]
        small[slot + 1 : slot + 2, :] += total[:, HALF:]

    wait_all(loads[:3])

    @pl.loop(0, LEN // TILE)
    def enter(i):
        rows = tile_rows(i)
        valid = (rows_iota(TILE) + i * TILE < length).astype(F32)
        grad = gy[rows, :].astype(F32) * valid
        hat, scale = norm_stats(resid_two[rows, :])
        note(0, grad * hat)
        note(2, grad)
        two = norm_grad(grad, hat, scale, second_gain[one, :])
        note(4, two)
        d_two[rows, :] = two
        d_group[rows, :] = two.astype(BF)
        hat, _ = norm_stats(resid[rows, :])
        normed_low[rows, :] = (hat * first_gain[one, :] + first_shift[one, :]).astype(BF)

    wait_all(loads[3:5])
    for g in range(2):
        @pl.loop(0, HIDDEN // 256)
        def feed(k):
            hidden = pl.ds(pl.multiple_of(g * HIDDEN + k * 256, 256), 256)
            d_act = dot_nt(d_group[:, g * HALF : (g + 1) * HALF], down[hidden, :])
            d_pre[:, hidden] = (d_act * slope[:, hidden].astype(F32)).astype(BF)

        if g == 0:
            second[1]()
    first[1]()
    first[2]()
    wait_all(loads[5:])

    @pl.loop(0, LEN // 256)
    def back(i):
        rows = tile_rows(i, 256)
        got = []
        for g in range(2):
            hidden = slice(g * HIDDEN, (g + 1) * HIDDEN)
            got.append(dot(d_pre[rows, hidden], up[hidden, :]).astype(BF).astype(F32))
        d_normed = d_two[rows, :] + jnp.concatenate(got, axis=1)
        hat, scale = norm_stats(resid[rows, :])
        note(6, d_normed * hat)
        note(8, d_normed)
        d_resid[rows, :] = norm_grad(d_normed, hat, scale, first_gain[one, :])

    stores = [moves.start(d_resid, d_resid_out)]
    second[2]()
    first[3]()
    first[4]()
    ones = jnp.ones((8, LEN), BF)
    for k in range(8):
        small[10 + k : 11 + k, :] = dot(ones, d_pre[:, k * HALF : (k + 1) * HALF])[0:1, :]

    for g in range(2):
        @pl.loop(0, 4)
        def grad(y):
            if g == 0:
                steps_in(y, (2, second[3]))
            hidden = lanes_at(g * HIDDEN + y * HALF, HALF)
            cols = slice(g * HALF, (g + 1) * HALF)
            d_up = dot_tn(d_pre[:, hidden], normed_low[:, cols])
            d_down = dot_tn(acted[:, hidden], d_group[:, cols])
            for d in range(16):
                x, z, core = d // 4, g * 2 + (d // 2) % 2, d % 2
                piece = jnp.concatenate([d_up[24 * d : 24 * d + 24], d_down[24 * d : 24 * d + 24]], axis=0).astype(BF)
                for p in range(PARTS):
                    part_block(grads, p, core, x, y, z)[...] = piece[16 * p : 16 * p + 16]

        zs = pl.ds(2 * g, 2)
        for index in ((0, slice(None), slice(None), slice(None), zs), (1, slice(None), slice(None), zs),
                      (2, slice(None), zs)):
            stores.append(moves.start(grads.at[index], grads_out.at[index]))

    second[4]()
    first[5]()
    second[5]()
    second[6]()
    if comm:
        sends.finish()
    wait_all(stores)


def ffn_backward(layer, gy, kept, ffn, late, early_mid, w):
    up, down, acted, slope, resid_two = ffn
    ins = [(w.lengths, scalars())] + [(m, far()) for m in (gy, resid_two, kept.resid, slope, down, up, acted)]
    ins += [(m, whole()) for m in (w.first_gain, w.first_shift, w.second_gain)]
    outs = [(shape((LEN, D), F32), far()), (block_shape(16), far()), (shape((32, HALF), F32), whole())]
    scratch = [pltpu.VMEM(m.shape, m.dtype) for m in (gy, resid_two, kept.resid, slope, down, up, acted)]
    scratch += [pltpu.VMEM((LEN, D), F32), pltpu.VMEM(block_shape(16).shape, BF), pltpu.VMEM((LEN, D), F32),
                pltpu.VMEM((LEN, 2 * HIDDEN), BF), pltpu.VMEM((LEN, D), BF), pltpu.VMEM((LEN, D), BF), dma(16)]
    comm = {}
    if layer == 0:
        ins += [(late, far()), (early_mid, whole())]
        outs += [(shape((PARTS, EARLY // 24, LANES), BF), whole()), (shape((EARLY, HALF), BF), far())]
        scratch += first_scratch(32) + second_scratch(32) + [dma(72), dma(72)]
        comm = remote(3)
    return call(functools.partial(ffn_backward_kernel, layer), ins, outs, scratch, "bf", **comm)


def attention_backward_kernel(layer, *refs):
    first = layer == 0
    (lengths, splits, d_resid_in), kept_in, log_total, refs = refs[:3], refs[3:12], refs[12], refs[13:]
    (ffn_small, w_query, w_key, w_value, w_conv, w_point, w_out, w_depth, w_kernel, widen, spread, ffn_grads) = refs[:12]
    refs = refs[12:]
    if first:
        above, refs = refs[0], refs[1:]
    d_input_out, own, refs = *refs[:2], refs[2:]
    if first:
        (above_all, early_all, late_all, small_all), refs = refs[:4], refs[4:]
    else:
        early_mid, late_out, refs = *refs[:2], refs[2:]
    d_resid, kept, d_input, shared, refs = refs[0], refs[1:10], refs[10], refs[11], refs[12:]
    x_low, query, key_low, value_low, depth_low, key_conv, kernels, conv_pad, joined = kept
    (w_cat, point, out_w, d_proj, d_cat, d_join, query_low, d_att, mix_pad, depth_pad, small, d_tap, tap_rows,
     sems) = refs[:14]
    scratch, (send_sems, recv_sems), refs = refs[14:20], refs[20:22], refs[22:]
    length = lengths[my_row()]
    at = here()
    greet(at)
    moves = Moves(sems)
    load_first = [moves.start(d_resid_in, d_resid), moves.start(w_out.at[layer], out_w)]
    load = [moves.start(kept_in[n], kept[n]) for n in (8, 1, 2, 3, 6, 7, 5, 4, 0)]
    load_cat = moves.start_cat(layer, (w_query, w_key, w_value, w_conv), w_cat)
    load_point = moves.start(w_point.at[layer], point)
    sends = Sends(send_sems, recv_sems)
    scatter = Scatter(0, at, sends, ffn_grads, scratch)
    steps = scatter.steps()
    more, late, little = [lambda: None] * 7, [lambda: None] * 13, [lambda: None] * 5
    first_refs, refs = refs[:4], refs[4:]
    if first:
        early_mid, late_mid, refs = refs[0], refs[1], refs[2:]
        more = SecondSum(1, at, sends, above, above_all, refs[:4]).steps()
    early = FirstSum(2, at, sends, shared.at[pl.ds(0, EARLY)], early_mid, first_refs).steps()
    if first:
        early += SecondSum(3, at, sends, early_mid, early_all, refs[4:8]).steps()
        late = FirstSum(4, at, sends, shared.at[pl.ds(EARLY, EARLY)], late_mid, refs[8:12]).steps()
        late += SecondSum(5, at, sends, late_mid, late_all, refs[12:16]).steps()
        little = SmallSum(6, at, sends, refs[16], refs[17], refs[18]).steps(small_all)
    else:
        early += [lambda: None] * 7
    met()
    steps[0]()
    more[0]()
    clear_edges(mix_pad, depth_pad)
    small[...] = jnp.zeros_like(small)
    small[SMALL_FFN : SMALL_FFN + 18, :] = ffn_small[0:18, :]
    shared[SMALL_AT:, :] = jnp.zeros((SHARED_ROWS - SMALL_AT, HALF), BF)
    tap_weights(layer, w_kernel, tap_rows)

    def note(slot, value):
        total = jnp.sum(value, axis=0, keepdims=True)
        for n in range(total.shape[1] // HALF):
            small[slot + n : slot + n + 1, :] += total[:, n * HALF : (n + 1) * HALF]

    wait_all(load_first)

    @pl.loop(0, LEN // TILE)
    def enter(i):
        rows = tile_rows(i)
        low = d_resid[rows, :].astype(BF)
        d_proj[rows, :] = low
        note(SMALL_BIAS + 5, low.astype(F32))

    for c in range(0, D, 256):
        d_join[:, c : c + 256] = dot_nt(d_proj[...], out_w[c : c + 256, :]).astype(BF)
    mix_pad[pl.ds(8, LEN), :] = d_join[:, HALF:].astype(F32)
    load[0].wait()

    @pl.loop(0, D // 256)
    def out_grad(c):
        part = dot_tn(joined[:, lanes_at(c * 256, 256)], d_proj[...])
        for n in range(2):
            shared[chunk(n * D + c * 256, 256), :] = part[:, n * HALF : (n + 1) * HALF].astype(BF)

    more[1]()
    wait_all(load[1:4])
    query_low[...] = query[...].astype(BF)

    @pl.loop(0, HEADS // 2)
    def attend(pair):
        steps_in(pair, (1, steps[1], steps[2]), (2, steps[3], steps[4], more[2]))
        lanes = lanes_at(pair * 128)
        keys = key_low[:, lanes]
        values = value_low[:, lanes]
        scaled = keys * jnp.asarray(SCORE_SCALE, BF)
        keys_t = jnp.transpose(keys.astype(F32)).astype(BF)
        side = lax.broadcasted_iota(jnp.int32, (LEN, 128), 1) // HEAD
        nothing = jnp.zeros_like(keys)
        d_keys = [None, None]
        d_values = [None, None]
        for block in range(2):
            cols = slice(block * 256, block * 256 + 256)
            queries = query_low[cols, lanes]
            d_context = d_join[cols, lanes]
            pieces = []
            for head in range(2):
                scores = dot_nt(jnp.where(side == head, scaled, nothing), queries)
                scores = jnp.where(rows_iota(LEN, 256) < length, scores, MASK_VALUE)
                probs = jnp.exp(scores - log_total[pair * 2 + head, :, cols])
                d_probs = dot_nt(jnp.where(side == head, values, nothing), d_context)
                weighted = probs * d_probs
                row_dot = jnp.sum(weighted, axis=0, keepdims=True)
                d_scores = (weighted - probs * row_dot).astype(BF)
                pieces.append(dot(keys_t[head * HEAD : (head + 1) * HEAD, :], d_scores))
                part = dot(d_scores, queries)
                d_keys[head] = part if block == 0 else d_keys[head] + part
                part = dot(probs.astype(BF), d_context)
                d_values[head] = part if block == 0 else d_values[head] + part
            d_att[cols, lanes] = jnp.transpose(jnp.concatenate(pieces, axis=0)) * SCORE_SCALE
        d_cat[:, lanes_at(HALF + pair * 128)] = (jnp.where(side == 0, d_keys[0], d_keys[1]) * SCORE_SCALE).astype(BF)
        d_cat[:, lanes_at(2 * HALF + pair * 128)] = jnp.where(side == 0, d_values[0], d_values[1]).astype(BF)

    wait_all(load[7:])

    @pl.loop(0, D // 256)
    def key_grad(c):
        low = x_low[:, lanes_at(c * 256, 256)]
        for n in range(2):
            part = dot_tn(low, d_cat[:, (n + 1) * HALF : (n + 2) * HALF])
            shared[chunk(1536 + n * D + c * 256, 256), :] = part.astype(BF)

    early[0]()
    more[3]()
    wait_all(load[4:7])

    @pl.loop(0, LEN // TILE)
    def taps(i):
        steps_in(i, (3, early[1], early[2]))
        rows = tile_rows(i)
        around = pl.ds(pl.multiple_of(i * TILE, TILE), TILE + 16)
        padded = tile_rows(i, TILE, 8)
        mix = mix_pad[padded, :]
        window = conv_pad[around, :]
        mix_window = mix_pad[around, :]
        d_kernel, d_conv = [], jnp.zeros((TILE, HALF), F32)
        dotted = jnp.zeros((TILE, TAPW), F32)
        for j in range(KERNEL):
            part = dot_nt((mix * window[4 + j : 4 + j + TILE]).astype(BF), widen[...])
            d_kernel.append(part)
            dotted += part * kernels[padded, j * TAPW : (j + 1) * TAPW]
            share = kernels[around, j * TAPW : (j + 1) * TAPW][12 - j : 12 - j + TILE]
            d_conv += dot(share.astype(BF), widen[...]) * mix_window[12 - j : 12 - j + TILE]
        d_cat[rows, 3 * HALF :] = d_conv.astype(BF)
        wide = [kernels[padded, j * TAPW : (j + 1) * TAPW] * (d_kernel[j] - dotted) for j in range(KERNEL)]
        d_logit = dot_nt(jnp.concatenate(wide, axis=1).astype(BF), spread[...]).astype(BF)
        d_tap[rows, :] = d_logit
        d_mixed = dot(d_logit, tap_rows[...].astype(BF))
        q = query[rows, :]
        key = key_conv[rows, :]
        d_keyconv = (d_mixed * q).astype(BF)
        d_cat[rows, :HALF] = (d_att[rows, :] + d_mixed * key).astype(BF)
        note(SMALL_BIAS + 2, d_keyconv.astype(F32))
        cat = d_cat[rows, :].astype(F32)
        note(SMALL_BIAS, cat[:, :HALF])
        note(SMALL_BIAS + 1, cat[:, 2 * HALF : 3 * HALF])
        note(SMALL_BIAS + 3, cat[:, 3 * HALF :])
        small[SMALL_BIAS + 4 : SMALL_BIAS + 5, :TAPW] += jnp.sum(d_logit.astype(F32), axis=0, keepdims=True)
        d_join[rows, HALF:] = d_keyconv
        d_join[rows, :HALF] = (key * q).astype(BF)

    early[3]()
    early[4]()
    shared[TAPS_AT : TAPS_AT + 64, :] = dot_tn(d_tap[...], d_join[:, :HALF])[:64].astype(BF)
    load_point.wait()
    for c in range(0, D, 256):
        depth_pad[pl.ds(8, LEN), c : c + 256] = dot_nt(d_join[:, HALF:], point[c : c + 256, :])

    @pl.loop(0, D // 256)
    def cat_grad(c):
        lanes = lanes_at(c * 256, 256)
        for n, k in enumerate((0, 3)):
            part = dot_tn(x_low[:, lanes], d_cat[:, k * HALF : (k + 1) * HALF])
            shared[chunk(EARLY + n * D + c * 256, 256), :] = part.astype(BF)
        part = dot_tn(depth_low[:, lanes], d_join[:, HALF:])
        shared[chunk(POINT_AT + c * 256, 256), :] = part.astype(BF)

    late[0]()
    steps[5]()
    more[4]()
    wait_all(load_cat)
    stores = []
    for n in range(3):
        cols = slice(n * 256, n * 256 + 256)
        d_input[:, cols] = d_resid[:, cols] + dot_nt(d_cat[...], w_cat[cols, :])
        if n == 1:
            late[1]()
            late[2]()
            more[5]()
        elif n == 2:
            late[3]()
            late[4]()
            steps[6]()

        @pl.loop(0, LEN // TILE)
        def leave(i):
            rows = tile_rows(i)
            window = depth_pad[pl.ds(pl.multiple_of(i * TILE, TILE), TILE + 16), cols]
            low = x_low[rows, cols].astype(F32)
            total = d_input[rows, cols]
            for j in range(KERNEL):
                moved = window[12 - j : 12 - j + TILE]
                total += w_depth[j, layer : layer + 1, cols].astype(F32) * moved
                tap = jnp.sum(low * moved, axis=0, keepdims=True)
                if n == 0:
                    small[SMALL_DEPTH + j : SMALL_DEPTH + j + 1, 0:256] += tap
                elif n == 1:
                    small[SMALL_DEPTH + j : SMALL_DEPTH + j + 1, 256:] += tap[:, :128]
                    small[SMALL_DEPTH + 9 + j : SMALL_DEPTH + 10 + j, :128] += tap[:, 128:]
                else:
                    small[SMALL_DEPTH + 9 + j : SMALL_DEPTH + 10 + j, 128:] += tap
            d_input[rows, cols] = total

    if first:
        @pl.loop(0, LEN // TILE)
        def seg_grad(i):
            rows = tile_rows(i)
            place = rows_iota(TILE) + i * TILE
            grad = d_input[rows, :] * (place < length).astype(F32)
            later = (place > splits[my_row()]).astype(F32)
            note(SMALL_SEG + 2, grad * later)
            note(SMALL_SEG, grad * (1.0 - later))
            d_input[rows, :] = grad

    if first:
        refs[16][...] = small[...].astype(BF)
    else:
        shared[SMALL_AT : SMALL_AT + SMALL, :] = small[...].astype(BF)
        stores.append(moves.start(shared.at[pl.ds(EARLY, EARLY)], late_out))
    little[0]()
    stores.append(moves.start(d_input, d_input_out))
    early[5]()
    early[6]()
    more[6]()
    little[1]()
    late[5]()
    late[6]()
    early[7]()
    steps[7]()
    little[2]()
    late[7]()
    early[8]()
    little[3]()
    late[8]()
    early[9]()
    late[9]()
    little[4]()
    early[10]()
    early[11]()
    for p in range(PARTS):
        own[p] = scatter.own(p)[...]
    late[10]()
    late[11]()
    early[12]()
    late[12]()
    sends.finish()
    wait_all(stores)


def attention_backward(layer, d_resid, ffn_small, ffn_grads, above, kept, w):
    ins = [(w.lengths, scalars()), (w.split_at, scalars()), (d_resid, far())] + [(m, far()) for m in kept[:9]]
    ins += [(kept.log_total, whole()), (ffn_small, whole())]
    ins += [(m, far()) for m in (w.w_query, w.w_key, w.w_value, w.w_conv, w.w_point, w.w_out)]
    ins += [(m, whole()) for m in (w.w_depth, w.w_kernel, widen_matrix(), tap_matrix())] + [(ffn_grads, far())]
    outs = [(shape((LEN, D), F32), far()), (shape((PARTS, 16, LANES), BF), whole())]
    if layer == 0:
        ins += [(above, whole())]
        outs += [(shape((EARLY, HALF), BF), far())] * 3 + [(shape((SMALL, HALF), BF), whole())]
    else:
        outs += [(shape((PARTS, EARLY // 24, LANES), BF), whole()), (shape((EARLY, HALF), BF), far())]
    scratch = [pltpu.VMEM((LEN, D), F32)] + [pltpu.VMEM(*s) for s in KEPT_SHAPES[:9]]
    scratch += [pltpu.VMEM((LEN, D), F32), pltpu.VMEM((SHARED_ROWS, HALF), BF), pltpu.VMEM((D, 4 * HALF), BF),
                pltpu.VMEM((D, HALF), BF), pltpu.VMEM((D, D), BF), pltpu.VMEM((LEN, D), BF),
                pltpu.VMEM((LEN, 4 * HALF), BF), pltpu.VMEM((LEN, D), BF), pltpu.VMEM((LEN, HALF), BF),
                pltpu.VMEM((LEN, HALF), F32), pltpu.VMEM((PADDED, HALF), F32), pltpu.VMEM((PADDED, D), F32),
                pltpu.VMEM((SMALL, HALF), F32), pltpu.VMEM((LEN, TAPW), BF), pltpu.VMEM((TAPW, HALF), F32), dma(24)]
    sends = 256 if layer == 0 else 64
    scratch += scatter_scratch(16) + [dma(sends), dma(sends)] + first_scratch(32)
    if layer == 0:
        scratch += [pltpu.VMEM((PARTS, EARLY // 24, LANES), BF)] * 2
        scratch += second_scratch(32) * 2 + first_scratch(32) + second_scratch(32)
        scratch += [pltpu.VMEM((SMALL, HALF), BF), pltpu.VMEM((PARTS, 16, LANES), BF),
                    pltpu.VMEM((PARTS, 3, 4, 16, LANES), BF)]
    return call(functools.partial(attention_backward_kernel, layer), ins, outs, scratch, "ba", **remote(4 + layer))


def hand_out_kernel(early_0, late_0, early_1, late_1, small_0, ffn_0, ffn_1, *refs):
    (seg, w_query, b_query, w_key, w_value, b_value, w_depth, w_point, b_keyconv, w_kernel, b_kernel, w_conv, b_conv,
     w_out, b_out, first_gain, first_shift, w_up, b_up, w_down, b_down, second_gain, second_shift) = refs[:23]
    low, high, load_sems, store_sems = refs[23:]
    group = lax.axis_index("grp")
    place = my_row() - group * 64
    loads, stores = Moves(load_sems), Moves(store_sems)
    for layer in range(LAYERS):
        for n in range(8):
            rows = pl.ds(n * D, D)
            source = (early_0, late_0, early_1, late_1)[2 * layer + n // 4].at[pl.ds(n % 4 * D, D)]
            loads.start(source, low.at[layer, rows])
    for layer in range(LAYERS):
        for n in range(7):
            loads.all[layer * 8 + n].wait()

            @pl.loop(0, D // 256)
            def widen(c):
                high[layer * 7 + n, tile_rows(c, 256), :] = low[layer, tile_rows(c + 3 * n, 256), :].astype(F32)

            out = (w_out, w_out, w_key, w_value, w_query, w_conv, w_point)[n].at[layer]
            if n < 2:
                out = out.at[:, pl.ds(n * HALF, HALF)]
            stores.start(high.at[layer * 7 + n], out)
    smalls, taps, ups = [], [], []
    for layer, ffn in enumerate((ffn_0, ffn_1)):
        loads.all[layer * 8 + 7].wait()
        taps.append(low[layer, TAPS_AT : TAPS_AT + 64, :].astype(F32))
        smalls.append((low[layer, SMALL_AT : SMALL_AT + SMALL, :] if layer else small_0[...]).astype(F32))
        rows = jnp.concatenate([ffn[p].astype(F32) for p in range(PARTS)], axis=0)
        w_up[layer, 0] = rows[:24]
        w_down[layer, 0] = rows[24:]
        mine = jnp.sum(jnp.where(rows_iota(8, HALF) == group * 4 + place // 16,
                                 smalls[layer][SMALL_FFN + 10 : SMALL_FFN + 18], 0.0), axis=0, keepdims=True)
        mine = jnp.broadcast_to(mine, (8, HALF))
        b_up[layer] = pltpu.roll(mine, (HALF - (place % 16) * 24) % HALF, 1)[:1, :24]

    def both(start, n=1):
        return jnp.concatenate(
            [jnp.concatenate([s[start + k : start + k + 1] for k in range(n)], axis=1) for s in smalls], axis=0)

    for j in range(KERNEL):
        w_depth[j] = jnp.concatenate([both(SMALL_DEPTH + j), both(SMALL_DEPTH + 9 + j)], axis=1)
    for j in range(HEADS * KERNEL):
        w_kernel[j] = jnp.concatenate([t[j : j + 1] for t in taps], axis=0)
    for n, out in enumerate((second_gain, second_shift, b_down, first_gain, first_shift)):
        out[...] = both(SMALL_FFN + 2 * n, 2)
    for n, out in enumerate((b_query, b_value, b_keyconv, b_conv)):
        out[...] = both(SMALL_BIAS + n)
    b_kernel[...] = both(SMALL_BIAS + 4)[:, : HEADS * KERNEL]
    b_out[...] = both(SMALL_BIAS + 5, 2)
    for n in range(2):
        s = smalls[0][SMALL_SEG + 2 * n : SMALL_SEG + 2 * n + 2]
        seg[n : n + 1, :] = jnp.concatenate([s[0:1], s[1:2]], axis=1)
    wait_all(stores.all)


def hand_out(shared, small, ffn):
    proj, half_row, full_row = (LAYERS, D, HALF), (LAYERS, HALF), (LAYERS, D)
    shapes = [(2, D), proj, half_row, proj, proj, half_row, (KERNEL, LAYERS, D), proj, half_row,
              (HEADS * KERNEL, LAYERS, HALF), (LAYERS, HEADS * KERNEL), proj, half_row, (LAYERS, D, D), full_row,
              full_row, full_row, (LAYERS, 1, 24, HALF), (LAYERS, 1, 24), (LAYERS, 1, 24, HALF), full_row, full_row,
              full_row]
    big = (proj, (LAYERS, D, D))
    outs = list(call(
        hand_out_kernel,
        [(m, far()) for m in shared] + [(m, whole()) for m in (small, *ffn)],
        [(shape(s, F32), far() if s in big else whole()) for s in shapes],
        [pltpu.VMEM((LAYERS, SHARED_ROWS, HALF), BF), pltpu.VMEM((14, D, HALF), F32), dma(16), dma(14)],
        "hand_out",
    ))
    outs[6] = jnp.swapaxes(outs[6], 0, 1)
    outs[9] = jnp.transpose(outs[9], (1, 2, 0))
    outs[17] = jnp.swapaxes(outs[17], 2, 3)
    return tuple(outs)


def shards(*args):
    w = Params(*args)
    w = w._replace(w_depth=jnp.swapaxes(w.w_depth, 0, 1), w_kernel=jnp.transpose(w.w_kernel, (2, 0, 1)))
    pieces = jnp.concatenate([jnp.swapaxes(w.w_up[:, 0], 1, 2), w.down_weight[:, 0]], axis=1)
    bias = jnp.pad(w.b_up[:, 0], ((0, 16 - LAYERS), (0, LANES - w.b_up.shape[2])))
    pieces = jnp.concatenate([pieces.reshape(LAYERS * PARTS, 16, LANES), bias[None]])
    x, kept, ffn = w.hidden, [], []
    for layer in range(LAYERS):
        outs = attention_forward(layer, x, pieces if layer == 0 else planes, w)
        kept.append(Kept(*outs[:11]))
        if layer == 0:
            bias = outs[12]
        *more, x = ffn_forward(layer, kept[layer].resid, outs[11], bias, pieces, w)
        if layer == 0:
            planes = x
            *more, x = more
        ffn.append(more)
    output, grad = x, w.cotangent
    d_resid, ffn_grads, small = ffn_backward(1, grad, kept[1], ffn[1], None, None, w)
    grad, ffn_1, early_mid, late = attention_backward(1, d_resid, small, ffn_grads, None, kept[1], w)
    d_resid, ffn_grads, small, late_mid, early_1 = ffn_backward(0, grad, kept[0], ffn[0], late, early_mid, w)
    grad, ffn_0, late_1, early_0, late_0, small_0 = attention_backward(
        0, d_resid, small, ffn_grads, late_mid, kept[0], w)
    return (output, grad) + hand_out((early_0, late_0, early_1, late_1), small_0, (ffn_0, ffn_1))


def solution(mesh):
    finer = Mesh(mesh.devices.reshape(mesh.shape["grp"], 4, 4, 2, 2), GRP_CH)
    rows, up = P(GRP_CH, None), P(None, "grp", None, CH)
    bias, down = P(None, "grp", CH), P(None, "grp", CH, None)
    placed = Params(*[P()] * len(Params._fields))._replace(
        hidden=rows, cotangent=rows, w_up=up, b_up=bias, down_weight=down)
    given = [P()] * 23
    given[17:20] = [up, bias, down]
    return jax.shard_map(
        shards,
        mesh=finer,
        in_specs=tuple(placed),
        out_specs=(rows, rows, *given),
        check_vma=False,
    )
```

```python
import functools
from typing import NamedTuple

import jax
import jax.numpy as jnp
import ml_dtypes
import numpy as np
from jax import lax
from jax.experimental import pallas as pl
from jax.experimental.pallas import tpu as pltpu
from jax.sharding import Mesh
from jax.sharding import PartitionSpec as P

HEADS = 6
HEAD = 64
KERNEL = 9
LAYERS = 2
LEN = 512
CH = ("ch_0", "ch_1", "ch_2", "ch_3")
GRP_CH = ("grp",) + CH
EPSILON = 1e-06
SCORE_SCALE = 0.125
MASK_VALUE = -1000000000.0
BF, F32 = jnp.bfloat16, jnp.float32
MESH = pl.DeviceIdType.MESH
LANES = 384
PARTS = 3
ORDERS = ("xyz", "yzx", "zxy")


def here():
    x, y = lax.axis_index("ch_1"), lax.axis_index("ch_0")
    z = lax.axis_index("grp") * 2 + lax.axis_index("ch_2")
    return {"x": x, "y": y, "z": z, "core": lax.axis_index("ch_3")}


def device_at(axis, place):
    if axis == "x":
        return {"ch_1": place}
    if axis == "y":
        return {"ch_0": place}
    if axis == "z":
        return {"grp": place // 2, "ch_2": place % 2}
    return {"ch_3": place}


def greet(at):
    peers = [("core", 1 - at["core"])]
    for axis in "xyz":
        peers += [(axis, (at[axis] + turn) % 4) for turn in (1, 2, 3)]
    for axis, place in peers:
        pl.semaphore_signal(
            pltpu.get_barrier_semaphore(), inc=1, device_id=device_at(axis, place), device_id_type=MESH)


def met():
    pl.semaphore_wait(pltpu.get_barrier_semaphore(), 10)


class Sends:
    def __init__(self, send_sems, recv_sems):
        self.send_sems, self.recv_sems, self.made = send_sems, recv_sems, {}

    def copy(self, key):
        number, make = self.made[key]
        src, dst, axis, place = make()
        return pltpu.make_async_remote_copy(
            src_ref=src, dst_ref=dst, send_sem=self.send_sems.at[number], recv_sem=self.recv_sems.at[number],
            device_id=device_at(axis, place), device_id_type=MESH)

    def start(self, key, make):
        if key not in self.made:
            self.made[key] = (len(self.made), make)
        self.copy(key).start()

    def arrived(self, *keys):
        for key in keys:
            self.copy(key).wait_recv()

    def finish(self):
        for key in self.made:
            self.copy(key).wait_send()


def all_in(lead, work):
    @pl.loop(0, int(np.prod(lead)))
    def one(i):
        at, rest = [], i
        for n in reversed(lead):
            at.append(rest % n)
            rest = rest // n
        work(tuple(reversed(at)))


class Scatter:
    def __init__(self, name, at, sends, x, scratch):
        self.name, self.at, self.sends, self.x = name, at, sends, x
        self.sums, self.core_in, self.bufs, self.load_sem = scratch[0], scratch[1], scratch[2:5], scratch[5]

    def load(self):
        return pltpu.make_async_copy(self.x.at[:, self.at["core"]], self.sums, self.load_sem.at[0])

    def place(self, p, s, turn):
        return (self.at[ORDERS[p][s]] + turn) % 4

    def block(self, p, s, turn):
        lead = [self.at[ORDERS[p][n]] for n in range(s)]
        return self.sums.at[(p, *lead, self.place(p, s, turn))]

    def begin(self):
        self.load().start()
        for turn in (2, 1, 3, 0):
            for p in range(PARTS):
                self.sends.start((self.name, 3, p, turn), lambda p=p, turn=turn: (
                    self.x.at[p, 1 - self.at["core"], self.place(p, 0, turn)],
                    self.core_in.at[p, self.place(p, 0, turn)], "core", 1 - self.at["core"]))

    def take(self, turn):
        for p in range(PARTS):
            self.sends.arrived((self.name, 3, p, turn))
            mine, other = self.block(p, 0, turn), self.core_in.at[p, self.place(p, 0, turn)]

            def add(at):
                mine[at] = mine[at] + other[at]

            all_in(mine.shape[:1], add)
            if turn:
                self.send(p, 0, turn)

    def send(self, p, s, turn):
        self.sends.start((self.name, s, p, turn), lambda: (
            self.block(p, s, turn), self.bufs[s].at[p, turn - 1], ORDERS[p][s], self.place(p, s, turn)))

    def onward(self, s):
        for p in range(PARTS):
            self.join(p, s - 1)
            for turn in (2, 1, 3):
                self.send(p, s, turn)

    def join(self, p, s):
        for turn in (1, 3, 2):
            self.sends.arrived((self.name, s, p, turn))
        mine, came = self.block(p, s, 0), self.bufs[s].at[p]

        def add(at):
            total = mine[at].astype(F32)
            for n in range(3):
                total += came[(n, *at)].astype(F32)
            mine[at] = total.astype(BF)

        if len(mine.shape) > 2:
            all_in(mine.shape[:1], add)
        else:
            add((Ellipsis,))

    def steps(self):
        def start():
            self.load().wait()
            self.take(2)

        return [self.begin, start, lambda: self.take(1), lambda: self.take(3), lambda: self.take(0),
                lambda: self.onward(1), lambda: self.onward(2), lambda: [self.join(p, 2) for p in range(PARTS)] and None]

    def own(self, p):
        return self.sums.at[(p, *[self.at[axis] for axis in ORDERS[p]])]


def scatter_scratch(rows):
    lead = (PARTS, 4, 4, 4)
    return [pltpu.VMEM(lead + (rows, LANES), BF), pltpu.VMEM(lead + (rows, LANES), BF),
            pltpu.VMEM((PARTS, 3, 4, 4, rows, LANES), BF), pltpu.VMEM((PARTS, 3, 4, rows, LANES), BF),
            pltpu.VMEM((PARTS, 3, rows, LANES), BF), dma(1)]


def chunk(start, size):
    return pl.ds(pl.multiple_of(start, 16), size)


class FirstSum:
    def __init__(self, name, at, sends, x, mid, scratch):
        self.name, self.at, self.sends, self.x, self.mid = name, at, sends, x, mid
        self.sums, self.core_in, self.came, self.load_sem = scratch
        self.c = x.shape[0] // (PARTS * 32)

    def place(self, p, turn):
        return (self.at[ORDERS[p][0]] + turn) % 4

    def loads(self):
        c = self.c
        return [pltpu.make_async_copy(self.x.at[chunk((p * 2 + self.at["core"]) * 16 * c, 16 * c)], self.sums.at[p],
                                      self.load_sem.at[p]) for p in range(PARTS)]

    def begin(self):
        c = self.c
        for load in self.loads():
            load.start()
        for turn in (2, 1, 3, 0):
            for p in range(PARTS):
                def make(p=p, turn=turn):
                    start = self.place(p, turn) * 4 * c
                    other = 1 - self.at["core"]
                    return (self.x.at[chunk((p * 2 + other) * 16 * c + start, 4 * c)],
                            self.core_in.at[p, chunk(start, 4 * c)], "core", other)

                self.sends.start((self.name, 3, p, turn), make)

    def take(self, turn):
        size = 4 * self.c
        for p in range(PARTS):
            self.sends.arrived((self.name, 3, p, turn))
            start = self.place(p, turn) * size

            @pl.loop(0, size // 64)
            def add(i):
                rows = chunk(start + i * 64, 64)
                self.sums[p, rows] = self.sums[p, rows] + self.core_in[p, rows]

            if turn:
                self.sends.start((self.name, 0, p, turn), lambda p=p: (
                    self.sums.at[p, chunk(self.place(p, turn) * size, size)], self.came.at[p, turn - 1], ORDERS[p][0],
                    self.place(p, turn)))

    def join(self):
        size = 4 * self.c
        for p in range(PARTS):
            for turn in (1, 3, 2):
                self.sends.arrived((self.name, 0, p, turn))
            start = self.place(p, 0) * size

            @pl.loop(0, size // 64)
            def add(i):
                rows = chunk(i * 64, 64)
                total = self.sums[p, chunk(start + i * 64, 64)].astype(F32)
                for n in range(3):
                    total += self.came[p, n, rows].astype(F32)
                self.mid[p, rows] = total.astype(BF)

    def steps(self):
        def start():
            for load in self.loads():
                load.wait()
            self.take(2)

        return [self.begin, start, lambda: self.take(1), lambda: self.take(3), lambda: self.take(0), self.join]


def first_scratch(c):
    return [pltpu.VMEM((PARTS, 16 * c, LANES), BF), pltpu.VMEM((PARTS, 16 * c, LANES), BF),
            pltpu.VMEM((PARTS, 3, 4 * c, LANES), BF), dma(PARTS)]


class SecondSum:
    def __init__(self, name, at, sends, mid, gathered, scratch):
        self.name, self.at, self.sends, self.mid, self.gathered = name, at, sends, mid, gathered
        self.came, self.slots, self.final, self.sems = scratch
        self.c = mid.shape[1] // 4

    def place(self, p, s, turn):
        return (self.at[ORDERS[p][s]] + turn) % 4

    def rows(self, p, first, second=None):
        c = self.c
        start = (p * 2 + self.at["core"]) * 16 * c + self.place(p, 0, first) * 4 * c
        if second is None:
            return self.gathered.at[chunk(start, 4 * c)]
        return self.gathered.at[chunk(start + self.place(p, 1, second) * c, c)]

    def scatter(self):
        c = self.c
        for p in range(PARTS):
            for turn in (2, 1, 3):
                self.sends.start((self.name, 1, p, turn), lambda p=p, turn=turn: (
                    self.mid.at[p, chunk(self.place(p, 1, turn) * c, c)], self.came.at[p, turn - 1], ORDERS[p][1],
                    self.place(p, 1, turn)))

    def share(self):
        for p in range(PARTS):
            for turn in (1, 3, 2):
                self.sends.arrived((self.name, 1, p, turn))
            total = self.mid[p, chunk(self.place(p, 1, 0) * self.c, self.c)].astype(F32)
            for n in range(3):
                total += self.came[p, n].astype(F32)
            self.slots[p, self.at[ORDERS[p][2]]] = total.astype(BF)
            for turn in (2, 1, 3):
                def make(p=p, turn=turn):
                    slot = self.slots.at[p, self.at[ORDERS[p][2]]]
                    return slot, slot, ORDERS[p][2], self.place(p, 2, turn)

                self.sends.start((self.name, 2, p, turn), make)

    def puts(self):
        return [pltpu.make_async_copy(self.final.at[p], self.rows(p, 0, 0), self.sems.at[p]) for p in range(PARTS)]

    def settle(self):
        for p in range(PARTS):
            for turn in (1, 3, 2):
                self.sends.arrived((self.name, 2, p, turn))
            total = self.slots[p, 0].astype(F32) + self.slots[p, 1].astype(F32)
            self.final[p] = (total + self.slots[p, 2].astype(F32) + self.slots[p, 3].astype(F32)).astype(BF)
            for turn in (2, 1, 3):
                self.sends.start((self.name, 4, p, turn), lambda p=p, turn=turn: (
                    self.final.at[p], self.rows(p, 0, 0), ORDERS[p][1], self.place(p, 1, turn)))
        for put in self.puts():
            put.start()

    def across(self, p, turn):
        def make():
            ref = self.rows(p, turn)
            return ref, ref, "core", 1 - self.at["core"]

        self.sends.start((self.name, 6, p, turn), make)

    def near(self):
        for put in self.puts():
            put.wait()
        for p in range(PARTS):
            for turn in (1, 3, 2):
                self.sends.arrived((self.name, 4, p, turn))
            for turn in (2, 1, 3):
                def make(p=p, turn=turn):
                    ref = self.rows(p, 0)
                    return ref, ref, ORDERS[p][0], self.place(p, 0, turn)

                self.sends.start((self.name, 5, p, turn), make)
            self.across(p, 0)

    def over(self, *turns):
        for turn in turns:
            for p in range(PARTS):
                self.sends.arrived((self.name, 5, p, turn))
                self.across(p, 4 - turn)

    def end(self):
        for turn in (0, 3, 1, 2):
            for p in range(PARTS):
                self.sends.arrived((self.name, 6, p, turn))

    def steps(self):
        return [self.scatter, self.share, self.settle, self.near, lambda: self.over(1, 3), lambda: self.over(2), self.end]


def second_scratch(c):
    return [pltpu.VMEM((PARTS, 3, c, LANES), BF), pltpu.VMEM((PARTS, 4, c, LANES), BF),
            pltpu.VMEM((PARTS, c, LANES), BF), dma(PARTS)]


class Gather:
    def __init__(self, name, at, sends, parts, sems):
        self.name, self.at, self.sends, self.parts, self.sems = name, at, sends, parts, sems

    def place(self, p, s, turn):
        return (self.at[self.parts[p][3][s]] + turn) % 4

    def in_plane(self, p):
        _, plane, _, order = self.parts[p]
        return plane.at[self.at[order[1]], self.at[order[2]]]

    def block(self, p, turn):
        return self.parts[p][2].at[self.at["core"], self.place(p, 0, turn)]

    def puts(self):
        return [pltpu.make_async_copy(part[0], self.in_plane(p), self.sems.at[p]) for p, part in enumerate(self.parts)]

    def last_puts(self):
        return [pltpu.make_async_copy(part[1], self.block(p, 0), self.sems.at[p]) for p, part in enumerate(self.parts)]

    def send(self, s, pick):
        for turn in (2, 1, 3):
            for p in range(len(self.parts)):
                self.sends.start((self.name, s, p, turn), lambda p=p, turn=turn: (
                    *pick(p), self.parts[p][3][s], self.place(p, s, turn)))

    def arrived(self, s, *turns):
        for turn in turns:
            for p in range(len(self.parts)):
                self.sends.arrived((self.name, s, p, turn))

    def across(self, turn):
        for p in range(len(self.parts)):
            def make(p=p):
                ref = self.block(p, turn)
                return self.parts[p][1] if turn == 0 else ref, ref, "core", 1 - self.at["core"]

            self.sends.start((self.name, 3, p, turn), make)

    def plane_steps(self):
        def first():
            for put in self.puts():
                put.start()
            self.send(2, lambda p: (self.parts[p][0], self.in_plane(p)))

        def second():
            for put in self.puts():
                put.wait()
            self.arrived(2, 1, 3, 2)

            def row(p):
                ref = self.parts[p][1].at[self.at[self.parts[p][3][1]]]
                return ref, ref

            self.send(1, row)

        return [first, second, lambda: self.arrived(1, 1, 3, 2)]

    def whole_steps(self):
        def first():
            for put in self.last_puts():
                put.start()
            self.send(0, lambda p: (self.parts[p][1], self.block(p, 0)))
            self.across(0)

        def more():
            self.arrived(0, 1)
            self.across(3)
            self.arrived(0, 3)
            self.across(1)

        def rest():
            self.arrived(0, 2)
            self.across(2)

        def end():
            self.arrived(3, 0, 3, 1, 2)
            for put in self.last_puts():
                put.wait()

        return [first, more, rest, end]


class SmallSum:
    def __init__(self, name, at, sends, x, core_in, slots):
        self.name, self.at, self.sends, self.x, self.core_in, self.slots = name, at, sends, x, core_in, slots

    def begin(self):
        for p in range(PARTS):
            self.sends.start((self.name, 3, p, 0), lambda p=p: (
                self.x.at[pl.ds(16 * p, 16)], self.core_in.at[p], "core", 1 - self.at["core"]))

    def total(self, p, s):
        if s == 0:
            self.sends.arrived((self.name, 3, p, 0))
            return self.x[16 * p : 16 * p + 16].astype(F32) + self.core_in[p].astype(F32)
        for turn in (1, 3, 2):
            self.sends.arrived((self.name, s - 1, p, turn))
        slots = self.slots.at[p, s - 1]
        return slots[0].astype(F32) + slots[1].astype(F32) + slots[2].astype(F32) + slots[3].astype(F32)

    def stage(self, s):
        for p in range(PARTS):
            self.slots[p, s, self.at[ORDERS[p][s]]] = self.total(p, s).astype(BF)
            for turn in (2, 1, 3):
                def make(p=p, turn=turn):
                    slot = self.slots.at[p, s, self.at[ORDERS[p][s]]]
                    return slot, slot, ORDERS[p][s], (self.at[ORDERS[p][s]] + turn) % 4

                self.sends.start((self.name, s, p, turn), make)

    def steps(self, out):
        def end():
            for p in range(PARTS):
                out[16 * p : 16 * p + 16] = self.total(p, 3).astype(BF)

        return [self.begin, lambda: self.stage(0), lambda: self.stage(1), lambda: self.stage(2), end]


def steps_in(i, *table):
    for turn, *steps in table:
        @pl.when(i == turn)
        def run():
            for step in steps:
                step()


D = 768
HALF = 384
HIDDEN = 1536
TILE = 128
TAPW = 128
PADDED = LEN + 16
SHARED_ROWS = 6144
VMEM_BYTES = 60 << 20
EARLY = 3072
POINT_AT, TAPS_AT, SMALL_AT = EARLY + 1536, EARLY + 2304, EARLY + 2368
SMALL_DEPTH, SMALL_FFN, SMALL_BIAS, SMALL_SEG, SMALL = 0, 18, 36, 43, 48


class Params(NamedTuple):
    hidden: jax.Array
    cotangent: jax.Array
    lengths: jax.Array
    split_at: jax.Array
    seg_table: jax.Array
    w_query: jax.Array
    b_query: jax.Array
    w_key: jax.Array
    w_value: jax.Array
    b_value: jax.Array
    w_depth: jax.Array
    w_point: jax.Array
    b_keyconv: jax.Array
    w_kernel: jax.Array
    b_kernel: jax.Array
    w_conv: jax.Array
    b_conv: jax.Array
    w_out: jax.Array
    b_out: jax.Array
    first_gain: jax.Array
    first_shift: jax.Array
    w_up: jax.Array
    b_up: jax.Array
    down_weight: jax.Array
    b_down: jax.Array
    second_gain: jax.Array
    second_shift: jax.Array


KEPT_SHAPES = (((LEN, D), BF), ((LEN, HALF), F32), ((LEN, HALF), BF), ((LEN, HALF), BF), ((LEN, D), BF),
               ((LEN, HALF), F32), ((PADDED, KERNEL * TAPW), F32), ((PADDED, HALF), F32), ((LEN, D), BF),
               ((LEN, D), F32))


def dims(lhs, rhs):
    return (((lhs,), (rhs,)), ((), ()))


def dot(a, b):
    return lax.dot_general(a, b, dims(1, 0), preferred_element_type=F32)


def dot_nt(a, b):
    return lax.dot_general(a, b, dims(1, 1), preferred_element_type=F32)


def dot_tn(a, b):
    return lax.dot_general(a, b, dims(0, 0), preferred_element_type=F32)


def tile_rows(i, n=TILE, start=0):
    return pl.ds(pl.multiple_of(i * n + start, 8 if start % 16 else 16), n)


def lanes_at(start, n=128):
    return pl.ds(pl.multiple_of(start, 128), n)


def rows_iota(n, width=1):
    return lax.broadcasted_iota(jnp.int32, (n, width), 0)


class Moves:
    def __init__(self, sems):
        self.sems, self.all = sems, []

    def start(self, src, dst):
        copy = pltpu.make_async_copy(src, dst, self.sems.at[len(self.all)])
        copy.start()
        self.all.append(copy)
        return copy

    def start_cat(self, layer, matrices, w_cat):
        return [self.start(ref.at[layer], w_cat.at[:, pl.ds(n * HALF, HALF)]) for n, ref in enumerate(matrices)]


def wait_all(copies):
    for copy in copies:
        copy.wait()


def my_row():
    row = lax.axis_index("grp")
    for name, size in zip(CH, (4, 4, 2, 2)):
        row = row * size + lax.axis_index(name)
    return row


def widen_matrix():
    lane = np.arange(HALF)[None, :] // HEAD
    return (np.arange(TAPW)[:, None] == lane).astype(ml_dtypes.bfloat16)


def tap_matrix():
    out = np.zeros((TAPW, KERNEL * TAPW), np.float32)
    for h in range(HEADS):
        for j in range(KERNEL):
            out[h * KERNEL + j, j * TAPW + h] = 1.0
    return out.astype(ml_dtypes.bfloat16)


def norm_stats(residual):
    mean = jnp.mean(residual, axis=-1, keepdims=True)
    center = residual - mean
    scale = lax.rsqrt(jnp.mean(center * center, axis=-1, keepdims=True) + EPSILON)
    return center * scale, scale


def norm_grad(gy, hat, scale, gain):
    d_hat = gy * gain
    mean_one = jnp.mean(d_hat, axis=-1, keepdims=True)
    mean_two = jnp.mean(d_hat * hat, axis=-1, keepdims=True)
    return scale * (d_hat - mean_one - hat * mean_two)


def gelu_both(pre):
    base = 1.0 + (0.3275911 * 0.7071067811865476) * jnp.abs(pre)
    t = pl.reciprocal(base, approx=True)
    t = t * (2.0 - base * t)
    poly = t * (0.127414796 + t * (-0.142248368 + t * (0.7107068705 + t * (-0.7265760135 + t * 0.5307027145))))
    bell = jnp.exp(-0.5 * pre * pre)
    tail = poly * bell
    cdf = jnp.where(pre >= 0, 1.0 - tail, tail)
    return pre * cdf, cdf + pre * (bell * 0.3989422804014327)


def far():
    return pl.BlockSpec(memory_space=pl.ANY)


def whole():
    return pl.BlockSpec(memory_space=pltpu.VMEM)


def scalars():
    return pl.BlockSpec(memory_space=pltpu.SMEM)


def dma(n):
    return pltpu.SemaphoreType.DMA((n,))


def shape(dims, dtype):
    return jax.ShapeDtypeStruct(dims, dtype)


def block_shape(rows, lanes=LANES):
    return shape((PARTS, 2, 4, 4, 4, rows, lanes), BF)


def call(kernel, ins, outs, scratch, name, **comm):
    return pl.pallas_call(
        kernel,
        out_shape=[out for out, _ in outs],
        in_specs=[place for _, place in ins],
        out_specs=[place for _, place in outs],
        scratch_shapes=scratch,
        compiler_params=pltpu.CompilerParams(vmem_limit_bytes=VMEM_BYTES, **comm),
        name=name,
    )(*[array for array, _ in ins])


def vmem(*shapes):
    return [pltpu.VMEM(*s) for s in shapes]


class Points(dict):
    def at(self, point):
        for step in self.get(point, ()):
            step()

    def turn(self, point, i):
        for (name, turn), steps in [(key, s) for key, s in self.items() if isinstance(key, tuple)]:
            if name == point:
                steps_in(i, (turn, *steps))


def remote(number):
    return {"collective_id": number, "has_side_effects": True}


def tap_weights(layer, w_kernel, rows):
    rows[...] = jnp.zeros_like(rows)
    for n in range(HEADS * KERNEL):
        rows[n : n + 1, :] = w_kernel[n].astype(F32)[layer : layer + 1, :]


def clear_edges(*refs):
    for ref in refs:
        ref[pl.ds(0, 8), :] = jnp.zeros((8, ref.shape[1]), F32)
        ref[pl.ds(LEN + 8, 8), :] = jnp.zeros((8, ref.shape[1]), F32)


ENTER, DEPTH, ATTEND, END, UNPACK, FEED, BACK, GRAD, OUT, KEY, TAPS, CAT, LEAVE = range(13)

FORWARD_WEIGHTS = 14
FA_SCRATCH = [((LEN, D), BF), ((D, 4 * HALF), BF), ((D, HALF), BF), ((D, D), BF), ((PADDED, D), F32),
              ((LEN, HALF), BF), ((LEN, HALF), BF), ((TAPW, HALF), F32), ((HALF, KERNEL * TAPW), BF),
              ((8, KERNEL * TAPW), F32)]


def attention_forward_body(layer, length, split, x_in, seg, weights, x_all, resid, kept_out, log_total, points, *refs):
    first = layer == 0
    (w_query, w_key, w_value, w_conv, w_point, w_out, w_depth, w_kernel, b_query, b_value, b_conv, b_keyconv, b_kernel,
     b_out, widen, spread) = weights
    kept, refs = refs[:9], refs[9:]
    x_low, query, key_low, value_low, depth_low, key_conv, kernels, conv_pad, joined = kept
    hidden, w_cat, point, out_w, x_pad, query_low, mixed_low, tap_rows, taps_w, tap_bias, sems = refs
    one = slice(layer, layer + 1)
    moves = Moves(sems)
    load_x = [moves.start(x_in, hidden)] if first else []
    load_cat = moves.start_cat(layer, (w_query, w_key, w_value, w_conv), w_cat)
    load_rest = [moves.start(w_point.at[layer], point), moves.start(w_out.at[layer], out_w)]
    clear_edges(x_pad, conv_pad, kernels)
    tap_weights(layer, w_kernel, tap_rows)
    for c in range(0, KERNEL * TAPW, 384):
        taps_w[:, c : c + 384] = dot_tn(tap_rows[...].astype(BF), spread[:, c : c + 384]).astype(BF)
    tap_bias[...] = jnp.zeros_like(tap_bias)
    tap_bias[0:1, 0 : HEADS * KERNEL] = b_kernel[one, :]
    left, bias = tap_bias[:, :TAPW], jnp.zeros((8, KERNEL * TAPW), F32)
    for _ in range(3):
        bias += dot(left.astype(BF), spread[...])
        left = left - left.astype(BF).astype(F32)
    tap_bias[...] = bias

    wait_all(load_x)
    points.at(ENTER)

    @pl.loop(0, LEN // TILE)
    def enter(i):
        rows = tile_rows(i)
        if first:
            place = rows_iota(TILE) + i * TILE
            x = hidden[rows, :].astype(F32) + jnp.where(place > split, seg[1:2, :], seg[0:1, :])
            x = x * (place < length).astype(F32)
            x_all[rows, :] = x
        else:
            x = x_all[rows, :]
        low = x.astype(BF)
        x_low[rows, :] = low
        x_pad[tile_rows(i, TILE, 8), :] = low.astype(F32)

    wait_all(load_cat)
    for n in range(6):
        proj = dot(x_low[...], w_cat[:, n * 256 : n * 256 + 256])
        for h in range(2):
            which, c = (2 * n + h) // 3, (2 * n + h) % 3 * 128
            cols = slice(c, c + 128)
            part = proj[:, h * 128 : h * 128 + 128]
            if which == 0:
                part += b_query[one, cols]
                query[:, cols] = part
                query_low[:, cols] = part.astype(BF)
            elif which == 1:
                key_low[:, cols] = part.astype(BF)
            elif which == 2:
                value_low[:, cols] = (part + b_value[one, cols]).astype(BF)
            else:
                conv_pad[pl.ds(8, LEN), cols] = part + b_conv[one, cols]
    stores = [moves.start(kept[n], kept_out[n]) for n in (0, 1, 2, 3, 7)]

    @pl.loop(0, LEN // TILE)
    def depth(i):
        rows = tile_rows(i)
        around = pl.ds(pl.multiple_of(i * TILE, TILE), TILE + 16)
        for c in range(0, D, 256):
            window = x_pad[around, c : c + 256]
            total = jnp.zeros((TILE, 256), F32)
            for j in range(KERNEL):
                total += w_depth[j, one, c : c + 256].astype(F32) * window[4 + j : 4 + j + TILE]
            depth_low[rows, c : c + 256] = total.astype(BF)

    points.at(DEPTH)
    wait_all(load_rest)
    for c, n in ((0, 256), (256, 128)):
        cols = slice(c, c + n)
        key = dot(depth_low[...], point[:, cols]) + b_keyconv[one, cols]
        key_conv[:, cols] = key
        mixed_low[:, cols] = (key * query[:, cols]).astype(BF)
    for c in range(0, KERNEL * TAPW, 384):
        cols = slice(c, c + 384)
        kernels[pl.ds(8, LEN), cols] = dot(mixed_low[...], taps_w[:, cols]) + tap_bias[0:1, cols]
    stores += [moves.start(kept[n], kept_out[n]) for n in (4, 5)]

    @pl.loop(0, LEN // TILE)
    def convolve(i):
        rows = tile_rows(i)
        around = pl.ds(pl.multiple_of(i * TILE, TILE), TILE + 16)
        padded = tile_rows(i, TILE, 8)
        taps = [kernels[padded, j * TAPW : (j + 1) * TAPW] for j in range(KERNEL)]
        peak = functools.reduce(jnp.maximum, taps)
        taps = [jnp.exp(t - peak) for t in taps]
        share = 1.0 / sum(taps)
        window = conv_pad[around, :]
        mix = jnp.zeros((TILE, HALF), F32)
        for j in range(KERNEL):
            tap = taps[j] * share
            kernels[padded, j * TAPW : (j + 1) * TAPW] = tap
            mix += dot(tap.astype(BF), widen[...]) * window[4 + j : 4 + j + TILE]
        joined[rows, HALF:] = mix.astype(BF)

    stores += [moves.start(kept[6], kept_out[6])]

    @pl.loop(0, HEADS // 2)
    def attend(pair):
        points.turn(ATTEND, pair)
        lanes = lanes_at(pair * 128)
        keys = key_low[:, lanes] * jnp.asarray(SCORE_SCALE, BF)
        side = lax.broadcasted_iota(jnp.int32, (LEN, 128), 1) // HEAD
        values = jnp.transpose(value_low[:, lanes].astype(F32)).astype(BF)
        for block in range(2):
            cols = slice(block * 256, block * 256 + 256)
            queries = query_low[cols, lanes]
            pieces_t = []
            for head in range(2):
                mine = jnp.where(side == head, keys, jnp.zeros_like(keys))
                scores = dot_nt(mine, queries)
                scores = jnp.where(rows_iota(LEN, 256) < length, scores, MASK_VALUE)
                peak = jnp.max(scores, axis=0, keepdims=True)
                probs = jnp.exp(scores - peak)
                total = jnp.sum(probs, axis=0, keepdims=True)
                log_total[pair * 2 + head, :, cols] = peak + jnp.log(total)
                probs = (probs * (1.0 / total)).astype(BF)
                pieces_t.append(dot(values[head * HEAD : (head + 1) * HEAD, :], probs))
            joined[cols, lanes] = jnp.transpose(jnp.concatenate(pieces_t, axis=0)).astype(BF)

    stores += [moves.start(kept[8], kept_out[8])]
    points.at(ATTEND)
    for c in range(0, D, 256):
        cols = slice(c, c + 256)
        resid[:, cols] = x_all[:, cols] + dot(joined[...], out_w[:, cols]) + b_out[one, cols]
    points.at(END)
    wait_all(stores)


PLANES = (PARTS, 4, 4, 16, LANES)


def part_block(ref, p, core, x, y, z):
    if p == 0:
        return ref.at[0, core, x, y, z]
    if p == 1:
        return ref.at[1, core, y, z, x]
    return ref.at[2, core, z, x, y]


FFN_SHAPES = [((2 * HIDDEN, HALF), BF)] * 2 + [((LEN, 2 * HIDDEN), BF)] * 2 + [((LEN, D), F32)]
FF_SCRATCH = [((LEN, D), F32), ((LEN, D), BF), ((LEN, 512), F32), ((2, 64, TAPW), F32), ((1, 2 * HIDDEN), F32)]


def ffn_forward_body(layer, length, gathered, bias_all, norms, resid, x_next, outs, ffn, points, *refs):
    first_gain, first_shift, b_down, second_gain, second_shift = norms
    up, down, acted, slope, resid_two = ffn
    normed_rows, low, pre, bias_rows, bias, sems, block_sems = refs
    one = slice(layer, layer + 1)
    moves = Moves(sems)

    @pl.loop(0, LEN // TILE)
    def enter(i):
        rows = tile_rows(i)
        hat, _ = norm_stats(resid[rows, :])
        normed = hat * first_gain[one, :] + first_shift[one, :]
        normed_rows[rows, :] = normed
        low[rows, :] = normed.astype(BF)

    points.at(ENTER)

    @pl.loop(0, 64)
    def unpack(chip):
        z, y, x = (chip // 32) * 2 + chip % 2, (chip // 8) % 4, (chip // 2) % 4
        ups, downs = [], []
        for core in range(2):
            piece = jnp.concatenate(
                [part_block(gathered, p, core, x, y, z)[...].astype(F32) for p in range(PARTS)], axis=0)
            ups.append(piece[:24])
            downs.append(piece[24:])
            bias_rows[core, pl.ds(chip, 1), :] = bias_all[core, x, y, z].astype(F32)[one, :]
        rows = tile_rows(chip, 48)
        up[rows, :] = jnp.concatenate(ups, axis=0).astype(BF)
        down[rows, :] = jnp.concatenate(downs, axis=0).astype(BF)

    stores = [moves.start(up, outs[0]), moves.start(down, outs[1])] if outs else []
    points.at(UNPACK)
    for c in range(0, 2 * HIDDEN, 512):
        spot = lax.broadcasted_iota(jnp.int32, (64, 512), 1) + c
        slot = (lax.broadcasted_iota(jnp.int32, (TAPW, 512), 1) + c) % 24
        repeat = (slot == rows_iota(TAPW, 512)).astype(F32).astype(BF)
        total = jnp.zeros((1, 512), F32)
        for core in range(2):
            spread = dot(bias_rows[core].astype(BF), repeat)
            mine = spot // 24 == 2 * rows_iota(64, 512) + core
            total += jnp.sum(jnp.where(mine, spread, 0.0), axis=0, keepdims=True)
        bias[:, c : c + 512] = total

    def block_stores(n):
        cols = lanes_at(n * 512, 512)
        return [pltpu.make_async_copy(src.at[:, cols], out.at[:, cols], block_sems.at[2 * n + m])
                for m, (src, out) in enumerate(((acted, outs[2]), (slope, outs[3])))]

    for g in range(2):
        @pl.loop(0, HIDDEN // 512)
        def feed(k):
            at = g * HIDDEN + k * 512
            hidden = pl.ds(pl.multiple_of(at, 512), 512)
            pre[...] = dot_nt(low[:, g * HALF : (g + 1) * HALF], up[hidden, :]) + bias[:, hidden]

            @pl.loop(0, LEN // 32)
            def act(i):
                few = tile_rows(i, 32)
                for c in range(0, 512, 256):
                    value, grad = gelu_both(pre[few, c : c + 256])
                    cols = lanes_at(at + c, 256)
                    acted[few, cols] = value.astype(BF)
                    slope[few, cols] = grad.astype(BF)

            if outs:
                for store in block_stores(g * (HIDDEN // 512) + k):
                    store.start()

        points.at(FEED + 100 * g)

    @pl.loop(0, LEN // 256)
    def leave(i):
        rows = tile_rows(i, 256)
        out = []
        for g in range(2):
            hidden = slice(g * HIDDEN, (g + 1) * HIDDEN)
            out.append(dot(acted[rows, hidden], down[hidden, :]).astype(BF).astype(F32))
        two = normed_rows[rows, :] + jnp.concatenate(out, axis=1) + b_down[one, :]
        resid_two[rows, :] = two
        hat, _ = norm_stats(two)
        valid = (rows_iota(256) + i * 256 < length).astype(F32)
        x_next[rows, :] = (hat * second_gain[one, :] + second_shift[one, :]) * valid

    points.at(END)
    if outs:
        stores.append(moves.start(resid_two, outs[4]))
        for n in range(2 * HIDDEN // 512):
            wait_all(block_stores(n))
    wait_all(stores)


BF_SCRATCH = [(block_shape(16).shape, BF), ((LEN, D), F32), ((LEN, 2 * HIDDEN), BF), ((LEN, D), BF),
              ((LEN, D), BF)]


def ffn_backward_body(layer, length, norms, gy, ffn, resid, d_resid, outs, waits, points, *refs):
    first_gain, first_shift, _, second_gain, _ = norms
    up, down, acted, slope, resid_two = ffn
    d_resid_out, grads_out, small = outs
    grads, d_two, d_pre, d_group, normed_low, sems = refs
    one = slice(layer, layer + 1)
    moves = Moves(sems)
    small[...] = jnp.zeros_like(small)

    def note(slot, value):
        total = jnp.sum(value, axis=0, keepdims=True)
        small[slot : slot + 1, :] += total[:, :HALF]
        small[slot + 1 : slot + 2, :] += total[:, HALF:]

    wait_all(waits[0])

    @pl.loop(0, LEN // TILE)
    def enter(i):
        rows = tile_rows(i)
        valid = (rows_iota(TILE) + i * TILE < length).astype(F32)
        grad = gy[rows, :].astype(F32) * valid
        hat, scale = norm_stats(resid_two[rows, :])
        note(0, grad * hat)
        note(2, grad)
        two = norm_grad(grad, hat, scale, second_gain[one, :])
        note(4, two)
        d_two[rows, :] = two
        d_group[rows, :] = two.astype(BF)
        hat, _ = norm_stats(resid[rows, :])
        normed_low[rows, :] = (hat * first_gain[one, :] + first_shift[one, :]).astype(BF)

    points.at(ENTER)
    wait_all(waits[1])
    for g in range(2):
        @pl.loop(0, HIDDEN // 256)
        def feed(k):
            hidden = pl.ds(pl.multiple_of(g * HIDDEN + k * 256, 256), 256)
            d_act = dot_nt(d_group[:, g * HALF : (g + 1) * HALF], down[hidden, :])
            d_pre[:, hidden] = (d_act * slope[:, hidden].astype(F32)).astype(BF)

        points.at(FEED + 100 * g)

    wait_all(waits[2])

    @pl.loop(0, LEN // 256)
    def back(i):
        rows = tile_rows(i, 256)
        got = []
        for g in range(2):
            hidden = slice(g * HIDDEN, (g + 1) * HIDDEN)
            got.append(dot(d_pre[rows, hidden], up[hidden, :]).astype(BF).astype(F32))
        d_normed = d_two[rows, :] + jnp.concatenate(got, axis=1)
        hat, scale = norm_stats(resid[rows, :])
        note(6, d_normed * hat)
        note(8, d_normed)
        d_resid[rows, :] = norm_grad(d_normed, hat, scale, first_gain[one, :])

    stores = [moves.start(d_resid, d_resid_out)] if d_resid_out is not None else []
    points.at(BACK)
    ones = jnp.ones((8, LEN), BF)
    for k in range(8):
        small[10 + k : 11 + k, :] = dot(ones, d_pre[:, k * HALF : (k + 1) * HALF])[0:1, :]

    for g in range(2):
        @pl.loop(0, 4)
        def grad(y):
            points.turn(GRAD + 100 * g, y)
            hidden = lanes_at(g * HIDDEN + y * HALF, HALF)
            cols = slice(g * HALF, (g + 1) * HALF)
            d_up = dot_tn(d_pre[:, hidden], normed_low[:, cols])
            d_down = dot_tn(acted[:, hidden], d_group[:, cols])
            for d in range(16):
                x, z, core = d // 4, g * 2 + (d // 2) % 2, d % 2
                piece = jnp.concatenate([d_up[24 * d : 24 * d + 24], d_down[24 * d : 24 * d + 24]], axis=0).astype(BF)
                for p in range(PARTS):
                    part_block(grads, p, core, x, y, z)[...] = piece[16 * p : 16 * p + 16]

        zs = pl.ds(2 * g, 2)
        for index in ((0, slice(None), slice(None), slice(None), zs), (1, slice(None), slice(None), zs),
                      (2, slice(None), zs)):
            stores.append(moves.start(grads.at[index], grads_out.at[index]))

    points.at(END)
    wait_all(stores)


BA_SCRATCH = [((D, 4 * HALF), BF), ((D, HALF), BF), ((D, D), BF), ((LEN, D), BF), ((LEN, 4 * HALF), BF), ((LEN, D), BF),
              ((LEN, HALF), BF), ((LEN, HALF), F32), ((PADDED, HALF), F32), ((PADDED, D), F32), ((SMALL, HALF), F32),
              ((LEN, TAPW), BF), ((TAPW, HALF), F32)]


def attention_backward_body(layer, length, split, d_resid, waits, kept_in, log_total, ffn_small, weights, shared, d_input,
                            small_out, points, *refs):
    first = layer == 0
    w_query, w_key, w_value, w_conv, w_point, w_out, w_depth, w_kernel, widen, spread = weights
    kept, refs = refs[:9], refs[9:]
    x_low, query, key_low, value_low, depth_low, key_conv, kernels, conv_pad, joined = kept
    (w_cat, point, out_w, d_proj, d_cat, d_join, query_low, d_att, mix_pad, depth_pad, small, d_tap, tap_rows,
     sems) = refs
    moves = Moves(sems)
    load_first = [*waits, moves.start(w_out.at[layer], out_w)]
    load = [moves.start(kept_in[n], kept[n]) for n in (8, 1, 2, 3, 6, 7, 5, 4, 0)]
    load_cat = moves.start_cat(layer, (w_query, w_key, w_value, w_conv), w_cat)
    load_point = moves.start(w_point.at[layer], point)
    clear_edges(mix_pad, depth_pad)
    small[...] = jnp.zeros_like(small)
    small[SMALL_FFN : SMALL_FFN + 18, :] = ffn_small[0:18, :]
    shared[SMALL_AT:, :] = jnp.zeros((SHARED_ROWS - SMALL_AT, HALF), BF)
    tap_weights(layer, w_kernel, tap_rows)

    def note(slot, value):
        total = jnp.sum(value, axis=0, keepdims=True)
        for n in range(total.shape[1] // HALF):
            small[slot + n : slot + n + 1, :] += total[:, n * HALF : (n + 1) * HALF]

    points.at(ENTER)
    wait_all(load_first)

    @pl.loop(0, LEN // TILE)
    def enter(i):
        rows = tile_rows(i)
        low = d_resid[rows, :].astype(BF)
        d_proj[rows, :] = low
        note(SMALL_BIAS + 5, low.astype(F32))

    for c in range(0, D, 256):
        d_join[:, c : c + 256] = dot_nt(d_proj[...], out_w[c : c + 256, :]).astype(BF)
    mix_pad[pl.ds(8, LEN), :] = d_join[:, HALF:].astype(F32)
    load[0].wait()

    @pl.loop(0, D // 256)
    def out_grad(c):
        part = dot_tn(joined[:, lanes_at(c * 256, 256)], d_proj[...])
        for n in range(2):
            shared[chunk(n * D + c * 256, 256), :] = part[:, n * HALF : (n + 1) * HALF].astype(BF)

    points.at(OUT)
    wait_all(load[1:4])
    query_low[...] = query[...].astype(BF)

    @pl.loop(0, HEADS // 2)
    def attend(pair):
        points.turn(ATTEND, pair)
        lanes = lanes_at(pair * 128)
        keys = key_low[:, lanes]
        values = value_low[:, lanes]
        scaled = keys * jnp.asarray(SCORE_SCALE, BF)
        keys_t = jnp.transpose(keys.astype(F32)).astype(BF)
        side = lax.broadcasted_iota(jnp.int32, (LEN, 128), 1) // HEAD
        nothing = jnp.zeros_like(keys)
        d_keys = [None, None]
        d_values = [None, None]
        for block in range(2):
            cols = slice(block * 256, block * 256 + 256)
            queries = query_low[cols, lanes]
            d_context = d_join[cols, lanes]
            pieces = []
            for head in range(2):
                scores = dot_nt(jnp.where(side == head, scaled, nothing), queries)
                scores = jnp.where(rows_iota(LEN, 256) < length, scores, MASK_VALUE)
                probs = jnp.exp(scores - log_total[pair * 2 + head, :, cols])
                d_probs = dot_nt(jnp.where(side == head, values, nothing), d_context)
                weighted = probs * d_probs
                row_dot = jnp.sum(weighted, axis=0, keepdims=True)
                d_scores = (weighted - probs * row_dot).astype(BF)
                pieces.append(dot(keys_t[head * HEAD : (head + 1) * HEAD, :], d_scores))
                part = dot(d_scores, queries)
                d_keys[head] = part if block == 0 else d_keys[head] + part
                part = dot(probs.astype(BF), d_context)
                d_values[head] = part if block == 0 else d_values[head] + part
            d_att[cols, lanes] = jnp.transpose(jnp.concatenate(pieces, axis=0)) * SCORE_SCALE
        d_cat[:, lanes_at(HALF + pair * 128)] = (jnp.where(side == 0, d_keys[0], d_keys[1]) * SCORE_SCALE).astype(BF)
        d_cat[:, lanes_at(2 * HALF + pair * 128)] = jnp.where(side == 0, d_values[0], d_values[1]).astype(BF)

    wait_all(load[7:])

    @pl.loop(0, D // 256)
    def key_grad(c):
        low = x_low[:, lanes_at(c * 256, 256)]
        for n in range(2):
            part = dot_tn(low, d_cat[:, (n + 1) * HALF : (n + 2) * HALF])
            shared[chunk(1536 + n * D + c * 256, 256), :] = part.astype(BF)

    points.at(KEY)
    wait_all(load[4:7])

    @pl.loop(0, LEN // TILE)
    def taps(i):
        points.turn(TAPS, i)
        rows = tile_rows(i)
        around = pl.ds(pl.multiple_of(i * TILE, TILE), TILE + 16)
        padded = tile_rows(i, TILE, 8)
        mix = mix_pad[padded, :]
        window = conv_pad[around, :]
        mix_window = mix_pad[around, :]
        d_kernel, d_conv = [], jnp.zeros((TILE, HALF), F32)
        dotted = jnp.zeros((TILE, TAPW), F32)
        for j in range(KERNEL):
            part = dot_nt((mix * window[4 + j : 4 + j + TILE]).astype(BF), widen[...])
            d_kernel.append(part)
            dotted += part * kernels[padded, j * TAPW : (j + 1) * TAPW]
            share = kernels[around, j * TAPW : (j + 1) * TAPW][12 - j : 12 - j + TILE]
            d_conv += dot(share.astype(BF), widen[...]) * mix_window[12 - j : 12 - j + TILE]
        d_cat[rows, 3 * HALF :] = d_conv.astype(BF)
        wide = [kernels[padded, j * TAPW : (j + 1) * TAPW] * (d_kernel[j] - dotted) for j in range(KERNEL)]
        d_logit = dot_nt(jnp.concatenate(wide, axis=1).astype(BF), spread[...]).astype(BF)
        d_tap[rows, :] = d_logit
        d_mixed = dot(d_logit, tap_rows[...].astype(BF))
        q = query[rows, :]
        key = key_conv[rows, :]
        d_keyconv = (d_mixed * q).astype(BF)
        d_cat[rows, :HALF] = (d_att[rows, :] + d_mixed * key).astype(BF)
        note(SMALL_BIAS + 2, d_keyconv.astype(F32))
        cat = d_cat[rows, :].astype(F32)
        note(SMALL_BIAS, cat[:, :HALF])
        note(SMALL_BIAS + 1, cat[:, 2 * HALF : 3 * HALF])
        note(SMALL_BIAS + 3, cat[:, 3 * HALF :])
        small[SMALL_BIAS + 4 : SMALL_BIAS + 5, :TAPW] += jnp.sum(d_logit.astype(F32), axis=0, keepdims=True)
        d_join[rows, HALF:] = d_keyconv
        d_join[rows, :HALF] = (key * q).astype(BF)

    points.at(TAPS)
    shared[TAPS_AT : TAPS_AT + 64, :] = dot_tn(d_tap[...], d_join[:, :HALF])[:64].astype(BF)
    load_point.wait()
    for c in range(0, D, 256):
        depth_pad[pl.ds(8, LEN), c : c + 256] = dot_nt(d_join[:, HALF:], point[c : c + 256, :])

    @pl.loop(0, D // 256)
    def cat_grad(c):
        lanes = lanes_at(c * 256, 256)
        for n, k in enumerate((0, 3)):
            part = dot_tn(x_low[:, lanes], d_cat[:, k * HALF : (k + 1) * HALF])
            shared[chunk(EARLY + n * D + c * 256, 256), :] = part.astype(BF)
        part = dot_tn(depth_low[:, lanes], d_join[:, HALF:])
        shared[chunk(POINT_AT + c * 256, 256), :] = part.astype(BF)

    points.at(CAT)
    wait_all(load_cat)
    for n in range(3):
        cols = slice(n * 256, n * 256 + 256)
        d_input[:, cols] = d_resid[:, cols] + dot_nt(d_cat[...], w_cat[cols, :])
        points.at(LEAVE + 100 * n)

        @pl.loop(0, LEN // TILE)
        def leave(i):
            rows = tile_rows(i)
            window = depth_pad[pl.ds(pl.multiple_of(i * TILE, TILE), TILE + 16), cols]
            low = x_low[rows, cols].astype(F32)
            total = d_input[rows, cols]
            for j in range(KERNEL):
                moved = window[12 - j : 12 - j + TILE]
                total += w_depth[j, layer : layer + 1, cols].astype(F32) * moved
                tap = jnp.sum(low * moved, axis=0, keepdims=True)
                if n == 0:
                    small[SMALL_DEPTH + j : SMALL_DEPTH + j + 1, 0:256] += tap
                elif n == 1:
                    small[SMALL_DEPTH + j : SMALL_DEPTH + j + 1, 256:] += tap[:, :128]
                    small[SMALL_DEPTH + 9 + j : SMALL_DEPTH + 10 + j, :128] += tap[:, 128:]
                else:
                    small[SMALL_DEPTH + 9 + j : SMALL_DEPTH + 10 + j, 128:] += tap
            d_input[rows, cols] = total

    if first:
        @pl.loop(0, LEN // TILE)
        def seg_grad(i):
            rows = tile_rows(i)
            place = rows_iota(TILE) + i * TILE
            grad = d_input[rows, :] * (place < length).astype(F32)
            later = (place > split).astype(F32)
            note(SMALL_SEG + 2, grad * later)
            note(SMALL_SEG, grad * (1.0 - later))
            d_input[rows, :] = grad

    small_out[...] = small[...].astype(BF)
    points.at(END)


def forward_kernel(*refs):
    (lengths, splits, hidden, seg, cotangent, pieces), weights, norms = refs[:6], refs[6:22], refs[22:27]
    refs = refs[27:]
    kept_out = refs[:10], refs[10:19]
    log_totals, ffn_out, refs = refs[19:21], refs[21:26], refs[26:]
    output, d_resid_out, grads_out, small, refs = *refs[:4], refs[4:]
    (x_all, resid, gathered_0, gathered_1, planes_0, planes_1, bias_all, bias_plane, sems, own_sems, send_sems,
     recv_sems) = refs
    at = here()
    greet(at)
    length, split = lengths[my_row()], splits[my_row()]
    moves = Moves(sems)
    sends = Sends(send_sems, recv_sems)
    gathered, planes = (gathered_0, gathered_1), (planes_0, planes_1)
    plane, whole_of = [], []
    for layer in range(LAYERS):
        parts = [(pieces.at[layer * PARTS + p], planes[layer].at[p], gathered[layer].at[p], ORDERS[p])
                 for p in range(PARTS)]
        if layer == 0:
            parts.append((pieces.at[LAYERS * PARTS, :, pl.ds(0, TAPW)], bias_plane, bias_all, ORDERS[0]))
        gather = Gather(layer, at, sends, parts, own_sems.at[pl.ds(4 * layer, 4)])
        plane.append(gather.plane_steps())
        whole_of.append(gather.whole_steps())
    (a0, a1, a2), (b0, b1, b2, b3) = plane[0], whole_of[0]
    (c0, c1, c2), (d0, d1, d2, d3) = plane[1], whole_of[1]
    met()
    a0()
    points = (
        (Points({ENTER: (a1,), DEPTH: (a2, b0), ATTEND: (b1,), END: (b2,)}),
         Points({ENTER: (b3,), UNPACK: (c0,), FEED: (c1,), END: (c2, d0)})),
        (Points({(ATTEND, 1): (d1,), (ATTEND, 2): (d2,)}), Points({ENTER: (d3,)})),
    )
    stores = []
    for layer in range(LAYERS):
        pl.run_scoped(
            lambda *s: attention_forward_body(layer, length, split, hidden, seg, weights, x_all, resid, kept_out[layer],
                                              log_totals[layer], points[layer][0], *s),
            *vmem(*KEPT_SHAPES[:9], *FA_SCRATCH), dma(24))
        if layer == 0:
            stores.append(moves.start(resid, kept_out[0][9]))

            def feed(*s):
                ffn_forward_body(0, length, gathered_0, bias_all, norms, resid, x_all, ffn_out, s[:5], points[0][1], *s[5:])

            pl.run_scoped(feed, *vmem(*FFN_SHAPES, *FF_SCRATCH), dma(4), dma(12))
            wait_all(stores)
        else:
            def feed_both(gy, *s):
                ffn, s = s[:5], s[5:]
                load = moves.start(cotangent, gy)
                n = len(FF_SCRATCH) + 2
                ffn_forward_body(1, length, gathered_1, bias_all, norms, resid, x_all, None, ffn, points[1][1], *s[:n])
                stores.append(moves.start(x_all, output))
                ffn_backward_body(1, length, norms, gy, ffn, resid, s[n], (d_resid_out, grads_out, small), ([load], [], []),
                                  Points(), *s[n + 1 :])
                stores[-1].wait()

            pl.run_scoped(feed_both, *vmem(((LEN, D), BF), *FFN_SHAPES, *FF_SCRATCH), dma(1), dma(1),
                          *vmem(((LEN, D), F32), *BF_SCRATCH), dma(16))
    sends.finish()


def projections(w):
    return [(m, far()) for m in (w.w_query, w.w_key, w.w_value, w.w_conv, w.w_point, w.w_out)]


def norm_params(w):
    return [(m, whole()) for m in (w.first_gain, w.first_shift, w.b_down, w.second_gain, w.second_shift)]


def forward(pieces, w):
    ins = [(w.lengths, scalars()), (w.split_at, scalars()), (w.hidden, far()), (w.seg_table, whole()),
           (w.cotangent, far()), (pieces, far())] + projections(w)
    ins += [(m, whole()) for m in (w.w_depth, w.w_kernel, w.b_query, w.b_value, w.b_conv, w.b_keyconv, w.b_kernel,
                                   w.b_out, widen_matrix(), tap_matrix())] + norm_params(w)
    outs = [(shape(*s), far()) for s in KEPT_SHAPES + KEPT_SHAPES[:9]]
    outs += [(shape((HEADS, 1, LEN), F32), whole())] * 2 + [(shape(*s), far()) for s in FFN_SHAPES]
    outs += [(shape((LEN, D), F32), far())] * 2 + [(block_shape(16), far()), (shape((32, HALF), F32), whole())]
    plane, gathered = ((PARTS, 4, 4, 16, LANES), BF), (block_shape(16).shape, BF)
    scratch = vmem(((LEN, D), F32), ((LEN, D), F32), gathered, gathered, plane, plane, ((2, 4, 4, 4, 16, TAPW), BF),
                   ((4, 4, 16, TAPW), BF))
    scratch += [dma(4), dma(8), dma(112), dma(112)]
    outs = call(forward_kernel, ins, outs, scratch, "forward", **remote(1))
    return (*outs[:10], outs[19]), (*outs[10:19], outs[20]), outs[21:26], outs[26:]


def first_sums(at, sends, shared, mids, scratch):
    return [FirstSum(n, at, sends, shared.at[pl.ds(n * EARLY, EARLY)], mids[n], scratch[4 * n : 4 * n + 4]).steps()
            for n in range(2)]


def second_sums(name, at, sends, mids, gathered, scratch):
    return [SecondSum(name + n, at, sends, mids[n], gathered[n], scratch[4 * n : 4 * n + 4]).steps() for n in range(2)]


def backward_ins(kept, w):
    ins = [(w.lengths, scalars()), (w.split_at, scalars())] + [(m, far()) for m in kept[:9]]
    ins += [(kept[-1], whole())] + projections(w)
    return ins + [(m, whole()) for m in (w.w_depth, w.w_kernel, widen_matrix(), tap_matrix())]


GROUP, MIDS, SMALLS = shape((EARLY, HALF), BF), shape((PARTS, EARLY // 24, LANES), BF), shape((SMALL, HALF), BF)
OWN = shape((PARTS, 16, LANES), BF)


def middle_kernel(*refs):
    (lengths, splits), kept_in, log_total, refs = refs[:2], refs[2:11], refs[11], refs[12:]
    weights, ffn_small, d_resid_in, ffn_grads, refs = refs[:10], refs[10], refs[11], refs[12], refs[13:]
    d_input_out, own, early_mid, late_mid, small, refs = *refs[:5], refs[5:]
    d_input, shared, d_resid, refs = *refs[:3], refs[3:]
    sum_refs, scatter_refs, (sems, send_sems, recv_sems) = refs[:8], refs[8:14], refs[14:]
    at = here()
    greet(at)
    length, split = lengths[my_row()], splits[my_row()]
    moves = Moves(sems)
    load = moves.start(d_resid_in, d_resid)
    sends = Sends(send_sems, recv_sems)
    scatter = Scatter(5, at, sends, ffn_grads, scatter_refs)
    f = scatter.steps()
    e, l = first_sums(at, sends, shared, (early_mid, late_mid), sum_refs)
    met()
    points = Points({ENTER: (f[0],), (ATTEND, 2): (f[1], f[2]), KEY: (f[3], f[4], e[0]), (TAPS, 3): (e[1], e[2]),
                     TAPS: (e[3], e[4]), CAT: (f[5], l[0]), LEAVE + 100: (l[1], l[2]), LEAVE + 200: (l[3], l[4], f[6]),
                     END: (e[5], f[7])})
    pl.run_scoped(
        lambda *refs: attention_backward_body(1, length, split, d_resid, [load], kept_in, log_total, ffn_small, weights,
                                              shared, d_input, small, points, *refs),
        *vmem(*KEPT_SHAPES[:9], *BA_SCRATCH), dma(24))
    store = moves.start(d_input, d_input_out)
    for p in range(PARTS):
        own[p] = scatter.own(p)[...]
    l[5]()
    sends.finish()
    store.wait()


def middle(d_resid, kept, ffn_small, ffn_grads, w):
    ins = backward_ins(kept, w) + [(ffn_small, whole()), (d_resid, far()), (ffn_grads, far())]
    outs = [(shape((LEN, D), F32), far())] + [(m, whole()) for m in (OWN, MIDS, MIDS, SMALLS)]
    scratch = vmem(((LEN, D), F32), ((SHARED_ROWS, HALF), BF), ((LEN, D), F32))
    scratch += first_scratch(32) * 2 + scatter_scratch(16)
    return call(middle_kernel, ins, outs, scratch + [dma(2), dma(96), dma(96)], "middle", **remote(2))


def last_kernel(*refs):
    (lengths, splits), kept_in, log_total, refs = refs[:2], refs[2:11], refs[11], refs[12:]
    weights, gy_in, ffn_in, resid_in, norms, refs = refs[:10], refs[10], refs[11:16], refs[16], refs[17:22], refs[22:]
    above_mids, above_small, refs = refs[:2], refs[2], refs[3:]
    d_input_out, grads_out, ffn_small_out, own, refs = *refs[:4], refs[4:]
    above_all, above_small_all, mine_all, small_all, refs = refs[:2], refs[2], refs[3:5], refs[5], refs[6:]
    d_input, d_resid, shared, mids, refs = *refs[:3], refs[3:5], refs[5:]
    sum_refs, second_refs, above_refs, refs = refs[:8], refs[8:16], refs[16:24], refs[24:]
    small, small_refs, above_small_refs, scatter_refs, refs = refs[0], refs[1:3], refs[3:5], refs[5:11], refs[11:]
    sems, send_sems, recv_sems = refs
    at = here()
    greet(at)
    length, split = lengths[my_row()], splits[my_row()]
    moves = Moves(sems)
    sends = Sends(send_sems, recv_sems)
    scatter = Scatter(7, at, sends, grads_out, scatter_refs)
    f = scatter.steps()
    a, b = second_sums(2, at, sends, above_mids, above_all, above_refs)
    c = SmallSum(4, at, sends, above_small, *above_small_refs).steps(above_small_all)
    e, l = first_sums(at, sends, shared, mids, sum_refs)
    more = second_sums(5, at, sends, mids, mine_all, second_refs)
    e, l = e + more[0], l + more[1]
    s = SmallSum(8, at, sends, small, *small_refs).steps(small_all)
    points = Points({FEED + 100: (a[1], b[1]), (GRAD, 1): (a[2], b[2], c[1]), END: (a[3], b[3])})

    def feed(gy, up, down, acted, slope, two, resid, load_sems, *refs):
        loads = Moves(load_sems)
        pairs = ((gy_in, gy), (ffn_in[4], two), (resid_in, resid), (ffn_in[3], slope), (ffn_in[1], down), (ffn_in[0], up),
                 (ffn_in[2], acted))
        loads = [loads.start(*pair) for pair in pairs]
        met()
        for step in (a[0], b[0], c[0]):
            step()
        ffn_backward_body(0, length, norms, gy, (up, down, acted, slope, two), resid, d_resid,
                          (None, grads_out, ffn_small_out), (loads[:3], loads[3:5], loads[5:]), points, *refs)

    pl.run_scoped(feed, *vmem(((LEN, D), F32), *FFN_SHAPES, ((LEN, D), F32)), dma(8), *vmem(*BF_SCRATCH), dma(16))
    points = Points({ENTER: (c[2], f[0]), (ATTEND, 2): (a[4], b[4], f[1]), KEY: (f[2], e[0]), (TAPS, 1): (a[5], b[5], f[3]),
                     (TAPS, 2): (f[4],), (TAPS, 3): (e[1], e[2]), TAPS: (e[3], e[4], c[3]), CAT: (l[0], a[6], b[6]),
                     LEAVE: (e[5], e[6], l[1], l[2]), LEAVE + 100: (l[3], l[4], f[5]), LEAVE + 200: (e[7], f[6]),
                     END: (s[0], e[8], f[7], c[4])})
    pl.run_scoped(
        lambda *refs: attention_backward_body(0, length, split, d_resid, [], kept_in, log_total, ffn_small_out, weights,
                                              shared, d_input, small, points, *refs),
        *vmem(*KEPT_SHAPES[:9], *BA_SCRATCH), dma(24))
    store = moves.start(d_input, d_input_out)
    for step in (l[5], l[6], s[1], e[9], l[7], s[2], l[8], s[3], l[9], s[4], e[10], e[11]):
        step()
    for p in range(PARTS):
        own[p] = scatter.own(p)[...]
    for step in (l[10], l[11], e[12], l[12]):
        step()
    sends.finish()
    store.wait()


def last(gy, kept, ffn, resid, mids, small, w):
    ins = backward_ins(kept, w) + [(m, far()) for m in (gy, *ffn, resid)] + norm_params(w)
    ins += [(m, whole()) for m in (*mids, small)]
    outs = [(shape((LEN, D), F32), far()), (block_shape(16), far()), (shape((32, HALF), F32), whole()), (OWN, whole()), (GROUP, far()),
            (GROUP, far()), (SMALLS, whole()), (GROUP, far()), (GROUP, far()), (SMALLS, whole())]
    scratch = vmem(((LEN, D), F32), ((LEN, D), F32), ((SHARED_ROWS, HALF), BF), (MIDS.shape, BF), (MIDS.shape, BF))
    scratch += first_scratch(32) * 2 + second_scratch(32) * 4
    scratch += vmem((SMALLS.shape, BF)) + vmem((OWN.shape, BF), ((PARTS, 3, 4, 16, LANES), BF)) * 2 + scatter_scratch(16)
    return call(last_kernel, ins, outs, scratch + [dma(1), dma(336), dma(336)], "last", **remote(3))


def hand_out_kernel(early_0, late_0, early_1, late_1, small_0, small_1, ffn_0, ffn_1, *refs):
    (seg, w_query, b_query, w_key, w_value, b_value, w_depth, w_point, b_keyconv, w_kernel, b_kernel, w_conv, b_conv,
     w_out, b_out, first_gain, first_shift, w_up, b_up, w_down, b_down, second_gain, second_shift) = refs[:23]
    low, high, load_sems, store_sems = refs[23:]
    group = lax.axis_index("grp")
    place = my_row() - group * 64
    loads, stores = Moves(load_sems), Moves(store_sems)
    for layer in range(LAYERS):
        for n in range(8):
            rows = pl.ds(n * D, D)
            source = (early_0, late_0, early_1, late_1)[2 * layer + n // 4].at[pl.ds(n % 4 * D, D)]
            loads.start(source, low.at[layer, rows])
    for layer in range(LAYERS):
        for n in range(7):
            loads.all[layer * 8 + n].wait()

            @pl.loop(0, D // 256)
            def widen(c):
                high[layer * 7 + n, tile_rows(c, 256), :] = low[layer, tile_rows(c + 3 * n, 256), :].astype(F32)

            out = (w_out, w_out, w_key, w_value, w_query, w_conv, w_point)[n].at[layer]
            if n < 2:
                out = out.at[:, pl.ds(n * HALF, HALF)]
            stores.start(high.at[layer * 7 + n], out)
    smalls, taps, ups = [], [], []
    for layer, ffn in enumerate((ffn_0, ffn_1)):
        loads.all[layer * 8 + 7].wait()
        taps.append(low[layer, TAPS_AT : TAPS_AT + 64, :].astype(F32))
        smalls.append((small_0, small_1)[layer][...].astype(F32))
        rows = jnp.concatenate([ffn[p].astype(F32) for p in range(PARTS)], axis=0)
        w_up[layer, 0] = rows[:24]
        w_down[layer, 0] = rows[24:]
        mine = jnp.sum(jnp.where(rows_iota(8, HALF) == group * 4 + place // 16,
                                 smalls[layer][SMALL_FFN + 10 : SMALL_FFN + 18], 0.0), axis=0, keepdims=True)
        mine = jnp.broadcast_to(mine, (8, HALF))
        b_up[layer] = pltpu.roll(mine, (HALF - (place % 16) * 24) % HALF, 1)[:1, :24]

    def both(start, n=1):
        return jnp.concatenate(
            [jnp.concatenate([s[start + k : start + k + 1] for k in range(n)], axis=1) for s in smalls], axis=0)

    for j in range(KERNEL):
        w_depth[j] = jnp.concatenate([both(SMALL_DEPTH + j), both(SMALL_DEPTH + 9 + j)], axis=1)
    for j in range(HEADS * KERNEL):
        w_kernel[j] = jnp.concatenate([t[j : j + 1] for t in taps], axis=0)
    for n, out in enumerate((second_gain, second_shift, b_down, first_gain, first_shift)):
        out[...] = both(SMALL_FFN + 2 * n, 2)
    for n, out in enumerate((b_query, b_value, b_keyconv, b_conv)):
        out[...] = both(SMALL_BIAS + n)
    b_kernel[...] = both(SMALL_BIAS + 4)[:, : HEADS * KERNEL]
    b_out[...] = both(SMALL_BIAS + 5, 2)
    for n in range(2):
        s = smalls[0][SMALL_SEG + 2 * n : SMALL_SEG + 2 * n + 2]
        seg[n : n + 1, :] = jnp.concatenate([s[0:1], s[1:2]], axis=1)
    wait_all(stores.all)


def hand_out(shared, small, ffn):
    proj, half_row, full_row = (LAYERS, D, HALF), (LAYERS, HALF), (LAYERS, D)
    shapes = [(2, D), proj, half_row, proj, proj, half_row, (KERNEL, LAYERS, D), proj, half_row,
              (HEADS * KERNEL, LAYERS, HALF), (LAYERS, HEADS * KERNEL), proj, half_row, (LAYERS, D, D), full_row,
              full_row, full_row, (LAYERS, 1, 24, HALF), (LAYERS, 1, 24), (LAYERS, 1, 24, HALF), full_row, full_row,
              full_row]
    big = (proj, (LAYERS, D, D))
    outs = list(call(
        hand_out_kernel,
        [(m, far()) for m in shared] + [(m, whole()) for m in (*small, *ffn)],
        [(shape(s, F32), far() if s in big else whole()) for s in shapes],
        [pltpu.VMEM((LAYERS, SHARED_ROWS, HALF), BF), pltpu.VMEM((14, D, HALF), F32), dma(16), dma(14)],
        "hand_out",
    ))
    outs[6] = jnp.swapaxes(outs[6], 0, 1)
    outs[9] = jnp.transpose(outs[9], (1, 2, 0))
    outs[17] = jnp.swapaxes(outs[17], 2, 3)
    return tuple(outs)


def shards(*args):
    w = Params(*args)
    w = w._replace(w_depth=jnp.swapaxes(w.w_depth, 0, 1), w_kernel=jnp.transpose(w.w_kernel, (2, 0, 1)))
    pieces = jnp.concatenate([jnp.swapaxes(w.w_up[:, 0], 1, 2), w.down_weight[:, 0]], axis=1)
    bias = jnp.pad(w.b_up[:, 0], ((0, 16 - LAYERS), (0, LANES - w.b_up.shape[2])))
    pieces = jnp.concatenate([pieces.reshape(LAYERS * PARTS, 16, LANES), bias[None]])
    kept_0, kept_1, ffn, (output, d_resid, ffn_grads, small) = forward(pieces, w)
    grad, ffn_1, *mids, small = middle(d_resid, kept_1, small, ffn_grads, w)
    grad, _, _, ffn_0, early_1, late_1, small_1, early_0, late_0, small_0 = last(
        grad, kept_0, ffn, kept_0[9], mids, small, w)
    return (output, grad) + hand_out((early_0, late_0, early_1, late_1), (small_0, small_1), (ffn_0, ffn_1))


def solution(mesh):
    finer = Mesh(mesh.devices.reshape(mesh.shape["grp"], 4, 4, 2, 2), GRP_CH)
    rows, up = P(GRP_CH, None), P(None, "grp", None, CH)
    bias, down = P(None, "grp", CH), P(None, "grp", CH, None)
    placed = Params(*[P()] * len(Params._fields))._replace(
        hidden=rows, cotangent=rows, w_up=up, b_up=bias, down_weight=down)
    given = [P()] * 23
    given[17:20] = [up, bias, down]
    return jax.shard_map(
        shards,
        mesh=finer,
        in_specs=tuple(placed),
        out_specs=(rows, rows, *given),
        check_vma=False,
    )
```

```python
import functools
from typing import NamedTuple

import jax
import jax.numpy as jnp
import ml_dtypes
import numpy as np
from jax import lax
from jax.experimental import pallas as pl
from jax.experimental.pallas import tpu as pltpu
from jax.sharding import Mesh
from jax.sharding import PartitionSpec as P

HEADS = 6
HEAD = 64
KERNEL = 9
LAYERS = 2
LEN = 512
CH = ("ch_0", "ch_1", "ch_2", "ch_3")
GRP_CH = ("grp",) + CH
EPSILON = 1e-06
SCORE_SCALE = 0.125
MASK_VALUE = -1000000000.0
BF, F32 = jnp.bfloat16, jnp.float32
MESH = pl.DeviceIdType.MESH
LANES = 384
PARTS = 3
ORDERS = ("xyz", "yzx", "zxy")


def here():
    x, y = lax.axis_index("ch_1"), lax.axis_index("ch_0")
    z = lax.axis_index("grp") * 2 + lax.axis_index("ch_2")
    return {"x": x, "y": y, "z": z, "core": lax.axis_index("ch_3")}


def device_at(axis, place):
    if axis == "x":
        return {"ch_1": place}
    if axis == "y":
        return {"ch_0": place}
    if axis == "z":
        return {"grp": place // 2, "ch_2": place % 2}
    return {"ch_3": place}


def greet(at):
    peers = [("core", 1 - at["core"])]
    for axis in "xyz":
        peers += [(axis, (at[axis] + turn) % 4) for turn in (1, 2, 3)]
    for axis, place in peers:
        pl.semaphore_signal(
            pltpu.get_barrier_semaphore(), inc=1, device_id=device_at(axis, place), device_id_type=MESH)


def met():
    pl.semaphore_wait(pltpu.get_barrier_semaphore(), 10)


class Sends:
    def __init__(self, send_sems, recv_sems):
        self.send_sems, self.recv_sems, self.made = send_sems, recv_sems, {}

    def copy(self, key):
        number, make = self.made[key]
        src, dst, axis, place = make()
        return pltpu.make_async_remote_copy(
            src_ref=src, dst_ref=dst, send_sem=self.send_sems.at[number], recv_sem=self.recv_sems.at[number],
            device_id=device_at(axis, place), device_id_type=MESH)

    def start(self, key, make):
        if key not in self.made:
            self.made[key] = (len(self.made), make)
        self.copy(key).start()

    def arrived(self, *keys):
        for key in keys:
            self.copy(key).wait_recv()

    def finish(self):
        for key in self.made:
            self.copy(key).wait_send()


def all_in(lead, work):
    @pl.loop(0, int(np.prod(lead)))
    def one(i):
        at, rest = [], i
        for n in reversed(lead):
            at.append(rest % n)
            rest = rest // n
        work(tuple(reversed(at)))


class Scatter:
    def __init__(self, name, at, sends, x, scratch):
        self.name, self.at, self.sends, self.x = name, at, sends, x
        self.sums, self.core_in, self.bufs, self.load_sem = scratch[0], scratch[1], scratch[2:5], scratch[5]

    def load(self):
        return pltpu.make_async_copy(self.x.at[:, self.at["core"]], self.sums, self.load_sem.at[0])

    def place(self, p, s, turn):
        return (self.at[ORDERS[p][s]] + turn) % 4

    def block(self, p, s, turn):
        lead = [self.at[ORDERS[p][n]] for n in range(s)]
        return self.sums.at[(p, *lead, self.place(p, s, turn))]

    def begin(self):
        self.load().start()
        for turn in (2, 1, 3, 0):
            for p in range(PARTS):
                self.sends.start((self.name, 3, p, turn), lambda p=p, turn=turn: (
                    self.x.at[p, 1 - self.at["core"], self.place(p, 0, turn)],
                    self.core_in.at[p, self.place(p, 0, turn)], "core", 1 - self.at["core"]))

    def take(self, turn):
        for p in range(PARTS):
            self.sends.arrived((self.name, 3, p, turn))
            mine, other = self.block(p, 0, turn), self.core_in.at[p, self.place(p, 0, turn)]

            def add(at):
                mine[at] = mine[at] + other[at]

            all_in(mine.shape[:1], add)
            if turn:
                self.send(p, 0, turn)

    def send(self, p, s, turn):
        self.sends.start((self.name, s, p, turn), lambda: (
            self.block(p, s, turn), self.bufs[s].at[p, turn - 1], ORDERS[p][s], self.place(p, s, turn)))

    def onward(self, s):
        for p in range(PARTS):
            self.join(p, s - 1)
            for turn in (2, 1, 3):
                self.send(p, s, turn)

    def join(self, p, s):
        for turn in (1, 3, 2):
            self.sends.arrived((self.name, s, p, turn))
        mine, came = self.block(p, s, 0), self.bufs[s].at[p]

        def add(at):
            total = mine[at].astype(F32)
            for n in range(3):
                total += came[(n, *at)].astype(F32)
            mine[at] = total.astype(BF)

        if len(mine.shape) > 2:
            all_in(mine.shape[:1], add)
        else:
            add((Ellipsis,))

    def steps(self):
        def start():
            self.load().wait()
            self.take(2)

        return [self.begin, start, lambda: self.take(1), lambda: self.take(3), lambda: self.take(0),
                lambda: self.onward(1), lambda: self.onward(2), lambda: [self.join(p, 2) for p in range(PARTS)] and None]

    def own(self, p):
        return self.sums.at[(p, *[self.at[axis] for axis in ORDERS[p]])]


def scatter_scratch(rows):
    lead = (PARTS, 4, 4, 4)
    return [pltpu.VMEM(lead + (rows, LANES), BF), pltpu.VMEM(lead + (rows, LANES), BF),
            pltpu.VMEM((PARTS, 3, 4, 4, rows, LANES), BF), pltpu.VMEM((PARTS, 3, 4, rows, LANES), BF),
            pltpu.VMEM((PARTS, 3, rows, LANES), BF), dma(1)]


def chunk(start, size):
    return pl.ds(pl.multiple_of(start, 16), size)


class FirstSum:
    def __init__(self, name, at, sends, x, mid, scratch):
        self.name, self.at, self.sends, self.x, self.mid = name, at, sends, x, mid
        self.sums, self.core_in, self.came, self.load_sem = scratch
        self.c = x.shape[0] // (PARTS * 32)

    def place(self, p, turn):
        return (self.at[ORDERS[p][0]] + turn) % 4

    def loads(self):
        c = self.c
        return [pltpu.make_async_copy(self.x.at[chunk((p * 2 + self.at["core"]) * 16 * c, 16 * c)], self.sums.at[p],
                                      self.load_sem.at[p]) for p in range(PARTS)]

    def begin(self):
        c = self.c
        for load in self.loads():
            load.start()
        for turn in (2, 1, 3, 0):
            for p in range(PARTS):
                def make(p=p, turn=turn):
                    start = self.place(p, turn) * 4 * c
                    other = 1 - self.at["core"]
                    return (self.x.at[chunk((p * 2 + other) * 16 * c + start, 4 * c)],
                            self.core_in.at[p, chunk(start, 4 * c)], "core", other)

                self.sends.start((self.name, 3, p, turn), make)

    def take(self, turn):
        size = 4 * self.c
        for p in range(PARTS):
            self.sends.arrived((self.name, 3, p, turn))
            start = self.place(p, turn) * size

            @pl.loop(0, size // 64)
            def add(i):
                rows = chunk(start + i * 64, 64)
                self.sums[p, rows] = self.sums[p, rows] + self.core_in[p, rows]

            if turn:
                self.sends.start((self.name, 0, p, turn), lambda p=p: (
                    self.sums.at[p, chunk(self.place(p, turn) * size, size)], self.came.at[p, turn - 1], ORDERS[p][0],
                    self.place(p, turn)))

    def join(self):
        size = 4 * self.c
        for p in range(PARTS):
            for turn in (1, 3, 2):
                self.sends.arrived((self.name, 0, p, turn))
            start = self.place(p, 0) * size

            @pl.loop(0, size // 64)
            def add(i):
                rows = chunk(i * 64, 64)
                total = self.sums[p, chunk(start + i * 64, 64)].astype(F32)
                for n in range(3):
                    total += self.came[p, n, rows].astype(F32)
                self.mid[p, rows] = total.astype(BF)

    def steps(self):
        def start():
            for load in self.loads():
                load.wait()
            self.take(2)

        return [self.begin, start, lambda: self.take(1), lambda: self.take(3), lambda: self.take(0), self.join]


def first_scratch(c):
    return [pltpu.VMEM((PARTS, 16 * c, LANES), BF), pltpu.VMEM((PARTS, 16 * c, LANES), BF),
            pltpu.VMEM((PARTS, 3, 4 * c, LANES), BF), dma(PARTS)]


class SecondSum:
    def __init__(self, name, at, sends, mid, gathered, scratch):
        self.name, self.at, self.sends, self.mid, self.gathered = name, at, sends, mid, gathered
        self.came, self.slots, self.final, self.sems = scratch
        self.c = mid.shape[1] // 4

    def place(self, p, s, turn):
        return (self.at[ORDERS[p][s]] + turn) % 4

    def rows(self, p, first, second=None):
        c = self.c
        start = (p * 2 + self.at["core"]) * 16 * c + self.place(p, 0, first) * 4 * c
        if second is None:
            return self.gathered.at[chunk(start, 4 * c)]
        return self.gathered.at[chunk(start + self.place(p, 1, second) * c, c)]

    def scatter(self):
        c = self.c
        for p in range(PARTS):
            for turn in (2, 1, 3):
                self.sends.start((self.name, 1, p, turn), lambda p=p, turn=turn: (
                    self.mid.at[p, chunk(self.place(p, 1, turn) * c, c)], self.came.at[p, turn - 1], ORDERS[p][1],
                    self.place(p, 1, turn)))

    def share(self):
        for p in range(PARTS):
            for turn in (1, 3, 2):
                self.sends.arrived((self.name, 1, p, turn))
            total = self.mid[p, chunk(self.place(p, 1, 0) * self.c, self.c)].astype(F32)
            for n in range(3):
                total += self.came[p, n].astype(F32)
            self.slots[p, self.at[ORDERS[p][2]]] = total.astype(BF)
            for turn in (2, 1, 3):
                def make(p=p, turn=turn):
                    slot = self.slots.at[p, self.at[ORDERS[p][2]]]
                    return slot, slot, ORDERS[p][2], self.place(p, 2, turn)

                self.sends.start((self.name, 2, p, turn), make)

    def puts(self):
        return [pltpu.make_async_copy(self.final.at[p], self.rows(p, 0, 0), self.sems.at[p]) for p in range(PARTS)]

    def settle(self):
        for p in range(PARTS):
            for turn in (1, 3, 2):
                self.sends.arrived((self.name, 2, p, turn))
            total = self.slots[p, 0].astype(F32) + self.slots[p, 1].astype(F32)
            self.final[p] = (total + self.slots[p, 2].astype(F32) + self.slots[p, 3].astype(F32)).astype(BF)
            for turn in (2, 1, 3):
                self.sends.start((self.name, 4, p, turn), lambda p=p, turn=turn: (
                    self.final.at[p], self.rows(p, 0, 0), ORDERS[p][1], self.place(p, 1, turn)))
        for put in self.puts():
            put.start()

    def across(self, p, turn):
        def make():
            ref = self.rows(p, turn)
            return ref, ref, "core", 1 - self.at["core"]

        self.sends.start((self.name, 6, p, turn), make)

    def near(self):
        for put in self.puts():
            put.wait()
        for p in range(PARTS):
            for turn in (1, 3, 2):
                self.sends.arrived((self.name, 4, p, turn))
            for turn in (2, 1, 3):
                def make(p=p, turn=turn):
                    ref = self.rows(p, 0)
                    return ref, ref, ORDERS[p][0], self.place(p, 0, turn)

                self.sends.start((self.name, 5, p, turn), make)
            self.across(p, 0)

    def over(self, *turns):
        for turn in turns:
            for p in range(PARTS):
                self.sends.arrived((self.name, 5, p, turn))
                self.across(p, 4 - turn)

    def end(self):
        for turn in (0, 3, 1, 2):
            for p in range(PARTS):
                self.sends.arrived((self.name, 6, p, turn))

    def steps(self):
        return [self.scatter, self.share, self.settle, self.near, lambda: self.over(1, 3), lambda: self.over(2), self.end]


def second_scratch(c):
    return [pltpu.VMEM((PARTS, 3, c, LANES), BF), pltpu.VMEM((PARTS, 4, c, LANES), BF),
            pltpu.VMEM((PARTS, c, LANES), BF), dma(PARTS)]


class Gather:
    def __init__(self, name, at, sends, parts, sems):
        self.name, self.at, self.sends, self.parts, self.sems = name, at, sends, parts, sems

    def place(self, p, s, turn):
        return (self.at[self.parts[p][3][s]] + turn) % 4

    def in_plane(self, p):
        _, plane, _, order = self.parts[p]
        return plane.at[self.at[order[1]], self.at[order[2]]]

    def block(self, p, turn):
        return self.parts[p][2].at[self.at["core"], self.place(p, 0, turn)]

    def puts(self):
        return [pltpu.make_async_copy(part[0], self.in_plane(p), self.sems.at[p]) for p, part in enumerate(self.parts)]

    def last_puts(self):
        return [pltpu.make_async_copy(part[1], self.block(p, 0), self.sems.at[p]) for p, part in enumerate(self.parts)]

    def send(self, s, pick):
        for turn in (2, 1, 3):
            for p in range(len(self.parts)):
                self.sends.start((self.name, s, p, turn), lambda p=p, turn=turn: (
                    *pick(p), self.parts[p][3][s], self.place(p, s, turn)))

    def arrived(self, s, *turns):
        for turn in turns:
            for p in range(len(self.parts)):
                self.sends.arrived((self.name, s, p, turn))

    def across(self, turn):
        for p in range(len(self.parts)):
            def make(p=p):
                ref = self.block(p, turn)
                return self.parts[p][1] if turn == 0 else ref, ref, "core", 1 - self.at["core"]

            self.sends.start((self.name, 3, p, turn), make)

    def plane_steps(self):
        def first():
            for put in self.puts():
                put.start()
            self.send(2, lambda p: (self.parts[p][0], self.in_plane(p)))

        def second():
            for put in self.puts():
                put.wait()
            self.arrived(2, 1, 3, 2)

            def row(p):
                ref = self.parts[p][1].at[self.at[self.parts[p][3][1]]]
                return ref, ref

            self.send(1, row)

        return [first, second, lambda: self.arrived(1, 1, 3, 2)]

    def whole_steps(self):
        def first():
            for put in self.last_puts():
                put.start()
            self.send(0, lambda p: (self.parts[p][1], self.block(p, 0)))
            self.across(0)

        def more():
            self.arrived(0, 1)
            self.across(3)
            self.arrived(0, 3)
            self.across(1)

        def rest():
            self.arrived(0, 2)
            self.across(2)

        def end():
            self.arrived(3, 0, 3, 1, 2)
            for put in self.last_puts():
                put.wait()

        return [first, more, rest, end]


class SmallSum:
    def __init__(self, name, at, sends, x, core_in, slots):
        self.name, self.at, self.sends, self.x, self.core_in, self.slots = name, at, sends, x, core_in, slots

    def begin(self):
        for p in range(PARTS):
            self.sends.start((self.name, 3, p, 0), lambda p=p: (
                self.x.at[pl.ds(16 * p, 16)], self.core_in.at[p], "core", 1 - self.at["core"]))

    def total(self, p, s):
        if s == 0:
            self.sends.arrived((self.name, 3, p, 0))
            return self.x[16 * p : 16 * p + 16].astype(F32) + self.core_in[p].astype(F32)
        for turn in (1, 3, 2):
            self.sends.arrived((self.name, s - 1, p, turn))
        slots = self.slots.at[p, s - 1]
        return slots[0].astype(F32) + slots[1].astype(F32) + slots[2].astype(F32) + slots[3].astype(F32)

    def stage(self, s):
        for p in range(PARTS):
            self.slots[p, s, self.at[ORDERS[p][s]]] = self.total(p, s).astype(BF)
            for turn in (2, 1, 3):
                def make(p=p, turn=turn):
                    slot = self.slots.at[p, s, self.at[ORDERS[p][s]]]
                    return slot, slot, ORDERS[p][s], (self.at[ORDERS[p][s]] + turn) % 4

                self.sends.start((self.name, s, p, turn), make)

    def steps(self, out):
        def end():
            for p in range(PARTS):
                out[16 * p : 16 * p + 16] = self.total(p, 3).astype(BF)

        return [self.begin, lambda: self.stage(0), lambda: self.stage(1), lambda: self.stage(2), end]


def steps_in(i, *table):
    for turn, *steps in table:
        @pl.when(i == turn)
        def run():
            for step in steps:
                step()


D = 768
HALF = 384
HIDDEN = 1536
TILE = 128
TAPW = 128
PADDED = LEN + 16
SHARED_ROWS = 6144
VMEM_BYTES = 60 << 20
EARLY = 3072
POINT_AT, TAPS_AT, SMALL_AT = EARLY + 1536, EARLY + 2304, EARLY + 2368
SMALL_DEPTH, SMALL_FFN, SMALL_BIAS, SMALL_SEG, SMALL = 0, 18, 36, 43, 48


class Params(NamedTuple):
    hidden: jax.Array
    cotangent: jax.Array
    lengths: jax.Array
    split_at: jax.Array
    seg_table: jax.Array
    w_query: jax.Array
    b_query: jax.Array
    w_key: jax.Array
    w_value: jax.Array
    b_value: jax.Array
    w_depth: jax.Array
    w_point: jax.Array
    b_keyconv: jax.Array
    w_kernel: jax.Array
    b_kernel: jax.Array
    w_conv: jax.Array
    b_conv: jax.Array
    w_out: jax.Array
    b_out: jax.Array
    first_gain: jax.Array
    first_shift: jax.Array
    w_up: jax.Array
    b_up: jax.Array
    down_weight: jax.Array
    b_down: jax.Array
    second_gain: jax.Array
    second_shift: jax.Array


KEPT_SHAPES = (((LEN, D), BF), ((LEN, HALF), F32), ((LEN, HALF), BF), ((LEN, HALF), BF), ((LEN, D), BF),
               ((LEN, HALF), F32), ((PADDED, KERNEL * TAPW), F32), ((PADDED, HALF), F32), ((LEN, D), BF),
               ((LEN, D), F32))


def dims(lhs, rhs):
    return (((lhs,), (rhs,)), ((), ()))


def dot(a, b):
    return lax.dot_general(a, b, dims(1, 0), preferred_element_type=F32)


def dot_nt(a, b):
    return lax.dot_general(a, b, dims(1, 1), preferred_element_type=F32)


def dot_tn(a, b):
    return lax.dot_general(a, b, dims(0, 0), preferred_element_type=F32)


def tile_rows(i, n=TILE, start=0):
    return pl.ds(pl.multiple_of(i * n + start, 8 if start % 16 else 16), n)


def lanes_at(start, n=128):
    return pl.ds(pl.multiple_of(start, 128), n)


def rows_iota(n, width=1):
    return lax.broadcasted_iota(jnp.int32, (n, width), 0)


class Moves:
    def __init__(self, sems):
        self.sems, self.all = sems, []

    def start(self, src, dst):
        copy = pltpu.make_async_copy(src, dst, self.sems.at[len(self.all)])
        copy.start()
        self.all.append(copy)
        return copy

    def start_cat(self, layer, matrices, w_cat):
        return [self.start(ref.at[layer], w_cat.at[:, pl.ds(n * HALF, HALF)]) for n, ref in enumerate(matrices)]


def wait_all(copies):
    for copy in copies:
        copy.wait()


def my_row():
    row = lax.axis_index("grp")
    for name, size in zip(CH, (4, 4, 2, 2)):
        row = row * size + lax.axis_index(name)
    return row


def widen_matrix():
    lane = np.arange(HALF)[None, :] // HEAD
    return (np.arange(TAPW)[:, None] == lane).astype(ml_dtypes.bfloat16)


def tap_matrix():
    out = np.zeros((TAPW, KERNEL * TAPW), np.float32)
    for h in range(HEADS):
        for j in range(KERNEL):
            out[h * KERNEL + j, j * TAPW + h] = 1.0
    return out.astype(ml_dtypes.bfloat16)


def norm_stats(residual):
    mean = jnp.mean(residual, axis=-1, keepdims=True)
    center = residual - mean
    scale = lax.rsqrt(jnp.mean(center * center, axis=-1, keepdims=True) + EPSILON)
    return center * scale, scale


def norm_grad(gy, hat, scale, gain):
    d_hat = gy * gain
    mean_one = jnp.mean(d_hat, axis=-1, keepdims=True)
    mean_two = jnp.mean(d_hat * hat, axis=-1, keepdims=True)
    return scale * (d_hat - mean_one - hat * mean_two)


def gelu_both(pre):
    base = 1.0 + (0.3275911 * 0.7071067811865476) * jnp.abs(pre)
    t = pl.reciprocal(base, approx=True)
    t = t * (2.0 - base * t)
    poly = t * (0.127414796 + t * (-0.142248368 + t * (0.7107068705 + t * (-0.7265760135 + t * 0.5307027145))))
    bell = jnp.exp2((-0.5 * 1.4426950408889634) * (pre * pre))
    tail = poly * bell
    cdf = jnp.where(pre >= 0, 1.0 - tail, tail)
    return pre * cdf, cdf + pre * (bell * 0.3989422804014327)


def moved(window, start, n):
    size = window.shape[0]
    return pltpu.roll(window, (size - start) % size, 0)[:n]


def masked(scores, start, length):
    if start + scores.shape[0] <= 259:
        return scores
    return jnp.where(rows_iota(*scores.shape) + start < length, scores, MASK_VALUE)


def far():
    return pl.BlockSpec(memory_space=pl.ANY)


def whole():
    return pl.BlockSpec(memory_space=pltpu.VMEM)


def scalars():
    return pl.BlockSpec(memory_space=pltpu.SMEM)


def dma(n):
    return pltpu.SemaphoreType.DMA((n,))


def shape(dims, dtype):
    return jax.ShapeDtypeStruct(dims, dtype)


def block_shape(rows, lanes=LANES):
    return shape((PARTS, 2, 4, 4, 4, rows, lanes), BF)


def call(kernel, ins, outs, scratch, name, **comm):
    return pl.pallas_call(
        kernel,
        out_shape=[out for out, _ in outs],
        in_specs=[place for _, place in ins],
        out_specs=[place for _, place in outs],
        scratch_shapes=scratch,
        compiler_params=pltpu.CompilerParams(vmem_limit_bytes=VMEM_BYTES, **comm),
        name=name,
    )(*[array for array, _ in ins])


def vmem(*shapes):
    return [pltpu.VMEM(*s) for s in shapes]


class Points(dict):
    def at(self, point):
        for step in self.get(point, ()):
            step()

    def turn(self, point, i):
        for (name, turn), steps in [(key, s) for key, s in self.items() if isinstance(key, tuple)]:
            if name == point:
                steps_in(i, (turn, *steps))


def remote(number):
    return {"collective_id": number, "has_side_effects": True}


def tap_weights(layer, w_kernel, rows):
    rows[...] = jnp.zeros_like(rows)
    for n in range(HEADS * KERNEL):
        rows[n : n + 1, :] = w_kernel[n].astype(F32)[layer : layer + 1, :]


def clear_edges(*refs):
    for ref in refs:
        ref[pl.ds(0, 8), :] = jnp.zeros((8, ref.shape[1]), F32)
        ref[pl.ds(LEN + 8, 8), :] = jnp.zeros((8, ref.shape[1]), F32)


ENTER, DEPTH, ATTEND, END, UNPACK, FEED, BACK, GRAD, OUT, KEY, TAPS, CAT, LEAVE = range(13)

FORWARD_WEIGHTS = 14
FA_SCRATCH = [((LEN, D), BF), ((D, 4 * HALF), BF), ((D, HALF), BF), ((D, D), BF), ((PADDED, D), F32),
              ((LEN, HALF), BF), ((LEN, HALF), BF), ((TAPW, HALF), F32), ((HALF, KERNEL * TAPW), BF),
              ((8, KERNEL * TAPW), F32)]


def attention_forward_body(layer, length, split, x_in, seg, weights, x_all, resid, kept_out, log_total, points, *refs):
    first = layer == 0
    (w_query, w_key, w_value, w_conv, w_point, w_out, w_depth, w_kernel, b_query, b_value, b_conv, b_keyconv, b_kernel,
     b_out, widen, spread) = weights
    kept, refs = refs[:9], refs[9:]
    x_low, query, key_low, value_low, depth_low, key_conv, kernels, conv_pad, joined = kept
    hidden, w_cat, point, out_w, x_pad, query_low, mixed_low, tap_rows, taps_w, tap_bias, sems = refs
    one = slice(layer, layer + 1)
    moves = Moves(sems)
    load_x = [moves.start(x_in, hidden)] if first else []
    load_cat = moves.start_cat(layer, (w_query, w_key, w_value, w_conv), w_cat)
    load_rest = [moves.start(w_point.at[layer], point), moves.start(w_out.at[layer], out_w)]
    clear_edges(x_pad, conv_pad, kernels)
    tap_weights(layer, w_kernel, tap_rows)
    for c in range(0, KERNEL * TAPW, 384):
        taps_w[:, c : c + 384] = dot_tn(tap_rows[...].astype(BF), spread[:, c : c + 384]).astype(BF)
    tap_bias[...] = jnp.zeros_like(tap_bias)
    tap_bias[0:1, 0 : HEADS * KERNEL] = b_kernel[one, :]
    left, bias = tap_bias[:, :TAPW], jnp.zeros((8, KERNEL * TAPW), F32)
    for _ in range(3):
        bias += dot(left.astype(BF), spread[...])
        left = left - left.astype(BF).astype(F32)
    tap_bias[...] = bias

    wait_all(load_x)
    points.at(ENTER)

    @pl.loop(0, LEN // TILE)
    def enter(i):
        rows = tile_rows(i)
        if first:
            place = rows_iota(TILE) + i * TILE
            x = hidden[rows, :].astype(F32) + jnp.where(place > split, seg[1:2, :], seg[0:1, :])
            x = x * (place < length).astype(F32)
            x_all[rows, :] = x
        else:
            x = x_all[rows, :]
        low = x.astype(BF)
        x_low[rows, :] = low
        x_pad[tile_rows(i, TILE, 8), :] = low.astype(F32)

    wait_all(load_cat)
    for n in range(6):
        proj = dot(x_low[...], w_cat[:, n * 256 : n * 256 + 256])
        for h in range(2):
            which, c = (2 * n + h) // 3, (2 * n + h) % 3 * 128
            cols = slice(c, c + 128)
            part = proj[:, h * 128 : h * 128 + 128]
            if which == 0:
                part += b_query[one, cols]
                query[:, cols] = part
                query_low[:, cols] = part.astype(BF)
            elif which == 1:
                key_low[:, cols] = part.astype(BF)
            elif which == 2:
                value_low[:, cols] = (part + b_value[one, cols]).astype(BF)
            else:
                conv_pad[pl.ds(8, LEN), cols] = part + b_conv[one, cols]
    stores = [moves.start(kept[n], kept_out[n]) for n in (0, 1, 2, 3, 7)]
    points.at(OUT)

    @pl.loop(0, LEN // TILE)
    def depth(i):
        rows = tile_rows(i)
        around = pl.ds(pl.multiple_of(i * TILE, TILE), TILE + 16)
        for c in range(0, D, 128):
            cols = slice(c, c + 128)
            window = x_pad[around, cols]
            total = jnp.zeros((TILE, 128), F32)
            for j in range(KERNEL):
                total += w_depth[j, one, cols].astype(F32) * moved(window, 4 + j, TILE)
            depth_low[rows, cols] = total.astype(BF)

    points.at(DEPTH)
    wait_all(load_rest)
    for c, n in ((0, 256), (256, 128)):
        cols = slice(c, c + n)
        key = dot(depth_low[...], point[:, cols]) + b_keyconv[one, cols]
        key_conv[:, cols] = key
        mixed_low[:, cols] = (key * query[:, cols]).astype(BF)
    for c in range(0, KERNEL * TAPW, 384):
        cols = slice(c, c + 384)
        kernels[pl.ds(8, LEN), cols] = dot(mixed_low[...], taps_w[:, cols]) + tap_bias[0:1, cols]
    stores += [moves.start(kept[n], kept_out[n]) for n in (4, 5)]

    @pl.loop(0, LEN // 256)
    def convolve(i):
        rows = tile_rows(i, 256)
        around = pl.ds(pl.multiple_of(i * 256, 256), 256 + 16)
        padded = tile_rows(i, 256, 8)
        taps = [kernels[padded, j * TAPW : (j + 1) * TAPW] for j in range(KERNEL)]
        peak = functools.reduce(jnp.maximum, taps)
        taps = [jnp.exp(t - peak) for t in taps]
        share = 1.0 / sum(taps)
        window = conv_pad[around, :]
        mix = jnp.zeros((256, HALF), F32)
        for j in range(KERNEL):
            tap = taps[j] * share
            kernels[padded, j * TAPW : (j + 1) * TAPW] = tap
            mix += dot(tap.astype(BF), widen[...]) * moved(window, 4 + j, 256)
        joined[rows, HALF:] = mix.astype(BF)

    stores += [moves.start(kept[6], kept_out[6])]

    @pl.loop(0, HEADS // 2)
    def attend(pair):
        points.turn(ATTEND, pair)
        lanes = lanes_at(pair * 128)
        keys = key_low[:, lanes] * jnp.asarray(SCORE_SCALE, BF)
        side = lax.broadcasted_iota(jnp.int32, (LEN, 128), 1) // HEAD
        values = jnp.transpose(value_low[:, lanes].astype(F32)).astype(BF)
        queries = query_low[:, lanes]
        context = []
        for head in range(2):
            mine = jnp.where(side == head, keys, jnp.zeros_like(keys))
            scores = [masked(dot_nt(mine[c : c + 128], queries), c, length) for c in range(0, LEN, 128)]
            peak = functools.reduce(jnp.maximum, [jnp.max(s, axis=0, keepdims=True) for s in scores])
            probs = [jnp.exp(s - peak) for s in scores]
            total = sum(jnp.sum(p, axis=0, keepdims=True) for p in probs)
            log_total[pair * 2 + head] = peak + jnp.log(total)
            share = 1.0 / total
            probs = jnp.concatenate([(p * share).astype(BF) for p in probs], axis=0)
            context.append(dot(values[head * HEAD : (head + 1) * HEAD, :], probs))
        joined[:, lanes] = jnp.transpose(jnp.concatenate(context, axis=0)).astype(BF)

    stores += [moves.start(kept[8], kept_out[8])]
    points.at(ATTEND)
    for c in range(0, D, 256):
        cols = slice(c, c + 256)
        resid[:, cols] = x_all[:, cols] + dot(joined[...], out_w[:, cols]) + b_out[one, cols]
    points.at(END)
    wait_all(stores)


PLANES = (PARTS, 4, 4, 16, LANES)


def part_block(ref, p, core, x, y, z):
    if p == 0:
        return ref.at[0, core, x, y, z]
    if p == 1:
        return ref.at[1, core, y, z, x]
    return ref.at[2, core, z, x, y]


FFN_SHAPES = [((2 * HIDDEN, HALF), BF)] * 2 + [((LEN, 2 * HIDDEN), BF)] * 2 + [((LEN, D), F32)]
FF_SCRATCH = [((LEN, D), F32), ((LEN, D), BF), ((LEN, 512), F32), ((2, 64, TAPW), F32), ((1, 2 * HIDDEN), F32)]


def ffn_forward_body(layer, length, gathered, bias_all, norms, resid, x_next, outs, ffn, points, *refs):
    first_gain, first_shift, b_down, second_gain, second_shift = norms
    up, down, acted, slope, resid_two = ffn
    normed_rows, low, pre, bias_rows, bias, sems, block_sems = refs
    one = slice(layer, layer + 1)
    moves = Moves(sems)

    @pl.loop(0, LEN // TILE)
    def enter(i):
        rows = tile_rows(i)
        hat, _ = norm_stats(resid[rows, :])
        normed = hat * first_gain[one, :] + first_shift[one, :]
        normed_rows[rows, :] = normed
        low[rows, :] = normed.astype(BF)

    points.at(ENTER)

    @pl.loop(0, 64)
    def unpack(chip):
        z, y, x = (chip // 32) * 2 + chip % 2, (chip // 8) % 4, (chip // 2) % 4
        ups, downs = [], []
        for core in range(2):
            piece = jnp.concatenate(
                [part_block(gathered, p, core, x, y, z)[...].astype(F32) for p in range(PARTS)], axis=0)
            ups.append(piece[:24])
            downs.append(piece[24:])
            bias_rows[core, pl.ds(chip, 1), :] = bias_all[core, x, y, z].astype(F32)[one, :]
        rows = tile_rows(chip, 48)
        up[rows, :] = jnp.concatenate(ups, axis=0).astype(BF)
        down[rows, :] = jnp.concatenate(downs, axis=0).astype(BF)

    stores = [moves.start(up, outs[0]), moves.start(down, outs[1])] if outs else []
    points.at(UNPACK)
    for c in range(0, 2 * HIDDEN, 512):
        spot = lax.broadcasted_iota(jnp.int32, (64, 512), 1) + c
        slot = (lax.broadcasted_iota(jnp.int32, (TAPW, 512), 1) + c) % 24
        repeat = (slot == rows_iota(TAPW, 512)).astype(F32).astype(BF)
        total = jnp.zeros((1, 512), F32)
        for core in range(2):
            spread = dot(bias_rows[core].astype(BF), repeat)
            mine = spot // 24 == 2 * rows_iota(64, 512) + core
            total += jnp.sum(jnp.where(mine, spread, 0.0), axis=0, keepdims=True)
        bias[:, c : c + 512] = total

    def block_stores(n):
        cols = lanes_at(n * 512, 512)
        return [pltpu.make_async_copy(src.at[:, cols], out.at[:, cols], block_sems.at[2 * n + m])
                for m, (src, out) in enumerate(((acted, outs[2]), (slope, outs[3])))]

    for g in range(2):
        @pl.loop(0, HIDDEN // 512)
        def feed(k):
            at = g * HIDDEN + k * 512
            hidden = pl.ds(pl.multiple_of(at, 512), 512)
            pre[...] = dot_nt(low[:, g * HALF : (g + 1) * HALF], up[hidden, :]) + bias[:, hidden]

            @pl.loop(0, LEN // TILE)
            def act(i):
                few = tile_rows(i)
                for c in range(0, 512, 128):
                    value, grad = gelu_both(pre[few, c : c + 128])
                    cols = lanes_at(at + c)
                    acted[few, cols] = value.astype(BF)
                    slope[few, cols] = grad.astype(BF)

            if outs:
                for store in block_stores(g * (HIDDEN // 512) + k):
                    store.start()

        points.at(FEED + 100 * g)

    @pl.loop(0, LEN // 256)
    def leave(i):
        rows = tile_rows(i, 256)
        out = []
        for g in range(2):
            hidden = slice(g * HIDDEN, (g + 1) * HIDDEN)
            out.append(dot(acted[rows, hidden], down[hidden, :]).astype(BF).astype(F32))
        two = normed_rows[rows, :] + jnp.concatenate(out, axis=1) + b_down[one, :]
        resid_two[rows, :] = two
        hat, _ = norm_stats(two)
        valid = (rows_iota(256) + i * 256 < length).astype(F32)
        x_next[rows, :] = (hat * second_gain[one, :] + second_shift[one, :]) * valid

    points.at(END)
    if outs:
        stores.append(moves.start(resid_two, outs[4]))
        for n in range(2 * HIDDEN // 512):
            wait_all(block_stores(n))
    wait_all(stores)


BF_SCRATCH = [(block_shape(16).shape, BF), ((LEN, D), F32), ((LEN, 2 * HIDDEN), BF), ((LEN, D), BF),
              ((LEN, D), BF)]


def ffn_backward_body(layer, length, norms, gy, ffn, resid, d_resid, outs, waits, points, *refs):
    first_gain, first_shift, _, second_gain, _ = norms
    up, down, acted, slope, resid_two = ffn
    d_resid_out, grads_out, small = outs
    grads, d_two, d_pre, d_group, normed_low, sems = refs
    one = slice(layer, layer + 1)
    moves = Moves(sems)
    small[...] = jnp.zeros_like(small)

    def note(slot, value):
        total = jnp.sum(value, axis=0, keepdims=True)
        small[slot : slot + 1, :] += total[:, :HALF]
        small[slot + 1 : slot + 2, :] += total[:, HALF:]

    wait_all(waits[0])

    @pl.loop(0, LEN // TILE)
    def enter(i):
        rows = tile_rows(i)
        valid = (rows_iota(TILE) + i * TILE < length).astype(F32)
        grad = gy[rows, :].astype(F32) * valid
        hat, scale = norm_stats(resid_two[rows, :])
        note(0, grad * hat)
        note(2, grad)
        two = norm_grad(grad, hat, scale, second_gain[one, :])
        note(4, two)
        d_two[rows, :] = two
        d_group[rows, :] = two.astype(BF)
        hat, _ = norm_stats(resid[rows, :])
        normed_low[rows, :] = (hat * first_gain[one, :] + first_shift[one, :]).astype(BF)

    points.at(ENTER)
    wait_all(waits[1])
    for g in range(2):
        @pl.loop(0, HIDDEN // 256)
        def feed(k):
            hidden = pl.ds(pl.multiple_of(g * HIDDEN + k * 256, 256), 256)
            d_act = dot_nt(d_group[:, g * HALF : (g + 1) * HALF], down[hidden, :])
            d_pre[:, hidden] = (d_act * slope[:, hidden].astype(F32)).astype(BF)

        points.at(FEED + 100 * g)

    wait_all(waits[2])

    @pl.loop(0, LEN // 256)
    def back(i):
        rows = tile_rows(i, 256)
        got = []
        for g in range(2):
            hidden = slice(g * HIDDEN, (g + 1) * HIDDEN)
            got.append(dot(d_pre[rows, hidden], up[hidden, :]).astype(BF).astype(F32))
        d_normed = d_two[rows, :] + jnp.concatenate(got, axis=1)
        hat, scale = norm_stats(resid[rows, :])
        note(6, d_normed * hat)
        note(8, d_normed)
        d_resid[rows, :] = norm_grad(d_normed, hat, scale, first_gain[one, :])

    stores = [moves.start(d_resid, d_resid_out)] if d_resid_out is not None else []
    points.at(BACK)
    ones = jnp.ones((8, LEN), BF)
    for k in range(8):
        small[10 + k : 11 + k, :] = dot(ones, d_pre[:, k * HALF : (k + 1) * HALF])[0:1, :]

    for g in range(2):
        @pl.loop(0, 4)
        def grad(y):
            points.turn(GRAD + 100 * g, y)
            hidden = lanes_at(g * HIDDEN + y * HALF, HALF)
            cols = slice(g * HALF, (g + 1) * HALF)
            d_up = dot_tn(d_pre[:, hidden], normed_low[:, cols])
            d_down = dot_tn(acted[:, hidden], d_group[:, cols])
            for d in range(16):
                x, z, core = d // 4, g * 2 + (d // 2) % 2, d % 2
                piece = jnp.concatenate([d_up[24 * d : 24 * d + 24], d_down[24 * d : 24 * d + 24]], axis=0).astype(BF)
                for p in range(PARTS):
                    part_block(grads, p, core, x, y, z)[...] = piece[16 * p : 16 * p + 16]

        zs = pl.ds(2 * g, 2)
        for index in ((0, slice(None), slice(None), slice(None), zs), (1, slice(None), slice(None), zs),
                      (2, slice(None), zs)):
            stores.append(moves.start(grads.at[index], grads_out.at[index]))

    points.at(END)
    wait_all(stores)


BA_SCRATCH = [((D, 4 * HALF), BF), ((D, HALF), BF), ((D, D), BF), ((LEN, D), BF), ((LEN, 4 * HALF), BF), ((LEN, D), BF),
              ((LEN, HALF), BF), ((LEN, HALF), F32), ((PADDED, HALF), F32), ((PADDED, D), F32), ((SMALL, HALF), F32),
              ((LEN, TAPW), BF), ((TAPW, HALF), F32)]


def attention_backward_body(layer, length, split, d_resid, waits, kept_in, log_total, ffn_small, weights, shared, d_input,
                            small_out, points, *refs):
    first = layer == 0
    w_query, w_key, w_value, w_conv, w_point, w_out, w_depth, w_kernel, widen, spread = weights
    kept, refs = refs[:9], refs[9:]
    x_low, query, key_low, value_low, depth_low, key_conv, kernels, conv_pad, joined = kept
    (w_cat, point, out_w, d_proj, d_cat, d_join, query_low, d_att, mix_pad, depth_pad, small, d_tap, tap_rows,
     sems) = refs
    moves = Moves(sems)
    load_first = [*waits, moves.start(w_out.at[layer], out_w)]
    load = [moves.start(kept_in[n], kept[n]) for n in (8, 1, 2, 3, 6, 7, 5, 4, 0)]
    load_cat = moves.start_cat(layer, (w_query, w_key, w_value, w_conv), w_cat)
    load_point = moves.start(w_point.at[layer], point)
    clear_edges(mix_pad, depth_pad)
    small[...] = jnp.zeros_like(small)
    small[SMALL_FFN : SMALL_FFN + 18, :] = ffn_small[0:18, :]
    shared[SMALL_AT:, :] = jnp.zeros((SHARED_ROWS - SMALL_AT, HALF), BF)
    tap_weights(layer, w_kernel, tap_rows)

    def note(slot, value):
        total = jnp.sum(value, axis=0, keepdims=True)
        for n in range(total.shape[1] // HALF):
            small[slot + n : slot + n + 1, :] += total[:, n * HALF : (n + 1) * HALF]

    points.at(ENTER)
    wait_all(load_first)

    @pl.loop(0, LEN // TILE)
    def enter(i):
        rows = tile_rows(i)
        low = d_resid[rows, :].astype(BF)
        d_proj[rows, :] = low
        note(SMALL_BIAS + 5, low.astype(F32))

    for c in range(0, D, 256):
        d_join[:, c : c + 256] = dot_nt(d_proj[...], out_w[c : c + 256, :]).astype(BF)
    mix_pad[pl.ds(8, LEN), :] = d_join[:, HALF:].astype(F32)
    load[0].wait()

    @pl.loop(0, D // 256)
    def out_grad(c):
        part = dot_tn(joined[:, lanes_at(c * 256, 256)], d_proj[...])
        for n in range(2):
            shared[chunk(n * D + c * 256, 256), :] = part[:, n * HALF : (n + 1) * HALF].astype(BF)

    points.at(OUT)
    wait_all(load[1:4])
    query_low[...] = query[...].astype(BF)

    @pl.loop(0, HEADS // 2)
    def attend(pair):
        points.turn(ATTEND, pair)
        lanes = lanes_at(pair * 128)
        keys = key_low[:, lanes]
        values = value_low[:, lanes]
        scaled = keys * jnp.asarray(SCORE_SCALE, BF)
        keys_t = jnp.transpose(keys.astype(F32)).astype(BF)
        side = lax.broadcasted_iota(jnp.int32, (LEN, 128), 1) // HEAD
        nothing = jnp.zeros_like(keys)
        queries = query_low[:, lanes]
        d_context = d_join[:, lanes]
        d_queries, d_keys, d_values = [], [], []
        for head in range(2):
            key, value = jnp.where(side == head, scaled, nothing), jnp.where(side == head, values, nothing)
            total = log_total[pair * 2 + head]
            probs, weighted = [], []
            for c in range(0, LEN, 128):
                probs.append(jnp.exp(masked(dot_nt(key[c : c + 128], queries), c, length) - total))
                weighted.append(probs[-1] * dot_nt(value[c : c + 128], d_context))
            row_dot = sum(jnp.sum(w, axis=0, keepdims=True) for w in weighted)
            d_scores = jnp.concatenate([(w - p * row_dot).astype(BF) for w, p in zip(weighted, probs)], axis=0)
            probs = jnp.concatenate([p.astype(BF) for p in probs], axis=0)
            d_queries.append(dot(keys_t[head * HEAD : (head + 1) * HEAD, :], d_scores))
            d_keys.append(dot(d_scores, queries))
            d_values.append(dot(probs, d_context))
        d_att[:, lanes] = jnp.transpose(jnp.concatenate(d_queries, axis=0)) * SCORE_SCALE
        d_cat[:, lanes_at(HALF + pair * 128)] = (jnp.where(side == 0, d_keys[0], d_keys[1]) * SCORE_SCALE).astype(BF)
        d_cat[:, lanes_at(2 * HALF + pair * 128)] = jnp.where(side == 0, d_values[0], d_values[1]).astype(BF)

    wait_all(load[7:])

    @pl.loop(0, D // 256)
    def key_grad(c):
        low = x_low[:, lanes_at(c * 256, 256)]
        for n in range(2):
            part = dot_tn(low, d_cat[:, (n + 1) * HALF : (n + 2) * HALF])
            shared[chunk(1536 + n * D + c * 256, 256), :] = part.astype(BF)

    points.at(KEY)
    wait_all(load[4:7])

    @pl.loop(0, LEN // 256)
    def taps(i):
        points.turn(TAPS, i)
        rows = tile_rows(i, 256)
        around = pl.ds(pl.multiple_of(i * 256, 256), 256 + 16)
        padded = tile_rows(i, 256, 8)
        mix = mix_pad[padded, :]
        window = conv_pad[around, :]
        mix_window = mix_pad[around, :]
        d_kernel, d_conv = [], jnp.zeros((256, HALF), F32)
        dotted = jnp.zeros((256, TAPW), F32)
        for j in range(KERNEL):
            part = dot_nt((mix * moved(window, 4 + j, 256)).astype(BF), widen[...])
            d_kernel.append(part)
            dotted += part * kernels[padded, j * TAPW : (j + 1) * TAPW]
            share = moved(kernels[around, j * TAPW : (j + 1) * TAPW], 12 - j, 256)
            d_conv += dot(share.astype(BF), widen[...]) * moved(mix_window, 12 - j, 256)
        d_cat[rows, 3 * HALF :] = d_conv.astype(BF)
        wide = [kernels[padded, j * TAPW : (j + 1) * TAPW] * (d_kernel[j] - dotted) for j in range(KERNEL)]
        d_logit = dot_nt(jnp.concatenate(wide, axis=1).astype(BF), spread[...]).astype(BF)
        d_tap[rows, :] = d_logit
        d_mixed = dot(d_logit, tap_rows[...].astype(BF))
        q = query[rows, :]
        key = key_conv[rows, :]
        d_keyconv = (d_mixed * q).astype(BF)
        d_cat[rows, :HALF] = (d_att[rows, :] + d_mixed * key).astype(BF)
        note(SMALL_BIAS + 2, d_keyconv.astype(F32))
        cat = d_cat[rows, :].astype(F32)
        note(SMALL_BIAS, cat[:, :HALF])
        note(SMALL_BIAS + 1, cat[:, 2 * HALF : 3 * HALF])
        note(SMALL_BIAS + 3, cat[:, 3 * HALF :])
        small[SMALL_BIAS + 4 : SMALL_BIAS + 5, :TAPW] += jnp.sum(d_logit.astype(F32), axis=0, keepdims=True)
        d_join[rows, HALF:] = d_keyconv
        d_join[rows, :HALF] = (key * q).astype(BF)

    points.at(TAPS)
    shared[TAPS_AT : TAPS_AT + 64, :] = dot_tn(d_tap[...], d_join[:, :HALF])[:64].astype(BF)
    load_point.wait()
    for c in range(0, D, 256):
        depth_pad[pl.ds(8, LEN), c : c + 256] = dot_nt(d_join[:, HALF:], point[c : c + 256, :])

    @pl.loop(0, D // 256)
    def cat_grad(c):
        lanes = lanes_at(c * 256, 256)
        for n, k in enumerate((0, 3)):
            part = dot_tn(x_low[:, lanes], d_cat[:, k * HALF : (k + 1) * HALF])
            shared[chunk(EARLY + n * D + c * 256, 256), :] = part.astype(BF)
        part = dot_tn(depth_low[:, lanes], d_join[:, HALF:])
        shared[chunk(POINT_AT + c * 256, 256), :] = part.astype(BF)

    points.at(CAT)
    wait_all(load_cat)
    for n in range(3):
        cols = slice(n * 256, n * 256 + 256)
        d_input[:, cols] = d_resid[:, cols] + dot_nt(d_cat[...], w_cat[cols, :])
        points.at(LEAVE + 100 * n)

        for half in range(2):
            c = n * 256 + half * 128
            cols, slot = slice(c, c + 128), SMALL_DEPTH + 9 * (c // HALF)
            lanes = slice(c % HALF, c % HALF + 128)

            @pl.loop(0, LEN // TILE)
            def leave(i):
                rows = tile_rows(i)
                window = depth_pad[pl.ds(pl.multiple_of(i * TILE, TILE), TILE + 16), cols]
                low = x_low[rows, cols].astype(F32)
                total = d_input[rows, cols]
                for j in range(KERNEL):
                    part = moved(window, 12 - j, TILE)
                    total += w_depth[j, layer : layer + 1, cols].astype(F32) * part
                    small[slot + j : slot + j + 1, lanes] += jnp.sum(low * part, axis=0, keepdims=True)
                d_input[rows, cols] = total

    if first:
        @pl.loop(0, LEN // TILE)
        def seg_grad(i):
            rows = tile_rows(i)
            place = rows_iota(TILE) + i * TILE
            grad = d_input[rows, :] * (place < length).astype(F32)
            later = (place > split).astype(F32)
            note(SMALL_SEG + 2, grad * later)
            note(SMALL_SEG, grad * (1.0 - later))
            d_input[rows, :] = grad

    small_out[...] = small[...].astype(BF)
    points.at(END)


def forward_kernel(*refs):
    (lengths, splits, hidden, seg, cotangent, pieces), weights, norms = refs[:6], refs[6:22], refs[22:27]
    refs = refs[27:]
    kept_out = refs[:10], refs[10:19]
    log_totals, ffn_out, refs = refs[19:21], refs[21:26], refs[26:]
    output, d_resid_out, grads_out, small, refs = *refs[:4], refs[4:]
    (x_all, resid, gathered_0, gathered_1, planes_0, planes_1, bias_all, bias_plane, sems, own_sems, send_sems,
     recv_sems) = refs
    at = here()
    greet(at)
    length, split = lengths[my_row()], splits[my_row()]
    moves = Moves(sems)
    sends = Sends(send_sems, recv_sems)
    gathered, planes = (gathered_0, gathered_1), (planes_0, planes_1)
    plane, whole_of = [], []
    for layer in range(LAYERS):
        parts = [(pieces.at[layer * PARTS + p], planes[layer].at[p], gathered[layer].at[p], ORDERS[p])
                 for p in range(PARTS)]
        if layer == 0:
            parts.append((pieces.at[LAYERS * PARTS, :, pl.ds(0, TAPW)], bias_plane, bias_all, ORDERS[0]))
        gather = Gather(layer, at, sends, parts, own_sems.at[pl.ds(4 * layer, 4)])
        plane.append(gather.plane_steps())
        whole_of.append(gather.whole_steps())
    (a0, a1, a2), (b0, b1, b2, b3) = plane[0], whole_of[0]
    (c0, c1, c2), (d0, d1, d2, d3) = plane[1], whole_of[1]
    met()
    a0()
    points = (
        (Points({ENTER: (a1,), OUT: (a2, b0), ATTEND: (b1,), END: (b2,)}),
         Points({ENTER: (b3,), UNPACK: (c0,), FEED: (c1,), END: (c2, d0)})),
        (Points({(ATTEND, 1): (d1,), (ATTEND, 2): (d2,)}), Points({ENTER: (d3,)})),
    )
    stores = []
    for layer in range(LAYERS):
        pl.run_scoped(
            lambda *s: attention_forward_body(layer, length, split, hidden, seg, weights, x_all, resid, kept_out[layer],
                                              log_totals[layer], points[layer][0], *s),
            *vmem(*KEPT_SHAPES[:9], *FA_SCRATCH), dma(24))
        if layer == 0:
            stores.append(moves.start(resid, kept_out[0][9]))

            def feed(*s):
                ffn_forward_body(0, length, gathered_0, bias_all, norms, resid, x_all, ffn_out, s[:5], points[0][1], *s[5:])

            pl.run_scoped(feed, *vmem(*FFN_SHAPES, *FF_SCRATCH), dma(4), dma(12))
            wait_all(stores)
        else:
            def feed_both(gy, *s):
                ffn, s = s[:5], s[5:]
                load = moves.start(cotangent, gy)
                n = len(FF_SCRATCH) + 2
                ffn_forward_body(1, length, gathered_1, bias_all, norms, resid, x_all, None, ffn, points[1][1], *s[:n])
                stores.append(moves.start(x_all, output))
                ffn_backward_body(1, length, norms, gy, ffn, resid, s[n], (d_resid_out, grads_out, small), ([load], [], []),
                                  Points(), *s[n + 1 :])
                stores[-1].wait()

            pl.run_scoped(feed_both, *vmem(((LEN, D), BF), *FFN_SHAPES, *FF_SCRATCH), dma(1), dma(1),
                          *vmem(((LEN, D), F32), *BF_SCRATCH), dma(16))
    sends.finish()


def projections(w):
    return [(m, far()) for m in (w.w_query, w.w_key, w.w_value, w.w_conv, w.w_point, w.w_out)]


def norm_params(w):
    return [(m, whole()) for m in (w.first_gain, w.first_shift, w.b_down, w.second_gain, w.second_shift)]


def forward(pieces, w):
    ins = [(w.lengths, scalars()), (w.split_at, scalars()), (w.hidden, far()), (w.seg_table, whole()),
           (w.cotangent, far()), (pieces, far())] + projections(w)
    ins += [(m, whole()) for m in (w.w_depth, w.w_kernel, w.b_query, w.b_value, w.b_conv, w.b_keyconv, w.b_kernel,
                                   w.b_out, widen_matrix(), tap_matrix())] + norm_params(w)
    outs = [(shape(*s), far()) for s in KEPT_SHAPES + KEPT_SHAPES[:9]]
    outs += [(shape((HEADS, 1, LEN), F32), whole())] * 2 + [(shape(*s), far()) for s in FFN_SHAPES]
    outs += [(shape((LEN, D), F32), far())] * 2 + [(block_shape(16), far()), (shape((32, HALF), F32), whole())]
    plane, gathered = ((PARTS, 4, 4, 16, LANES), BF), (block_shape(16).shape, BF)
    scratch = vmem(((LEN, D), F32), ((LEN, D), F32), gathered, gathered, plane, plane, ((2, 4, 4, 4, 16, TAPW), BF),
                   ((4, 4, 16, TAPW), BF))
    scratch += [dma(4), dma(8), dma(112), dma(112)]
    outs = call(forward_kernel, ins, outs, scratch, "forward", **remote(1))
    return (*outs[:10], outs[19]), (*outs[10:19], outs[20]), outs[21:26], outs[26:]


def first_sums(at, sends, shared, mids, scratch):
    return [FirstSum(n, at, sends, shared.at[pl.ds(n * EARLY, EARLY)], mids[n], scratch[4 * n : 4 * n + 4]).steps()
            for n in range(2)]


def second_sums(name, at, sends, mids, gathered, scratch):
    return [SecondSum(name + n, at, sends, mids[n], gathered[n], scratch[4 * n : 4 * n + 4]).steps() for n in range(2)]


def backward_ins(kept, w):
    ins = [(w.lengths, scalars()), (w.split_at, scalars())] + [(m, far()) for m in kept[:9]]
    ins += [(kept[-1], whole())] + projections(w)
    return ins + [(m, whole()) for m in (w.w_depth, w.w_kernel, widen_matrix(), tap_matrix())]


GROUP, MIDS, SMALLS = shape((EARLY, HALF), BF), shape((PARTS, EARLY // 24, LANES), BF), shape((SMALL, HALF), BF)
OWN = shape((PARTS, 16, LANES), BF)


def middle_kernel(*refs):
    (lengths, splits), kept_in, log_total, refs = refs[:2], refs[2:11], refs[11], refs[12:]
    weights, ffn_small, d_resid_in, ffn_grads, refs = refs[:10], refs[10], refs[11], refs[12], refs[13:]
    d_input_out, own, early_mid, late_mid, small, refs = *refs[:5], refs[5:]
    d_input, shared, d_resid, refs = *refs[:3], refs[3:]
    sum_refs, scatter_refs, (sems, send_sems, recv_sems) = refs[:8], refs[8:14], refs[14:]
    at = here()
    greet(at)
    length, split = lengths[my_row()], splits[my_row()]
    moves = Moves(sems)
    load = moves.start(d_resid_in, d_resid)
    sends = Sends(send_sems, recv_sems)
    scatter = Scatter(5, at, sends, ffn_grads, scatter_refs)
    f = scatter.steps()
    e, l = first_sums(at, sends, shared, (early_mid, late_mid), sum_refs)
    met()
    points = Points({ENTER: (f[0],), (ATTEND, 2): (f[1], f[2]), KEY: (f[3], f[4], e[0]), TAPS: (e[1], e[2]),
                     CAT: (e[3], e[4], f[5], l[0]), LEAVE: (l[1], l[2]), LEAVE + 100: (l[3], l[4]),
                     LEAVE + 200: (f[6],), END: (e[5],)})
    pl.run_scoped(
        lambda *refs: attention_backward_body(1, length, split, d_resid, [load], kept_in, log_total, ffn_small, weights,
                                              shared, d_input, small, points, *refs),
        *vmem(*KEPT_SHAPES[:9], *BA_SCRATCH), dma(24))
    store = moves.start(d_input, d_input_out)
    f[7]()
    for p in range(PARTS):
        own[p] = scatter.own(p)[...]
    l[5]()
    sends.finish()
    store.wait()


def middle(d_resid, kept, ffn_small, ffn_grads, w):
    ins = backward_ins(kept, w) + [(ffn_small, whole()), (d_resid, far()), (ffn_grads, far())]
    outs = [(shape((LEN, D), F32), far())] + [(m, whole()) for m in (OWN, MIDS, MIDS, SMALLS)]
    scratch = vmem(((LEN, D), F32), ((SHARED_ROWS, HALF), BF), ((LEN, D), F32))
    scratch += first_scratch(32) * 2 + scatter_scratch(16)
    return call(middle_kernel, ins, outs, scratch + [dma(2), dma(96), dma(96)], "middle", **remote(2))


def last_kernel(*refs):
    (lengths, splits), kept_in, log_total, refs = refs[:2], refs[2:11], refs[11], refs[12:]
    weights, gy_in, ffn_in, resid_in, norms, refs = refs[:10], refs[10], refs[11:16], refs[16], refs[17:22], refs[22:]
    above_mids, above_small, refs = refs[:2], refs[2], refs[3:]
    d_input_out, grads_out, ffn_small_out, own, refs = *refs[:4], refs[4:]
    above_all, above_small_all, mine_all, small_all, refs = refs[:2], refs[2], refs[3:5], refs[5], refs[6:]
    d_input, d_resid, shared, mids, refs = *refs[:3], refs[3:5], refs[5:]
    sum_refs, second_refs, above_refs, refs = refs[:8], refs[8:16], refs[16:24], refs[24:]
    small, small_refs, above_small_refs, scatter_refs, refs = refs[0], refs[1:3], refs[3:5], refs[5:11], refs[11:]
    sems, send_sems, recv_sems = refs
    at = here()
    greet(at)
    length, split = lengths[my_row()], splits[my_row()]
    moves = Moves(sems)
    sends = Sends(send_sems, recv_sems)
    scatter = Scatter(7, at, sends, grads_out, scatter_refs)
    f = scatter.steps()
    a, b = second_sums(2, at, sends, above_mids, above_all, above_refs)
    c = SmallSum(4, at, sends, above_small, *above_small_refs).steps(above_small_all)
    e, l = first_sums(at, sends, shared, mids, sum_refs)
    more = second_sums(5, at, sends, mids, mine_all, second_refs)
    e, l = e + more[0], l + more[1]
    s = SmallSum(8, at, sends, small, *small_refs).steps(small_all)
    points = Points({FEED + 100: (a[1], b[1]), (GRAD, 1): (a[2], b[2], c[1]), END: (a[3], b[3])})

    def feed(gy, up, down, acted, slope, two, resid, load_sems, *refs):
        loads = Moves(load_sems)
        pairs = ((gy_in, gy), (ffn_in[4], two), (resid_in, resid), (ffn_in[3], slope), (ffn_in[1], down), (ffn_in[0], up),
                 (ffn_in[2], acted))
        loads = [loads.start(*pair) for pair in pairs]
        met()
        for step in (a[0], b[0], c[0]):
            step()
        ffn_backward_body(0, length, norms, gy, (up, down, acted, slope, two), resid, d_resid,
                          (None, grads_out, ffn_small_out), (loads[:3], loads[3:5], loads[5:]), points, *refs)

    pl.run_scoped(feed, *vmem(((LEN, D), F32), *FFN_SHAPES, ((LEN, D), F32)), dma(8), *vmem(*BF_SCRATCH), dma(16))
    points = Points({ENTER: (c[2], f[0]), (ATTEND, 0): (f[1],), (ATTEND, 1): (f[2],), (ATTEND, 2): (f[3], a[4], b[4]),
                     KEY: (f[4], e[0]), (TAPS, 1): (a[5], b[5]), TAPS: (e[1], e[2], c[3]),
                     CAT: (e[3], e[4], l[0], a[6], b[6]), LEAVE: (l[1], l[2]), LEAVE + 100: (l[3], l[4]),
                     LEAVE + 200: (f[5], e[5], e[6]), END: (s[0], c[4])})
    pl.run_scoped(
        lambda *refs: attention_backward_body(0, length, split, d_resid, [], kept_in, log_total, ffn_small_out, weights,
                                              shared, d_input, small, points, *refs),
        *vmem(*KEPT_SHAPES[:9], *BA_SCRATCH), dma(24))
    store = moves.start(d_input, d_input_out)
    for step in (l[5], l[6], s[1], e[7], f[6], l[7], s[2], e[8], f[7], l[8], s[3], e[9], l[9], s[4], e[10], e[11]):
        step()
    for p in range(PARTS):
        own[p] = scatter.own(p)[...]
    for step in (l[10], l[11], e[12], l[12]):
        step()
    sends.finish()
    store.wait()


def last(gy, kept, ffn, resid, mids, small, w):
    ins = backward_ins(kept, w) + [(m, far()) for m in (gy, *ffn, resid)] + norm_params(w)
    ins += [(m, whole()) for m in (*mids, small)]
    outs = [(shape((LEN, D), F32), far()), (block_shape(16), far()), (shape((32, HALF), F32), whole()), (OWN, whole()), (GROUP, far()),
            (GROUP, far()), (SMALLS, whole()), (GROUP, far()), (GROUP, far()), (SMALLS, whole())]
    scratch = vmem(((LEN, D), F32), ((LEN, D), F32), ((SHARED_ROWS, HALF), BF), (MIDS.shape, BF), (MIDS.shape, BF))
    scratch += first_scratch(32) * 2 + second_scratch(32) * 4
    scratch += vmem((SMALLS.shape, BF)) + vmem((OWN.shape, BF), ((PARTS, 3, 4, 16, LANES), BF)) * 2 + scatter_scratch(16)
    return call(last_kernel, ins, outs, scratch + [dma(1), dma(336), dma(336)], "last", **remote(3))


def hand_out_kernel(early_0, late_0, early_1, late_1, small_0, small_1, ffn_0, ffn_1, *refs):
    (seg, w_query, b_query, w_key, w_value, b_value, w_depth, w_point, b_keyconv, w_kernel, b_kernel, w_conv, b_conv,
     w_out, b_out, first_gain, first_shift, w_up, b_up, w_down, b_down, second_gain, second_shift) = refs[:23]
    low, high, load_sems, store_sems = refs[23:]
    group = lax.axis_index("grp")
    place = my_row() - group * 64
    loads, stores = Moves(load_sems), Moves(store_sems)
    for layer in range(LAYERS):
        for n in range(8):
            rows = pl.ds(n * D, D)
            source = (early_0, late_0, early_1, late_1)[2 * layer + n // 4].at[pl.ds(n % 4 * D, D)]
            loads.start(source, low.at[layer, rows])
    for layer in range(LAYERS):
        for n in range(7):
            loads.all[layer * 8 + n].wait()

            @pl.loop(0, D // 256)
            def widen(c):
                high[layer * 7 + n, tile_rows(c, 256), :] = low[layer, tile_rows(c + 3 * n, 256), :].astype(F32)

            out = (w_out, w_out, w_key, w_value, w_query, w_conv, w_point)[n].at[layer]
            if n < 2:
                out = out.at[:, pl.ds(n * HALF, HALF)]
            stores.start(high.at[layer * 7 + n], out)
    smalls, taps = [], []
    for layer, ffn in enumerate((ffn_0, ffn_1)):
        loads.all[layer * 8 + 7].wait()
        taps.append(low[layer, TAPS_AT : TAPS_AT + 64, :].astype(F32))
        smalls.append((small_0, small_1)[layer][...].astype(F32))
        rows = jnp.concatenate([ffn[p].astype(F32) for p in range(PARTS)], axis=0)
        w_up[layer, 0] = rows[:24]
        w_down[layer, 0] = rows[24:]
        mine = jnp.sum(jnp.where(rows_iota(8, HALF) == group * 4 + place // 16,
                                 smalls[layer][SMALL_FFN + 10 : SMALL_FFN + 18], 0.0), axis=0, keepdims=True)
        mine = jnp.broadcast_to(mine, (8, HALF))
        b_up[layer] = pltpu.roll(mine, (HALF - (place % 16) * 24) % HALF, 1)[:1, :24]

    def both(start, n=1):
        return jnp.concatenate(
            [jnp.concatenate([s[start + k : start + k + 1] for k in range(n)], axis=1) for s in smalls], axis=0)

    for j in range(KERNEL):
        w_depth[j] = jnp.concatenate([both(SMALL_DEPTH + j), both(SMALL_DEPTH + 9 + j)], axis=1)
    for j in range(HEADS * KERNEL):
        w_kernel[j] = jnp.concatenate([t[j : j + 1] for t in taps], axis=0)
    for n, out in enumerate((second_gain, second_shift, b_down, first_gain, first_shift)):
        out[...] = both(SMALL_FFN + 2 * n, 2)
    for n, out in enumerate((b_query, b_value, b_keyconv, b_conv)):
        out[...] = both(SMALL_BIAS + n)
    b_kernel[...] = both(SMALL_BIAS + 4)[:, : HEADS * KERNEL]
    b_out[...] = both(SMALL_BIAS + 5, 2)
    for n in range(2):
        s = smalls[0][SMALL_SEG + 2 * n : SMALL_SEG + 2 * n + 2]
        seg[n : n + 1, :] = jnp.concatenate([s[0:1], s[1:2]], axis=1)
    wait_all(stores.all)


def hand_out(shared, small, ffn):
    proj, half_row, full_row = (LAYERS, D, HALF), (LAYERS, HALF), (LAYERS, D)
    shapes = [(2, D), proj, half_row, proj, proj, half_row, (KERNEL, LAYERS, D), proj, half_row,
              (HEADS * KERNEL, LAYERS, HALF), (LAYERS, HEADS * KERNEL), proj, half_row, (LAYERS, D, D), full_row,
              full_row, full_row, (LAYERS, 1, 24, HALF), (LAYERS, 1, 24), (LAYERS, 1, 24, HALF), full_row, full_row,
              full_row]
    big = (proj, (LAYERS, D, D))
    outs = list(call(
        hand_out_kernel,
        [(m, far()) for m in shared] + [(m, whole()) for m in (*small, *ffn)],
        [(shape(s, F32), far() if s in big else whole()) for s in shapes],
        [pltpu.VMEM((LAYERS, SHARED_ROWS, HALF), BF), pltpu.VMEM((14, D, HALF), F32), dma(16), dma(14)],
        "hand_out",
    ))
    outs[6] = jnp.swapaxes(outs[6], 0, 1)
    outs[9] = jnp.transpose(outs[9], (1, 2, 0))
    outs[17] = jnp.swapaxes(outs[17], 2, 3)
    return tuple(outs)


def shards(*args):
    w = Params(*args)
    w = w._replace(w_depth=jnp.swapaxes(w.w_depth, 0, 1), w_kernel=jnp.transpose(w.w_kernel, (2, 0, 1)))
    pieces = jnp.concatenate([jnp.swapaxes(w.w_up[:, 0], 1, 2), w.down_weight[:, 0]], axis=1)
    bias = jnp.pad(w.b_up[:, 0], ((0, 16 - LAYERS), (0, LANES - w.b_up.shape[2])))
    pieces = jnp.concatenate([pieces.reshape(LAYERS * PARTS, 16, LANES), bias[None]])
    kept_0, kept_1, ffn, (output, d_resid, ffn_grads, small) = forward(pieces, w)
    grad, ffn_1, *mids, small = middle(d_resid, kept_1, small, ffn_grads, w)
    grad, _, _, ffn_0, early_1, late_1, small_1, early_0, late_0, small_0 = last(
        grad, kept_0, ffn, kept_0[9], mids, small, w)
    return (output, grad) + hand_out((early_0, late_0, early_1, late_1), (small_0, small_1), (ffn_0, ffn_1))


def solution(mesh):
    finer = Mesh(mesh.devices.reshape(mesh.shape["grp"], 4, 4, 2, 2), GRP_CH)
    rows, up = P(GRP_CH, None), P(None, "grp", None, CH)
    bias, down = P(None, "grp", CH), P(None, "grp", CH, None)
    placed = Params(*[P()] * len(Params._fields))._replace(
        hidden=rows, cotangent=rows, w_up=up, b_up=bias, down_weight=down)
    given = [P()] * 23
    given[17:20] = [up, bias, down]
    return jax.shard_map(
        shards,
        mesh=finer,
        in_specs=tuple(placed),
        out_specs=(rows, rows, *given),
        check_vma=False,
    )
```

```python
import functools
from typing import NamedTuple

import jax
import jax.numpy as jnp
import ml_dtypes
import numpy as np
from jax import lax
from jax.experimental import pallas as pl
from jax.experimental.pallas import tpu as pltpu
from jax.sharding import Mesh
from jax.sharding import PartitionSpec as P

HEADS = 6
HEAD = 64
KERNEL = 9
LAYERS = 2
LEN = 512
CH = ("ch_0", "ch_1", "ch_2", "ch_3")
GRP_CH = ("grp",) + CH
EPSILON = 1e-06
SCORE_SCALE = 0.125
MASK_VALUE = -1000000000.0
BF, F32 = jnp.bfloat16, jnp.float32
MESH = pl.DeviceIdType.MESH
LANES = 384
PARTS = 3
ORDERS = ("xyz", "yzx", "zxy")


def here():
    x, y = lax.axis_index("ch_1"), lax.axis_index("ch_0")
    z = lax.axis_index("grp") * 2 + lax.axis_index("ch_2")
    return {"x": x, "y": y, "z": z, "core": lax.axis_index("ch_3")}


def device_at(axis, place):
    if axis == "x":
        return {"ch_1": place}
    if axis == "y":
        return {"ch_0": place}
    if axis == "z":
        return {"grp": place // 2, "ch_2": place % 2}
    return {"ch_3": place}


def greet(at):
    peers = [("core", 1 - at["core"])]
    for axis in "xyz":
        peers += [(axis, (at[axis] + turn) % 4) for turn in (1, 2, 3)]
    for axis, place in peers:
        pl.semaphore_signal(
            pltpu.get_barrier_semaphore(), inc=1, device_id=device_at(axis, place), device_id_type=MESH)


def met():
    pl.semaphore_wait(pltpu.get_barrier_semaphore(), 10)


class Sends:
    def __init__(self, send_sems, recv_sems):
        self.send_sems, self.recv_sems, self.made = send_sems, recv_sems, {}

    def copy(self, key):
        number, make = self.made[key]
        src, dst, axis, place = make()
        return pltpu.make_async_remote_copy(
            src_ref=src, dst_ref=dst, send_sem=self.send_sems.at[number], recv_sem=self.recv_sems.at[number],
            device_id=device_at(axis, place), device_id_type=MESH)

    def start(self, key, make):
        if key not in self.made:
            self.made[key] = (len(self.made), make)
        self.copy(key).start()

    def arrived(self, *keys):
        for key in keys:
            self.copy(key).wait_recv()

    def finish(self):
        for key in self.made:
            self.copy(key).wait_send()


def all_in(lead, work):
    @pl.loop(0, int(np.prod(lead)))
    def one(i):
        at, rest = [], i
        for n in reversed(lead):
            at.append(rest % n)
            rest = rest // n
        work(tuple(reversed(at)))


class Scatter:
    def __init__(self, name, at, sends, x, scratch):
        self.name, self.at, self.sends, self.x = name, at, sends, x
        self.sums, self.core_in, self.bufs, self.load_sem = scratch[0], scratch[1], scratch[2:5], scratch[5]

    def load(self):
        return pltpu.make_async_copy(self.x.at[:, self.at["core"]], self.sums, self.load_sem.at[0])

    def place(self, p, s, turn):
        return (self.at[ORDERS[p][s]] + turn) % 4

    def block(self, p, s, turn):
        lead = [self.at[ORDERS[p][n]] for n in range(s)]
        return self.sums.at[(p, *lead, self.place(p, s, turn))]

    def begin(self):
        self.load().start()
        for turn in (2, 1, 3, 0):
            for p in range(PARTS):
                self.sends.start((self.name, 3, p, turn), lambda p=p, turn=turn: (
                    self.x.at[p, 1 - self.at["core"], self.place(p, 0, turn)],
                    self.core_in.at[p, self.place(p, 0, turn)], "core", 1 - self.at["core"]))

    def take(self, turn):
        for p in range(PARTS):
            self.sends.arrived((self.name, 3, p, turn))
            mine, other = self.block(p, 0, turn), self.core_in.at[p, self.place(p, 0, turn)]

            def add(at):
                mine[at] = mine[at] + other[at]

            all_in(mine.shape[:1], add)
            if turn:
                self.send(p, 0, turn)

    def send(self, p, s, turn):
        self.sends.start((self.name, s, p, turn), lambda: (
            self.block(p, s, turn), self.bufs[s].at[p, turn - 1], ORDERS[p][s], self.place(p, s, turn)))

    def onward(self, s):
        for p in range(PARTS):
            self.join(p, s - 1)
            for turn in (2, 1, 3):
                self.send(p, s, turn)

    def join(self, p, s):
        for turn in (1, 3, 2):
            self.sends.arrived((self.name, s, p, turn))
        mine, came = self.block(p, s, 0), self.bufs[s].at[p]

        def add(at):
            total = mine[at].astype(F32)
            for n in range(3):
                total += came[(n, *at)].astype(F32)
            mine[at] = total.astype(BF)

        if len(mine.shape) > 2:
            all_in(mine.shape[:1], add)
        else:
            add((Ellipsis,))

    def steps(self):
        def start():
            self.load().wait()
            self.take(2)

        return [self.begin, start, lambda: self.take(1), lambda: self.take(3), lambda: self.take(0),
                lambda: self.onward(1), lambda: self.onward(2), lambda: [self.join(p, 2) for p in range(PARTS)] and None]

    def own(self, p):
        return self.sums.at[(p, *[self.at[axis] for axis in ORDERS[p]])]


def scatter_scratch(rows):
    lead = (PARTS, 4, 4, 4)
    return [pltpu.VMEM(lead + (rows, LANES), BF), pltpu.VMEM(lead + (rows, LANES), BF),
            pltpu.VMEM((PARTS, 3, 4, 4, rows, LANES), BF), pltpu.VMEM((PARTS, 3, 4, rows, LANES), BF),
            pltpu.VMEM((PARTS, 3, rows, LANES), BF), dma(1)]


def chunk(start, size):
    return pl.ds(pl.multiple_of(start, 16), size)


class FirstSum:
    def __init__(self, name, at, sends, x, mid, scratch):
        self.name, self.at, self.sends, self.x, self.mid = name, at, sends, x, mid
        self.sums, self.core_in, self.came, self.load_sem = scratch
        self.c = x.shape[0] // (PARTS * 32)

    def place(self, p, turn):
        return (self.at[ORDERS[p][0]] + turn) % 4

    def loads(self):
        c = self.c
        return [pltpu.make_async_copy(self.x.at[chunk((p * 2 + self.at["core"]) * 16 * c, 16 * c)], self.sums.at[p],
                                      self.load_sem.at[p]) for p in range(PARTS)]

    def begin(self):
        c = self.c
        for load in self.loads():
            load.start()
        for turn in (2, 1, 3, 0):
            for p in range(PARTS):
                def make(p=p, turn=turn):
                    start = self.place(p, turn) * 4 * c
                    other = 1 - self.at["core"]
                    return (self.x.at[chunk((p * 2 + other) * 16 * c + start, 4 * c)],
                            self.core_in.at[p, chunk(start, 4 * c)], "core", other)

                self.sends.start((self.name, 3, p, turn), make)

    def take(self, turn):
        size = 4 * self.c
        for p in range(PARTS):
            self.sends.arrived((self.name, 3, p, turn))
            start = self.place(p, turn) * size

            @pl.loop(0, size // 64)
            def add(i):
                rows = chunk(start + i * 64, 64)
                self.sums[p, rows] = self.sums[p, rows] + self.core_in[p, rows]

            if turn:
                self.sends.start((self.name, 0, p, turn), lambda p=p: (
                    self.sums.at[p, chunk(self.place(p, turn) * size, size)], self.came.at[p, turn - 1], ORDERS[p][0],
                    self.place(p, turn)))

    def join(self):
        size = 4 * self.c
        for p in range(PARTS):
            for turn in (1, 3, 2):
                self.sends.arrived((self.name, 0, p, turn))
            start = self.place(p, 0) * size

            @pl.loop(0, size // 64)
            def add(i):
                rows = chunk(i * 64, 64)
                total = self.sums[p, chunk(start + i * 64, 64)].astype(F32)
                for n in range(3):
                    total += self.came[p, n, rows].astype(F32)
                self.mid[p, rows] = total.astype(BF)

    def steps(self):
        def start():
            for load in self.loads():
                load.wait()
            self.take(2)

        return [self.begin, start, lambda: self.take(1), lambda: self.take(3), lambda: self.take(0), self.join]


def first_scratch(c):
    return [pltpu.VMEM((PARTS, 16 * c, LANES), BF), pltpu.VMEM((PARTS, 16 * c, LANES), BF),
            pltpu.VMEM((PARTS, 3, 4 * c, LANES), BF), dma(PARTS)]


class SecondSum:
    def __init__(self, name, at, sends, mid, gathered, scratch):
        self.name, self.at, self.sends, self.mid, self.gathered = name, at, sends, mid, gathered
        self.came, self.slots, self.final, self.sems = scratch
        self.c = mid.shape[1] // 4

    def place(self, p, s, turn):
        return (self.at[ORDERS[p][s]] + turn) % 4

    def rows(self, p, first, second=None):
        c = self.c
        start = (p * 2 + self.at["core"]) * 16 * c + self.place(p, 0, first) * 4 * c
        if second is None:
            return self.gathered.at[chunk(start, 4 * c)]
        return self.gathered.at[chunk(start + self.place(p, 1, second) * c, c)]

    def scatter(self):
        c = self.c
        for p in range(PARTS):
            for turn in (2, 1, 3):
                self.sends.start((self.name, 1, p, turn), lambda p=p, turn=turn: (
                    self.mid.at[p, chunk(self.place(p, 1, turn) * c, c)], self.came.at[p, turn - 1], ORDERS[p][1],
                    self.place(p, 1, turn)))

    def share(self):
        for p in range(PARTS):
            for turn in (1, 3, 2):
                self.sends.arrived((self.name, 1, p, turn))
            total = self.mid[p, chunk(self.place(p, 1, 0) * self.c, self.c)].astype(F32)
            for n in range(3):
                total += self.came[p, n].astype(F32)
            self.slots[p, self.at[ORDERS[p][2]]] = total.astype(BF)
            for turn in (2, 1, 3):
                def make(p=p, turn=turn):
                    slot = self.slots.at[p, self.at[ORDERS[p][2]]]
                    return slot, slot, ORDERS[p][2], self.place(p, 2, turn)

                self.sends.start((self.name, 2, p, turn), make)

    def puts(self):
        return [pltpu.make_async_copy(self.final.at[p], self.rows(p, 0, 0), self.sems.at[p]) for p in range(PARTS)]

    def settle(self):
        for p in range(PARTS):
            for turn in (1, 3, 2):
                self.sends.arrived((self.name, 2, p, turn))
            total = self.slots[p, 0].astype(F32) + self.slots[p, 1].astype(F32)
            self.final[p] = (total + self.slots[p, 2].astype(F32) + self.slots[p, 3].astype(F32)).astype(BF)
            for turn in (2, 1, 3):
                self.sends.start((self.name, 4, p, turn), lambda p=p, turn=turn: (
                    self.final.at[p], self.rows(p, 0, 0), ORDERS[p][1], self.place(p, 1, turn)))
        for put in self.puts():
            put.start()

    def across(self, p, turn):
        def make():
            ref = self.rows(p, turn)
            return ref, ref, "core", 1 - self.at["core"]

        self.sends.start((self.name, 6, p, turn), make)

    def near(self):
        for put in self.puts():
            put.wait()
        for p in range(PARTS):
            for turn in (1, 3, 2):
                self.sends.arrived((self.name, 4, p, turn))
            for turn in (2, 1, 3):
                def make(p=p, turn=turn):
                    ref = self.rows(p, 0)
                    return ref, ref, ORDERS[p][0], self.place(p, 0, turn)

                self.sends.start((self.name, 5, p, turn), make)
            self.across(p, 0)

    def over(self, *turns):
        for turn in turns:
            for p in range(PARTS):
                self.sends.arrived((self.name, 5, p, turn))
                self.across(p, 4 - turn)

    def end(self):
        for turn in (0, 3, 1, 2):
            for p in range(PARTS):
                self.sends.arrived((self.name, 6, p, turn))

    def steps(self):
        return [self.scatter, self.share, self.settle, self.near, lambda: self.over(1, 3), lambda: self.over(2), self.end]


def second_scratch(c):
    return [pltpu.VMEM((PARTS, 3, c, LANES), BF), pltpu.VMEM((PARTS, 4, c, LANES), BF),
            pltpu.VMEM((PARTS, c, LANES), BF), dma(PARTS)]


class Gather:
    def __init__(self, name, at, sends, parts, sems):
        self.name, self.at, self.sends, self.parts, self.sems = name, at, sends, parts, sems

    def place(self, p, s, turn):
        return (self.at[self.parts[p][3][s]] + turn) % 4

    def in_plane(self, p):
        _, plane, _, order = self.parts[p]
        return plane.at[self.at[order[1]], self.at[order[2]]]

    def block(self, p, turn):
        return self.parts[p][2].at[self.at["core"], self.place(p, 0, turn)]

    def puts(self):
        return [pltpu.make_async_copy(part[0], self.in_plane(p), self.sems.at[p]) for p, part in enumerate(self.parts)]

    def last_puts(self):
        return [pltpu.make_async_copy(part[1], self.block(p, 0), self.sems.at[p]) for p, part in enumerate(self.parts)]

    def send(self, s, pick):
        for turn in (2, 1, 3):
            for p in range(len(self.parts)):
                self.sends.start((self.name, s, p, turn), lambda p=p, turn=turn: (
                    *pick(p), self.parts[p][3][s], self.place(p, s, turn)))

    def arrived(self, s, *turns):
        for turn in turns:
            for p in range(len(self.parts)):
                self.sends.arrived((self.name, s, p, turn))

    def across(self, turn):
        for p in range(len(self.parts)):
            def make(p=p):
                ref = self.block(p, turn)
                return self.parts[p][1] if turn == 0 else ref, ref, "core", 1 - self.at["core"]

            self.sends.start((self.name, 3, p, turn), make)

    def plane_steps(self):
        def first():
            for put in self.puts():
                put.start()
            self.send(2, lambda p: (self.parts[p][0], self.in_plane(p)))

        def second():
            for put in self.puts():
                put.wait()
            self.arrived(2, 1, 3, 2)

            def row(p):
                ref = self.parts[p][1].at[self.at[self.parts[p][3][1]]]
                return ref, ref

            self.send(1, row)

        return [first, second, lambda: self.arrived(1, 1, 3, 2)]

    def whole_steps(self):
        def first():
            for put in self.last_puts():
                put.start()
            self.send(0, lambda p: (self.parts[p][1], self.block(p, 0)))
            self.across(0)

        def more():
            self.arrived(0, 1)
            self.across(3)
            self.arrived(0, 3)
            self.across(1)

        def rest():
            self.arrived(0, 2)
            self.across(2)

        def end():
            self.arrived(3, 0, 3, 1, 2)
            for put in self.last_puts():
                put.wait()

        return [first, more, rest, end]


class SmallSum:
    def __init__(self, name, at, sends, x, core_in, slots):
        self.name, self.at, self.sends, self.x, self.core_in, self.slots = name, at, sends, x, core_in, slots

    def begin(self):
        for p in range(PARTS):
            self.sends.start((self.name, 3, p, 0), lambda p=p: (
                self.x.at[pl.ds(16 * p, 16)], self.core_in.at[p], "core", 1 - self.at["core"]))

    def total(self, p, s):
        if s == 0:
            self.sends.arrived((self.name, 3, p, 0))
            return self.x[16 * p : 16 * p + 16].astype(F32) + self.core_in[p].astype(F32)
        for turn in (1, 3, 2):
            self.sends.arrived((self.name, s - 1, p, turn))
        slots = self.slots.at[p, s - 1]
        return slots[0].astype(F32) + slots[1].astype(F32) + slots[2].astype(F32) + slots[3].astype(F32)

    def stage(self, s):
        for p in range(PARTS):
            self.slots[p, s, self.at[ORDERS[p][s]]] = self.total(p, s).astype(BF)
            for turn in (2, 1, 3):
                def make(p=p, turn=turn):
                    slot = self.slots.at[p, s, self.at[ORDERS[p][s]]]
                    return slot, slot, ORDERS[p][s], (self.at[ORDERS[p][s]] + turn) % 4

                self.sends.start((self.name, s, p, turn), make)

    def steps(self, out):
        def end():
            for p in range(PARTS):
                out[16 * p : 16 * p + 16] = self.total(p, 3).astype(BF)

        return [self.begin, lambda: self.stage(0), lambda: self.stage(1), lambda: self.stage(2), end]


def steps_in(i, *table):
    for turn, *steps in table:
        @pl.when(i == turn)
        def run():
            for step in steps:
                step()


D = 768
HALF = 384
HIDDEN = 1536
TILE = 128
TAPW = 128
PADDED = LEN + 16
SHARED_ROWS = 6144
VMEM_BYTES = 60 << 20
EARLY = 3072
POINT_AT, TAPS_AT, SMALL_AT = EARLY + 1536, EARLY + 2304, EARLY + 2368
SMALL_DEPTH, SMALL_FFN, SMALL_BIAS, SMALL_SEG, SMALL = 0, 18, 36, 43, 48


class Params(NamedTuple):
    hidden: jax.Array
    cotangent: jax.Array
    lengths: jax.Array
    split_at: jax.Array
    seg_table: jax.Array
    w_query: jax.Array
    b_query: jax.Array
    w_key: jax.Array
    w_value: jax.Array
    b_value: jax.Array
    w_depth: jax.Array
    w_point: jax.Array
    b_keyconv: jax.Array
    w_kernel: jax.Array
    b_kernel: jax.Array
    w_conv: jax.Array
    b_conv: jax.Array
    w_out: jax.Array
    b_out: jax.Array
    first_gain: jax.Array
    first_shift: jax.Array
    w_up: jax.Array
    b_up: jax.Array
    down_weight: jax.Array
    b_down: jax.Array
    second_gain: jax.Array
    second_shift: jax.Array


KEPT_SHAPES = (((LEN, D), BF), ((LEN, HALF), F32), ((LEN, HALF), BF), ((LEN, HALF), BF), ((LEN, D), BF),
               ((LEN, HALF), F32), ((PADDED, KERNEL * TAPW), F32), ((PADDED, HALF), F32), ((LEN, D), BF),
               ((LEN, D), F32))


def dims(lhs, rhs):
    return (((lhs,), (rhs,)), ((), ()))


def dot(a, b):
    return lax.dot_general(a, b, dims(1, 0), preferred_element_type=F32)


def dot_nt(a, b):
    return lax.dot_general(a, b, dims(1, 1), preferred_element_type=F32)


def dot_tn(a, b):
    return lax.dot_general(a, b, dims(0, 0), preferred_element_type=F32)


def tile_rows(i, n=TILE, start=0):
    return pl.ds(pl.multiple_of(i * n + start, 8 if start % 16 else 16), n)


def lanes_at(start, n=128):
    return pl.ds(pl.multiple_of(start, 128), n)


def rows_iota(n, width=1):
    return lax.broadcasted_iota(jnp.int32, (n, width), 0)


class Moves:
    def __init__(self, sems):
        self.sems, self.all = sems, []

    def start(self, src, dst):
        copy = pltpu.make_async_copy(src, dst, self.sems.at[len(self.all)])
        copy.start()
        self.all.append(copy)
        return copy

    def start_cat(self, layer, matrices, w_cat):
        return [self.start(ref.at[layer], w_cat.at[:, pl.ds(n * HALF, HALF)]) for n, ref in enumerate(matrices)]


def wait_all(copies):
    for copy in copies:
        copy.wait()


def my_row():
    row = lax.axis_index("grp")
    for name, size in zip(CH, (4, 4, 2, 2)):
        row = row * size + lax.axis_index(name)
    return row


def widen_matrix():
    lane = np.arange(HALF)[None, :] // HEAD
    return (np.arange(TAPW)[:, None] == lane).astype(ml_dtypes.bfloat16)


def tap_matrix():
    out = np.zeros((TAPW, KERNEL * TAPW), np.float32)
    for h in range(HEADS):
        for j in range(KERNEL):
            out[h * KERNEL + j, j * TAPW + h] = 1.0
    return out.astype(ml_dtypes.bfloat16)


def norm_stats(residual):
    mean = jnp.mean(residual, axis=-1, keepdims=True)
    center = residual - mean
    scale = lax.rsqrt(jnp.mean(center * center, axis=-1, keepdims=True) + EPSILON)
    return center * scale, scale


def norm_grad(gy, hat, scale, gain):
    d_hat = gy * gain
    mean_one = jnp.mean(d_hat, axis=-1, keepdims=True)
    mean_two = jnp.mean(d_hat * hat, axis=-1, keepdims=True)
    return scale * (d_hat - mean_one - hat * mean_two)


def gelu_both(pre):
    base = 1.0 + (0.3275911 * 0.7071067811865476) * jnp.abs(pre)
    t = pl.reciprocal(base, approx=True)
    t = t * (2.0 - base * t)
    poly = t * (0.127414796 + t * (-0.142248368 + t * (0.7107068705 + t * (-0.7265760135 + t * 0.5307027145))))
    bell = jnp.exp2((-0.5 * 1.4426950408889634) * (pre * pre))
    tail = poly * bell
    cdf = jnp.where(pre >= 0, 1.0 - tail, tail)
    return pre * cdf, cdf + pre * (bell * 0.3989422804014327)


def moved(window, start, n):
    size = window.shape[0]
    return pltpu.roll(window, (size - start) % size, 0)[:n]


def masked(scores, start, length):
    if start + scores.shape[0] <= 259:
        return scores
    return jnp.where(rows_iota(*scores.shape) + start < length, scores, MASK_VALUE)


def far():
    return pl.BlockSpec(memory_space=pl.ANY)


def whole():
    return pl.BlockSpec(memory_space=pltpu.VMEM)


def scalars():
    return pl.BlockSpec(memory_space=pltpu.SMEM)


def dma(n):
    return pltpu.SemaphoreType.DMA((n,))


def shape(dims, dtype):
    return jax.ShapeDtypeStruct(dims, dtype)


def block_shape(rows, lanes=LANES):
    return shape((PARTS, 2, 4, 4, 4, rows, lanes), BF)


def call(kernel, ins, outs, scratch, name, **comm):
    return pl.pallas_call(
        kernel,
        out_shape=[out for out, _ in outs],
        in_specs=[place for _, place in ins],
        out_specs=[place for _, place in outs],
        scratch_shapes=scratch,
        compiler_params=pltpu.CompilerParams(vmem_limit_bytes=VMEM_BYTES, **comm),
        name=name,
    )(*[array for array, _ in ins])


def vmem(*shapes):
    return [pltpu.VMEM(*s) for s in shapes]


class Points(dict):
    def at(self, point):
        for step in self.get(point, ()):
            step()

    def turn(self, point, i):
        for (name, turn), steps in [(key, s) for key, s in self.items() if isinstance(key, tuple)]:
            if name == point:
                steps_in(i, (turn, *steps))


def remote(number):
    return {"collective_id": number, "has_side_effects": True}


def tap_weights(layer, w_kernel, rows):
    rows[...] = jnp.zeros_like(rows)
    for n in range(HEADS * KERNEL):
        rows[n : n + 1, :] = w_kernel[n].astype(F32)[layer : layer + 1, :]


def clear_edges(*refs):
    for ref in refs:
        ref[pl.ds(0, 8), :] = jnp.zeros((8, ref.shape[1]), F32)
        ref[pl.ds(LEN + 8, 8), :] = jnp.zeros((8, ref.shape[1]), F32)


ENTER, DEPTH, ATTEND, END, UNPACK, FEED, BACK, GRAD, OUT, KEY, TAPS, CAT, LEAVE = range(13)

FORWARD_WEIGHTS = 14
FA_SCRATCH = [((LEN, D), BF), ((D, 4 * HALF), BF), ((D, HALF), BF), ((D, D), BF), ((PADDED, D), F32),
              ((LEN, HALF), BF), ((LEN, HALF), BF), ((TAPW, HALF), F32), ((HALF, KERNEL * TAPW), BF),
              ((8, KERNEL * TAPW), F32)]


def attention_forward_body(layer, length, split, x_in, seg, weights, x_all, resid, kept_out, log_total, points, *refs):
    first = layer == 0
    (w_query, w_key, w_value, w_conv, w_point, w_out, w_depth, w_kernel, b_query, b_value, b_conv, b_keyconv, b_kernel,
     b_out, widen, spread) = weights
    kept, refs = refs[:9], refs[9:]
    x_low, query, key_low, value_low, depth_low, key_conv, kernels, conv_pad, joined = kept
    hidden, w_cat, point, out_w, x_pad, query_low, mixed_low, tap_rows, taps_w, tap_bias, sems = refs
    one = slice(layer, layer + 1)
    moves = Moves(sems)
    load_x = [moves.start(x_in, hidden)] if first else []
    load_cat = moves.start_cat(layer, (w_query, w_key, w_value, w_conv), w_cat)
    load_rest = [moves.start(w_point.at[layer], point), moves.start(w_out.at[layer], out_w)]
    clear_edges(x_pad, conv_pad, kernels)
    tap_weights(layer, w_kernel, tap_rows)
    for c in range(0, KERNEL * TAPW, 384):
        taps_w[:, c : c + 384] = dot_tn(tap_rows[...].astype(BF), spread[:, c : c + 384]).astype(BF)
    tap_bias[...] = jnp.zeros_like(tap_bias)
    tap_bias[0:1, 0 : HEADS * KERNEL] = b_kernel[one, :]
    left, bias = tap_bias[:, :TAPW], jnp.zeros((8, KERNEL * TAPW), F32)
    for _ in range(3):
        bias += dot(left.astype(BF), spread[...])
        left = left - left.astype(BF).astype(F32)
    tap_bias[...] = bias

    wait_all(load_x)
    points.at(ENTER)

    @pl.loop(0, LEN // TILE)
    def enter(i):
        rows = tile_rows(i)
        if first:
            place = rows_iota(TILE) + i * TILE
            x = hidden[rows, :].astype(F32) + jnp.where(place > split, seg[1:2, :], seg[0:1, :])
            x = x * (place < length).astype(F32)
            x_all[rows, :] = x
        else:
            x = x_all[rows, :]
        low = x.astype(BF)
        x_low[rows, :] = low
        x_pad[tile_rows(i, TILE, 8), :] = low.astype(F32)

    wait_all(load_cat)
    for n in range(6):
        proj = dot(x_low[...], w_cat[:, n * 256 : n * 256 + 256])
        for h in range(2):
            which, c = (2 * n + h) // 3, (2 * n + h) % 3 * 128
            cols = slice(c, c + 128)
            part = proj[:, h * 128 : h * 128 + 128]
            if which == 0:
                part += b_query[one, cols]
                query[:, cols] = part
                query_low[:, cols] = part.astype(BF)
            elif which == 1:
                key_low[:, cols] = part.astype(BF)
            elif which == 2:
                value_low[:, cols] = (part + b_value[one, cols]).astype(BF)
            else:
                conv_pad[pl.ds(8, LEN), cols] = part + b_conv[one, cols]
    stores = [moves.start(kept[n], kept_out[n]) for n in (0, 1, 2, 3, 7)]
    points.at(OUT)

    @pl.loop(0, LEN // TILE)
    def depth(i):
        rows = tile_rows(i)
        around = pl.ds(pl.multiple_of(i * TILE, TILE), TILE + 16)
        for c in range(0, D, 128):
            cols = slice(c, c + 128)
            window = x_pad[around, cols]
            total = jnp.zeros((TILE, 128), F32)
            for j in range(KERNEL):
                total += w_depth[j, one, cols].astype(F32) * moved(window, 4 + j, TILE)
            depth_low[rows, cols] = total.astype(BF)

    points.at(DEPTH)
    wait_all(load_rest)
    for c, n in ((0, 256), (256, 128)):
        cols = slice(c, c + n)
        key = dot(depth_low[...], point[:, cols]) + b_keyconv[one, cols]
        key_conv[:, cols] = key
        mixed_low[:, cols] = (key * query[:, cols]).astype(BF)
    for c in range(0, KERNEL * TAPW, 384):
        cols = slice(c, c + 384)
        kernels[pl.ds(8, LEN), cols] = dot(mixed_low[...], taps_w[:, cols]) + tap_bias[0:1, cols]
    stores += [moves.start(kept[n], kept_out[n]) for n in (4, 5)]

    @pl.loop(0, LEN // 256)
    def convolve(i):
        rows = tile_rows(i, 256)
        around = pl.ds(pl.multiple_of(i * 256, 256), 256 + 16)
        padded = tile_rows(i, 256, 8)
        taps = [kernels[padded, j * TAPW : (j + 1) * TAPW] for j in range(KERNEL)]
        peak = functools.reduce(jnp.maximum, taps)
        taps = [jnp.exp(t - peak) for t in taps]
        share = 1.0 / sum(taps)
        window = conv_pad[around, :]
        mix = jnp.zeros((256, HALF), F32)
        for j in range(KERNEL):
            tap = taps[j] * share
            kernels[padded, j * TAPW : (j + 1) * TAPW] = tap
            mix += dot(tap.astype(BF), widen[...]) * moved(window, 4 + j, 256)
        joined[rows, HALF:] = mix.astype(BF)

    stores += [moves.start(kept[6], kept_out[6])]

    @pl.loop(0, HEADS // 2)
    def attend(pair):
        points.turn(ATTEND, pair)
        lanes = lanes_at(pair * 128)
        keys = key_low[:, lanes] * jnp.asarray(SCORE_SCALE, BF)
        side = lax.broadcasted_iota(jnp.int32, (LEN, 128), 1) // HEAD
        values = jnp.transpose(value_low[:, lanes].astype(F32)).astype(BF)
        queries = query_low[:, lanes]
        context = []
        for head in range(2):
            mine = jnp.where(side == head, keys, jnp.zeros_like(keys))
            scores = [masked(dot_nt(mine[c : c + 128], queries), c, length) for c in range(0, LEN, 128)]
            peak = functools.reduce(jnp.maximum, [jnp.max(s, axis=0, keepdims=True) for s in scores])
            probs = [jnp.exp(s - peak) for s in scores]
            total = sum(jnp.sum(p, axis=0, keepdims=True) for p in probs)
            log_total[pair * 2 + head] = peak + jnp.log(total)
            share = 1.0 / total
            probs = jnp.concatenate([(p * share).astype(BF) for p in probs], axis=0)
            context.append(dot(values[head * HEAD : (head + 1) * HEAD, :], probs))
        joined[:, lanes] = jnp.transpose(jnp.concatenate(context, axis=0)).astype(BF)

    stores += [moves.start(kept[8], kept_out[8])]
    points.at(ATTEND)
    for c in range(0, D, 256):
        cols = slice(c, c + 256)
        resid[:, cols] = x_all[:, cols] + dot(joined[...], out_w[:, cols]) + b_out[one, cols]
    points.at(END)
    wait_all(stores)


PLANES = (PARTS, 4, 4, 16, LANES)


def part_block(ref, p, core, x, y, z):
    if p == 0:
        return ref.at[0, core, x, y, z]
    if p == 1:
        return ref.at[1, core, y, z, x]
    return ref.at[2, core, z, x, y]


FFN_SHAPES = [((2 * HIDDEN, HALF), BF)] * 2 + [((LEN, 2 * HIDDEN), BF)] * 2 + [((LEN, D), F32)]
FF_SCRATCH = [((LEN, D), F32), ((LEN, D), BF), ((LEN, 512), F32), ((2, 64, TAPW), F32), ((1, 2 * HIDDEN), F32)]


def ffn_forward_body(layer, length, gathered, bias_all, norms, resid, x_next, outs, ffn, points, *refs):
    first_gain, first_shift, b_down, second_gain, second_shift = norms
    up, down, acted, slope, resid_two = ffn
    normed_rows, low, pre, bias_rows, bias, sems, block_sems = refs
    one = slice(layer, layer + 1)
    moves = Moves(sems)

    @pl.loop(0, LEN // TILE)
    def enter(i):
        rows = tile_rows(i)
        hat, _ = norm_stats(resid[rows, :])
        normed = hat * first_gain[one, :] + first_shift[one, :]
        normed_rows[rows, :] = normed
        low[rows, :] = normed.astype(BF)

    points.at(ENTER)

    @pl.loop(0, 64)
    def unpack(chip):
        z, y, x = (chip // 32) * 2 + chip % 2, (chip // 8) % 4, (chip // 2) % 4
        ups, downs = [], []
        for core in range(2):
            piece = jnp.concatenate(
                [part_block(gathered, p, core, x, y, z)[...].astype(F32) for p in range(PARTS)], axis=0)
            ups.append(piece[:24])
            downs.append(piece[24:])
            bias_rows[core, pl.ds(chip, 1), :] = bias_all[core, x, y, z].astype(F32)[one, :]
        rows = tile_rows(chip, 48)
        up[rows, :] = jnp.concatenate(ups, axis=0).astype(BF)
        down[rows, :] = jnp.concatenate(downs, axis=0).astype(BF)

    stores = [moves.start(up, outs[0]), moves.start(down, outs[1])] if outs else []
    points.at(UNPACK)
    for c in range(0, 2 * HIDDEN, 512):
        spot = lax.broadcasted_iota(jnp.int32, (64, 512), 1) + c
        slot = (lax.broadcasted_iota(jnp.int32, (TAPW, 512), 1) + c) % 24
        repeat = (slot == rows_iota(TAPW, 512)).astype(F32).astype(BF)
        total = jnp.zeros((1, 512), F32)
        for core in range(2):
            spread = dot(bias_rows[core].astype(BF), repeat)
            mine = spot // 24 == 2 * rows_iota(64, 512) + core
            total += jnp.sum(jnp.where(mine, spread, 0.0), axis=0, keepdims=True)
        bias[:, c : c + 512] = total

    def block_stores(n):
        cols = lanes_at(n * 512, 512)
        return [pltpu.make_async_copy(src.at[:, cols], out.at[:, cols], block_sems.at[2 * n + m])
                for m, (src, out) in enumerate(((acted, outs[2]), (slope, outs[3])))]

    for g in range(2):
        @pl.loop(0, HIDDEN // 512)
        def feed(k):
            at = g * HIDDEN + k * 512
            hidden = pl.ds(pl.multiple_of(at, 512), 512)
            pre[...] = dot_nt(low[:, g * HALF : (g + 1) * HALF], up[hidden, :]) + bias[:, hidden]

            @pl.loop(0, LEN // TILE)
            def act(i):
                few = tile_rows(i)
                for c in range(0, 512, 128):
                    value, grad = gelu_both(pre[few, c : c + 128])
                    cols = lanes_at(at + c)
                    acted[few, cols] = value.astype(BF)
                    slope[few, cols] = grad.astype(BF)

            if outs:
                for store in block_stores(g * (HIDDEN // 512) + k):
                    store.start()

        points.at(FEED + 100 * g)

    @pl.loop(0, LEN // 256)
    def leave(i):
        rows = tile_rows(i, 256)
        out = []
        for g in range(2):
            hidden = slice(g * HIDDEN, (g + 1) * HIDDEN)
            out.append(dot(acted[rows, hidden], down[hidden, :]).astype(BF).astype(F32))
        two = normed_rows[rows, :] + jnp.concatenate(out, axis=1) + b_down[one, :]
        resid_two[rows, :] = two
        hat, _ = norm_stats(two)
        valid = (rows_iota(256) + i * 256 < length).astype(F32)
        x_next[rows, :] = (hat * second_gain[one, :] + second_shift[one, :]) * valid

    points.at(END)
    if outs:
        stores.append(moves.start(resid_two, outs[4]))
        for n in range(2 * HIDDEN // 512):
            wait_all(block_stores(n))
    wait_all(stores)


BF_SCRATCH = [(block_shape(16).shape, BF), ((LEN, D), F32), ((LEN, 2 * HIDDEN), BF), ((LEN, D), BF),
              ((LEN, D), BF)]


def ffn_backward_body(layer, length, norms, gy, ffn, resid, d_resid, outs, waits, points, *refs):
    first_gain, first_shift, _, second_gain, _ = norms
    up, down, acted, slope, resid_two = ffn
    d_resid_out, grads_out, small = outs
    grads, d_two, d_pre, d_group, normed_low, sems = refs
    one = slice(layer, layer + 1)
    moves = Moves(sems)
    small[...] = jnp.zeros_like(small)

    def note(slot, value):
        total = jnp.sum(value, axis=0, keepdims=True)
        small[slot : slot + 1, :] += total[:, :HALF]
        small[slot + 1 : slot + 2, :] += total[:, HALF:]

    wait_all(waits[0])

    @pl.loop(0, LEN // TILE)
    def enter(i):
        rows = tile_rows(i)
        valid = (rows_iota(TILE) + i * TILE < length).astype(F32)
        grad = gy[rows, :].astype(F32) * valid
        hat, scale = norm_stats(resid_two[rows, :])
        note(0, grad * hat)
        note(2, grad)
        two = norm_grad(grad, hat, scale, second_gain[one, :])
        note(4, two)
        d_two[rows, :] = two
        d_group[rows, :] = two.astype(BF)
        hat, _ = norm_stats(resid[rows, :])
        normed_low[rows, :] = (hat * first_gain[one, :] + first_shift[one, :]).astype(BF)

    points.at(ENTER)
    wait_all(waits[1])
    for g in range(2):
        @pl.loop(0, HIDDEN // 256)
        def feed(k):
            hidden = pl.ds(pl.multiple_of(g * HIDDEN + k * 256, 256), 256)
            d_act = dot_nt(d_group[:, g * HALF : (g + 1) * HALF], down[hidden, :])
            d_pre[:, hidden] = (d_act * slope[:, hidden].astype(F32)).astype(BF)

        points.at(FEED + 100 * g)

    wait_all(waits[2])

    @pl.loop(0, LEN // 256)
    def back(i):
        rows = tile_rows(i, 256)
        got = []
        for g in range(2):
            hidden = slice(g * HIDDEN, (g + 1) * HIDDEN)
            got.append(dot(d_pre[rows, hidden], up[hidden, :]).astype(BF).astype(F32))
        d_normed = d_two[rows, :] + jnp.concatenate(got, axis=1)
        hat, scale = norm_stats(resid[rows, :])
        note(6, d_normed * hat)
        note(8, d_normed)
        d_resid[rows, :] = norm_grad(d_normed, hat, scale, first_gain[one, :])

    stores = [moves.start(d_resid, d_resid_out)] if d_resid_out is not None else []
    points.at(BACK)
    ones = jnp.ones((8, LEN), BF)
    for k in range(8):
        small[10 + k : 11 + k, :] = dot(ones, d_pre[:, k * HALF : (k + 1) * HALF])[0:1, :]

    for g in range(2):
        @pl.loop(0, 4)
        def grad(y):
            points.turn(GRAD + 100 * g, y)
            hidden = lanes_at(g * HIDDEN + y * HALF, HALF)
            cols = slice(g * HALF, (g + 1) * HALF)
            d_up = dot_tn(d_pre[:, hidden], normed_low[:, cols])
            d_down = dot_tn(acted[:, hidden], d_group[:, cols])
            for d in range(16):
                x, z, core = d // 4, g * 2 + (d // 2) % 2, d % 2
                piece = jnp.concatenate([d_up[24 * d : 24 * d + 24], d_down[24 * d : 24 * d + 24]], axis=0).astype(BF)
                for p in range(PARTS):
                    part_block(grads, p, core, x, y, z)[...] = piece[16 * p : 16 * p + 16]

        zs = pl.ds(2 * g, 2)
        for index in ((0, slice(None), slice(None), slice(None), zs), (1, slice(None), slice(None), zs),
                      (2, slice(None), zs)):
            stores.append(moves.start(grads.at[index], grads_out.at[index]))

    points.at(END)
    wait_all(stores)


BA_SCRATCH = [((D, 4 * HALF), BF), ((D, HALF), BF), ((D, D), BF), ((LEN, D), BF), ((LEN, 4 * HALF), BF), ((LEN, D), BF),
              ((LEN, HALF), BF), ((LEN, HALF), F32), ((PADDED, HALF), F32), ((PADDED, D), F32), ((SMALL, HALF), F32),
              ((LEN, TAPW), BF), ((TAPW, HALF), F32)]


def attention_backward_body(layer, length, split, d_resid, waits, kept_in, log_total, ffn_small, weights, shared, d_input,
                            small_out, points, *refs):
    first = layer == 0
    w_query, w_key, w_value, w_conv, w_point, w_out, w_depth, w_kernel, widen, spread = weights
    kept, refs = refs[:9], refs[9:]
    x_low, query, key_low, value_low, depth_low, key_conv, kernels, conv_pad, joined = kept
    (w_cat, point, out_w, d_proj, d_cat, d_join, query_low, d_att, mix_pad, depth_pad, small, d_tap, tap_rows,
     sems) = refs
    moves = Moves(sems)
    load_first = [*waits, moves.start(w_out.at[layer], out_w)]
    load = [moves.start(kept_in[n], kept[n]) for n in (8, 1, 2, 3, 6, 7, 5, 4, 0)]
    load_cat = moves.start_cat(layer, (w_query, w_key, w_value, w_conv), w_cat)
    load_point = moves.start(w_point.at[layer], point)
    clear_edges(mix_pad, depth_pad)
    small[...] = jnp.zeros_like(small)
    small[SMALL_FFN : SMALL_FFN + 18, :] = ffn_small[0:18, :]
    shared[SMALL_AT:, :] = jnp.zeros((SHARED_ROWS - SMALL_AT, HALF), BF)
    tap_weights(layer, w_kernel, tap_rows)

    def note(slot, value):
        total = jnp.sum(value, axis=0, keepdims=True)
        for n in range(total.shape[1] // HALF):
            small[slot + n : slot + n + 1, :] += total[:, n * HALF : (n + 1) * HALF]

    points.at(ENTER)
    wait_all(load_first)

    @pl.loop(0, LEN // TILE)
    def enter(i):
        rows = tile_rows(i)
        low = d_resid[rows, :].astype(BF)
        d_proj[rows, :] = low
        note(SMALL_BIAS + 5, low.astype(F32))

    for c in range(0, D, 256):
        d_join[:, c : c + 256] = dot_nt(d_proj[...], out_w[c : c + 256, :]).astype(BF)
    mix_pad[pl.ds(8, LEN), :] = d_join[:, HALF:].astype(F32)
    load[0].wait()

    @pl.loop(0, D // 256)
    def out_grad(c):
        part = dot_tn(joined[:, lanes_at(c * 256, 256)], d_proj[...])
        for n in range(2):
            shared[chunk(n * D + c * 256, 256), :] = part[:, n * HALF : (n + 1) * HALF].astype(BF)

    points.at(OUT)
    wait_all(load[1:4])
    query_low[...] = query[...].astype(BF)

    @pl.loop(0, HEADS // 2)
    def attend(pair):
        points.turn(ATTEND, pair)
        lanes = lanes_at(pair * 128)
        keys = key_low[:, lanes]
        values = value_low[:, lanes]
        scaled = keys * jnp.asarray(SCORE_SCALE, BF)
        keys_t = jnp.transpose(keys.astype(F32)).astype(BF)
        side = lax.broadcasted_iota(jnp.int32, (LEN, 128), 1) // HEAD
        nothing = jnp.zeros_like(keys)
        queries = query_low[:, lanes]
        d_context = d_join[:, lanes]
        d_queries, d_keys, d_values = [], [], []
        for head in range(2):
            key, value = jnp.where(side == head, scaled, nothing), jnp.where(side == head, values, nothing)
            total = log_total[pair * 2 + head]
            probs, weighted = [], []
            for c in range(0, LEN, 128):
                probs.append(jnp.exp(masked(dot_nt(key[c : c + 128], queries), c, length) - total))
                weighted.append(probs[-1] * dot_nt(value[c : c + 128], d_context))
            row_dot = sum(jnp.sum(w, axis=0, keepdims=True) for w in weighted)
            d_scores = jnp.concatenate([(w - p * row_dot).astype(BF) for w, p in zip(weighted, probs)], axis=0)
            probs = jnp.concatenate([p.astype(BF) for p in probs], axis=0)
            d_queries.append(dot(keys_t[head * HEAD : (head + 1) * HEAD, :], d_scores))
            d_keys.append(dot(d_scores, queries))
            d_values.append(dot(probs, d_context))
        d_att[:, lanes] = jnp.transpose(jnp.concatenate(d_queries, axis=0)) * SCORE_SCALE
        d_cat[:, lanes_at(HALF + pair * 128)] = (jnp.where(side == 0, d_keys[0], d_keys[1]) * SCORE_SCALE).astype(BF)
        d_cat[:, lanes_at(2 * HALF + pair * 128)] = jnp.where(side == 0, d_values[0], d_values[1]).astype(BF)

    wait_all(load[7:])

    @pl.loop(0, D // 256)
    def key_grad(c):
        low = x_low[:, lanes_at(c * 256, 256)]
        for n in range(2):
            part = dot_tn(low, d_cat[:, (n + 1) * HALF : (n + 2) * HALF])
            shared[chunk(1536 + n * D + c * 256, 256), :] = part.astype(BF)

    points.at(KEY)
    wait_all(load[4:7])

    @pl.loop(0, LEN // 256)
    def taps(i):
        points.turn(TAPS, i)
        rows = tile_rows(i, 256)
        around = pl.ds(pl.multiple_of(i * 256, 256), 256 + 16)
        padded = tile_rows(i, 256, 8)
        mix = mix_pad[padded, :]
        window = conv_pad[around, :]
        mix_window = mix_pad[around, :]
        d_kernel, d_conv = [], jnp.zeros((256, HALF), F32)
        dotted = jnp.zeros((256, TAPW), F32)
        for j in range(KERNEL):
            part = dot_nt((mix * moved(window, 4 + j, 256)).astype(BF), widen[...])
            d_kernel.append(part)
            dotted += part * kernels[padded, j * TAPW : (j + 1) * TAPW]
            share = moved(kernels[around, j * TAPW : (j + 1) * TAPW], 12 - j, 256)
            d_conv += dot(share.astype(BF), widen[...]) * moved(mix_window, 12 - j, 256)
        d_cat[rows, 3 * HALF :] = d_conv.astype(BF)
        wide = [kernels[padded, j * TAPW : (j + 1) * TAPW] * (d_kernel[j] - dotted) for j in range(KERNEL)]
        d_logit = dot_nt(jnp.concatenate(wide, axis=1).astype(BF), spread[...]).astype(BF)
        d_tap[rows, :] = d_logit
        d_mixed = dot(d_logit, tap_rows[...].astype(BF))
        q = query[rows, :]
        key = key_conv[rows, :]
        d_keyconv = (d_mixed * q).astype(BF)
        d_cat[rows, :HALF] = (d_att[rows, :] + d_mixed * key).astype(BF)
        note(SMALL_BIAS + 2, d_keyconv.astype(F32))
        cat = d_cat[rows, :].astype(F32)
        note(SMALL_BIAS, cat[:, :HALF])
        note(SMALL_BIAS + 1, cat[:, 2 * HALF : 3 * HALF])
        note(SMALL_BIAS + 3, cat[:, 3 * HALF :])
        small[SMALL_BIAS + 4 : SMALL_BIAS + 5, :TAPW] += jnp.sum(d_logit.astype(F32), axis=0, keepdims=True)
        d_join[rows, HALF:] = d_keyconv
        d_join[rows, :HALF] = (key * q).astype(BF)

    points.at(TAPS)
    shared[TAPS_AT : TAPS_AT + 64, :] = dot_tn(d_tap[...], d_join[:, :HALF])[:64].astype(BF)
    load_point.wait()
    for c in range(0, D, 256):
        depth_pad[pl.ds(8, LEN), c : c + 256] = dot_nt(d_join[:, HALF:], point[c : c + 256, :])

    @pl.loop(0, D // 256)
    def cat_grad(c):
        lanes = lanes_at(c * 256, 256)
        for n, k in enumerate((0, 3)):
            part = dot_tn(x_low[:, lanes], d_cat[:, k * HALF : (k + 1) * HALF])
            shared[chunk(EARLY + n * D + c * 256, 256), :] = part.astype(BF)
        part = dot_tn(depth_low[:, lanes], d_join[:, HALF:])
        shared[chunk(POINT_AT + c * 256, 256), :] = part.astype(BF)

    points.at(CAT)
    wait_all(load_cat)
    for n in range(3):
        cols = slice(n * 256, n * 256 + 256)
        d_input[:, cols] = d_resid[:, cols] + dot_nt(d_cat[...], w_cat[cols, :])
        points.at(LEAVE + 100 * n)

        for half in range(2):
            c = n * 256 + half * 128
            cols, slot = slice(c, c + 128), SMALL_DEPTH + 9 * (c // HALF)
            lanes = slice(c % HALF, c % HALF + 128)

            @pl.loop(0, LEN // TILE)
            def leave(i):
                rows = tile_rows(i)
                window = depth_pad[pl.ds(pl.multiple_of(i * TILE, TILE), TILE + 16), cols]
                low = x_low[rows, cols].astype(F32)
                total = d_input[rows, cols]
                for j in range(KERNEL):
                    part = moved(window, 12 - j, TILE)
                    total += w_depth[j, layer : layer + 1, cols].astype(F32) * part
                    small[slot + j : slot + j + 1, lanes] += jnp.sum(low * part, axis=0, keepdims=True)
                d_input[rows, cols] = total

    if first:
        @pl.loop(0, LEN // TILE)
        def seg_grad(i):
            rows = tile_rows(i)
            place = rows_iota(TILE) + i * TILE
            grad = d_input[rows, :] * (place < length).astype(F32)
            later = (place > split).astype(F32)
            note(SMALL_SEG + 2, grad * later)
            note(SMALL_SEG, grad * (1.0 - later))
            d_input[rows, :] = grad

    small_out[...] = small[...].astype(BF)
    points.at(END)


def forward_kernel(*refs):
    (lengths, splits, hidden, seg, cotangent), weights, norms = refs[:5], refs[5:21], refs[21:26]
    (w_up, down_weight, b_up), refs = refs[26:29], refs[29:]
    kept_out = refs[:10], refs[10:19]
    log_totals, ffn_out, refs = refs[19:21], refs[21:26], refs[26:]
    output, d_resid_out, grads_out, small, refs = *refs[:4], refs[4:]
    (x_all, resid, gathered_0, gathered_1, planes_0, planes_1, bias_all, bias_plane, pieces, bias_wide, bias_piece, sems,
     own_sems, send_sems, recv_sems) = refs
    at = here()
    greet(at)
    for layer in range(LAYERS):
        rows = jnp.concatenate([w_up[layer].astype(F32), down_weight[layer].astype(F32)], axis=0).astype(BF)
        for p in range(PARTS):
            pieces[layer * PARTS + p] = rows[16 * p : 16 * p + 16]
    bias_wide[...] = jnp.zeros_like(bias_wide)
    bias_wide[0:LAYERS, 0 : b_up.shape[1]] = b_up[...].astype(F32)
    bias_piece[...] = bias_wide[...].astype(BF)
    length, split = lengths[my_row()], splits[my_row()]
    moves = Moves(sems)
    sends = Sends(send_sems, recv_sems)
    gathered, planes = (gathered_0, gathered_1), (planes_0, planes_1)
    plane, whole_of = [], []
    for layer in range(LAYERS):
        parts = [(pieces.at[layer * PARTS + p], planes[layer].at[p], gathered[layer].at[p], ORDERS[p])
                 for p in range(PARTS)]
        if layer == 0:
            parts.append((bias_piece, bias_plane, bias_all, ORDERS[0]))
        gather = Gather(layer, at, sends, parts, own_sems.at[pl.ds(4 * layer, 4)])
        plane.append(gather.plane_steps())
        whole_of.append(gather.whole_steps())
    (a0, a1, a2), (b0, b1, b2, b3) = plane[0], whole_of[0]
    (c0, c1, c2), (d0, d1, d2, d3) = plane[1], whole_of[1]
    met()
    a0()
    points = (
        (Points({ENTER: (a1,), OUT: (a2, b0), ATTEND: (b1,), END: (b2,)}),
         Points({ENTER: (b3,), UNPACK: (c0,), FEED: (c1,), FEED + 100: (c2, d0)})),
        (Points({(ATTEND, 1): (d1,), (ATTEND, 2): (d2,)}), Points({ENTER: (d3,)})),
    )
    stores = []
    for layer in range(LAYERS):
        pl.run_scoped(
            lambda *s: attention_forward_body(layer, length, split, hidden, seg, weights, x_all, resid, kept_out[layer],
                                              log_totals[layer], points[layer][0], *s),
            *vmem(*KEPT_SHAPES[:9], *FA_SCRATCH), dma(24))
        if layer == 0:
            stores.append(moves.start(resid, kept_out[0][9]))

            def feed(*s):
                ffn_forward_body(0, length, gathered_0, bias_all, norms, resid, x_all, ffn_out, s[:5], points[0][1], *s[5:])

            pl.run_scoped(feed, *vmem(*FFN_SHAPES, *FF_SCRATCH), dma(4), dma(12))
            wait_all(stores)
        else:
            def feed_both(gy, *s):
                ffn, s = s[:5], s[5:]
                load = moves.start(cotangent, gy)
                n = len(FF_SCRATCH) + 2
                ffn_forward_body(1, length, gathered_1, bias_all, norms, resid, x_all, None, ffn, points[1][1], *s[:n])
                stores.append(moves.start(x_all, output))
                ffn_backward_body(1, length, norms, gy, ffn, resid, s[n], (d_resid_out, grads_out, small), ([load], [], []),
                                  Points(), *s[n + 1 :])
                stores[-1].wait()

            pl.run_scoped(feed_both, *vmem(((LEN, D), BF), *FFN_SHAPES, *FF_SCRATCH), dma(1), dma(1),
                          *vmem(((LEN, D), F32), *BF_SCRATCH), dma(16))
    sends.finish()


def projections(w):
    return [(m, far()) for m in (w.w_query, w.w_key, w.w_value, w.w_conv, w.w_point, w.w_out)]


def norm_params(w):
    return [(m, whole()) for m in (w.first_gain, w.first_shift, w.b_down, w.second_gain, w.second_shift)]


def forward(w):
    ins = [(w.lengths, scalars()), (w.split_at, scalars()), (w.hidden, far()), (w.seg_table, whole()),
           (w.cotangent, far())] + projections(w)
    ins += [(m, whole()) for m in (w.w_depth, w.w_kernel, w.b_query, w.b_value, w.b_conv, w.b_keyconv, w.b_kernel,
                                   w.b_out, widen_matrix(), tap_matrix())] + norm_params(w)
    ins += [(m, whole()) for m in (jnp.swapaxes(w.w_up[:, 0], 1, 2), w.down_weight[:, 0], w.b_up[:, 0])]
    outs = [(shape(*s), far()) for s in KEPT_SHAPES + KEPT_SHAPES[:9]]
    outs += [(shape((HEADS, 1, LEN), F32), whole())] * 2 + [(shape(*s), far()) for s in FFN_SHAPES]
    outs += [(shape((LEN, D), F32), far())] * 2 + [(block_shape(16), far()), (shape((32, HALF), F32), whole())]
    plane, gathered = ((PARTS, 4, 4, 16, LANES), BF), (block_shape(16).shape, BF)
    scratch = vmem(((LEN, D), F32), ((LEN, D), F32), gathered, gathered, plane, plane, ((2, 4, 4, 4, 16, TAPW), BF),
                   ((4, 4, 16, TAPW), BF), ((LAYERS * PARTS, 16, LANES), BF), ((16, TAPW), F32), ((16, TAPW), BF))
    scratch += [dma(4), dma(8), dma(112), dma(112)]
    outs = call(forward_kernel, ins, outs, scratch, "forward", **remote(1))
    return (*outs[:10], outs[19]), (*outs[10:19], outs[20]), outs[21:26], outs[26:]


def first_sums(at, sends, shared, mids, scratch):
    return [FirstSum(n, at, sends, shared.at[pl.ds(n * EARLY, EARLY)], mids[n], scratch[4 * n : 4 * n + 4]).steps()
            for n in range(2)]


def second_sums(name, at, sends, mids, gathered, scratch):
    return [SecondSum(name + n, at, sends, mids[n], gathered[n], scratch[4 * n : 4 * n + 4]).steps() for n in range(2)]


def backward_ins(kept, w):
    ins = [(w.lengths, scalars()), (w.split_at, scalars())] + [(m, far()) for m in kept[:9]]
    ins += [(kept[-1], whole())] + projections(w)
    return ins + [(m, whole()) for m in (w.w_depth, w.w_kernel, widen_matrix(), tap_matrix())]


GROUP, MIDS, SMALLS = shape((EARLY, HALF), BF), shape((PARTS, EARLY // 24, LANES), BF), shape((SMALL, HALF), BF)
OWN = shape((PARTS, 16, LANES), BF)


def middle_kernel(*refs):
    (lengths, splits), kept_in, log_total, refs = refs[:2], refs[2:11], refs[11], refs[12:]
    weights, ffn_small, d_resid_in, ffn_grads, refs = refs[:10], refs[10], refs[11], refs[12], refs[13:]
    d_input_out, own, early_mid, late_mid, small, refs = *refs[:5], refs[5:]
    d_input, shared, d_resid, refs = *refs[:3], refs[3:]
    sum_refs, scatter_refs, (sems, send_sems, recv_sems) = refs[:8], refs[8:14], refs[14:]
    at = here()
    greet(at)
    length, split = lengths[my_row()], splits[my_row()]
    moves = Moves(sems)
    load = moves.start(d_resid_in, d_resid)
    sends = Sends(send_sems, recv_sems)
    scatter = Scatter(5, at, sends, ffn_grads, scatter_refs)
    f = scatter.steps()
    e, l = first_sums(at, sends, shared, (early_mid, late_mid), sum_refs)
    met()
    points = Points({ENTER: (f[0],), (ATTEND, 2): (f[1], f[2]), KEY: (f[3], f[4], e[0]), TAPS: (e[1], e[2]),
                     CAT: (e[3], e[4], f[5], l[0]), LEAVE: (l[1], l[2]), LEAVE + 100: (l[3], l[4]),
                     LEAVE + 200: (f[6],), END: (e[5],)})
    pl.run_scoped(
        lambda *refs: attention_backward_body(1, length, split, d_resid, [load], kept_in, log_total, ffn_small, weights,
                                              shared, d_input, small, points, *refs),
        *vmem(*KEPT_SHAPES[:9], *BA_SCRATCH), dma(24))
    store = moves.start(d_input, d_input_out)
    f[7]()
    for p in range(PARTS):
        own[p] = scatter.own(p)[...]
    l[5]()
    sends.finish()
    store.wait()


def middle(d_resid, kept, ffn_small, ffn_grads, w):
    ins = backward_ins(kept, w) + [(ffn_small, whole()), (d_resid, far()), (ffn_grads, far())]
    outs = [(shape((LEN, D), F32), far())] + [(m, whole()) for m in (OWN, MIDS, MIDS, SMALLS)]
    scratch = vmem(((LEN, D), F32), ((SHARED_ROWS, HALF), BF), ((LEN, D), F32))
    scratch += first_scratch(32) * 2 + scatter_scratch(16)
    return call(middle_kernel, ins, outs, scratch + [dma(2), dma(96), dma(96)], "middle", **remote(2))


def last_kernel(*refs):
    (lengths, splits), kept_in, log_total, refs = refs[:2], refs[2:11], refs[11], refs[12:]
    weights, gy_in, ffn_in, resid_in, norms, refs = refs[:10], refs[10], refs[11:16], refs[16], refs[17:22], refs[22:]
    above_mids, above_small, refs = refs[:2], refs[2], refs[3:]
    d_input_out, grads_out, ffn_small_out, own, refs = *refs[:4], refs[4:]
    above_all, above_small_all, mine_all, small_all, refs = refs[:2], refs[2], refs[3:5], refs[5], refs[6:]
    d_input, d_resid, shared, mids, refs = *refs[:3], refs[3:5], refs[5:]
    sum_refs, second_refs, above_refs, refs = refs[:8], refs[8:16], refs[16:24], refs[24:]
    small, small_refs, above_small_refs, scatter_refs, refs = refs[0], refs[1:3], refs[3:5], refs[5:11], refs[11:]
    sems, send_sems, recv_sems = refs
    at = here()
    greet(at)
    length, split = lengths[my_row()], splits[my_row()]
    moves = Moves(sems)
    sends = Sends(send_sems, recv_sems)
    scatter = Scatter(7, at, sends, grads_out, scatter_refs)
    f = scatter.steps()
    a, b = second_sums(2, at, sends, above_mids, above_all, above_refs)
    c = SmallSum(4, at, sends, above_small, *above_small_refs).steps(above_small_all)
    e, l = first_sums(at, sends, shared, mids, sum_refs)
    more = second_sums(5, at, sends, mids, mine_all, second_refs)
    e, l = e + more[0], l + more[1]
    s = SmallSum(8, at, sends, small, *small_refs).steps(small_all)
    points = Points({FEED + 100: (a[1], b[1]), (GRAD, 1): (a[2], b[2], c[1]), END: (a[3], b[3])})

    def feed(gy, up, down, acted, slope, two, resid, load_sems, *refs):
        loads = Moves(load_sems)
        pairs = ((gy_in, gy), (ffn_in[4], two), (resid_in, resid), (ffn_in[3], slope), (ffn_in[1], down), (ffn_in[0], up),
                 (ffn_in[2], acted))
        loads = [loads.start(*pair) for pair in pairs]
        met()
        for step in (a[0], b[0], c[0]):
            step()
        ffn_backward_body(0, length, norms, gy, (up, down, acted, slope, two), resid, d_resid,
                          (None, grads_out, ffn_small_out), (loads[:3], loads[3:5], loads[5:]), points, *refs)

    pl.run_scoped(feed, *vmem(((LEN, D), F32), *FFN_SHAPES, ((LEN, D), F32)), dma(8), *vmem(*BF_SCRATCH), dma(16))
    points = Points({ENTER: (c[2], f[0]), (ATTEND, 2): (f[1], f[2]), KEY: (f[3], f[4], e[0], a[4], b[4]),
                     (TAPS, 1): (a[5], b[5]), TAPS: (e[1], e[2], c[3]), CAT: (e[3], e[4], l[0], a[6], b[6]),
                     LEAVE: (l[1], l[2]), LEAVE + 100: (l[3], l[4]), LEAVE + 200: (e[5], e[6]), END: (s[0], c[4])})
    pl.run_scoped(
        lambda *refs: attention_backward_body(0, length, split, d_resid, [], kept_in, log_total, ffn_small_out, weights,
                                              shared, d_input, small, points, *refs),
        *vmem(*KEPT_SHAPES[:9], *BA_SCRATCH), dma(24))
    store = moves.start(d_input, d_input_out)
    for step in (l[5], l[6], s[1], e[7], f[5], l[7], s[2], e[8], f[6], l[8], s[3], e[9], l[9], s[4], f[7], e[10], e[11]):
        step()
    for p in range(PARTS):
        own[p] = scatter.own(p)[...]
    for step in (l[10], l[11], e[12], l[12]):
        step()
    sends.finish()
    store.wait()


def last(gy, kept, ffn, resid, mids, small, w):
    ins = backward_ins(kept, w) + [(m, far()) for m in (gy, *ffn, resid)] + norm_params(w)
    ins += [(m, whole()) for m in (*mids, small)]
    outs = [(shape((LEN, D), F32), far()), (block_shape(16), far()), (shape((32, HALF), F32), whole()), (OWN, whole()), (GROUP, far()),
            (GROUP, far()), (SMALLS, whole()), (GROUP, far()), (GROUP, far()), (SMALLS, whole())]
    scratch = vmem(((LEN, D), F32), ((LEN, D), F32), ((SHARED_ROWS, HALF), BF), (MIDS.shape, BF), (MIDS.shape, BF))
    scratch += first_scratch(32) * 2 + second_scratch(32) * 4
    scratch += vmem((SMALLS.shape, BF)) + vmem((OWN.shape, BF), ((PARTS, 3, 4, 16, LANES), BF)) * 2 + scatter_scratch(16)
    return call(last_kernel, ins, outs, scratch + [dma(1), dma(336), dma(336)], "last", **remote(3))


def hand_out_kernel(early_0, late_0, early_1, late_1, small_0, small_1, ffn_0, ffn_1, *refs):
    (seg, w_query, b_query, w_key, w_value, b_value, w_depth, w_point, b_keyconv, w_kernel, b_kernel, w_conv, b_conv,
     w_out, b_out, first_gain, first_shift, w_up, b_up, w_down, b_down, second_gain, second_shift) = refs[:23]
    low, high, load_sems, store_sems = refs[23:]
    group = lax.axis_index("grp")
    place = my_row() - group * 64
    loads, stores = Moves(load_sems), Moves(store_sems)
    for layer in range(LAYERS):
        for n in range(8):
            rows = pl.ds(n * D, D)
            source = (early_0, late_0, early_1, late_1)[2 * layer + n // 4].at[pl.ds(n % 4 * D, D)]
            loads.start(source, low.at[layer, rows])
    for layer in range(LAYERS):
        for n in range(7):
            loads.all[layer * 8 + n].wait()

            @pl.loop(0, D // 256)
            def widen(c):
                high[layer * 7 + n, tile_rows(c, 256), :] = low[layer, tile_rows(c + 3 * n, 256), :].astype(F32)

            out = (w_out, w_out, w_key, w_value, w_query, w_conv, w_point)[n].at[layer]
            if n < 2:
                out = out.at[:, pl.ds(n * HALF, HALF)]
            stores.start(high.at[layer * 7 + n], out)
    smalls, taps = [], []
    for layer, ffn in enumerate((ffn_0, ffn_1)):
        loads.all[layer * 8 + 7].wait()
        taps.append(low[layer, TAPS_AT : TAPS_AT + 64, :].astype(F32))
        smalls.append((small_0, small_1)[layer][...].astype(F32))
        rows = jnp.concatenate([ffn[p].astype(F32) for p in range(PARTS)], axis=0)
        w_up[layer, 0] = rows[:24]
        w_down[layer, 0] = rows[24:]
        mine = jnp.sum(jnp.where(rows_iota(8, HALF) == group * 4 + place // 16,
                                 smalls[layer][SMALL_FFN + 10 : SMALL_FFN + 18], 0.0), axis=0, keepdims=True)
        mine = jnp.broadcast_to(mine, (8, HALF))
        b_up[layer] = pltpu.roll(mine, (HALF - (place % 16) * 24) % HALF, 1)[:1, :24]

    def both(start, n=1):
        return jnp.concatenate(
            [jnp.concatenate([s[start + k : start + k + 1] for k in range(n)], axis=1) for s in smalls], axis=0)

    for j in range(KERNEL):
        w_depth[j] = jnp.concatenate([both(SMALL_DEPTH + j), both(SMALL_DEPTH + 9 + j)], axis=1)
    for j in range(HEADS * KERNEL):
        w_kernel[j] = jnp.concatenate([t[j : j + 1] for t in taps], axis=0)
    for n, out in enumerate((second_gain, second_shift, b_down, first_gain, first_shift)):
        out[...] = both(SMALL_FFN + 2 * n, 2)
    for n, out in enumerate((b_query, b_value, b_keyconv, b_conv)):
        out[...] = both(SMALL_BIAS + n)
    b_kernel[...] = both(SMALL_BIAS + 4)[:, : HEADS * KERNEL]
    b_out[...] = both(SMALL_BIAS + 5, 2)
    for n in range(2):
        s = smalls[0][SMALL_SEG + 2 * n : SMALL_SEG + 2 * n + 2]
        seg[n : n + 1, :] = jnp.concatenate([s[0:1], s[1:2]], axis=1)
    wait_all(stores.all)


def hand_out(shared, small, ffn):
    proj, half_row, full_row = (LAYERS, D, HALF), (LAYERS, HALF), (LAYERS, D)
    shapes = [(2, D), proj, half_row, proj, proj, half_row, (KERNEL, LAYERS, D), proj, half_row,
              (HEADS * KERNEL, LAYERS, HALF), (LAYERS, HEADS * KERNEL), proj, half_row, (LAYERS, D, D), full_row,
              full_row, full_row, (LAYERS, 1, 24, HALF), (LAYERS, 1, 24), (LAYERS, 1, 24, HALF), full_row, full_row,
              full_row]
    big = (proj, (LAYERS, D, D))
    outs = list(call(
        hand_out_kernel,
        [(m, far()) for m in shared] + [(m, whole()) for m in (*small, *ffn)],
        [(shape(s, F32), far() if s in big else whole()) for s in shapes],
        [pltpu.VMEM((LAYERS, SHARED_ROWS, HALF), BF), pltpu.VMEM((14, D, HALF), F32), dma(16), dma(14)],
        "hand_out",
    ))
    outs[6] = jnp.swapaxes(outs[6], 0, 1)
    outs[9] = jnp.transpose(outs[9], (1, 2, 0))
    outs[17] = jnp.swapaxes(outs[17], 2, 3)
    return tuple(outs)


def shards(*args):
    w = Params(*args)
    w = w._replace(w_depth=jnp.swapaxes(w.w_depth, 0, 1), w_kernel=jnp.transpose(w.w_kernel, (2, 0, 1)))
    kept_0, kept_1, ffn, (output, d_resid, ffn_grads, small) = forward(w)
    grad, ffn_1, *mids, small = middle(d_resid, kept_1, small, ffn_grads, w)
    grad, _, _, ffn_0, early_1, late_1, small_1, early_0, late_0, small_0 = last(
        grad, kept_0, ffn, kept_0[9], mids, small, w)
    return (output, grad) + hand_out((early_0, late_0, early_1, late_1), (small_0, small_1), (ffn_0, ffn_1))


def solution(mesh):
    finer = Mesh(mesh.devices.reshape(mesh.shape["grp"], 4, 4, 2, 2), GRP_CH)
    rows, up = P(GRP_CH, None), P(None, "grp", None, CH)
    bias, down = P(None, "grp", CH), P(None, "grp", CH, None)
    placed = Params(*[P()] * len(Params._fields))._replace(
        hidden=rows, cotangent=rows, w_up=up, b_up=bias, down_weight=down)
    given = [P()] * 23
    given[17:20] = [up, bias, down]
    return jax.shard_map(
        shards,
        mesh=finer,
        in_specs=tuple(placed),
        out_specs=(rows, rows, *given),
        check_vma=False,
    )
```

```python
import functools
from typing import NamedTuple

import jax
import jax.numpy as jnp
import ml_dtypes
import numpy as np
from jax import lax
from jax.experimental import pallas as pl
from jax.experimental.pallas import tpu as pltpu
from jax.sharding import Mesh
from jax.sharding import PartitionSpec as P

HEADS = 6
HEAD = 64
KERNEL = 9
LAYERS = 2
LEN = 512
CH = ("ch_0", "ch_1", "ch_2", "ch_3")
GRP_CH = ("grp",) + CH
EPSILON = 1e-06
SCORE_SCALE = 0.125
MASK_VALUE = -1000000000.0
BF, F32 = jnp.bfloat16, jnp.float32
MESH = pl.DeviceIdType.MESH
LANES = 384
PARTS = 3
ORDERS = ("xyz", "yzx", "zxy")


def here():
    x, y = lax.axis_index("ch_1"), lax.axis_index("ch_0")
    z = lax.axis_index("grp") * 2 + lax.axis_index("ch_2")
    return {"x": x, "y": y, "z": z, "core": lax.axis_index("ch_3")}


def device_at(axis, place):
    if axis == "x":
        return {"ch_1": place}
    if axis == "y":
        return {"ch_0": place}
    if axis == "z":
        return {"grp": place // 2, "ch_2": place % 2}
    return {"ch_3": place}


def greet(at):
    peers = [("core", 1 - at["core"])]
    for axis in "xyz":
        peers += [(axis, (at[axis] + turn) % 4) for turn in (1, 2, 3)]
    for axis, place in peers:
        pl.semaphore_signal(
            pltpu.get_barrier_semaphore(), inc=1, device_id=device_at(axis, place), device_id_type=MESH)


def met():
    pl.semaphore_wait(pltpu.get_barrier_semaphore(), 10)


class Sends:
    def __init__(self, send_sems, recv_sems):
        self.send_sems, self.recv_sems, self.made = send_sems, recv_sems, {}

    def copy(self, key):
        number, make = self.made[key]
        src, dst, axis, place = make()
        return pltpu.make_async_remote_copy(
            src_ref=src, dst_ref=dst, send_sem=self.send_sems.at[number], recv_sem=self.recv_sems.at[number],
            device_id=device_at(axis, place), device_id_type=MESH)

    def start(self, key, make):
        if key not in self.made:
            self.made[key] = (len(self.made), make)
        self.copy(key).start()

    def arrived(self, *keys):
        for key in keys:
            self.copy(key).wait_recv()

    def finish(self):
        for key in self.made:
            self.copy(key).wait_send()


def all_in(lead, work):
    @pl.loop(0, int(np.prod(lead)))
    def one(i):
        at, rest = [], i
        for n in reversed(lead):
            at.append(rest % n)
            rest = rest // n
        work(tuple(reversed(at)))


class Scatter:
    def __init__(self, name, at, sends, x, scratch):
        self.name, self.at, self.sends, self.x = name, at, sends, x
        self.sums, self.core_in, self.bufs, self.load_sem = scratch[0], scratch[1], scratch[2:5], scratch[5]

    def load(self):
        return pltpu.make_async_copy(self.x.at[:, self.at["core"]], self.sums, self.load_sem.at[0])

    def place(self, p, s, turn):
        return (self.at[ORDERS[p][s]] + turn) % 4

    def block(self, p, s, turn):
        lead = [self.at[ORDERS[p][n]] for n in range(s)]
        return self.sums.at[(p, *lead, self.place(p, s, turn))]

    def begin(self):
        self.load().start()
        for turn in (2, 1, 3, 0):
            for p in range(PARTS):
                self.sends.start((self.name, 3, p, turn), lambda p=p, turn=turn: (
                    self.x.at[p, 1 - self.at["core"], self.place(p, 0, turn)],
                    self.core_in.at[p, self.place(p, 0, turn)], "core", 1 - self.at["core"]))

    def take(self, turn):
        for p in range(PARTS):
            self.sends.arrived((self.name, 3, p, turn))
            mine, other = self.block(p, 0, turn), self.core_in.at[p, self.place(p, 0, turn)]

            def add(at):
                mine[at] = mine[at] + other[at]

            all_in(mine.shape[:1], add)
            if turn:
                self.send(p, 0, turn)

    def send(self, p, s, turn):
        self.sends.start((self.name, s, p, turn), lambda: (
            self.block(p, s, turn), self.bufs[s].at[p, turn - 1], ORDERS[p][s], self.place(p, s, turn)))

    def onward(self, s):
        for p in range(PARTS):
            self.join(p, s - 1)
            for turn in (2, 1, 3):
                self.send(p, s, turn)

    def join(self, p, s):
        for turn in (1, 3, 2):
            self.sends.arrived((self.name, s, p, turn))
        mine, came = self.block(p, s, 0), self.bufs[s].at[p]

        def add(at):
            total = mine[at].astype(F32)
            for n in range(3):
                total += came[(n, *at)].astype(F32)
            mine[at] = total.astype(BF)

        if len(mine.shape) > 2:
            all_in(mine.shape[:1], add)
        else:
            add((Ellipsis,))

    def steps(self):
        def start():
            self.load().wait()
            self.take(2)

        return [self.begin, start, lambda: self.take(1), lambda: self.take(3), lambda: self.take(0),
                lambda: self.onward(1), lambda: self.onward(2), lambda: [self.join(p, 2) for p in range(PARTS)] and None]

    def own(self, p):
        return self.sums.at[(p, *[self.at[axis] for axis in ORDERS[p]])]


def scatter_scratch(rows):
    lead = (PARTS, 4, 4, 4)
    return [pltpu.VMEM(lead + (rows, LANES), BF), pltpu.VMEM(lead + (rows, LANES), BF),
            pltpu.VMEM((PARTS, 3, 4, 4, rows, LANES), BF), pltpu.VMEM((PARTS, 3, 4, rows, LANES), BF),
            pltpu.VMEM((PARTS, 3, rows, LANES), BF), dma(1)]


def chunk(start, size):
    return pl.ds(pl.multiple_of(start, 16), size)


class FirstSum:
    def __init__(self, name, at, sends, x, mid, scratch):
        self.name, self.at, self.sends, self.x, self.mid = name, at, sends, x, mid
        self.sums, self.core_in, self.came, self.load_sem = scratch
        self.c = x.shape[0] // (PARTS * 32)

    def place(self, p, turn):
        return (self.at[ORDERS[p][0]] + turn) % 4

    def loads(self):
        c = self.c
        return [pltpu.make_async_copy(self.x.at[chunk((p * 2 + self.at["core"]) * 16 * c, 16 * c)], self.sums.at[p],
                                      self.load_sem.at[p]) for p in range(PARTS)]

    def begin(self):
        c = self.c
        for load in self.loads():
            load.start()
        for turn in (2, 1, 3, 0):
            for p in range(PARTS):
                def make(p=p, turn=turn):
                    start = self.place(p, turn) * 4 * c
                    other = 1 - self.at["core"]
                    return (self.x.at[chunk((p * 2 + other) * 16 * c + start, 4 * c)],
                            self.core_in.at[p, chunk(start, 4 * c)], "core", other)

                self.sends.start((self.name, 3, p, turn), make)

    def take(self, turn):
        size = 4 * self.c
        for p in range(PARTS):
            self.sends.arrived((self.name, 3, p, turn))
            start = self.place(p, turn) * size

            @pl.loop(0, size // 64)
            def add(i):
                rows = chunk(start + i * 64, 64)
                self.sums[p, rows] = self.sums[p, rows] + self.core_in[p, rows]

            if turn:
                self.sends.start((self.name, 0, p, turn), lambda p=p: (
                    self.sums.at[p, chunk(self.place(p, turn) * size, size)], self.came.at[p, turn - 1], ORDERS[p][0],
                    self.place(p, turn)))

    def join(self):
        size = 4 * self.c
        for p in range(PARTS):
            for turn in (1, 3, 2):
                self.sends.arrived((self.name, 0, p, turn))
            start = self.place(p, 0) * size

            @pl.loop(0, size // 64)
            def add(i):
                rows = chunk(i * 64, 64)
                total = self.sums[p, chunk(start + i * 64, 64)].astype(F32)
                for n in range(3):
                    total += self.came[p, n, rows].astype(F32)
                self.mid[p, rows] = total.astype(BF)

    def steps(self):
        def start():
            for load in self.loads():
                load.wait()
            self.take(2)

        return [self.begin, start, lambda: self.take(1), lambda: self.take(3), lambda: self.take(0), self.join]


def first_scratch(c):
    return [pltpu.VMEM((PARTS, 16 * c, LANES), BF), pltpu.VMEM((PARTS, 16 * c, LANES), BF),
            pltpu.VMEM((PARTS, 3, 4 * c, LANES), BF), dma(PARTS)]


class SecondSum:
    def __init__(self, name, at, sends, mid, gathered, scratch):
        self.name, self.at, self.sends, self.mid, self.gathered = name, at, sends, mid, gathered
        self.came, self.slots, self.final, self.sems = scratch
        self.c = mid.shape[1] // 4

    def place(self, p, s, turn):
        return (self.at[ORDERS[p][s]] + turn) % 4

    def rows(self, p, first, second=None):
        c = self.c
        start = (p * 2 + self.at["core"]) * 16 * c + self.place(p, 0, first) * 4 * c
        if second is None:
            return self.gathered.at[chunk(start, 4 * c)]
        return self.gathered.at[chunk(start + self.place(p, 1, second) * c, c)]

    def scatter(self):
        c = self.c
        for p in range(PARTS):
            for turn in (2, 1, 3):
                self.sends.start((self.name, 1, p, turn), lambda p=p, turn=turn: (
                    self.mid.at[p, chunk(self.place(p, 1, turn) * c, c)], self.came.at[p, turn - 1], ORDERS[p][1],
                    self.place(p, 1, turn)))

    def share(self):
        for p in range(PARTS):
            for turn in (1, 3, 2):
                self.sends.arrived((self.name, 1, p, turn))
            total = self.mid[p, chunk(self.place(p, 1, 0) * self.c, self.c)].astype(F32)
            for n in range(3):
                total += self.came[p, n].astype(F32)
            self.slots[p, self.at[ORDERS[p][2]]] = total.astype(BF)
            for turn in (2, 1, 3):
                def make(p=p, turn=turn):
                    slot = self.slots.at[p, self.at[ORDERS[p][2]]]
                    return slot, slot, ORDERS[p][2], self.place(p, 2, turn)

                self.sends.start((self.name, 2, p, turn), make)

    def puts(self):
        return [pltpu.make_async_copy(self.final.at[p], self.rows(p, 0, 0), self.sems.at[p]) for p in range(PARTS)]

    def settle(self):
        for p in range(PARTS):
            for turn in (1, 3, 2):
                self.sends.arrived((self.name, 2, p, turn))
            total = self.slots[p, 0].astype(F32) + self.slots[p, 1].astype(F32)
            self.final[p] = (total + self.slots[p, 2].astype(F32) + self.slots[p, 3].astype(F32)).astype(BF)
            for turn in (2, 1, 3):
                self.sends.start((self.name, 4, p, turn), lambda p=p, turn=turn: (
                    self.final.at[p], self.rows(p, 0, 0), ORDERS[p][1], self.place(p, 1, turn)))
        for put in self.puts():
            put.start()

    def across(self, p, turn):
        def make():
            ref = self.rows(p, turn)
            return ref, ref, "core", 1 - self.at["core"]

        self.sends.start((self.name, 6, p, turn), make)

    def near(self):
        for put in self.puts():
            put.wait()
        for p in range(PARTS):
            for turn in (1, 3, 2):
                self.sends.arrived((self.name, 4, p, turn))
            for turn in (2, 1, 3):
                def make(p=p, turn=turn):
                    ref = self.rows(p, 0)
                    return ref, ref, ORDERS[p][0], self.place(p, 0, turn)

                self.sends.start((self.name, 5, p, turn), make)
            self.across(p, 0)

    def over(self, *turns):
        for turn in turns:
            for p in range(PARTS):
                self.sends.arrived((self.name, 5, p, turn))
                self.across(p, 4 - turn)

    def end(self):
        for turn in (0, 3, 1, 2):
            for p in range(PARTS):
                self.sends.arrived((self.name, 6, p, turn))

    def steps(self):
        return [self.scatter, self.share, self.settle, self.near, lambda: self.over(1, 3), lambda: self.over(2), self.end]


def second_scratch(c):
    return [pltpu.VMEM((PARTS, 3, c, LANES), BF), pltpu.VMEM((PARTS, 4, c, LANES), BF),
            pltpu.VMEM((PARTS, c, LANES), BF), dma(PARTS)]


class Gather:
    def __init__(self, name, at, sends, parts, sems):
        self.name, self.at, self.sends, self.parts, self.sems = name, at, sends, parts, sems

    def place(self, p, s, turn):
        return (self.at[self.parts[p][3][s]] + turn) % 4

    def in_plane(self, p):
        _, plane, _, order = self.parts[p]
        return plane.at[self.at[order[1]], self.at[order[2]]]

    def block(self, p, turn):
        return self.parts[p][2].at[self.at["core"], self.place(p, 0, turn)]

    def puts(self):
        return [pltpu.make_async_copy(part[0], self.in_plane(p), self.sems.at[p]) for p, part in enumerate(self.parts)]

    def last_puts(self):
        return [pltpu.make_async_copy(part[1], self.block(p, 0), self.sems.at[p]) for p, part in enumerate(self.parts)]

    def send(self, s, pick):
        for turn in (2, 1, 3):
            for p in range(len(self.parts)):
                self.sends.start((self.name, s, p, turn), lambda p=p, turn=turn: (
                    *pick(p), self.parts[p][3][s], self.place(p, s, turn)))

    def arrived(self, s, *turns):
        for turn in turns:
            for p in range(len(self.parts)):
                self.sends.arrived((self.name, s, p, turn))

    def across(self, turn):
        for p in range(len(self.parts)):
            def make(p=p):
                ref = self.block(p, turn)
                return self.parts[p][1] if turn == 0 else ref, ref, "core", 1 - self.at["core"]

            self.sends.start((self.name, 3, p, turn), make)

    def plane_steps(self):
        def first():
            for put in self.puts():
                put.start()
            self.send(2, lambda p: (self.parts[p][0], self.in_plane(p)))

        def second():
            for put in self.puts():
                put.wait()
            self.arrived(2, 1, 3, 2)

            def row(p):
                ref = self.parts[p][1].at[self.at[self.parts[p][3][1]]]
                return ref, ref

            self.send(1, row)

        return [first, second, lambda: self.arrived(1, 1, 3, 2)]

    def whole_steps(self):
        def first():
            for put in self.last_puts():
                put.start()
            self.send(0, lambda p: (self.parts[p][1], self.block(p, 0)))
            self.across(0)

        def more():
            self.arrived(0, 1)
            self.across(3)
            self.arrived(0, 3)
            self.across(1)

        def rest():
            self.arrived(0, 2)
            self.across(2)

        def end():
            self.arrived(3, 0, 3, 1, 2)
            for put in self.last_puts():
                put.wait()

        return [first, more, rest, end]


class SmallSum:
    def __init__(self, name, at, sends, x, core_in, slots):
        self.name, self.at, self.sends, self.x, self.core_in, self.slots = name, at, sends, x, core_in, slots

    def begin(self):
        for p in range(PARTS):
            self.sends.start((self.name, 3, p, 0), lambda p=p: (
                self.x.at[pl.ds(16 * p, 16)], self.core_in.at[p], "core", 1 - self.at["core"]))

    def total(self, p, s):
        if s == 0:
            self.sends.arrived((self.name, 3, p, 0))
            return self.x[16 * p : 16 * p + 16].astype(F32) + self.core_in[p].astype(F32)
        for turn in (1, 3, 2):
            self.sends.arrived((self.name, s - 1, p, turn))
        slots = self.slots.at[p, s - 1]
        return slots[0].astype(F32) + slots[1].astype(F32) + slots[2].astype(F32) + slots[3].astype(F32)

    def stage(self, s):
        for p in range(PARTS):
            self.slots[p, s, self.at[ORDERS[p][s]]] = self.total(p, s).astype(BF)
            for turn in (2, 1, 3):
                def make(p=p, turn=turn):
                    slot = self.slots.at[p, s, self.at[ORDERS[p][s]]]
                    return slot, slot, ORDERS[p][s], (self.at[ORDERS[p][s]] + turn) % 4

                self.sends.start((self.name, s, p, turn), make)

    def steps(self, out):
        def end():
            for p in range(PARTS):
                out[16 * p : 16 * p + 16] = self.total(p, 3).astype(BF)

        return [self.begin, lambda: self.stage(0), lambda: self.stage(1), lambda: self.stage(2), end]


def steps_in(i, *table):
    for turn, *steps in table:
        @pl.when(i == turn)
        def run():
            for step in steps:
                step()


D = 768
HALF = 384
HIDDEN = 1536
TILE = 128
TAPW = 128
PADDED = LEN + 16
SHARED_ROWS = 6144
VMEM_BYTES = 60 << 20
EARLY = 3072
POINT_AT, TAPS_AT, SMALL_AT = EARLY + 1536, EARLY + 2304, EARLY + 2368
SMALL_DEPTH, SMALL_FFN, SMALL_BIAS, SMALL_SEG, SMALL = 0, 18, 36, 43, 48


class Params(NamedTuple):
    hidden: jax.Array
    cotangent: jax.Array
    lengths: jax.Array
    split_at: jax.Array
    seg_table: jax.Array
    w_query: jax.Array
    b_query: jax.Array
    w_key: jax.Array
    w_value: jax.Array
    b_value: jax.Array
    w_depth: jax.Array
    w_point: jax.Array
    b_keyconv: jax.Array
    w_kernel: jax.Array
    b_kernel: jax.Array
    w_conv: jax.Array
    b_conv: jax.Array
    w_out: jax.Array
    b_out: jax.Array
    first_gain: jax.Array
    first_shift: jax.Array
    w_up: jax.Array
    b_up: jax.Array
    down_weight: jax.Array
    b_down: jax.Array
    second_gain: jax.Array
    second_shift: jax.Array


KEPT_SHAPES = (((LEN, D), BF), ((LEN, HALF), F32), ((LEN, HALF), BF), ((LEN, HALF), BF), ((LEN, D), BF),
               ((LEN, HALF), F32), ((PADDED, KERNEL * TAPW), F32), ((PADDED, HALF), F32), ((LEN, D), BF),
               ((LEN, D), F32))


def dims(lhs, rhs):
    return (((lhs,), (rhs,)), ((), ()))


def dot(a, b):
    return lax.dot_general(a, b, dims(1, 0), preferred_element_type=F32)


def dot_nt(a, b):
    return lax.dot_general(a, b, dims(1, 1), preferred_element_type=F32)


def dot_tn(a, b):
    return lax.dot_general(a, b, dims(0, 0), preferred_element_type=F32)


def tile_rows(i, n=TILE, start=0):
    return pl.ds(pl.multiple_of(i * n + start, 8 if start % 16 else 16), n)


def lanes_at(start, n=128):
    return pl.ds(pl.multiple_of(start, 128), n)


def rows_iota(n, width=1):
    return lax.broadcasted_iota(jnp.int32, (n, width), 0)


class Moves:
    def __init__(self, sems):
        self.sems, self.all = sems, []

    def start(self, src, dst):
        copy = pltpu.make_async_copy(src, dst, self.sems.at[len(self.all)])
        copy.start()
        self.all.append(copy)
        return copy

    def start_cat(self, layer, matrices, w_cat):
        return [self.start(ref.at[layer], w_cat.at[:, pl.ds(n * HALF, HALF)]) for n, ref in enumerate(matrices)]


def wait_all(copies):
    for copy in copies:
        copy.wait()


def my_row():
    row = lax.axis_index("grp")
    for name, size in zip(CH, (4, 4, 2, 2)):
        row = row * size + lax.axis_index(name)
    return row


def widen_matrix():
    lane = np.arange(HALF)[None, :] // HEAD
    return (np.arange(TAPW)[:, None] == lane).astype(ml_dtypes.bfloat16)


def tap_matrix():
    out = np.zeros((TAPW, KERNEL * TAPW), np.float32)
    for h in range(HEADS):
        for j in range(KERNEL):
            out[h * KERNEL + j, j * TAPW + h] = 1.0
    return out.astype(ml_dtypes.bfloat16)


def norm_stats(residual):
    mean = jnp.mean(residual, axis=-1, keepdims=True)
    center = residual - mean
    scale = lax.rsqrt(jnp.mean(center * center, axis=-1, keepdims=True) + EPSILON)
    return center * scale, scale


def norm_grad(gy, hat, scale, gain):
    d_hat = gy * gain
    mean_one = jnp.mean(d_hat, axis=-1, keepdims=True)
    mean_two = jnp.mean(d_hat * hat, axis=-1, keepdims=True)
    return scale * (d_hat - mean_one - hat * mean_two)


def gelu_both(pre):
    base = 1.0 + (0.3275911 * 0.7071067811865476) * jnp.abs(pre)
    t = pl.reciprocal(base, approx=True)
    t = t * (2.0 - base * t)
    poly = t * (0.127414796 + t * (-0.142248368 + t * (0.7107068705 + t * (-0.7265760135 + t * 0.5307027145))))
    bell = jnp.exp2((-0.5 * 1.4426950408889634) * (pre * pre))
    tail = poly * bell
    cdf = jnp.where(pre >= 0, 1.0 - tail, tail)
    return pre * cdf, cdf + pre * (bell * 0.3989422804014327)


def moved(window, start, n):
    size = window.shape[0]
    return pltpu.roll(window, (size - start) % size, 0)[:n]


def masked(scores, start, length):
    if start + scores.shape[0] <= 259:
        return scores
    return jnp.where(rows_iota(*scores.shape) + start < length, scores, MASK_VALUE)


def far():
    return pl.BlockSpec(memory_space=pl.ANY)


def whole():
    return pl.BlockSpec(memory_space=pltpu.VMEM)


def scalars():
    return pl.BlockSpec(memory_space=pltpu.SMEM)


def dma(n):
    return pltpu.SemaphoreType.DMA((n,))


def shape(dims, dtype):
    return jax.ShapeDtypeStruct(dims, dtype)


def block_shape(rows, lanes=LANES):
    return shape((PARTS, 2, 4, 4, 4, rows, lanes), BF)


def call(kernel, ins, outs, scratch, name, **comm):
    return pl.pallas_call(
        kernel,
        out_shape=[out for out, _ in outs],
        in_specs=[place for _, place in ins],
        out_specs=[place for _, place in outs],
        scratch_shapes=scratch,
        compiler_params=pltpu.CompilerParams(vmem_limit_bytes=VMEM_BYTES, **comm),
        name=name,
    )(*[array for array, _ in ins])


def vmem(*shapes):
    return [pltpu.VMEM(*s) for s in shapes]


class Points(dict):
    def at(self, point):
        for step in self.get(point, ()):
            step()

    def turn(self, point, i):
        for (name, turn), steps in [(key, s) for key, s in self.items() if isinstance(key, tuple)]:
            if name == point:
                steps_in(i, (turn, *steps))


def remote(number):
    return {"collective_id": number, "has_side_effects": True}


def tap_weights(layer, w_kernel, rows):
    rows[...] = jnp.zeros_like(rows)
    for n in range(HEADS * KERNEL):
        rows[n : n + 1, :] = w_kernel[n].astype(F32)[layer : layer + 1, :]


def clear_edges(*refs):
    for ref in refs:
        ref[pl.ds(0, 8), :] = jnp.zeros((8, ref.shape[1]), F32)
        ref[pl.ds(LEN + 8, 8), :] = jnp.zeros((8, ref.shape[1]), F32)


ENTER, DEPTH, ATTEND, END, UNPACK, FEED, BACK, GRAD, OUT, KEY, TAPS, CAT, LEAVE = range(13)

FORWARD_WEIGHTS = 14
FA_SCRATCH = [((LEN, D), BF), ((D, 4 * HALF), BF), ((D, HALF), BF), ((D, D), BF), ((PADDED, D), F32),
              ((LEN, HALF), BF), ((LEN, HALF), BF), ((TAPW, HALF), F32), ((HALF, KERNEL * TAPW), BF),
              ((8, KERNEL * TAPW), F32)]


def attention_forward_body(layer, length, split, x_in, seg, weights, x_all, resid, kept_out, log_total, points, *refs):
    first = layer == 0
    (w_query, w_key, w_value, w_conv, w_point, w_out, w_depth, w_kernel, b_query, b_value, b_conv, b_keyconv, b_kernel,
     b_out, widen, spread) = weights
    kept, refs = refs[:9], refs[9:]
    x_low, query, key_low, value_low, depth_low, key_conv, kernels, conv_pad, joined = kept
    hidden, w_cat, point, out_w, x_pad, query_low, mixed_low, tap_rows, taps_w, tap_bias, sems = refs
    one = slice(layer, layer + 1)
    moves = Moves(sems)
    load_x = [moves.start(x_in, hidden)] if first else []
    load_cat = moves.start_cat(layer, (w_query, w_key, w_value, w_conv), w_cat)
    load_rest = [moves.start(w_point.at[layer], point), moves.start(w_out.at[layer], out_w)]
    clear_edges(x_pad, conv_pad, kernels)
    tap_weights(layer, w_kernel, tap_rows)
    for c in range(0, KERNEL * TAPW, 384):
        taps_w[:, c : c + 384] = dot_tn(tap_rows[...].astype(BF), spread[:, c : c + 384]).astype(BF)
    tap_bias[...] = jnp.zeros_like(tap_bias)
    tap_bias[0:1, 0 : HEADS * KERNEL] = b_kernel[one, :]
    left, bias = tap_bias[:, :TAPW], jnp.zeros((8, KERNEL * TAPW), F32)
    for _ in range(3):
        bias += dot(left.astype(BF), spread[...])
        left = left - left.astype(BF).astype(F32)
    tap_bias[...] = bias

    wait_all(load_x)
    points.at(ENTER)

    @pl.loop(0, LEN // TILE)
    def enter(i):
        rows = tile_rows(i)
        if first:
            place = rows_iota(TILE) + i * TILE
            x = hidden[rows, :].astype(F32) + jnp.where(place > split, seg[1:2, :], seg[0:1, :])
            x = x * (place < length).astype(F32)
            x_all[rows, :] = x
        else:
            x = x_all[rows, :]
        low = x.astype(BF)
        x_low[rows, :] = low
        x_pad[tile_rows(i, TILE, 8), :] = low.astype(F32)

    wait_all(load_cat)
    for n in range(6):
        proj = dot(x_low[...], w_cat[:, n * 256 : n * 256 + 256])
        for h in range(2):
            which, c = (2 * n + h) // 3, (2 * n + h) % 3 * 128
            cols = slice(c, c + 128)
            part = proj[:, h * 128 : h * 128 + 128]
            if which == 0:
                part += b_query[one, cols]
                query[:, cols] = part
                query_low[:, cols] = part.astype(BF)
            elif which == 1:
                key_low[:, cols] = part.astype(BF)
            elif which == 2:
                value_low[:, cols] = (part + b_value[one, cols]).astype(BF)
            else:
                conv_pad[pl.ds(8, LEN), cols] = part + b_conv[one, cols]
    stores = [moves.start(kept[n], kept_out[n]) for n in (0, 1, 2, 3, 7)]
    points.at(OUT)

    @pl.loop(0, LEN // TILE)
    def depth(i):
        rows = tile_rows(i)
        around = pl.ds(pl.multiple_of(i * TILE, TILE), TILE + 16)
        for c in range(0, D, 128):
            cols = slice(c, c + 128)
            window = x_pad[around, cols]
            total = jnp.zeros((TILE, 128), F32)
            for j in range(KERNEL):
                total += w_depth[j, one, cols].astype(F32) * moved(window, 4 + j, TILE)
            depth_low[rows, cols] = total.astype(BF)

    points.at(DEPTH)
    wait_all(load_rest)
    for c, n in ((0, 256), (256, 128)):
        cols = slice(c, c + n)
        key = dot(depth_low[...], point[:, cols]) + b_keyconv[one, cols]
        key_conv[:, cols] = key
        mixed_low[:, cols] = (key * query[:, cols]).astype(BF)
    for c in range(0, KERNEL * TAPW, 384):
        cols = slice(c, c + 384)
        kernels[pl.ds(8, LEN), cols] = dot(mixed_low[...], taps_w[:, cols]) + tap_bias[0:1, cols]
    stores += [moves.start(kept[n], kept_out[n]) for n in (4, 5)]

    @pl.loop(0, LEN // 256)
    def convolve(i):
        rows = tile_rows(i, 256)
        around = pl.ds(pl.multiple_of(i * 256, 256), 256 + 16)
        padded = tile_rows(i, 256, 8)
        taps = [kernels[padded, j * TAPW : (j + 1) * TAPW] for j in range(KERNEL)]
        peak = functools.reduce(jnp.maximum, taps)
        taps = [jnp.exp(t - peak) for t in taps]
        share = 1.0 / sum(taps)
        window = conv_pad[around, :]
        mix = jnp.zeros((256, HALF), F32)
        for j in range(KERNEL):
            tap = taps[j] * share
            kernels[padded, j * TAPW : (j + 1) * TAPW] = tap
            mix += dot(tap.astype(BF), widen[...]) * moved(window, 4 + j, 256)
        joined[rows, HALF:] = mix.astype(BF)

    stores += [moves.start(kept[6], kept_out[6])]

    @pl.loop(0, HEADS // 2)
    def attend(pair):
        points.turn(ATTEND, pair)
        lanes = lanes_at(pair * 128)
        keys = key_low[:, lanes] * jnp.asarray(SCORE_SCALE, BF)
        side = lax.broadcasted_iota(jnp.int32, (LEN, 128), 1) // HEAD
        values = jnp.transpose(value_low[:, lanes].astype(F32)).astype(BF)
        queries = query_low[:, lanes]
        context = []
        for head in range(2):
            mine = jnp.where(side == head, keys, jnp.zeros_like(keys))
            scores = [masked(dot_nt(mine[c : c + 128], queries), c, length) for c in range(0, LEN, 128)]
            peak = functools.reduce(jnp.maximum, [jnp.max(s, axis=0, keepdims=True) for s in scores])
            probs = [jnp.exp(s - peak) for s in scores]
            total = sum(jnp.sum(p, axis=0, keepdims=True) for p in probs)
            log_total[pair * 2 + head] = peak + jnp.log(total)
            share = 1.0 / total
            probs = jnp.concatenate([(p * share).astype(BF) for p in probs], axis=0)
            context.append(dot(values[head * HEAD : (head + 1) * HEAD, :], probs))
        joined[:, lanes] = jnp.transpose(jnp.concatenate(context, axis=0)).astype(BF)

    stores += [moves.start(kept[8], kept_out[8])]
    points.at(ATTEND)
    for c in range(0, D, 256):
        cols = slice(c, c + 256)
        resid[:, cols] = x_all[:, cols] + dot(joined[...], out_w[:, cols]) + b_out[one, cols]
    points.at(END)
    wait_all(stores)


PLANES = (PARTS, 4, 4, 16, LANES)


def part_block(ref, p, core, x, y, z):
    if p == 0:
        return ref.at[0, core, x, y, z]
    if p == 1:
        return ref.at[1, core, y, z, x]
    return ref.at[2, core, z, x, y]


FFN_SHAPES = [((2 * HIDDEN, HALF), BF)] * 2 + [((LEN, 2 * HIDDEN), BF)] * 2 + [((LEN, D), F32)]
FF_SCRATCH = [((LEN, D), F32), ((LEN, D), BF), ((2, 64, TAPW), F32), ((1, 2 * HIDDEN), F32)]


def ffn_forward_body(layer, length, gathered, bias_all, norms, resid, x_next, outs, ffn, points, *refs):
    first_gain, first_shift, b_down, second_gain, second_shift = norms
    up, down, acted, slope, resid_two = ffn
    normed_rows, low, bias_rows, bias, sems, block_sems = refs
    one = slice(layer, layer + 1)
    moves = Moves(sems)

    @pl.loop(0, LEN // TILE)
    def enter(i):
        rows = tile_rows(i)
        hat, _ = norm_stats(resid[rows, :])
        normed = hat * first_gain[one, :] + first_shift[one, :]
        normed_rows[rows, :] = normed
        low[rows, :] = normed.astype(BF)

    points.at(ENTER)

    @pl.loop(0, 64)
    def unpack(chip):
        z, y, x = (chip // 32) * 2 + chip % 2, (chip // 8) % 4, (chip // 2) % 4
        ups, downs = [], []
        for core in range(2):
            piece = jnp.concatenate(
                [part_block(gathered, p, core, x, y, z)[...].astype(F32) for p in range(PARTS)], axis=0)
            ups.append(piece[:24])
            downs.append(piece[24:])
            bias_rows[core, pl.ds(chip, 1), :] = bias_all[core, x, y, z].astype(F32)[one, :]
        rows = tile_rows(chip, 48)
        up[rows, :] = jnp.concatenate(ups, axis=0).astype(BF)
        down[rows, :] = jnp.concatenate(downs, axis=0).astype(BF)

    stores = [moves.start(up, outs[0]), moves.start(down, outs[1])] if outs else []
    points.at(UNPACK)
    for c in range(0, 2 * HIDDEN, 512):
        spot = lax.broadcasted_iota(jnp.int32, (64, 512), 1) + c
        slot = (lax.broadcasted_iota(jnp.int32, (TAPW, 512), 1) + c) % 24
        repeat = (slot == rows_iota(TAPW, 512)).astype(F32).astype(BF)
        total = jnp.zeros((1, 512), F32)
        for core in range(2):
            spread = dot(bias_rows[core].astype(BF), repeat)
            mine = spot // 24 == 2 * rows_iota(64, 512) + core
            total += jnp.sum(jnp.where(mine, spread, 0.0), axis=0, keepdims=True)
        bias[:, c : c + 512] = total

    def block_stores(n):
        cols = lanes_at(n * 512, 512)
        return [pltpu.make_async_copy(src.at[:, cols], out.at[:, cols], block_sems.at[2 * n + m])
                for m, (src, out) in enumerate(((acted, outs[2]), (slope, outs[3])))]

    for g in range(2):
        @pl.loop(0, HIDDEN // 512)
        def feed(k):
            at = g * HIDDEN + k * 512
            for c in range(0, 512, 128):
                hidden = lanes_at(at + c)
                pre = dot_nt(low[:, g * HALF : (g + 1) * HALF], up[hidden, :]) + bias[:, hidden]
                value, grad = gelu_both(pre)
                acted[:, hidden] = value.astype(BF)
                slope[:, hidden] = grad.astype(BF)

            if outs:
                for store in block_stores(g * (HIDDEN // 512) + k):
                    store.start()

        points.at(FEED + 100 * g)

    @pl.loop(0, LEN // 256)
    def leave(i):
        rows = tile_rows(i, 256)
        out = []
        for g in range(2):
            hidden = slice(g * HIDDEN, (g + 1) * HIDDEN)
            out.append(dot(acted[rows, hidden], down[hidden, :]).astype(BF).astype(F32))
        two = normed_rows[rows, :] + jnp.concatenate(out, axis=1) + b_down[one, :]
        resid_two[rows, :] = two
        hat, _ = norm_stats(two)
        valid = (rows_iota(256) + i * 256 < length).astype(F32)
        x_next[rows, :] = (hat * second_gain[one, :] + second_shift[one, :]) * valid

    points.at(END)
    if outs:
        stores.append(moves.start(resid_two, outs[4]))
        for n in range(2 * HIDDEN // 512):
            wait_all(block_stores(n))
    wait_all(stores)


BF_SCRATCH = [(block_shape(16).shape, BF), ((LEN, D), F32), ((LEN, 2 * HIDDEN), BF), ((LEN, D), BF),
              ((LEN, D), BF)]


def ffn_backward_body(layer, length, norms, gy, ffn, resid, d_resid, outs, waits, points, *refs):
    first_gain, first_shift, _, second_gain, _ = norms
    up, down, acted, slope, resid_two = ffn
    d_resid_out, grads_out, small = outs
    grads, d_two, d_pre, d_group, normed_low, sems = refs
    one = slice(layer, layer + 1)
    moves = Moves(sems)
    small[...] = jnp.zeros_like(small)

    def note(slot, value):
        total = jnp.sum(value, axis=0, keepdims=True)
        small[slot : slot + 1, :] += total[:, :HALF]
        small[slot + 1 : slot + 2, :] += total[:, HALF:]

    wait_all(waits[0])

    @pl.loop(0, LEN // TILE)
    def enter(i):
        rows = tile_rows(i)
        valid = (rows_iota(TILE) + i * TILE < length).astype(F32)
        grad = gy[rows, :].astype(F32) * valid
        hat, scale = norm_stats(resid_two[rows, :])
        note(0, grad * hat)
        note(2, grad)
        two = norm_grad(grad, hat, scale, second_gain[one, :])
        note(4, two)
        d_two[rows, :] = two
        d_group[rows, :] = two.astype(BF)
        hat, _ = norm_stats(resid[rows, :])
        normed_low[rows, :] = (hat * first_gain[one, :] + first_shift[one, :]).astype(BF)

    points.at(ENTER)
    wait_all(waits[1])
    for g in range(2):
        @pl.loop(0, HIDDEN // 256)
        def feed(k):
            hidden = pl.ds(pl.multiple_of(g * HIDDEN + k * 256, 256), 256)
            d_act = dot_nt(d_group[:, g * HALF : (g + 1) * HALF], down[hidden, :])
            d_pre[:, hidden] = (d_act * slope[:, hidden].astype(F32)).astype(BF)

        points.at(FEED + 100 * g)

    wait_all(waits[2])

    @pl.loop(0, LEN // 256)
    def back(i):
        rows = tile_rows(i, 256)
        got = []
        for g in range(2):
            hidden = slice(g * HIDDEN, (g + 1) * HIDDEN)
            got.append(dot(d_pre[rows, hidden], up[hidden, :]).astype(BF).astype(F32))
        d_normed = d_two[rows, :] + jnp.concatenate(got, axis=1)
        hat, scale = norm_stats(resid[rows, :])
        note(6, d_normed * hat)
        note(8, d_normed)
        d_resid[rows, :] = norm_grad(d_normed, hat, scale, first_gain[one, :])

    stores = [moves.start(d_resid, d_resid_out)] if d_resid_out is not None else []
    points.at(BACK)
    ones = jnp.ones((8, LEN), BF)
    for k in range(8):
        small[10 + k : 11 + k, :] = dot(ones, d_pre[:, k * HALF : (k + 1) * HALF])[0:1, :]

    for g in range(2):
        @pl.loop(0, 4)
        def grad(y):
            points.turn(GRAD + 100 * g, y)
            hidden = lanes_at(g * HIDDEN + y * HALF, HALF)
            cols = slice(g * HALF, (g + 1) * HALF)
            d_up = dot_tn(d_pre[:, hidden], normed_low[:, cols])
            d_down = dot_tn(acted[:, hidden], d_group[:, cols])
            for d in range(16):
                x, z, core = d // 4, g * 2 + (d // 2) % 2, d % 2
                piece = jnp.concatenate([d_up[24 * d : 24 * d + 24], d_down[24 * d : 24 * d + 24]], axis=0).astype(BF)
                for p in range(PARTS):
                    part_block(grads, p, core, x, y, z)[...] = piece[16 * p : 16 * p + 16]

        zs = pl.ds(2 * g, 2)
        for index in ((0, slice(None), slice(None), slice(None), zs), (1, slice(None), slice(None), zs),
                      (2, slice(None), zs)):
            stores.append(moves.start(grads.at[index], grads_out.at[index]))

    points.at(END)
    wait_all(stores)


BA_SCRATCH = [((D, 4 * HALF), BF), ((D, HALF), BF), ((D, D), BF), ((LEN, D), BF), ((LEN, 4 * HALF), BF), ((LEN, D), BF),
              ((LEN, HALF), BF), ((LEN, HALF), F32), ((PADDED, HALF), F32), ((PADDED, D), F32), ((SMALL, HALF), F32),
              ((LEN, TAPW), BF), ((TAPW, HALF), F32)]


def attention_backward_body(layer, length, split, d_resid, waits, kept_in, log_total, ffn_small, weights, shared, d_input,
                            small_out, points, *refs):
    first = layer == 0
    w_query, w_key, w_value, w_conv, w_point, w_out, w_depth, w_kernel, widen, spread = weights
    kept, refs = refs[:9], refs[9:]
    x_low, query, key_low, value_low, depth_low, key_conv, kernels, conv_pad, joined = kept
    (w_cat, point, out_w, d_proj, d_cat, d_join, query_low, d_att, mix_pad, depth_pad, small, d_tap, tap_rows,
     sems) = refs
    moves = Moves(sems)
    load_first = [*waits, moves.start(w_out.at[layer], out_w)]
    load = [moves.start(kept_in[n], kept[n]) for n in (8, 1, 2, 3, 6, 7, 5, 4, 0)]
    load_cat = moves.start_cat(layer, (w_query, w_key, w_value, w_conv), w_cat)
    load_point = moves.start(w_point.at[layer], point)
    clear_edges(mix_pad, depth_pad)
    small[...] = jnp.zeros_like(small)
    small[SMALL_FFN : SMALL_FFN + 18, :] = ffn_small[0:18, :]
    shared[SMALL_AT:, :] = jnp.zeros((SHARED_ROWS - SMALL_AT, HALF), BF)
    tap_weights(layer, w_kernel, tap_rows)

    def note(slot, value):
        total = jnp.sum(value, axis=0, keepdims=True)
        for n in range(total.shape[1] // HALF):
            small[slot + n : slot + n + 1, :] += total[:, n * HALF : (n + 1) * HALF]

    points.at(ENTER)
    wait_all(load_first)

    @pl.loop(0, LEN // TILE)
    def enter(i):
        rows = tile_rows(i)
        low = d_resid[rows, :].astype(BF)
        d_proj[rows, :] = low
        note(SMALL_BIAS + 5, low.astype(F32))

    for c in range(0, D, 256):
        d_join[:, c : c + 256] = dot_nt(d_proj[...], out_w[c : c + 256, :]).astype(BF)
    mix_pad[pl.ds(8, LEN), :] = d_join[:, HALF:].astype(F32)
    load[0].wait()

    @pl.loop(0, D // 256)
    def out_grad(c):
        part = dot_tn(joined[:, lanes_at(c * 256, 256)], d_proj[...])
        for n in range(2):
            shared[chunk(n * D + c * 256, 256), :] = part[:, n * HALF : (n + 1) * HALF].astype(BF)

    points.at(OUT)
    wait_all(load[1:4])
    query_low[...] = query[...].astype(BF)

    @pl.loop(0, HEADS // 2)
    def attend(pair):
        points.turn(ATTEND, pair)
        lanes = lanes_at(pair * 128)
        keys = key_low[:, lanes]
        values = value_low[:, lanes]
        scaled = keys * jnp.asarray(SCORE_SCALE, BF)
        keys_t = jnp.transpose(keys.astype(F32)).astype(BF)
        side = lax.broadcasted_iota(jnp.int32, (LEN, 128), 1) // HEAD
        nothing = jnp.zeros_like(keys)
        queries = query_low[:, lanes]
        d_context = d_join[:, lanes]
        d_queries, d_keys, d_values = [], [], []
        for head in range(2):
            key, value = jnp.where(side == head, scaled, nothing), jnp.where(side == head, values, nothing)
            total = log_total[pair * 2 + head]
            probs, weighted = [], []
            for c in range(0, LEN, 128):
                probs.append(jnp.exp(masked(dot_nt(key[c : c + 128], queries), c, length) - total))
                weighted.append(probs[-1] * dot_nt(value[c : c + 128], d_context))
            row_dot = sum(jnp.sum(w, axis=0, keepdims=True) for w in weighted)
            d_scores = jnp.concatenate([(w - p * row_dot).astype(BF) for w, p in zip(weighted, probs)], axis=0)
            probs = jnp.concatenate([p.astype(BF) for p in probs], axis=0)
            d_queries.append(dot(keys_t[head * HEAD : (head + 1) * HEAD, :], d_scores))
            d_keys.append(dot(d_scores, queries))
            d_values.append(dot(probs, d_context))
        d_att[:, lanes] = jnp.transpose(jnp.concatenate(d_queries, axis=0)) * SCORE_SCALE
        d_cat[:, lanes_at(HALF + pair * 128)] = (jnp.where(side == 0, d_keys[0], d_keys[1]) * SCORE_SCALE).astype(BF)
        d_cat[:, lanes_at(2 * HALF + pair * 128)] = jnp.where(side == 0, d_values[0], d_values[1]).astype(BF)

    wait_all(load[7:])

    @pl.loop(0, D // 256)
    def key_grad(c):
        low = x_low[:, lanes_at(c * 256, 256)]
        for n in range(2):
            part = dot_tn(low, d_cat[:, (n + 1) * HALF : (n + 2) * HALF])
            shared[chunk(1536 + n * D + c * 256, 256), :] = part.astype(BF)

    points.at(KEY)
    wait_all(load[4:7])

    @pl.loop(0, LEN // 256)
    def taps(i):
        points.turn(TAPS, i)
        rows = tile_rows(i, 256)
        around = pl.ds(pl.multiple_of(i * 256, 256), 256 + 16)
        padded = tile_rows(i, 256, 8)
        mix = mix_pad[padded, :]
        window = conv_pad[around, :]
        mix_window = mix_pad[around, :]
        d_kernel, d_conv = [], jnp.zeros((256, HALF), F32)
        dotted = jnp.zeros((256, TAPW), F32)
        for j in range(KERNEL):
            part = dot_nt((mix * moved(window, 4 + j, 256)).astype(BF), widen[...])
            d_kernel.append(part)
            dotted += part * kernels[padded, j * TAPW : (j + 1) * TAPW]
            share = moved(kernels[around, j * TAPW : (j + 1) * TAPW], 12 - j, 256)
            d_conv += dot(share.astype(BF), widen[...]) * moved(mix_window, 12 - j, 256)
        d_cat[rows, 3 * HALF :] = d_conv.astype(BF)
        wide = [kernels[padded, j * TAPW : (j + 1) * TAPW] * (d_kernel[j] - dotted) for j in range(KERNEL)]
        d_logit = dot_nt(jnp.concatenate(wide, axis=1).astype(BF), spread[...]).astype(BF)
        d_tap[rows, :] = d_logit
        d_mixed = dot(d_logit, tap_rows[...].astype(BF))
        q = query[rows, :]
        key = key_conv[rows, :]
        d_keyconv = (d_mixed * q).astype(BF)
        d_cat[rows, :HALF] = (d_att[rows, :] + d_mixed * key).astype(BF)
        note(SMALL_BIAS + 2, d_keyconv.astype(F32))
        cat = d_cat[rows, :].astype(F32)
        note(SMALL_BIAS, cat[:, :HALF])
        note(SMALL_BIAS + 1, cat[:, 2 * HALF : 3 * HALF])
        note(SMALL_BIAS + 3, cat[:, 3 * HALF :])
        small[SMALL_BIAS + 4 : SMALL_BIAS + 5, :TAPW] += jnp.sum(d_logit.astype(F32), axis=0, keepdims=True)
        d_join[rows, HALF:] = d_keyconv
        d_join[rows, :HALF] = (key * q).astype(BF)

    points.at(TAPS)
    shared[TAPS_AT : TAPS_AT + 64, :] = dot_tn(d_tap[...], d_join[:, :HALF])[:64].astype(BF)
    load_point.wait()
    for c in range(0, D, 256):
        depth_pad[pl.ds(8, LEN), c : c + 256] = dot_nt(d_join[:, HALF:], point[c : c + 256, :])

    @pl.loop(0, D // 256)
    def cat_grad(c):
        lanes = lanes_at(c * 256, 256)
        for n, k in enumerate((0, 3)):
            part = dot_tn(x_low[:, lanes], d_cat[:, k * HALF : (k + 1) * HALF])
            shared[chunk(EARLY + n * D + c * 256, 256), :] = part.astype(BF)
        part = dot_tn(depth_low[:, lanes], d_join[:, HALF:])
        shared[chunk(POINT_AT + c * 256, 256), :] = part.astype(BF)

    points.at(CAT)
    wait_all(load_cat)
    for n in range(3):
        cols = slice(n * 256, n * 256 + 256)
        d_input[:, cols] = d_resid[:, cols] + dot_nt(d_cat[...], w_cat[cols, :])
        points.at(LEAVE + 100 * n)

        for half in range(2):
            c = n * 256 + half * 128
            cols, slot = slice(c, c + 128), SMALL_DEPTH + 9 * (c // HALF)
            lanes = slice(c % HALF, c % HALF + 128)

            @pl.loop(0, LEN // TILE)
            def leave(i):
                rows = tile_rows(i)
                window = depth_pad[pl.ds(pl.multiple_of(i * TILE, TILE), TILE + 16), cols]
                low = x_low[rows, cols].astype(F32)
                total = d_input[rows, cols]
                for j in range(KERNEL):
                    part = moved(window, 12 - j, TILE)
                    total += w_depth[j, layer : layer + 1, cols].astype(F32) * part
                    small[slot + j : slot + j + 1, lanes] += jnp.sum(low * part, axis=0, keepdims=True)
                d_input[rows, cols] = total

    if first:
        @pl.loop(0, LEN // TILE)
        def seg_grad(i):
            rows = tile_rows(i)
            place = rows_iota(TILE) + i * TILE
            grad = d_input[rows, :] * (place < length).astype(F32)
            later = (place > split).astype(F32)
            note(SMALL_SEG + 2, grad * later)
            note(SMALL_SEG, grad * (1.0 - later))
            d_input[rows, :] = grad

    small_out[...] = small[...].astype(BF)
    points.at(END)


def forward_kernel(*refs):
    (lengths, splits, hidden, seg, cotangent), weights, norms = refs[:5], refs[5:21], refs[21:26]
    (w_up, down_weight, b_up), refs = refs[26:29], refs[29:]
    kept_out = refs[:10], refs[10:19]
    log_totals, ffn_out, refs = refs[19:21], refs[21:26], refs[26:]
    output, d_resid_out, grads_out, small, refs = *refs[:4], refs[4:]
    (x_all, resid, gathered_0, gathered_1, planes_0, planes_1, bias_all, bias_plane, pieces, bias_wide, bias_piece, sems,
     own_sems, send_sems, recv_sems) = refs
    at = here()
    greet(at)
    for layer in range(LAYERS):
        rows = jnp.concatenate([w_up[layer].astype(F32), down_weight[layer].astype(F32)], axis=0).astype(BF)
        for p in range(PARTS):
            pieces[layer * PARTS + p] = rows[16 * p : 16 * p + 16]
    bias_wide[...] = jnp.zeros_like(bias_wide)
    bias_wide[0:LAYERS, 0 : b_up.shape[1]] = b_up[...].astype(F32)
    bias_piece[...] = bias_wide[...].astype(BF)
    length, split = lengths[my_row()], splits[my_row()]
    moves = Moves(sems)
    sends = Sends(send_sems, recv_sems)
    gathered, planes = (gathered_0, gathered_1), (planes_0, planes_1)
    plane, whole_of = [], []
    for layer in range(LAYERS):
        parts = [(pieces.at[layer * PARTS + p], planes[layer].at[p], gathered[layer].at[p], ORDERS[p])
                 for p in range(PARTS)]
        if layer == 0:
            parts.append((bias_piece, bias_plane, bias_all, ORDERS[0]))
        gather = Gather(layer, at, sends, parts, own_sems.at[pl.ds(4 * layer, 4)])
        plane.append(gather.plane_steps())
        whole_of.append(gather.whole_steps())
    (a0, a1, a2), (b0, b1, b2, b3) = plane[0], whole_of[0]
    (c0, c1, c2), (d0, d1, d2, d3) = plane[1], whole_of[1]
    met()
    a0()
    points = (
        (Points({ENTER: (a1,), OUT: (a2, b0), ATTEND: (b1,), END: (b2,)}),
         Points({ENTER: (b3,), UNPACK: (c0,), FEED: (c1,), FEED + 100: (c2, d0)})),
        (Points({(ATTEND, 1): (d1,), (ATTEND, 2): (d2,)}), Points({ENTER: (d3,)})),
    )
    stores = []
    for layer in range(LAYERS):
        pl.run_scoped(
            lambda *s: attention_forward_body(layer, length, split, hidden, seg, weights, x_all, resid, kept_out[layer],
                                              log_totals[layer], points[layer][0], *s),
            *vmem(*KEPT_SHAPES[:9], *FA_SCRATCH), dma(24))
        if layer == 0:
            stores.append(moves.start(resid, kept_out[0][9]))

            def feed(*s):
                ffn_forward_body(0, length, gathered_0, bias_all, norms, resid, x_all, ffn_out, s[:5], points[0][1], *s[5:])

            pl.run_scoped(feed, *vmem(*FFN_SHAPES, *FF_SCRATCH), dma(4), dma(12))
            wait_all(stores)
        else:
            def feed_both(gy, *s):
                ffn, s = s[:5], s[5:]
                load = moves.start(cotangent, gy)
                n = len(FF_SCRATCH) + 2
                ffn_forward_body(1, length, gathered_1, bias_all, norms, resid, x_all, None, ffn, points[1][1], *s[:n])
                stores.append(moves.start(x_all, output))
                ffn_backward_body(1, length, norms, gy, ffn, resid, s[n], (d_resid_out, grads_out, small), ([load], [], []),
                                  Points(), *s[n + 1 :])
                stores[-1].wait()

            pl.run_scoped(feed_both, *vmem(((LEN, D), BF), *FFN_SHAPES, *FF_SCRATCH), dma(1), dma(1),
                          *vmem(((LEN, D), F32), *BF_SCRATCH), dma(16))
    sends.finish()


def projections(w):
    return [(m, far()) for m in (w.w_query, w.w_key, w.w_value, w.w_conv, w.w_point, w.w_out)]


def norm_params(w):
    return [(m, whole()) for m in (w.first_gain, w.first_shift, w.b_down, w.second_gain, w.second_shift)]


def forward(w):
    ins = [(w.lengths, scalars()), (w.split_at, scalars()), (w.hidden, far()), (w.seg_table, whole()),
           (w.cotangent, far())] + projections(w)
    ins += [(m, whole()) for m in (w.w_depth, w.w_kernel, w.b_query, w.b_value, w.b_conv, w.b_keyconv, w.b_kernel,
                                   w.b_out, widen_matrix(), tap_matrix())] + norm_params(w)
    ins += [(m, whole()) for m in (jnp.swapaxes(w.w_up[:, 0], 1, 2), w.down_weight[:, 0], w.b_up[:, 0])]
    outs = [(shape(*s), far()) for s in KEPT_SHAPES + KEPT_SHAPES[:9]]
    outs += [(shape((HEADS, 1, LEN), F32), whole())] * 2 + [(shape(*s), far()) for s in FFN_SHAPES]
    outs += [(shape((LEN, D), F32), far())] * 2 + [(block_shape(16), far()), (shape((32, HALF), F32), whole())]
    plane, gathered = ((PARTS, 4, 4, 16, LANES), BF), (block_shape(16).shape, BF)
    scratch = vmem(((LEN, D), F32), ((LEN, D), F32), gathered, gathered, plane, plane, ((2, 4, 4, 4, 16, TAPW), BF),
                   ((4, 4, 16, TAPW), BF), ((LAYERS * PARTS, 16, LANES), BF), ((16, TAPW), F32), ((16, TAPW), BF))
    scratch += [dma(4), dma(8), dma(112), dma(112)]
    outs = call(forward_kernel, ins, outs, scratch, "forward", **remote(1))
    return (*outs[:10], outs[19]), (*outs[10:19], outs[20]), outs[21:26], outs[26:]


def first_sums(at, sends, shared, mids, scratch):
    return [FirstSum(n, at, sends, shared.at[pl.ds(n * EARLY, EARLY)], mids[n], scratch[4 * n : 4 * n + 4]).steps()
            for n in range(2)]


def second_sums(name, at, sends, mids, gathered, scratch):
    return [SecondSum(name + n, at, sends, mids[n], gathered[n], scratch[4 * n : 4 * n + 4]).steps() for n in range(2)]


def backward_ins(kept, w):
    ins = [(w.lengths, scalars()), (w.split_at, scalars())] + [(m, far()) for m in kept[:9]]
    ins += [(kept[-1], whole())] + projections(w)
    return ins + [(m, whole()) for m in (w.w_depth, w.w_kernel, widen_matrix(), tap_matrix())]


GROUP, MIDS, SMALLS = shape((EARLY, HALF), BF), shape((PARTS, EARLY // 24, LANES), BF), shape((SMALL, HALF), BF)
OWN = shape((PARTS, 16, LANES), BF)


def middle_kernel(*refs):
    (lengths, splits), kept_in, log_total, refs = refs[:2], refs[2:11], refs[11], refs[12:]
    weights, ffn_small, d_resid_in, ffn_grads, refs = refs[:10], refs[10], refs[11], refs[12], refs[13:]
    d_input_out, own, early_mid, late_mid, small, refs = *refs[:5], refs[5:]
    d_input, shared, d_resid, refs = *refs[:3], refs[3:]
    sum_refs, scatter_refs, (sems, send_sems, recv_sems) = refs[:8], refs[8:14], refs[14:]
    at = here()
    greet(at)
    length, split = lengths[my_row()], splits[my_row()]
    moves = Moves(sems)
    load = moves.start(d_resid_in, d_resid)
    sends = Sends(send_sems, recv_sems)
    scatter = Scatter(5, at, sends, ffn_grads, scatter_refs)
    f = scatter.steps()
    e, l = first_sums(at, sends, shared, (early_mid, late_mid), sum_refs)
    met()
    points = Points({ENTER: (f[0],), (ATTEND, 2): (f[1], f[2]), KEY: (f[3], f[4], e[0]), TAPS: (e[1], e[2]),
                     CAT: (e[3], e[4], f[5], l[0]), LEAVE: (l[1], l[2]), LEAVE + 100: (l[3], l[4]),
                     LEAVE + 200: (f[6],), END: (e[5],)})
    pl.run_scoped(
        lambda *refs: attention_backward_body(1, length, split, d_resid, [load], kept_in, log_total, ffn_small, weights,
                                              shared, d_input, small, points, *refs),
        *vmem(*KEPT_SHAPES[:9], *BA_SCRATCH), dma(24))
    store = moves.start(d_input, d_input_out)
    f[7]()
    for p in range(PARTS):
        own[p] = scatter.own(p)[...]
    l[5]()
    sends.finish()
    store.wait()


def middle(d_resid, kept, ffn_small, ffn_grads, w):
    ins = backward_ins(kept, w) + [(ffn_small, whole()), (d_resid, far()), (ffn_grads, far())]
    outs = [(shape((LEN, D), F32), far())] + [(m, whole()) for m in (OWN, MIDS, MIDS, SMALLS)]
    scratch = vmem(((LEN, D), F32), ((SHARED_ROWS, HALF), BF), ((LEN, D), F32))
    scratch += first_scratch(32) * 2 + scatter_scratch(16)
    return call(middle_kernel, ins, outs, scratch + [dma(2), dma(96), dma(96)], "middle", **remote(2))


def last_kernel(*refs):
    (lengths, splits), kept_in, log_total, refs = refs[:2], refs[2:11], refs[11], refs[12:]
    weights, gy_in, ffn_in, resid_in, norms, refs = refs[:10], refs[10], refs[11:16], refs[16], refs[17:22], refs[22:]
    above_mids, above_small, refs = refs[:2], refs[2], refs[3:]
    d_input_out, grads_out, ffn_small_out, own, refs = *refs[:4], refs[4:]
    above_all, above_small_all, mine_all, small_all, refs = refs[:2], refs[2], refs[3:5], refs[5], refs[6:]
    d_input, d_resid, shared, mids, refs = *refs[:3], refs[3:5], refs[5:]
    sum_refs, second_refs, above_refs, refs = refs[:8], refs[8:16], refs[16:24], refs[24:]
    small, small_refs, above_small_refs, scatter_refs, refs = refs[0], refs[1:3], refs[3:5], refs[5:11], refs[11:]
    sems, send_sems, recv_sems = refs
    at = here()
    greet(at)
    length, split = lengths[my_row()], splits[my_row()]
    moves = Moves(sems)
    sends = Sends(send_sems, recv_sems)
    scatter = Scatter(7, at, sends, grads_out, scatter_refs)
    f = scatter.steps()
    a, b = second_sums(2, at, sends, above_mids, above_all, above_refs)
    c = SmallSum(4, at, sends, above_small, *above_small_refs).steps(above_small_all)
    e, l = first_sums(at, sends, shared, mids, sum_refs)
    more = second_sums(5, at, sends, mids, mine_all, second_refs)
    e, l = e + more[0], l + more[1]
    s = SmallSum(8, at, sends, small, *small_refs).steps(small_all)
    points = Points({FEED + 100: (a[1], b[1]), (GRAD, 1): (a[2], b[2], c[1]), END: (a[3], b[3])})

    def feed(gy, up, down, acted, slope, two, resid, load_sems, *refs):
        loads = Moves(load_sems)
        pairs = ((gy_in, gy), (ffn_in[4], two), (resid_in, resid), (ffn_in[3], slope), (ffn_in[1], down), (ffn_in[0], up),
                 (ffn_in[2], acted))
        loads = [loads.start(*pair) for pair in pairs]
        met()
        for step in (a[0], b[0], c[0]):
            step()
        ffn_backward_body(0, length, norms, gy, (up, down, acted, slope, two), resid, d_resid,
                          (None, grads_out, ffn_small_out), (loads[:3], loads[3:5], loads[5:]), points, *refs)

    pl.run_scoped(feed, *vmem(((LEN, D), F32), *FFN_SHAPES, ((LEN, D), F32)), dma(8), *vmem(*BF_SCRATCH), dma(16))
    points = Points({ENTER: (c[2], f[0]), (ATTEND, 2): (f[1], f[2]), KEY: (f[3], f[4], e[0], a[4], b[4]),
                     (TAPS, 1): (a[5], b[5]), TAPS: (e[1], e[2], c[3]), CAT: (e[3], e[4], l[0], a[6], b[6]),
                     LEAVE: (l[1], l[2]), LEAVE + 100: (l[3], l[4]), LEAVE + 200: (e[5], e[6]), END: (s[0], c[4])})
    pl.run_scoped(
        lambda *refs: attention_backward_body(0, length, split, d_resid, [], kept_in, log_total, ffn_small_out, weights,
                                              shared, d_input, small, points, *refs),
        *vmem(*KEPT_SHAPES[:9], *BA_SCRATCH), dma(24))
    store = moves.start(d_input, d_input_out)
    for step in (l[5], l[6], s[1], e[7], f[5], l[7], s[2], e[8], f[6], l[8], s[3], e[9], l[9], s[4], f[7], e[10], e[11]):
        step()
    for p in range(PARTS):
        own[p] = scatter.own(p)[...]
    for step in (l[10], l[11], e[12], l[12]):
        step()
    sends.finish()
    store.wait()


def last(gy, kept, ffn, resid, mids, small, w):
    ins = backward_ins(kept, w) + [(m, far()) for m in (gy, *ffn, resid)] + norm_params(w)
    ins += [(m, whole()) for m in (*mids, small)]
    outs = [(shape((LEN, D), F32), far()), (block_shape(16), far()), (shape((32, HALF), F32), whole()), (OWN, whole()), (GROUP, far()),
            (GROUP, far()), (SMALLS, whole()), (GROUP, far()), (GROUP, far()), (SMALLS, whole())]
    scratch = vmem(((LEN, D), F32), ((LEN, D), F32), ((SHARED_ROWS, HALF), BF), (MIDS.shape, BF), (MIDS.shape, BF))
    scratch += first_scratch(32) * 2 + second_scratch(32) * 4
    scratch += vmem((SMALLS.shape, BF)) + vmem((OWN.shape, BF), ((PARTS, 3, 4, 16, LANES), BF)) * 2 + scatter_scratch(16)
    return call(last_kernel, ins, outs, scratch + [dma(1), dma(336), dma(336)], "last", **remote(3))


def hand_out_kernel(early_0, late_0, early_1, late_1, small_0, small_1, ffn_0, ffn_1, *refs):
    (seg, w_query, b_query, w_key, w_value, b_value, w_depth, w_point, b_keyconv, w_kernel, b_kernel, w_conv, b_conv,
     w_out, b_out, first_gain, first_shift, w_up, b_up, w_down, b_down, second_gain, second_shift) = refs[:23]
    low, high, load_sems, store_sems = refs[23:]
    group = lax.axis_index("grp")
    place = my_row() - group * 64
    loads, stores = Moves(load_sems), Moves(store_sems)
    for layer in range(LAYERS):
        for n in range(8):
            rows = pl.ds(n * D, D)
            source = (early_0, late_0, early_1, late_1)[2 * layer + n // 4].at[pl.ds(n % 4 * D, D)]
            loads.start(source, low.at[layer, rows])
    for layer in range(LAYERS):
        for n in range(7):
            loads.all[layer * 8 + n].wait()

            @pl.loop(0, D // 256)
            def widen(c):
                high[layer * 7 + n, tile_rows(c, 256), :] = low[layer, tile_rows(c + 3 * n, 256), :].astype(F32)

            out = (w_out, w_out, w_key, w_value, w_query, w_conv, w_point)[n].at[layer]
            if n < 2:
                out = out.at[:, pl.ds(n * HALF, HALF)]
            stores.start(high.at[layer * 7 + n], out)
    smalls, taps = [], []
    for layer, ffn in enumerate((ffn_0, ffn_1)):
        loads.all[layer * 8 + 7].wait()
        taps.append(low[layer, TAPS_AT : TAPS_AT + 64, :].astype(F32))
        smalls.append((small_0, small_1)[layer][...].astype(F32))
        rows = jnp.concatenate([ffn[p].astype(F32) for p in range(PARTS)], axis=0)
        w_up[layer, 0] = rows[:24]
        w_down[layer, 0] = rows[24:]
        mine = jnp.sum(jnp.where(rows_iota(8, HALF) == group * 4 + place // 16,
                                 smalls[layer][SMALL_FFN + 10 : SMALL_FFN + 18], 0.0), axis=0, keepdims=True)
        mine = jnp.broadcast_to(mine, (8, HALF))
        b_up[layer] = pltpu.roll(mine, (HALF - (place % 16) * 24) % HALF, 1)[:1, :24]

    def both(start, n=1):
        return jnp.concatenate(
            [jnp.concatenate([s[start + k : start + k + 1] for k in range(n)], axis=1) for s in smalls], axis=0)

    for j in range(KERNEL):
        w_depth[j] = jnp.concatenate([both(SMALL_DEPTH + j), both(SMALL_DEPTH + 9 + j)], axis=1)
    for j in range(HEADS * KERNEL):
        w_kernel[j] = jnp.concatenate([t[j : j + 1] for t in taps], axis=0)
    for n, out in enumerate((second_gain, second_shift, b_down, first_gain, first_shift)):
        out[...] = both(SMALL_FFN + 2 * n, 2)
    for n, out in enumerate((b_query, b_value, b_keyconv, b_conv)):
        out[...] = both(SMALL_BIAS + n)
    b_kernel[...] = both(SMALL_BIAS + 4)[:, : HEADS * KERNEL]
    b_out[...] = both(SMALL_BIAS + 5, 2)
    for n in range(2):
        s = smalls[0][SMALL_SEG + 2 * n : SMALL_SEG + 2 * n + 2]
        seg[n : n + 1, :] = jnp.concatenate([s[0:1], s[1:2]], axis=1)
    wait_all(stores.all)


def hand_out(shared, small, ffn):
    proj, half_row, full_row = (LAYERS, D, HALF), (LAYERS, HALF), (LAYERS, D)
    shapes = [(2, D), proj, half_row, proj, proj, half_row, (KERNEL, LAYERS, D), proj, half_row,
              (HEADS * KERNEL, LAYERS, HALF), (LAYERS, HEADS * KERNEL), proj, half_row, (LAYERS, D, D), full_row,
              full_row, full_row, (LAYERS, 1, 24, HALF), (LAYERS, 1, 24), (LAYERS, 1, 24, HALF), full_row, full_row,
              full_row]
    big = (proj, (LAYERS, D, D))
    outs = list(call(
        hand_out_kernel,
        [(m, far()) for m in shared] + [(m, whole()) for m in (*small, *ffn)],
        [(shape(s, F32), far() if s in big else whole()) for s in shapes],
        [pltpu.VMEM((LAYERS, SHARED_ROWS, HALF), BF), pltpu.VMEM((14, D, HALF), F32), dma(16), dma(14)],
        "hand_out",
    ))
    outs[6] = jnp.swapaxes(outs[6], 0, 1)
    outs[9] = jnp.transpose(outs[9], (1, 2, 0))
    outs[17] = jnp.swapaxes(outs[17], 2, 3)
    return tuple(outs)


def shards(*args):
    w = Params(*args)
    w = w._replace(w_depth=jnp.swapaxes(w.w_depth, 0, 1), w_kernel=jnp.transpose(w.w_kernel, (2, 0, 1)))
    kept_0, kept_1, ffn, (output, d_resid, ffn_grads, small) = forward(w)
    grad, ffn_1, *mids, small = middle(d_resid, kept_1, small, ffn_grads, w)
    grad, _, _, ffn_0, early_1, late_1, small_1, early_0, late_0, small_0 = last(
        grad, kept_0, ffn, kept_0[9], mids, small, w)
    return (output, grad) + hand_out((early_0, late_0, early_1, late_1), (small_0, small_1), (ffn_0, ffn_1))


def solution(mesh):
    finer = Mesh(mesh.devices.reshape(mesh.shape["grp"], 4, 4, 2, 2), GRP_CH)
    rows, up = P(GRP_CH, None), P(None, "grp", None, CH)
    bias, down = P(None, "grp", CH), P(None, "grp", CH, None)
    placed = Params(*[P()] * len(Params._fields))._replace(
        hidden=rows, cotangent=rows, w_up=up, b_up=bias, down_weight=down)
    given = [P()] * 23
    given[17:20] = [up, bias, down]
    return jax.shard_map(
        shards,
        mesh=finer,
        in_specs=tuple(placed),
        out_specs=(rows, rows, *given),
        check_vma=False,
    )
```
